32 devices in a mesh: dp: 8 (over z, x), head: 4 (over y, core).
Axes of the slice: x: 2, y: 2, z: 4, core: 2. Of those that a mesh axis runs over, the one named last changes fastest.
Arguments:
- seg_large: int32 [8, 1536], P('dp'), may hold values from 0 to 9, never falling along the last dimension, each value on 1 to 197 neighbouring positions
- seg_small: int32 [8, 3584], P('dp'), may hold values from 0 to 9, never falling along the last dimension, each value on 1 to 401 neighbouring positions
- x_large: bfloat16 [8, 1536, 384], P('dp', 'head'), may hold values from -6 to 6
- x_small: bfloat16 [8, 3584, 192], P('dp', 'head'), may hold values from -6 to 6
- dy_large: bfloat16 [8, 1536, 384], P('dp', 'head'), may hold values from -6 to 6
- dy_small: bfloat16 [8, 3584, 192], P('dp', 'head'), may hold values from -6 to 6
- lb_norms: float32 [2, 2, 384], replicated, may hold values from -0.75 to 1.5, as said below
- lb_qkv: bfloat16 [384, 1152], replicated, may hold values from -0.3125 to 0.3125
- lb_out: bfloat16 [384, 384], replicated, may hold values from -4 to 4
- lb_up: bfloat16 [384, 1536], replicated, may hold values from -0.3125 to 0.3125
- lb_down: bfloat16 [1536, 384], replicated, may hold values from -0.15625 to 0.15625
- lb_bias: float32 [2, 384], replicated, may hold values from -1.2 to 1.2
- lb_upbias: float32 [1536], replicated, may hold values from -1.2 to 1.2
- sb_norms: float32 [2, 2, 192], replicated, may hold values from -0.75 to 1.5, as said below
- sb_qkv: bfloat16 [192, 576], replicated, may hold values from -0.4375 to 0.4375
- sb_out: bfloat16 [192, 192], replicated, may hold values from -4 to 4
- sb_up: bfloat16 [192, 768], replicated, may hold values from -0.4375 to 0.4375
- sb_down: bfloat16 [768, 192], replicated, may hold values from -0.21875 to 0.21875
- sb_bias: float32 [2, 192], replicated, may hold values from -1.2 to 1.2
- sb_upbias: float32 [768], replicated, may hold values from -1.2 to 1.2
- fl_norms: float32 [2, 768], replicated, may hold values from -0.75 to 1.5, as said below
- fl_proj: bfloat16 [384, 192], replicated, may hold values from -0.3125 to 0.3125
- fl_query: bfloat16 [192, 192], replicated, may hold values from -0.4375 to 0.4375
- fl_keyval: bfloat16 [192, 384], replicated, may hold values from -0.4375 to 0.4375
- fl_out: bfloat16 [192, 192], replicated, may hold values from -4 to 4
- fl_back: bfloat16 [192, 384], replicated, may hold values from -0.4375 to 0.4375
- fl_bias: float32 [768], replicated, may hold values from -1.2 to 1.2
- fs_norms: float32 [2, 960], replicated, may hold values from -0.75 to 1.5, as said below
- fs_proj: bfloat16 [192, 384], replicated, may hold values from -0.4375 to 0.4375
- fs_query: bfloat16 [384, 384], replicated, may hold values from -0.3125 to 0.3125
- fs_keyval: bfloat16 [384, 768], replicated, may hold values from -0.3125 to 0.3125
- fs_out: bfloat16 [384, 384], replicated, may hold values from -4 to 4
- fs_back: bfloat16 [384, 192], replicated, may hold values from -0.3125 to 0.3125
- fs_bias: float32 [960], replicated, may hold values from -1.2 to 1.2
Outputs:
- out_large: bfloat16 [8, 1536, 384], P('dp', 'head')
- out_small: bfloat16 [8, 3584, 192], P('dp', 'head')
- grad_x_large: bfloat16 [8, 1536, 384], P('dp', 'head')
- grad_x_small: bfloat16 [8, 3584, 192], P('dp', 'head')
- grad_lb_norms: float32 [2, 2, 384], replicated
- grad_lb_qkv: float32 [384, 1152], replicated
- grad_lb_out: float32 [384, 384], replicated
- grad_lb_up: float32 [384, 1536], replicated
- grad_lb_down: float32 [1536, 384], replicated
- grad_lb_bias: float32 [2, 384], replicated
- grad_lb_upbias: float32 [1536], replicated
- grad_sb_norms: float32 [2, 2, 192], replicated
- grad_sb_qkv: float32 [192, 576], replicated
- grad_sb_out: float32 [192, 192], replicated
- grad_sb_up: float32 [192, 768], replicated
- grad_sb_down: float32 [768, 192], replicated
- grad_sb_bias: float32 [2, 192], replicated
- grad_sb_upbias: float32 [768], replicated
- grad_fl_norms: float32 [2, 768], replicated
- grad_fl_proj: float32 [384, 192], replicated
- grad_fl_query: float32 [192, 192], replicated
- grad_fl_keyval: float32 [192, 384], replicated
- grad_fl_out: float32 [192, 192], replicated
- grad_fl_back: float32 [192, 384], replicated
- grad_fl_bias: float32 [768], replicated
- grad_fs_norms: float32 [2, 960], replicated
- grad_fs_proj: float32 [192, 384], replicated
- grad_fs_query: float32 [384, 384], replicated
- grad_fs_keyval: float32 [384, 768], replicated
- grad_fs_out: float32 [384, 384], replicated
- grad_fs_back: float32 [384, 192], replicated
- grad_fs_bias: float32 [960], replicated
The draws below stay inside these ranges and needn't reach their ends.
Inputs may be any that keep to these rules, and one draw needn't show every extreme that they name: `seg_large`: per sequence the image numbers of its patches never fall, every one of the 10 images has 1 to 197 patches and one has exactly 197; an image's first patch is its class token. `seg_small`: per sequence the image numbers of its patches never fall, every one of the 10 images has 1 to 401 patches and one has exactly 401; an image's first patch is its class token. `lb_norms`: index 0 of the second dimension holds gains, index 1 shifts. `sb_norms`: index 0 of the second dimension holds gains, index 1 shifts. `fl_norms`: row 0 gains, row 1 shifts. `fs_norms`: row 0 gains, row 1 shifts.
All inputs are finite; a program needn't handle non-finite values.
Results may differ from the reference program's by a relative error of at most 0.029.
Values may be sent and summed in bfloat16 or wider, within the bound.
No kernel may reach another device: no remote copies, remote signals or barrier semaphores. Data moves between devices by JAX's collectives and lax.ppermute only.
A program may use at most 192 MiB of HBM per device.

```python
import math
import jax
import jax.numpy as jnp
import numpy as np
from jax import lax

DL = 384
DS = 192
HEADS = 6
FL = 1536
FS = 768
IMGS = 10
TOK_L = 1536
TOK_S = 3584
MOST_L = 197
MOST_S = 401
SEQS = 8


def bell_pair(gain_key, shift_key, shape):
    gains = 1.0 + 0.2 * jax.random.truncated_normal(gain_key, -2.5, 2.5, shape, jnp.float32)
    shifts = 0.3 * jax.random.truncated_normal(shift_key, -2.5, 2.5, shape, jnp.float32)
    return (gains, shifts)


def draw_lb_norms(key, part):
    key = jax.random.fold_in(key, 11)
    gain_key, shift_key = jax.random.split(key)
    gains, shifts = bell_pair(gain_key, shift_key, (2, DL))
    return jnp.stack([gains, shifts], axis=1)


def draw_sb_norms(key, part):
    key = jax.random.fold_in(key, 12)
    gain_key, shift_key = jax.random.split(key)
    gains, shifts = bell_pair(gain_key, shift_key, (2, DS))
    return jnp.stack([gains, shifts], axis=1)


def draw_fl_norms(key, part):
    key = jax.random.fold_in(key, 13)
    gain_key, shift_key = jax.random.split(key)
    gains, shifts = bell_pair(gain_key, shift_key, (DL + 2 * DS,))
    return jnp.stack([gains, shifts], axis=0)


def draw_fs_norms(key, part):
    key = jax.random.fold_in(key, 14)
    gain_key, shift_key = jax.random.split(key)
    gains, shifts = bell_pair(gain_key, shift_key, (DS + 2 * DL,))
    return jnp.stack([gains, shifts], axis=0)


def block_levels(rng, dims, shards, smallest, top_value):
    level = 1.0
    for position, shards_of in shards:
        heights = jax.random.uniform(jax.random.fold_in(jax.random.fold_in(rng, 6), position), (shards_of,), jnp.float32, smallest / len(shards), top_value / len(shards))
        level = level * jnp.repeat(jnp.exp(heights), dims[position] // shards_of).reshape((-1,) + (1,) * (len(dims) - 1 - position))
    return level


def length_profile(amount, total, bound, lean):
    loads = [(1 << 20) // math.isqrt(grade ** lean) + 1 for grade in range(2, amount + 1)]
    surplus, holding = total - bound - (amount - 1), [1] * (amount - 1)
    while surplus > 0:
        free = [i for i in range(amount - 1) if holding[i] < bound]
        mass, left = sum([loads[i] for i in free]), surplus
        for i in free:
            more = min(bound - holding[i], max(1, left * loads[i] // mass), surplus)
            holding[i] = holding[i] + more
            surplus = surplus - more
    return np.array([bound] + holding)


def uneven_parts(own_key, amount, total, reach, lean):
    if amount == 2:
        one = jax.random.randint(own_key, (), max(1, total - reach), min(reach, total - 1) + 1)
        return jnp.stack([one, total - one])
    tallies = jnp.asarray(length_profile(amount, total, reach, lean), jnp.int32)
    twos = (amount - 1) // 2
    giver, sink = tallies[1:1 + 2 * twos:2], tallies[2:2 + 2 * twos:2]
    room = jnp.minimum(giver - 1, reach - sink)
    moved = jax.random.randint(jax.random.fold_in(own_key, 1), (twos,), 0, 1 << 20) % (room + 1)
    tallies = tallies.at[1:1 + 2 * twos:2].set(giver - moved).at[2:2 + 2 * twos:2].set(sink + moved)
    return tallies[jax.random.permutation(jax.random.fold_in(own_key, 2), amount)]


def centred(rng, dims, scale, most, shards=(), kind=jnp.bfloat16):
    loudness = block_levels(rng, dims, shards, -0.22, 0.18) if shards else 1.0
    drawn = jax.random.normal(rng, dims, jnp.float32) * scale * loudness
    return jnp.minimum(jnp.maximum(drawn, -most), most).astype(kind)


def setup_inputs(seed: int = 0) -> dict:
    keys = jax.random.split(jax.random.key(seed), 35)
    return {
        "seg_large": jax.vmap(lambda own: jnp.searchsorted(jnp.cumsum(uneven_parts(own, IMGS, TOK_L, MOST_L, 1)), jnp.arange(TOK_L), side="right"))(jax.random.split(keys[0], SEQS)).reshape((SEQS, TOK_L)).astype(jnp.int32),
        "seg_small": jax.vmap(lambda own: jnp.searchsorted(jnp.cumsum(uneven_parts(own, IMGS, TOK_S, MOST_S, 1)), jnp.arange(TOK_S), side="right"))(jax.random.split(keys[1], SEQS)).reshape((SEQS, TOK_S)).astype(jnp.int32),
        "x_large": centred(keys[2], (SEQS, TOK_L, DL), 1.0, 6.0, ((0, 8), (1, 4))),
        "x_small": centred(keys[3], (SEQS, TOK_S, DS), 1.0, 6.0, ((0, 8), (1, 4))),
        "dy_large": centred(keys[4], (SEQS, TOK_L, DL), 1.0, 6.0, ((0, 8), (1, 4))),
        "dy_small": centred(keys[5], (SEQS, TOK_S, DS), 1.0, 6.0, ((0, 8), (1, 4))),
        "lb_norms": draw_lb_norms(jax.random.fold_in(keys[34], 71), 0),
        "lb_qkv": centred(keys[7], (DL, 3 * DL), DL ** -0.5, 0.3125),
        "lb_out": centred(keys[8], (DL, DL), 2 ** -0.5, 4.0),
        "lb_up": centred(keys[9], (DL, FL), DL ** -0.5, 0.3125),
        "lb_down": centred(keys[10], (FL, DL), FL ** -0.5, 0.15625),
        "lb_bias": centred(keys[11], (2, DL), 0.3, 1.2, (), jnp.float32),
        "lb_upbias": centred(keys[12], (FL,), 0.3, 1.2, (), jnp.float32),
        "sb_norms": draw_sb_norms(jax.random.fold_in(keys[34], 71), 0),
        "sb_qkv": centred(keys[14], (DS, 3 * DS), DS ** -0.5, 0.4375),
        "sb_out": centred(keys[15], (DS, DS), 2 ** -0.5, 4.0),
        "sb_up": centred(keys[16], (DS, FS), DS ** -0.5, 0.4375),
        "sb_down": centred(keys[17], (FS, DS), FS ** -0.5, 0.21875),
        "sb_bias": centred(keys[18], (2, DS), 0.3, 1.2, (), jnp.float32),
        "sb_upbias": centred(keys[19], (FS,), 0.3, 1.2, (), jnp.float32),
        "fl_norms": draw_fl_norms(jax.random.fold_in(keys[34], 71), 0),
        "fl_proj": centred(keys[21], (DL, DS), DL ** -0.5, 0.3125),
        "fl_query": centred(keys[22], (DS, DS), DS ** -0.5, 0.4375),
        "fl_keyval": centred(keys[23], (DS, 2 * DS), DS ** -0.5, 0.4375),
        "fl_out": centred(keys[24], (DS, DS), 2 ** -0.5, 4.0),
        "fl_back": centred(keys[25], (DS, DL), DS ** -0.5, 0.4375),
        "fl_bias": centred(keys[26], (2 * DS + DL,), 0.3, 1.2, (), jnp.float32),
        "fs_norms": draw_fs_norms(jax.random.fold_in(keys[34], 71), 0),
        "fs_proj": centred(keys[28], (DS, DL), DS ** -0.5, 0.4375),
        "fs_query": centred(keys[29], (DL, DL), DL ** -0.5, 0.3125),
        "fs_keyval": centred(keys[30], (DL, 2 * DL), DL ** -0.5, 0.3125),
        "fs_out": centred(keys[31], (DL, DL), 2 ** -0.5, 4.0),
        "fs_back": centred(keys[32], (DL, DS), DL ** -0.5, 0.3125),
        "fs_bias": centred(keys[33], (2 * DL + DS,), 0.3, 1.2, (), jnp.float32),
    }


@jax.custom_vjp
def low(v):
    return lax.optimization_barrier(v.astype(jnp.bfloat16)).astype(jnp.float32)

@jax.custom_vjp
def low_back(v):
    return v

def low_keep(v):
    return (low(v), None)

def low_pass(kept, grad):
    return (grad,)

def back_keep(v):
    return (v, None)

def back_low(kept, grad):
    return (low(grad),)
low.defvjp(low_keep, low_pass)
low_back.defvjp(back_keep, back_low)
NORM_EPS = 1e-06
EXACT_PRECISION = lax.Precision.HIGHEST

def matmul(left, right):
    return jnp.dot(left, right, precision=EXACT_PRECISION)

def layer_norm(inputs, gain, shift):
    center = inputs - lax.optimization_barrier(jnp.mean(inputs, axis=-1, keepdims=True))
    spread = lax.optimization_barrier(jnp.mean(center * center, axis=-1, keepdims=True))
    return center * lax.rsqrt(spread + NORM_EPS) * gain + shift

def gelu_exact(inputs):
    return jax.nn.gelu(inputs, approximate=False)

def class_tokens(segment):
    segment = segment.astype(jnp.int32)
    shifted = jnp.concatenate([jnp.full((1,), -1, jnp.int32), segment[:-1]])
    is_first = segment != shifted
    images = jnp.arange(IMGS, dtype=jnp.int32)
    choose = jnp.logical_and(images[:, None] == segment[None, :], is_first[None, :])
    return (is_first, choose.astype(jnp.float32))

def softmax_rows(scores):
    maximum = lax.optimization_barrier(jnp.max(scores, axis=-1, keepdims=True))
    exp_terms = jnp.exp(scores - maximum)
    return exp_terms / lax.optimization_barrier(jnp.sum(exp_terms, axis=-1, keepdims=True))

def branch_block(inputs, segment, norm_params, w_qkv, w_out, w_up, w_down, bias_rows, up_bias):
    total_rows, model_width = inputs.shape
    head_dimension_width = model_width // HEADS
    normed = low(layer_norm(inputs, norm_params[0, 0], norm_params[0, 1]))
    projected = low_back(low(matmul(normed, w_qkv))).reshape(total_rows, 3, HEADS, head_dimension_width)
    scores = jnp.einsum('qhe,khe->hqk', projected[:, 0], projected[:, 1], precision=EXACT_PRECISION) * head_dimension_width ** (-0.5)
    scores = low_back(scores)
    scores = jnp.where((segment[:, None] == segment[None, :])[None], scores, -1e+30)
    attn_probs = low(softmax_rows(scores))
    heads_out = jnp.einsum('hqk,khe->qhe', attn_probs, projected[:, 2], precision=EXACT_PRECISION)
    heads_out = low_back(low(heads_out)).reshape(total_rows, model_width)
    mid_sum = inputs + low_back(matmul(heads_out, w_out) + bias_rows[0])
    normed_two = low(layer_norm(mid_sum, norm_params[1, 0], norm_params[1, 1]))
    hidden_act = low(gelu_exact(low_back(matmul(normed_two, w_up) + up_bias)))
    return low_back(low(mid_sum + matmul(hidden_act, w_down) + bias_rows[1]))

def cross_attend(a_rows, b_rows, seg_a, seg_b, norm_params, w_proj, w_query, w_keyval, w_out, w_back, bias_all):
    width_a = a_rows.shape[1]
    total_b, second_branch_width = b_rows.shape
    head_dimension_width = second_branch_width // HEADS
    score_scale = head_dimension_width ** (-0.5)
    is_first, choose = class_tokens(seg_a)
    first_b, _ = class_tokens(seg_b)
    lifted = layer_norm(matmul(choose, a_rows), norm_params[0, :width_a], norm_params[1, :width_a])
    moved_cls = matmul(low(gelu_exact(lifted)), w_proj) + bias_all[:second_branch_width]
    gain_b = norm_params[0, width_a:width_a + second_branch_width]
    shift_b = norm_params[1, width_a:width_a + second_branch_width]
    query_in = low(layer_norm(moved_cls, gain_b, shift_b))
    key_in = low(layer_norm(b_rows, gain_b, shift_b))
    queries = low_back(low(matmul(query_in, w_query))).reshape(IMGS, HEADS, head_dimension_width)
    self_pairs = low_back(low(matmul(query_in, w_keyval))).reshape(IMGS, 2, HEADS, head_dimension_width)
    key_values = low_back(low(matmul(key_in, w_keyval))).reshape(total_b, 2, HEADS, head_dimension_width)
    self_scores = jnp.einsum('qhe,qhe->hq', queries, self_pairs[:, 0], precision=EXACT_PRECISION) * score_scale
    patch_scores = jnp.einsum('qhe,khe->hqk', queries, key_values[:, 0], precision=EXACT_PRECISION) * score_scale
    scores = low_back(jnp.concatenate([self_scores[:, :, None], patch_scores], axis=2))
    images = jnp.arange(IMGS, dtype=jnp.int32)
    allowed = jnp.logical_and(images[:, None] == seg_b.astype(jnp.int32)[None, :], jnp.logical_not(first_b)[None, :])
    allowed = jnp.concatenate([jnp.ones((IMGS, 1), dtype=bool), allowed], axis=1)
    scores = jnp.where(allowed[None], scores, -1e+30)
    attn_probs = low(softmax_rows(scores))
    heads_out = jnp.transpose(attn_probs[:, :, 0])[:, :, None] * self_pairs[:, 1]
    heads_out = heads_out + jnp.einsum('hqk,khe->qhe', attn_probs[:, :, 1:], key_values[:, 1], precision=EXACT_PRECISION)
    heads_out = low_back(low(heads_out)).reshape(IMGS, second_branch_width)
    joined = moved_cls + low_back(matmul(heads_out, w_out) + bias_all[second_branch_width:2 * second_branch_width])
    reverted = layer_norm(joined, norm_params[0, width_a + second_branch_width:], norm_params[1, width_a + second_branch_width:])
    back_cls = matmul(low(gelu_exact(reverted)), w_back) + bias_all[2 * second_branch_width:]
    return jnp.where(is_first[:, None], matmul(choose.T, back_cls), a_rows)

def reference(seg_large, seg_small, x_large, x_small, dy_large, dy_small, lb_norms, lb_qkv, lb_out, lb_up, lb_down, lb_bias, lb_upbias, sb_norms, sb_qkv, sb_out, sb_up, sb_down, sb_bias, sb_upbias, fl_norms, fl_proj, fl_query, fl_keyval, fl_out, fl_back, fl_bias, fs_norms, fs_proj, fs_query, fs_keyval, fs_out, fs_back, fs_bias):
    params = tuple((item.astype(jnp.float32) for item in (lb_norms, lb_qkv, lb_out, lb_up, lb_down, lb_bias, lb_upbias, sb_norms, sb_qkv, sb_out, sb_up, sb_down, sb_bias, sb_upbias, fl_norms, fl_proj, fl_query, fl_keyval, fl_out, fl_back, fl_bias, fs_norms, fs_proj, fs_query, fs_keyval, fs_out, fs_back, fs_bias)))

    def forward(weights, large_in, small_in):

        def one_sequence(running, block_items):
            large_x, small_x, large_seg, small_seg = block_items
            large_y = branch_block(large_x, large_seg, weights[0], weights[1], weights[2], weights[3], weights[4], weights[5], weights[6])
            small_y = branch_block(small_x, small_seg, weights[7], weights[8], weights[9], weights[10], weights[11], weights[12], weights[13])
            large_out = cross_attend(large_y, small_y, large_seg, small_seg, weights[14], weights[15], weights[16], weights[17], weights[18], weights[19], weights[20])
            small_out = cross_attend(small_y, large_y, small_seg, large_seg, weights[21], weights[22], weights[23], weights[24], weights[25], weights[26], weights[27])
            return (running, (large_out, small_out))
        _, results = lax.scan(jax.checkpoint(one_sequence), jnp.zeros((), jnp.float32), (large_in, small_in, seg_large, seg_small))
        return results
    results, pullback = jax.vjp(forward, params, x_large.astype(jnp.float32), x_small.astype(jnp.float32))
    grad_params, grad_large, grad_small = pullback((dy_large.astype(jnp.float32), dy_small.astype(jnp.float32)))
    return (results[0].astype(jnp.bfloat16), results[1].astype(jnp.bfloat16), grad_large.astype(jnp.bfloat16), grad_small.astype(jnp.bfloat16), grad_params[0], grad_params[1], grad_params[2], grad_params[3], grad_params[4], grad_params[5], grad_params[6], grad_params[7], grad_params[8], grad_params[9], grad_params[10], grad_params[11], grad_params[12], grad_params[13], grad_params[14], grad_params[15], grad_params[16], grad_params[17], grad_params[18], grad_params[19], grad_params[20], grad_params[21], grad_params[22], grad_params[23], grad_params[24], grad_params[25], grad_params[26], grad_params[27])
```

```python
import functools
import math

import jax
import jax.numpy as jnp
from jax import lax
from jax.experimental import pallas as pl
from jax.experimental.pallas import tpu as pltpu
from jax.sharding import PartitionSpec as P

HEADS = 6
IMGS = 10
ROWS = 16
MOST_L = 197
MOST_S = 401
EPS = 1e-6
NEG = -1e30
LOG2E = math.log2(math.e)
F32 = jnp.float32
BF16 = jnp.bfloat16
VMEM = pl.BlockSpec(memory_space=pltpu.VMEM)
SMEM = pl.BlockSpec(memory_space=pltpu.SMEM)
ANY = pl.BlockSpec(memory_space=pl.ANY)


def round_up(value, unit):
    return -(-value // unit) * unit


class Branch:
    def __init__(self, rows, width, hidden, most):
        self.n = rows
        self.w = width
        self.f = hidden
        self.dh = width // HEADS
        self.halo = round_up(most - 1, 16)
        self.kw = self.halo + 16
        self.r = rows + 2 * self.halo
        self.t = rows // 128
        self.scale = self.dh ** (-0.5)
        self.turned = width % 128 != 0
        if width % 128 == 0:
            per = 128 // self.dh
            self.groups = [
                (i * 128, (i + 1) * 128, list(range(i * per, (i + 1) * per)))
                for i in range(width // 128)
            ]
        else:
            self.groups = [(0, width, list(range(HEADS)))]


def nn(a, b):
    return jnp.dot(a, b, preferred_element_type=F32)


def nt(a, b):
    return lax.dot_general(a, b, (((1,), (1,)), ((), ())), preferred_element_type=F32)


def tn(a, b):
    return lax.dot_general(a, b, (((0,), (0,)), ((), ())), preferred_element_type=F32)


def split(x):
    high = x.astype(BF16)
    return high, (x - high.astype(F32)).astype(BF16)


def nn_exact(a, b):
    return jnp.dot(a, b, preferred_element_type=F32, precision=lax.Precision.HIGHEST)


def nt_exact(a, b):
    return lax.dot_general(
        a,
        b,
        (((1,), (1,)), ((), ())),
        preferred_element_type=F32,
        precision=lax.Precision.HIGHEST,
    )


def normalize(x):
    center = x - jnp.mean(x, axis=-1, keepdims=True)
    rstd = lax.rsqrt(jnp.mean(center * center, axis=-1, keepdims=True) + EPS)
    return center * rstd, rstd


def norm_grad(unit, rstd, gain, upstream):
    scaled = upstream * gain
    mean_one = jnp.mean(scaled, axis=-1, keepdims=True)
    mean_two = jnp.mean(scaled * unit, axis=-1, keepdims=True)
    return (scaled - mean_one - unit * mean_two) * rstd


def col_sum(x):
    return jnp.sum(x, axis=0, keepdims=True)


def gelu_pair(x):
    cumulative = 0.5 * (1.0 + lax.erf(x * 0.7071067811865476))
    density = jnp.exp(-0.5 * x * x) * 0.3989422804014327
    return x * cumulative, cumulative + x * density


def iota(shape, dim):
    return lax.broadcasted_iota(jnp.int32, shape, dim)


def call(kernel, outs, ins, in_specs=None, scratch=(), flops=0, moved=0, out_specs=None):
    return pl.pallas_call(
        kernel,
        out_shape=outs,
        in_specs=[VMEM] * len(ins) if in_specs is None else in_specs,
        out_specs=jax.tree.map(lambda _: VMEM, outs) if out_specs is None else out_specs,
        scratch_shapes=list(scratch),
        compiler_params=pltpu.CompilerParams(vmem_limit_bytes=56 * 1024 * 1024),
        cost_estimate=pl.CostEstimate(flops=flops, bytes_accessed=moved, transcendentals=0),
    )(*ins)


def sds(shape, dtype):
    return jax.ShapeDtypeStruct(shape, dtype)


def mat_rows(rows, cols):
    return rows * cols // 128


def vec_rows(widths):
    return round_up(sum(round_up(w, 128) // 128 for w in widths), 16)


def layout(items, unit=32):
    at, row = {}, 0
    for name, rows in items:
        at[name] = row
        row += rows
    return at, round_up(row, unit)


def pack_mat(ref, at, rows, cols, value):
    low = value.astype(BF16)
    full = cols // 128
    for i in range(full):
        ref[at + i * rows : at + (i + 1) * rows, :] = low[:, i * 128 : (i + 1) * 128]
    if cols % 128:
        tail = low[:, full * 128 :]
        at = at + full * rows
        half = rows // 2
        ref[at : at + half, :] = jnp.concatenate([tail[:half], tail[half:]], axis=1)


def unpack_mat(ref, at, rows, cols, out):
    full = cols // 128
    for i in range(full):
        out[:, i * 128 : (i + 1) * 128] = ref[at + i * rows : at + (i + 1) * rows, :].astype(F32)
    if cols % 128:
        at = at + full * rows
        half = rows // 2
        block = ref[at : at + half, :].astype(F32)
        out[:half, full * 128 :] = block[:, :64]
        out[half:, full * 128 :] = block[:, 64:]


def vec_block(values):
    pieces = []
    for value in values:
        width = value.shape[1]
        for i in range(0, width, 128):
            piece = value[:, i : min(i + 128, width)]
            if piece.shape[1] < 128:
                piece = jnp.concatenate(
                    [piece, jnp.zeros((1, 128 - piece.shape[1]), F32)], axis=1
                )
            pieces.append(piece)
    total = round_up(len(pieces), 16)
    if total > len(pieces):
        pieces.append(jnp.zeros((total - len(pieces), 128), F32))
    return jnp.concatenate(pieces, axis=0)


def vecs_of(block, widths):
    out, i = [], 0
    for width in widths:
        parts = []
        for j in range(0, width, 128):
            parts.append(block[i : i + 1, : min(128, width - j)])
            i += 1
        out.append(parts[0] if len(parts) == 1 else jnp.concatenate(parts, axis=1))
    return out


def emit(src_ref, outs, index, sems):
    size = src_ref.shape[0] // len(outs)
    copies = []
    for d, out in enumerate(outs):
        at = pl.multiple_of((index ^ d) * size, 16)
        copies.append(pltpu.make_async_copy(src_ref.at[pl.ds(at, size)], out, sems.at[d]))
        copies[-1].start()
    for copy in copies:
        copy.wait()


def start_kernel(
    br_l,
    br_s,
    here_ref,
    seg_l_ref,
    seg_s_ref,
    xl_ref,
    xs_ref,
    dyl_ref,
    dys_ref,
    nl_ref,
    ns_ref,
    wl_ref,
    ws_ref,
    ql_ref,
    kl_ref,
    vl_ref,
    qs_ref,
    ks_ref,
    vs_ref,
    meta_l_ref,
    meta_s_ref,
    lane_l_ref,
    lane_s_ref,
    sub_l_ref,
    sub_s_ref,
    dcls_ref,
    vector_ref,
    scalar_ref,
    sem,
):
    col = 0
    dcls_ref[...] = jnp.zeros_like(dcls_ref)
    for br, seg_ref, dy_ref, meta_ref, lane_ref, sub_ref in (
        (br_l, seg_l_ref, dyl_ref, meta_l_ref, lane_l_ref, sub_l_ref),
        (br_s, seg_s_ref, dys_ref, meta_s_ref, lane_s_ref, sub_s_ref),
    ):
        own = here_ref[0] * br.n
        seg = seg_ref[...]
        image = iota((ROWS, seg.shape[1]), 0)
        starts = jnp.sum((seg < image).astype(jnp.int32), axis=1, keepdims=True)
        ends = jnp.sum((seg <= image).astype(jnp.int32), axis=1, keepdims=True)
        starts = jnp.broadcast_to(starts, (ROWS, 128))
        ends = jnp.broadcast_to(ends, (ROWS, 128))
        lane = iota((ROWS, 128), 1)
        diagonal = (lane - (lane // ROWS) * ROWS) == iota((ROWS, 128), 0)
        lo = jnp.sum(jnp.where(diagonal, starts, 0), axis=0, keepdims=True) - own
        hi = jnp.sum(jnp.where(diagonal, ends, 0), axis=0, keepdims=True) - own
        lane_ref[...] = jnp.concatenate([lo, hi, jnp.zeros((6, 128), jnp.int32)], axis=0)
        sub_ref[...] = starts - own
        real = iota((ROWS, 128), 0) < IMGS
        first = jnp.sum(jnp.where(real & (starts <= own), 1, 0), axis=0, keepdims=True) - 1
        last = jnp.sum(jnp.where(real & (starts < own + br.n), 1, 0), axis=0, keepdims=True) - 1
        vector_ref[0:ROWS, :] = starts
        vector_ref[ROWS : ROWS + 8, :] = jnp.concatenate(
            [first, last, jnp.zeros((6, 128), jnp.int32)], axis=0
        )
        copy = pltpu.make_async_copy(vector_ref, scalar_ref, sem)
        copy.start()
        copy.wait()
        for j in range(IMGS + 1):
            meta_ref[j] = scalar_ref[j, 0]
        meta_ref[11] = own
        meta_ref[12] = scalar_ref[ROWS, 0]
        meta_ref[13] = scalar_ref[ROWS + 1, 0]
        meta_ref[14] = 0
        meta_ref[15] = 0
        pick = (iota((ROWS, br.n), 1) == (starts - own)[:, 0:1]).astype(F32).astype(BF16)
        dcls_ref[:, col : col + br.w] = nn(pick, dy_ref[...])
        col += br.w
    for x_ref, norms_ref, w_ref, outs in (
        (xl_ref, nl_ref, wl_ref, (ql_ref, kl_ref, vl_ref)),
        (xs_ref, ns_ref, ws_ref, (qs_ref, ks_ref, vs_ref)),
    ):
        width = x_ref.shape[1]
        unit, _ = normalize(x_ref[...].astype(F32))
        normed = (unit * norms_ref[0, 0:1, :] + norms_ref[0, 1:2, :]).astype(BF16)
        for i, ref in enumerate(outs):
            ref[...] = nn(normed, w_ref[:, i * width : (i + 1) * width]).astype(BF16)


def head_mask(br, head, c0, c1):
    lane = iota((1, c1 - c0), 1) + c0
    return jnp.logical_and(lane >= head * br.dh, lane < (head + 1) * br.dh)


def stack_heads(br, rows, group):
    c0, c1, heads = group
    part = rows[:, c0:c1]
    zero = jnp.zeros_like(part)
    return jnp.concatenate(
        [jnp.where(head_mask(br, h, c0, c1), part, zero) for h in heads], axis=0
    )


def image_span(br, meta_ref, j):
    base = meta_ref[11]
    lo = meta_ref[j] - base
    hi = meta_ref[j + 1] - base
    k0 = pl.multiple_of(((lo + br.halo) // 16) * 16, 16)
    t0 = jnp.maximum(lo, 0) // 128
    t1 = (jnp.minimum(hi, br.n) + 127) // 128
    return lo, hi, k0, t0, t1


def forward_kernel(
    br,
    meta_ref,
    x_ref,
    xl_ref,
    xr_ref,
    q_ref,
    k_ref,
    v_ref,
    norms_ref,
    wqkv_ref,
    wout_ref,
    wup_ref,
    wdown_ref,
    bias_ref,
    upbias_ref,
    sub_ref,
    y_ref,
    cls_ref,
    kwin_ref,
    vwin_ref,
    lse_ref,
    ho_ref,
    mid_ref,
    n2_ref,
    hid_ref,
    slope_ref,
    ot_ref,
):
    n, w, f, dh, halo = br.n, br.w, br.f, br.dh, br.halo
    for ref, at in ((xl_ref, 0), (xr_ref, halo + n)):
        unit, _ = normalize(ref[...].astype(F32))
        normed = (unit * norms_ref[0, 0:1, :] + norms_ref[0, 1:2, :]).astype(BF16)
        kwin_ref[at : at + halo, :] = nn(normed, wqkv_ref[:, w : 2 * w]).astype(BF16)
        vwin_ref[at : at + halo, :] = nn(normed, wqkv_ref[:, 2 * w :]).astype(BF16)
    kwin_ref[halo : halo + n, :] = k_ref[...]
    vwin_ref[halo : halo + n, :] = v_ref[...]
    ot_ref[...] = jnp.zeros_like(ot_ref)
    lse_ref[...] = jnp.zeros_like(lse_ref)
    factor = br.scale * LOG2E

    def image(j, carry):
        lo, hi, k0, t0, t1 = image_span(br, meta_ref, j)
        keys = kwin_ref[pl.ds(k0, br.kw), :]
        values_t = vwin_ref[pl.ds(k0, br.kw), :].T
        row = iota((br.kw, 128), 0) + (k0 - br.halo)
        mask = jnp.logical_and(row >= lo, row < hi)

        def tile(t, carry):
            rows = q_ref[pl.ds(pl.multiple_of(t * 128, 128), 128), :]
            lane = iota((1, 128), 1) + t * 128
            inside = jnp.logical_and(lane >= lo, lane < hi)
            for group in br.groups:
                c0, c1, heads = group
                scores = nt(keys[:, c0:c1], stack_heads(br, rows, group))
                for i, h in enumerate(heads):
                    s = jnp.where(mask, scores[:, i * 128 : (i + 1) * 128] * factor, NEG)
                    top = jnp.max(s, axis=0, keepdims=True)
                    p = jnp.exp2(s - top)
                    total = col_sum(p)
                    o = nn(values_t[h * dh : (h + 1) * dh, :], p.astype(BF16))
                    ot_ref[t, h * dh : (h + 1) * dh, :] += o * jnp.where(inside, 1.0 / total, 0.0)
                    lse_ref[t, h : h + 1, :] = jnp.where(
                        inside, top + jnp.log2(total), lse_ref[t, h : h + 1, :]
                    )
            return carry

        return lax.fori_loop(t0, t1, tile, carry)

    lax.fori_loop(meta_ref[12], meta_ref[13] + 1, image, 0)
    for t in range(br.t):
        ho_ref[t * 128 : (t + 1) * 128, :] = ot_ref[t].T.astype(BF16)
    mid = x_ref[...].astype(F32) + (nn(ho_ref[...], wout_ref[...]) + bias_ref[0:1, :])
    mid_ref[...] = mid
    unit, _ = normalize(mid)
    normed = (unit * norms_ref[1, 0:1, :] + norms_ref[1, 1:2, :]).astype(BF16)
    n2_ref[...] = normed
    total = mid + bias_ref[1:2, :]
    step = 256
    upbias = upbias_ref[...].reshape(1, f)
    for c in range(0, f, step):
        pre = nn(normed, wup_ref[:, c : c + step]) + upbias[:, c : c + step]
        act, slope = gelu_pair(pre)
        act = act.astype(BF16)
        hid_ref[:, c : c + step] = act
        slope_ref[:, c : c + step] = slope.astype(BF16)
        if br.turned:
            total = total + nt(act, wdown_ref[:, c : c + step])
        else:
            total = total + nn(act, wdown_ref[c : c + step, :])
    y = total.astype(BF16)
    y_ref[...] = y
    pick = (iota((ROWS, n), 1) == sub_ref[:, 0:1]).astype(F32).astype(BF16)
    cls_ref[...] = nn(pick, y)


def ffn_back_kernel(
    br,
    at,
    index_ref,
    lane_ref,
    dy_ref,
    cross_ref,
    dcls_ref,
    hid_ref,
    slope_ref,
    n2_ref,
    mid_ref,
    ho_ref,
    norms_ref,
    wout_ref,
    wup_ref,
    wdown_ref,
    keep_ref,
    send_ref,
    dmid_ref,
    dheads_ref,
    vec_ref,
    pack_ref,
    sems,
):
    n, w, f = br.n, br.w, br.f
    c0 = at["col"]
    cls = dcls_ref[:, c0 : c0 + w].astype(BF16)
    hit = (iota((n, 128), 0) == lane_ref[0:1, :]).astype(F32)
    hit = jnp.where(iota((1, 128), 1) < IMGS, hit, 0.0)
    first = jnp.sum(hit, axis=1, keepdims=True) > 0.5
    placed = nn(hit[:, :ROWS].astype(BF16), cls)
    gy = jnp.where(first, placed, dy_ref[...].astype(F32) + cross_ref[...]).astype(BF16)
    gy_float = gy.astype(F32)
    dn2 = jnp.zeros((n, w), F32)
    step = 256
    upbias = []
    normed = n2_ref[...]
    if br.turned:
        gy_t = gy.T
    normed_t = normed.T
    if at["rows"] > at["end"]:
        pack_ref[at["end"] :, :] = jnp.zeros((at["rows"] - at["end"], 128), BF16)
    for i, c in enumerate(range(0, f, step)):
        if br.turned:
            dpre = nn(gy, wdown_ref[:, c : c + step])
        else:
            dpre = nt(gy, wdown_ref[c : c + step, :])
        dpre = (dpre * slope_ref[:, c : c + step].astype(F32)).astype(BF16)
        upbias.append(col_sum(dpre.astype(F32)))
        pack_mat(pack_ref, at["up"] + i * mat_rows(w, step), w, step, nn(normed_t, dpre))
        dn2 = dn2 + nt(dpre, wup_ref[:, c : c + step])
        if br.turned:
            down = nn(gy_t, hid_ref[:, c : c + step])
            pack_mat(pack_ref, at["down"] + i * mat_rows(w, step), w, step, down)
        else:
            down = tn(hid_ref[:, c : c + step], gy)
            for k in range(w // 128):
                a = at["down"] + k * f + c
                pack_ref[a : a + step, :] = down[:, k * 128 : (k + 1) * 128].astype(BF16)
    unit, rstd = normalize(mid_ref[...])
    dmid = gy_float + norm_grad(unit, rstd, norms_ref[1, 0:1, :], dn2)
    dmid_ref[...] = dmid
    dattn = dmid.astype(BF16)
    pack_mat(pack_ref, at["out"], w, w, tn(ho_ref[...], dattn))
    dheads_ref[...] = nt(dattn, wout_ref[...]).astype(BF16)
    vec_ref[...] = vec_block(
        [col_sum(dn2 * unit), col_sum(dn2), col_sum(dattn.astype(F32)), col_sum(gy_float)] + upbias
    )
    emit(pack_ref, (keep_ref, send_ref), index_ref[0], sems)


def attn_back_kernel(
    br,
    at,
    meta_ref,
    index_ref,
    q_ref,
    kwin_ref,
    vwin_ref,
    dheads_ref,
    lse_ref,
    x_ref,
    xl_ref,
    xr_ref,
    norms_ref,
    wqkv_ref,
    dmid_ref,
    vec_ref,
    keep_ref,
    send_ref,
    dx_ref,
    dxl_ref,
    dxr_ref,
    dk_ref,
    dv_ref,
    dqt_ref,
    dq_ref,
    p_ref,
    ds_ref,
    normed_ref,
    pack_ref,
    sems,
):
    n, w, dh, halo = br.n, br.w, br.dh, br.halo
    dk_ref[...] = jnp.zeros_like(dk_ref)
    dv_ref[...] = jnp.zeros_like(dv_ref)
    dqt_ref[...] = jnp.zeros_like(dqt_ref)
    factor = br.scale * LOG2E

    def image(j, carry):
        lo, hi, k0, t0, t1 = image_span(br, meta_ref, j)
        span = pl.ds(k0, br.kw)
        keys = kwin_ref[span, :]
        keys_t = keys.T
        values = vwin_ref[span, :]
        row = iota((br.kw, 128), 0) + (k0 - br.halo)
        mask = jnp.logical_and(row >= lo, row < hi)

        def tile(t, carry):
            here = pl.ds(pl.multiple_of(t * 128, 128), 128)
            rows = q_ref[here, :]
            outs = dheads_ref[here, :]
            lane = iota((1, 128), 1) + t * 128
            inside = jnp.logical_and(lane >= lo, lane < hi)
            for group in br.groups:
                c0, c1, heads = group
                queries = stack_heads(br, rows, group)
                upstream = stack_heads(br, outs, group)
                scores = nt(keys[:, c0:c1], queries)
                dprobs = nt(values[:, c0:c1], upstream)
                for i, h in enumerate(heads):
                    part = slice(i * 128, (i + 1) * 128)
                    lse = jnp.where(inside, lse_ref[t, h : h + 1, :], -NEG)
                    p = jnp.exp2(scores[:, part] * factor - lse)
                    p = jnp.where(mask, p, 0.0)
                    dp = dprobs[:, part]
                    ds = (p * (dp - col_sum(p * dp))).astype(BF16)
                    p_ref[:, part] = p.astype(BF16)
                    ds_ref[:, part] = ds
                    dqt_ref[t, h * dh : (h + 1) * dh, :] += nn(
                        keys_t[h * dh : (h + 1) * dh, :], ds
                    )
                size = 128 * len(heads)
                dv_ref[span, c0:c1] += nn(p_ref[:, :size], upstream)
                dk_ref[span, c0:c1] += nn(ds_ref[:, :size], queries)
            return carry

        return lax.fori_loop(t0, t1, tile, carry)

    lax.fori_loop(meta_ref[12], meta_ref[13] + 1, image, 0)
    for t in range(br.t):
        dq_ref[t * 128 : (t + 1) * 128, :] = (dqt_ref[t].T * br.scale).astype(BF16)
    dk = (dk_ref[...] * br.scale).astype(BF16)
    dv = dv_ref[...].astype(BF16)
    gain, shift = norms_ref[0, 0:1, :], norms_ref[0, 1:2, :]
    dgain = jnp.zeros((1, w), F32)
    dshift = jnp.zeros((1, w), F32)
    for ref, lo, size, out in (
        (xl_ref, 0, halo, dxl_ref),
        (x_ref, halo, n, dx_ref),
        (xr_ref, halo + n, halo, dxr_ref),
    ):
        unit, rstd = normalize(ref[...].astype(F32))
        normed_ref[lo : lo + size, :] = (unit * gain + shift).astype(BF16)
        up = nt(dk[lo : lo + size], wqkv_ref[:, w : 2 * w])
        up = up + nt(dv[lo : lo + size], wqkv_ref[:, 2 * w :])
        if out is dx_ref:
            up = up + nt(dq_ref[...], wqkv_ref[:, :w])
        dgain = dgain + col_sum(up * unit)
        dshift = dshift + col_sum(up)
        dx = norm_grad(unit, rstd, gain, up)
        if out is dx_ref:
            out[...] = dx + dmid_ref[...]
        else:
            out[...] = dx.astype(BF16)
    whole = jnp.concatenate(
        [
            tn(normed_ref[halo : halo + n, :], dq_ref[...]),
            tn(normed_ref[...], dk),
            tn(normed_ref[...], dv),
        ],
        axis=1,
    )
    pack_mat(pack_ref, at["qkv"], w, 3 * w, whole)
    block = vec_block([dgain, dshift])
    pack_ref[at["vec1"] : at["vec1"] + block.shape[0], :] = block.astype(BF16)
    pack_ref[at["vec2"] : at["vec2"] + vec_ref.shape[0], :] = vec_ref[...].astype(BF16)
    if at["rows"] > at["end"]:
        pack_ref[at["end"] :, :] = jnp.zeros((at["rows"] - at["end"], 128), BF16)
    emit(pack_ref, (keep_ref, send_ref), index_ref[0], sems)


class Cross:
    def __init__(self, wa, wb, rows_b):
        self.wa = wa
        self.wb = wb
        self.dh = wb // HEADS
        self.n = rows_b
        self.scale = self.dh ** (-0.5)
        self.proj = nt if wa > wb else nn
        self.proj_back = nn if wa > wb else nt
        self.back = nn if wa > wb else nt
        self.back_back = nt if wa > wb else nn

    def by_head(self):
        head = iota((128, self.wb), 0) // ROWS
        col = iota((128, self.wb), 1)
        return jnp.logical_and(col >= head * self.dh, col < (head + 1) * self.dh).astype(F32)

    def by_image(self):
        lane = iota((ROWS, 128), 1)
        return jnp.logical_and(
            lane - (lane // ROWS) * ROWS == iota((ROWS, 128), 0), lane < HEADS * ROWS
        ).astype(F32)


def spread(cx, low_rows):
    return jnp.concatenate([low_rows] * 8, axis=0) * cx.by_head().astype(low_rows.dtype)


def gather_heads(cx, wide):
    kept = wide * cx.by_head()
    total = kept[0:ROWS]
    for h in range(1, HEADS):
        total = total + kept[h * ROWS : (h + 1) * ROWS]
    return total


def to_lane(cx, rows):
    return col_sum(cx.by_image() * nt_exact(rows, cx.by_head()))


def from_lane(cx, lane):
    return nn_exact(cx.by_image() * lane, cx.by_head())


def cross_query(cx, cls, norms_ref, proj_ref, query_ref, keyval_ref, bias_ref, qa_ref, qb_ref):
    wa, wb = cx.wa, cx.wb
    unit_a, rstd_a = normalize(cls)
    lifted = unit_a * norms_ref[0:1, :wa] + norms_ref[1:2, :wa]
    act, slope = gelu_pair(lifted)
    act = act.astype(BF16)
    bias = bias_ref[...].reshape(1, bias_ref.shape[0])[:, :wb]
    moved = cx.proj(act, proj_ref[...]) + bias
    gain, shift = norms_ref[0:1, wa : wa + wb], norms_ref[1:2, wa : wa + wb]
    unit_q, rstd_q = normalize(moved)
    query_in = (unit_q * gain + shift).astype(BF16)
    fquery = nn(query_in, query_ref[...]).astype(BF16)
    kself = nn(query_in, keyval_ref[:, :wb]).astype(BF16)
    vself = nn(query_in, keyval_ref[:, wb:]).astype(BF16)
    for i, item in enumerate((unit_a, slope, act, jnp.broadcast_to(rstd_a, unit_a.shape))):
        qa_ref[i] = item.astype(F32)
    for i, item in enumerate(
        (moved, unit_q, query_in, fquery, kself, vself, jnp.broadcast_to(rstd_q, moved.shape))
    ):
        qb_ref[i] = item.astype(F32)
    return fquery


def allowed_rows(cx, lane_ref):
    row = iota((cx.n, 128), 0)
    return jnp.logical_and(row > lane_ref[0:1, :], row < lane_ref[1:2, :])


def keys_kernel(cxs, ys_ref, fln_ref, yl_ref, fsn_ref, ks_ref, kl_ref):
    for cx, y_ref, norms_ref, out_ref in (
        (cxs[0], ys_ref, fln_ref, ks_ref),
        (cxs[1], yl_ref, fsn_ref, kl_ref),
    ):
        wa, wb = cx.wa, cx.wb
        unit, _ = normalize(y_ref[...].astype(F32))
        out_ref[...] = (
            unit * norms_ref[0:1, wa : wa + wb] + norms_ref[1:2, wa : wa + wb]
        ).astype(BF16)


def cross_front_kernel(
    cxs,
    c0_ref,
    c1_ref,
    c2_ref,
    c3_ref,
    lane_s_ref,
    lane_l_ref,
    key_s_ref,
    key_l_ref,
    fln_ref,
    flp_ref,
    flq_ref,
    flk_ref,
    flb_ref,
    fsn_ref,
    fsp_ref,
    fsq_ref,
    fsk_ref,
    fsb_ref,
    part_ref,
    sc_l_ref,
    sc_s_ref,
    ab_l_ref,
    ab_s_ref,
    qa_l_ref,
    qb_l_ref,
    qa_s_ref,
    qb_s_ref,
):
    cls = c0_ref[...] + c1_ref[...] + c2_ref[...] + c3_ref[...]
    wl, ws = cxs[0].wa, cxs[1].wa
    col = 0
    stats = []
    for cx, rows, key_ref, lane_ref, keyval_ref, weights, kept, sc_ref, ab_ref in (
        (
            cxs[0],
            cls[:, :wl],
            key_s_ref,
            lane_s_ref,
            flk_ref,
            (fln_ref, flp_ref, flq_ref, flk_ref, flb_ref),
            (qa_l_ref, qb_l_ref),
            sc_l_ref,
            ab_l_ref,
        ),
        (
            cxs[1],
            cls[:, wl : wl + ws],
            key_l_ref,
            lane_l_ref,
            fsk_ref,
            (fsn_ref, fsp_ref, fsq_ref, fsk_ref, fsb_ref),
            (qa_s_ref, qb_s_ref),
            sc_s_ref,
            ab_s_ref,
        ),
    ):
        fquery = cross_query(cx, rows, *weights, *kept)
        absorbed = nt(spread(cx, fquery), keyval_ref[:, : cx.wb]).astype(BF16)
        ab_ref[...] = absorbed
        key = key_ref[...]
        allowed = allowed_rows(cx, lane_ref)
        scores = jnp.where(allowed, nt(key, absorbed) * (cx.scale * LOG2E), NEG)
        sc_ref[...] = scores
        top = jnp.max(scores, axis=0, keepdims=True)
        p = jnp.where(allowed, jnp.exp2(scores - top), 0.0)
        high, low = split(p)
        mixed_high, mixed_low = split(tn(high, key) + tn(low, key))
        value_part = keyval_ref[:, cx.wb :]
        out = gather_heads(cx, nn(mixed_high, value_part) + nn(mixed_low, value_part))
        part_ref[0:ROWS, col : col + cx.wb] = out
        col += cx.wb
        stats += [top, col_sum(p)]
    width = part_ref.shape[1]
    part_ref[0:ROWS, col:] = jnp.zeros((ROWS, width - col), F32)
    part_ref[ROWS:, :] = jnp.zeros((8, width), F32)
    part_ref[ROWS : ROWS + 4, :128] = jnp.concatenate(stats, axis=0)


def cross_back_kernel(
    cxs,
    share,
    g0_ref,
    g1_ref,
    g2_ref,
    g3_ref,
    p0_ref,
    p1_ref,
    p2_ref,
    p3_ref,
    lane_s_ref,
    lane_l_ref,
    ys_ref,
    yl_ref,
    key_s_ref,
    key_l_ref,
    sc_l_ref,
    sc_s_ref,
    ab_l_ref,
    ab_s_ref,
    qb_l_ref,
    qb_s_ref,
    fln_ref,
    flk_ref,
    flo_ref,
    flw_ref,
    flb_ref,
    fsn_ref,
    fsk_ref,
    fso_ref,
    fsw_ref,
    fsb_ref,
    dq_ref,
    cross_s_ref,
    cross_l_ref,
    out_s_ref,
    out_l_ref,
    rt_l_ref,
    rt_s_ref,
    gk_l_ref,
    gk_s_ref,
    vec_ref,
):
    dcls = g0_ref[...] + g1_ref[...] + g2_ref[...] + g3_ref[...]
    parts = [p0_ref, p1_ref, p2_ref, p3_ref]
    vecs = []
    col_b = 0
    col_a = 0
    for index, (
        cx,
        key_ref,
        y_ref,
        lane_ref,
        lane_a_ref,
        a_ref,
        out_ref,
        cross_ref,
        sc_ref,
        ab_ref,
        qb_ref,
        rt_ref,
        gk_ref,
        weights,
    ) in enumerate(
        (
            (
                cxs[0],
                key_s_ref,
                ys_ref,
                lane_s_ref,
                lane_l_ref,
                yl_ref,
                out_l_ref,
                cross_s_ref,
                sc_l_ref,
                ab_l_ref,
                qb_l_ref,
                rt_l_ref,
                gk_l_ref,
                (fln_ref, flk_ref, flo_ref, flw_ref, flb_ref),
            ),
            (
                cxs[1],
                key_l_ref,
                yl_ref,
                lane_l_ref,
                lane_s_ref,
                ys_ref,
                out_s_ref,
                cross_l_ref,
                sc_s_ref,
                ab_s_ref,
                qb_s_ref,
                rt_s_ref,
                gk_s_ref,
                (fsn_ref, fsk_ref, fso_ref, fsw_ref, fsb_ref),
            ),
        )
    ):
        norms_ref, keyval_ref, wout_ref, wback_ref, bias_ref = weights
        wa, wb = cx.wa, cx.wb
        bias = bias_ref[...].reshape(1, bias_ref.shape[0])
        moved, fquery, kself, vself = qb_ref[0], qb_ref[3], qb_ref[4], qb_ref[5]
        self_score = to_lane(cx, fquery * kself) * (cx.scale * LOG2E)
        tops = [p[ROWS + 2 * index : ROWS + 2 * index + 1, :128] for p in parts]
        sums = [p[ROWS + 2 * index + 1 : ROWS + 2 * index + 2, :128] for p in parts]
        top = self_score
        for item in tops:
            top = jnp.maximum(top, item)
        own = jnp.exp2(self_score - top)
        total = own
        weights_of = []
        for item, amount in zip(tops, sums):
            weight = jnp.exp2(item - top)
            weights_of.append(weight)
            total = total + amount * weight
        inverse = 1.0 / total
        p_self = own * inverse
        fheads = from_lane(cx, p_self) * vself
        for part, weight in zip(parts, weights_of):
            fheads = fheads + part[0:ROWS, col_b : col_b + wb] * from_lane(cx, weight * inverse)
        fheads_low = fheads.astype(BF16)
        joined = moved + (nn(fheads_low, wout_ref[...]) + bias[:, wb : 2 * wb])
        unit_r, rstd_r = normalize(joined)
        gain_r = norms_ref[0:1, wa + wb :]
        reverted = unit_r * gain_r + norms_ref[1:2, wa + wb :]
        act_r, slope_r = gelu_pair(reverted)
        act_r = act_r.astype(BF16)
        back = cx.back(act_r, wback_ref[...]) + bias[:, 2 * wb :]
        n_a = a_ref.shape[0]
        hit = (iota((n_a, 128), 0) == lane_a_ref[0:1, :]).astype(F32)
        hit = jnp.where(iota((1, 128), 1) < IMGS, hit, 0.0)
        first = jnp.sum(hit, axis=1, keepdims=True) > 0.5
        placed = nn(hit[:, :ROWS].astype(BF16), back.astype(BF16))
        result = jnp.where(first, placed, a_ref[...].astype(F32))
        out_ref[...] = (result.T if wa % 128 else result).astype(BF16)
        dback = dcls[:, col_a : col_a + wa]
        dback_low = dback.astype(BF16)
        drev = cx.back_back(dback_low, wback_ref[...]) * slope_r
        djoined = norm_grad(unit_r, rstd_r, gain_r, drev)
        dattn = djoined.astype(BF16)
        dheads_low = nt(dattn, wout_ref[...]).astype(BF16)
        dheads = dheads_low.astype(F32)
        delta = to_lane(cx, dheads * fheads)
        ds_self = p_self * (to_lane(cx, dheads * vself) - delta)
        ds_self_rows = from_lane(cx, ds_self.astype(BF16).astype(F32))
        p_self_rows = from_lane(cx, p_self.astype(BF16).astype(F32))
        upstream = spread(cx, dheads_low)
        absorbed_high, absorbed_low = split(nt(upstream, keyval_ref[:, wb:]))
        key = key_ref[...]
        allowed = allowed_rows(cx, lane_ref)
        p = jnp.where(allowed, jnp.exp2(sc_ref[...] - (top + jnp.log2(total))), 0.0)
        dp = nt(key, absorbed_high) + nt(key, absorbed_low)
        ds = (p * (dp - delta)).astype(BF16)
        p_low = p.astype(BF16)
        dkey = nn(ds, ab_ref[...]) * cx.scale + nn(p_low, absorbed_high)
        g_k = tn(ds, key)
        gk_ref[0] = g_k
        gk_ref[1] = tn(p_low, key)
        g_high, g_low = split(g_k)
        key_part = keyval_ref[:, :wb]
        dquery = gather_heads(cx, nn(g_high, key_part) + nn(g_low, key_part)) * cx.scale
        dq_ref[:, col_b : col_b + wb] = dquery + ds_self_rows * kself * (cx.scale * share)
        unit_b, rstd_b = normalize(y_ref[...].astype(F32))
        gain_b = norms_ref[0:1, wa : wa + wb]
        cross_ref[...] = norm_grad(unit_b, rstd_b, gain_b, dkey)
        for i, item in enumerate(
            (
                fheads_low,
                act_r,
                dattn,
                djoined,
                dheads_low,
                ds_self_rows * fquery * cx.scale,
                p_self_rows * dheads,
            )
        ):
            rt_ref[i] = item.astype(F32)
        vecs += [
            col_sum(dkey * unit_b),
            col_sum(drev * unit_r) * share,
            col_sum(dkey),
            col_sum(drev) * share,
        ]
        col_a += wa
        col_b += wb
    dq_ref[:, col_b:] = jnp.zeros((ROWS, dq_ref.shape[1] - col_b), F32)
    vec_ref[...] = vec_block(vecs)


def cross_query_back_kernel(
    cxs,
    share,
    d0_ref,
    d1_ref,
    d2_ref,
    d3_ref,
    qa_l_ref,
    qb_l_ref,
    rt_l_ref,
    fln_ref,
    flp_ref,
    flq_ref,
    flk_ref,
    qa_s_ref,
    qb_s_ref,
    rt_s_ref,
    fsn_ref,
    fsp_ref,
    fsq_ref,
    fsk_ref,
    dcls_ref,
    dm_l_ref,
    dm_s_ref,
    vec_ref,
):
    dquery_all = d0_ref[...] + d1_ref[...] + d2_ref[...] + d3_ref[...]
    col_a = col_b = 0
    vecs = []
    for cx, qa_ref, qb_ref, rt_ref, norms_ref, proj_ref, query_ref, keyval_ref, dm_ref in (
        (cxs[0], qa_l_ref, qb_l_ref, rt_l_ref, fln_ref, flp_ref, flq_ref, flk_ref, dm_l_ref),
        (cxs[1], qa_s_ref, qb_s_ref, rt_s_ref, fsn_ref, fsp_ref, fsq_ref, fsk_ref, dm_s_ref),
    ):
        wa, wb = cx.wa, cx.wb
        dquery = dquery_all[:, col_b : col_b + wb].astype(BF16)
        dkself = rt_ref[5].astype(BF16)
        dvself = rt_ref[6].astype(BF16)
        dquery_in = (
            nt(dquery, query_ref[...])
            + nt(dkself, keyval_ref[:, :wb])
            + nt(dvself, keyval_ref[:, wb:])
        )
        unit_q, rstd_q = qb_ref[1], qb_ref[6]
        gain = norms_ref[0:1, wa : wa + wb]
        dmoved = norm_grad(unit_q, rstd_q, gain, dquery_in) + rt_ref[3]
        high, low = split(dmoved)
        dlifted = (cx.proj_back(high, proj_ref[...]) + cx.proj_back(low, proj_ref[...])) * qa_ref[1]
        unit_a = qa_ref[0]
        dcls_ref[:, col_a : col_a + wa] = norm_grad(
            unit_a, qa_ref[3], norms_ref[0:1, :wa], dlifted
        )
        dm_ref[0] = dmoved
        dm_ref[1] = dquery.astype(F32)
        vecs += [
            col_sum(dlifted * unit_a) * share,
            col_sum(dquery_in * unit_q) * share,
            col_sum(dlifted) * share,
            col_sum(dquery_in) * share,
            col_sum(dmoved) * share,
            col_sum(rt_ref[2]) * share,
        ]
        col_a += wa
        col_b += wb
    dcls_ref[:, col_a:] = jnp.zeros((ROWS, dcls_ref.shape[1] - col_a), F32)
    vec_ref[...] = vec_block(vecs)


def cross_grads_kernel(
    cxs,
    ats,
    share,
    index_ref,
    g0_ref,
    g1_ref,
    g2_ref,
    g3_ref,
    vec1_ref,
    vec2_ref,
    qa_l_ref,
    qb_l_ref,
    rt_l_ref,
    gk_l_ref,
    dm_l_ref,
    qa_s_ref,
    qb_s_ref,
    rt_s_ref,
    gk_s_ref,
    dm_s_ref,
    keep_ref,
    send_ref,
    pack_ref,
    sems,
):
    dcls = g0_ref[...] + g1_ref[...] + g2_ref[...] + g3_ref[...]
    col_a = 0
    dbacks = []
    for cx, at, qa_ref, qb_ref, rt_ref, gk_ref, dm_ref in (
        (cxs[0], ats, qa_l_ref, qb_l_ref, rt_l_ref, gk_l_ref, dm_l_ref),
        (cxs[1], ats, qa_s_ref, qb_s_ref, rt_s_ref, gk_s_ref, dm_s_ref),
    ):
        wa, wb = cx.wa, cx.wb
        name = "l" if cx is cxs[0] else "s"
        dback = dcls[:, col_a : col_a + wa]
        dbacks.append(col_sum(dback) * share)
        dback = dback.astype(BF16)
        act, query_in, fquery = (
            qa_ref[2].astype(BF16),
            qb_ref[2].astype(BF16),
            qb_ref[3].astype(BF16),
        )
        fheads, act_r, dattn, dheads, dkself, dvself = (
            rt_ref[i].astype(BF16) for i in (0, 1, 2, 4, 5, 6)
        )
        dmoved = dm_ref[0].astype(BF16)
        if wa > wb:
            proj, back = tn(dmoved, act), tn(act_r, dback)
        else:
            proj, back = tn(act, dmoved), tn(dback, act_r)
        pack_mat(pack_ref, at["proj" + name], *proj.shape, proj * share)
        pack_mat(pack_ref, at["back" + name], *back.shape, back * share)
        query = tn(query_in, dm_ref[1].astype(BF16)) * share
        pack_mat(pack_ref, at["query" + name], wb, wb, query)
        pack_mat(pack_ref, at["out" + name], wb, wb, tn(fheads, dattn) * share)
        keys = (
            tn(gk_ref[0].astype(BF16), spread(cx, fquery)) * cx.scale
            + tn(query_in, dkself) * share
        )
        values = tn(gk_ref[1].astype(BF16), spread(cx, dheads)) + tn(query_in, dvself) * share
        pack_mat(pack_ref, at["keyval" + name], wb, 2 * wb, jnp.concatenate([keys, values], axis=1))
        col_a += wa
    for name, block in (
        ("vec1", vec1_ref[...]),
        ("vec2", vec2_ref[...]),
        ("vec3", vec_block(dbacks)),
    ):
        pack_ref[ats[name] : ats[name] + block.shape[0], :] = block.astype(BF16)
    if ats["rows"] > ats["end"]:
        pack_ref[ats["end"] :, :] = jnp.zeros((ats["rows"] - ats["end"], 128), BF16)
    emit(pack_ref, (keep_ref, send_ref), index_ref[0], sems)


def fold_kernel(counts, stage, rows, index_ref, *refs):
    total = sum(counts)
    ins, refs = refs[:total], refs[total:]
    outs, (sum_ref, sems) = refs[:-2], refs[-2:]
    at = i = 0
    for count in counts:
        value = ins[i][...].astype(F32)
        for other in ins[i + 1 : i + count]:
            value = value + other[...].astype(F32)
        size = value.shape[0]
        sum_ref[at : at + size, :] = value.astype(BF16)
        at += size
        i += count
    if rows > at:
        sum_ref[at:, :] = jnp.zeros((rows - at, 128), BF16)
    emit(sum_ref, outs, 0 if stage is None else index_ref[stage], sems)


def join_kernel(stage, index_ref, *refs):
    *parts, out_ref = refs
    for d, part in enumerate(parts):
        size = part.shape[0]
        at = pl.multiple_of((index_ref[stage] ^ d) * size, 16)
        out_ref[pl.ds(at, size), :] = part[...]


def settle_kernel(brs, *refs):
    ins, outs = refs[: 3 * len(brs)], refs[3 * len(brs) :]
    for i, br in enumerate(brs):
        dx_ref, left_ref, right_ref = ins[3 * i : 3 * i + 3]
        n, halo = br.n, br.halo
        rest = jnp.zeros((n - halo, br.w), F32)
        dx = dx_ref[...] + jnp.concatenate([left_ref[...].astype(F32), rest], axis=0)
        dx = dx + jnp.concatenate([rest, right_ref[...].astype(F32)], axis=0)
        outs[i][...] = (dx.T if br.turned else dx).astype(BF16)


def gather_packs(index, own_ref, got_ref, packs, sems):
    copies, at = [], 0
    for pack_ref in packs:
        half = pack_ref.shape[0] // 2
        for d, part in enumerate((own_ref, got_ref)):
            to = pl.multiple_of((index ^ d) * half, 16)
            copies.append(
                pltpu.make_async_copy(
                    part.at[pl.ds(at, half)], pack_ref.at[pl.ds(to, half)], sems.at[len(copies)]
                )
            )
            copies[-1].start()
        at += half
    for copy in copies:
        copy.wait()


def unpack_ffn_kernel(brs, ats, index_ref, own_ref, got_ref, *refs):
    outs, packs, sems = refs[:6], refs[6:8], refs[8]
    gather_packs(index_ref[0], own_ref, got_ref, packs, sems)
    for i, (br, at, ref) in enumerate(zip(brs, ats, packs)):
        out_ref, up_ref, down_ref = outs[3 * i : 3 * i + 3]
        w, f, step = br.w, br.f, 256
        unpack_mat(ref, at["out"], w, w, out_ref)
        for j, c in enumerate(range(0, f, step)):
            unpack_mat(ref, at["up"] + j * mat_rows(w, step), w, step, up_ref.at[:, c : c + step])
            if br.turned:
                unpack_mat(
                    ref, at["down"] + j * mat_rows(w, step), w, step, down_ref.at[:, c : c + step]
                )
        if not br.turned:
            unpack_mat(ref, at["down"], f, w, down_ref)


def unpack_qkv_kernel(brs, ats, index_ref, own_ref, got_ref, *refs):
    outs, packs, sems = refs[:8], refs[8:10], refs[10]
    gather_packs(index_ref[0], own_ref, got_ref, packs, sems)
    for i, (br, at, ref) in enumerate(zip(brs, ats, packs)):
        qkv_ref, norms_ref, bias_ref, upbias_ref = outs[4 * i : 4 * i + 4]
        w, f = br.w, br.f
        unpack_mat(ref, at["qkv"], w, 3 * w, qkv_ref)
        block = ref[at["vec1"] : at["vec1"] + vec_rows([w, w]), :].astype(F32)
        gain, shift = vecs_of(block, [w, w])
        norms_ref[0, 0:1, :] = gain
        norms_ref[0, 1:2, :] = shift
        block = ref[at["vec2"] : at["vec2"] + vec_rows([w] * 4 + [f]), :].astype(F32)
        gain, shift, bias0, bias1, upbias = vecs_of(block, [w] * 4 + [f])
        norms_ref[1, 0:1, :] = gain
        norms_ref[1, 1:2, :] = shift
        bias_ref[0:1, :] = bias0
        bias_ref[1:2, :] = bias1
        upbias_ref[...] = upbias.reshape(f)


def unpack_cross_kernel(cxs, at, index_ref, own_ref, got_ref, *refs):
    outs, ref, sems = refs[:14], refs[14], refs[15]
    gather_packs(index_ref[0], own_ref, got_ref, (ref,), sems)

    def vectors(name):
        widths = at["widths"][name]
        return vecs_of(ref[at[name] : at[name] + vec_rows(widths), :].astype(F32), widths)

    vec1, vec2, vec3 = vectors("vec1"), vectors("vec2"), vectors("vec3")
    for i, (cx, name) in enumerate(zip(cxs, "ls")):
        norms_ref, proj_ref, query_ref, keyval_ref, out_ref, back_ref, bias_ref = outs[
            7 * i : 7 * i + 7
        ]
        wa, wb = cx.wa, cx.wb
        less, more = min(wa, wb), max(wa, wb)
        unpack_mat(ref, at["proj" + name], less, more, proj_ref)
        unpack_mat(ref, at["query" + name], wb, wb, query_ref)
        unpack_mat(ref, at["keyval" + name], wb, 2 * wb, keyval_ref)
        unpack_mat(ref, at["out" + name], wb, wb, out_ref)
        unpack_mat(ref, at["back" + name], less, more, back_ref)
        gain_key, gain_rev, shift_key, shift_rev = vec1[4 * i : 4 * i + 4]
        gain_a, gain_q, shift_a, shift_q, bias_a, bias_b = vec2[6 * i : 6 * i + 6]
        norms_ref[0:1, :] = jnp.concatenate([gain_a, gain_q + gain_key, gain_rev], axis=1)
        norms_ref[1:2, :] = jnp.concatenate([shift_a, shift_q + shift_key, shift_rev], axis=1)
        bias_ref[...] = jnp.concatenate([bias_a, bias_b, vec3[i]], axis=1).reshape(wa + 2 * wb)


def stages():
    head = [("head", 1 << i) for i in range(lax.axis_size("head").bit_length() - 1)]
    dp = [("dp", 1 << i) for i in range(lax.axis_size("dp").bit_length() - 1)]
    found = [head[:1], dp[:1] + head[1:]]
    for i in range(1, len(dp), 2):
        found.append(dp[i : i + 2])
    return found


def index_of(stage):
    index = 0
    for k, (axis, bit) in enumerate(stage):
        index = index + ((lax.axis_index(axis) // bit) % 2 << k)
    return index


def swap(x, stage, d):
    heads = lax.axis_size("head")
    flip = {"dp": 0, "head": 0}
    for k, (axis, bit) in enumerate(stage):
        if d >> k & 1:
            flip[axis] |= bit
    pairs = [
        (i * heads + j, (i ^ flip["dp"]) * heads + (j ^ flip["head"]))
        for i in range(lax.axis_size("dp"))
        for j in range(heads)
    ]
    return lax.ppermute(x, ("dp", "head"), pairs)


def others(x):
    count = lax.axis_size("head")
    return [
        lax.ppermute(x, "head", [(i, i ^ d) for i in range(count)]) for d in range(1, count)
    ]


class Sum:
    def __init__(self, index, packs):
        self.index = index
        self.plan = stages()
        self.sizes = [1 << len(stage) for stage in self.plan]
        devices = lax.axis_size("dp") * lax.axis_size("head")
        self.rows = round_up(sum(keep.shape[0] for keep, _ in packs), devices // 2 * 16)
        self.counts = [2] * len(packs)
        self.ins = []
        for keep, send in packs:
            self.ins += [keep, swap(send, self.plan[0], 1)]

    def fold(self, s):
        last = s == len(self.plan)
        cuts = 1 if last else self.sizes[s]
        pieces = call(
            functools.partial(fold_kernel, self.counts, None if last else s, self.rows),
            (sds((self.rows // cuts, 128), BF16),) * cuts,
            (self.index, *self.ins),
            [SMEM] + [VMEM] * len(self.ins),
            [pltpu.VMEM((self.rows, 128), BF16), pltpu.SemaphoreType.DMA((cuts,))],
            out_specs=(ANY,) * cuts,
            moved=self.rows * 128 * 6,
        )
        self.rows = self.rows // cuts
        self.counts = [cuts]
        if last:
            self.whole = pieces[0]
            self.ins = self.sent(len(self.plan) - 1)
        else:
            self.ins = [pieces[0]] + [swap(pieces[d], self.plan[s], d) for d in range(1, cuts)]

    def sent(self, s):
        return [self.whole] + [swap(self.whole, self.plan[s], d) for d in range(1, self.sizes[s])]

    def join(self, s):
        self.whole = call(
            functools.partial(join_kernel, s),
            sds((self.whole.shape[0] * self.sizes[s], 128), BF16),
            (self.index, *self.ins),
            [SMEM] + [VMEM] * len(self.ins),
            moved=self.whole.shape[0] * self.sizes[s] * 512,
        )
        self.ins = self.sent(s - 1)

    def folds(self, first, last):
        for s in range(first, last + 1):
            self.fold(s)

    def joins(self):
        for s in range(len(self.plan) - 1, 0, -1):
            self.join(s)
        return self.ins


def after(first, then):
    return lax.optimization_barrier((first, then))[1]


def halos(x, size):
    count = lax.axis_size("head")
    left = lax.ppermute(x[-size:], "head", [(i, i + 1) for i in range(count - 1)])
    right = lax.ppermute(x[:size], "head", [(i + 1, i) for i in range(count - 1)])
    return left, right


def block_forward(br, meta, sub, x, halo, qkv, norms, w_qkv, w_out, w_up, w_down, bias, upbias):
    n, w, f = br.n, br.w, br.f
    outs = (
        sds((n, w), BF16),
        sds((ROWS, w), F32),
        sds((br.r, w), BF16),
        sds((br.r, w), BF16),
        sds((br.t, 8, 128), F32),
        sds((n, w), BF16),
        sds((n, w), F32),
        sds((n, w), BF16),
        sds((n, f), BF16),
        sds((n, f), BF16),
    )
    ins = (meta, x, *halo, *qkv, norms, w_qkv, w_out, w_up, w_down, bias, upbias, sub)
    return call(
        functools.partial(forward_kernel, br),
        outs,
        ins,
        [SMEM] + [VMEM] * (len(ins) - 1),
        [pltpu.VMEM((br.t, w, 128), F32)],
        flops=4 * n * w * f,
        moved=n * f * 8,
    )


def ffn_back(br, index, col, lane, dy, cross, dcls, kept, norms, w_out, w_up, w_down):
    n, w, f = br.n, br.w, br.f
    parts = [("up", mat_rows(w, f)), ("down", mat_rows(f, w)), ("out", mat_rows(w, w))]
    at, rows = layout(parts)
    at["rows"], at["end"], at["col"] = rows, sum(r for _, r in parts), col
    ins = (index, lane, dy, cross, dcls, *kept, norms, w_out, w_up, w_down)
    half = sds((rows // 2, 128), BF16)
    vec = sds((vec_rows([w] * 4 + [f]), 128), F32)
    keep, send, *outs = call(
        functools.partial(ffn_back_kernel, br, at),
        (half, half, sds((n, w), F32), sds((n, w), BF16), vec),
        ins,
        [SMEM] + [VMEM] * (len(ins) - 1),
        [pltpu.VMEM((rows, 128), BF16), pltpu.SemaphoreType.DMA((2,))],
        flops=8 * n * w * f,
        moved=n * f * 8,
        out_specs=(ANY, ANY, VMEM, VMEM, VMEM),
    )
    return at, (keep, send), outs


def attn_back(br, index, meta, q, kwin, vwin, dheads, lse, x, halo, norms, w_qkv, dmid, vec):
    n, w = br.n, br.w
    parts = [("qkv", mat_rows(w, 3 * w)), ("vec1", vec_rows([w, w])), ("vec2", vec.shape[0])]
    at, rows = layout(parts)
    at["rows"], at["end"] = rows, sum(r for _, r in parts)
    size = 128 * max(len(g[2]) for g in br.groups)
    ins = (meta, index, q, kwin, vwin, dheads, lse, x, *halo, norms, w_qkv, dmid, vec)
    half = sds((rows // 2, 128), BF16)
    keep, send, *outs = call(
        functools.partial(attn_back_kernel, br, at),
        (half, half, sds((n, w), F32), sds((br.halo, w), BF16), sds((br.halo, w), BF16)),
        ins,
        [SMEM, SMEM] + [VMEM] * (len(ins) - 2),
        [
            pltpu.VMEM((br.r, w), F32),
            pltpu.VMEM((br.r, w), F32),
            pltpu.VMEM((br.t, w, 128), F32),
            pltpu.VMEM((n, w), BF16),
            pltpu.VMEM((br.kw, size), BF16),
            pltpu.VMEM((br.kw, size), BF16),
            pltpu.VMEM((br.r, w), BF16),
            pltpu.VMEM((rows, 128), BF16),
            pltpu.SemaphoreType.DMA((2,)),
        ],
        flops=16 * n * w * 1024,
        moved=n * w * 32,
        out_specs=(ANY, ANY, VMEM, VMEM, VMEM),
    )
    return at, (keep, send), outs


def on_device(
    seg_large,
    seg_small,
    x_large,
    x_small,
    dy_large,
    dy_small,
    lb_norms,
    lb_qkv,
    lb_out,
    lb_up,
    lb_down,
    lb_bias,
    lb_upbias,
    sb_norms,
    sb_qkv,
    sb_out,
    sb_up,
    sb_down,
    sb_bias,
    sb_upbias,
    fl_norms,
    fl_proj,
    fl_query,
    fl_keyval,
    fl_out,
    fl_back,
    fl_bias,
    fs_norms,
    fs_proj,
    fs_query,
    fs_keyval,
    fs_out,
    fs_back,
    fs_bias,
):
    xl, xs, dyl, dys = x_large[0], x_small[0], dy_large[0], dy_small[0]
    large = Branch(*xl.shape, lb_up.shape[1], MOST_L)
    small = Branch(*xs.shape, sb_up.shape[1], MOST_S)
    cxs = (Cross(large.w, small.w, small.n), Cross(small.w, large.w, large.n))
    share = 1.0 / lax.axis_size("head")
    wide = round_up(large.w + small.w, 128)
    sb_down, fl_proj, fs_back = sb_down.T, fl_proj.T, fs_back.T
    found = [index_of(stage) for stage in stages()]
    index = jnp.stack(found + [jnp.int32(0)] * (7 - len(found)) + [lax.axis_index("head")])
    index = index.astype(jnp.int32)
    here = lax.axis_index("head").astype(jnp.int32)[None]

    halo_s = halos(xs, small.halo)
    halo_l = halos(xl, large.halo)
    words = sds((16,), jnp.int32)
    lanes = sds((8, 128), jnp.int32)
    subs = sds((ROWS, 128), jnp.int32)
    start = call(
        functools.partial(start_kernel, large, small),
        (sds((large.n, large.w), BF16),) * 3
        + (sds((small.n, small.w), BF16),) * 3
        + (words, words, lanes, lanes, subs, subs, sds((ROWS, wide), F32)),
        (here, seg_large, seg_small, xl, xs, dyl, dys, lb_norms, sb_norms, lb_qkv, sb_qkv),
        [SMEM] + [VMEM] * 10,
        [
            pltpu.VMEM((ROWS + 8, 128), jnp.int32),
            pltpu.SMEM((ROWS + 8, 128), jnp.int32),
            pltpu.SemaphoreType.DMA,
        ],
        out_specs=(VMEM,) * 6 + (SMEM, SMEM) + (VMEM,) * 5,
    )
    qkv_l, qkv_s = start[:3], start[3:6]
    meta_l, meta_s, lane_l, lane_s, sub_l, sub_s, dcls = start[6:]
    dcls_all = [dcls] + others(dcls)

    ys, cls_s, kwin_s, vwin_s, lse_s, ho_s, mid_s, n2_s, hid_s, slope_s = block_forward(
        small, meta_s, sub_s, xs, halo_s, qkv_s, sb_norms, sb_qkv, sb_out, sb_up, sb_down,
        sb_bias, sb_upbias,
    )
    yl, cls_l, kwin_l, vwin_l, lse_l, ho_l, mid_l, n2_l, hid_l, slope_l = block_forward(
        large, meta_l, sub_l, xl, halo_l, qkv_l, lb_norms, lb_qkv, lb_out, lb_up, lb_down,
        lb_bias, lb_upbias,
    )

    cls = jnp.concatenate(
        [cls_l, cls_s, jnp.zeros((ROWS, wide - large.w - small.w), F32)], axis=1
    )
    cls_all = [cls] + others(cls)
    key_s, key_l = call(
        functools.partial(keys_kernel, cxs),
        (sds((small.n, small.w), BF16), sds((large.n, large.w), BF16)),
        (ys, fl_norms, yl, fs_norms),
    )
    wl, ws = large.w, small.w
    part, sc_l, sc_s, ab_l, ab_s, qa_l, qb_l, qa_s, qb_s = call(
        functools.partial(cross_front_kernel, cxs),
        (
            sds((ROWS + 8, wide), F32),
            sds((small.n, 128), F32),
            sds((large.n, 128), F32),
            sds((128, ws), BF16),
            sds((128, wl), BF16),
            sds((4, ROWS, wl), F32),
            sds((7, ROWS, ws), F32),
            sds((4, ROWS, ws), F32),
            sds((7, ROWS, wl), F32),
        ),
        (
            *cls_all, lane_s, lane_l, key_s, key_l,
            fl_norms, fl_proj, fl_query, fl_keyval, fl_bias,
            fs_norms, fs_proj, fs_query, fs_keyval, fs_bias,
        ),
    )
    part_all = [part] + others(part)
    vec1 = [ws, ws, ws, ws, wl, wl, wl, wl]
    dquery, cross_s, cross_l, out_s, out_l, rt_l, rt_s, gk_l, gk_s, block1 = call(
        functools.partial(cross_back_kernel, cxs, share),
        (
            sds((ROWS, wide), F32),
            sds((small.n, ws), F32),
            sds((large.n, wl), F32),
            sds((ws, small.n) if small.turned else (small.n, ws), BF16),
            sds((large.n, wl), BF16),
            sds((7, ROWS, ws), F32),
            sds((7, ROWS, wl), F32),
            sds((2, 128, ws), F32),
            sds((2, 128, wl), F32),
            sds((vec_rows(vec1), 128), F32),
        ),
        (
            *dcls_all, *part_all, lane_s, lane_l, ys, yl, key_s, key_l,
            sc_l, sc_s, ab_l, ab_s, qb_l, qb_s,
            fl_norms, fl_keyval, fl_out, fl_back, fl_bias,
            fs_norms, fs_keyval, fs_out, fs_back, fs_bias,
        ),
    )
    dquery_all = [dquery] + others(dquery)
    vec2 = [wl, ws, wl, ws, ws, ws, ws, wl, ws, wl, wl, wl]
    dcls_new, dm_l, dm_s, block2 = call(
        functools.partial(cross_query_back_kernel, cxs, share),
        (
            sds((ROWS, wide), F32),
            sds((2, ROWS, ws), F32),
            sds((2, ROWS, wl), F32),
            sds((vec_rows(vec2), 128), F32),
        ),
        (
            *dquery_all, qa_l, qb_l, rt_l, fl_norms, fl_proj, fl_query, fl_keyval,
            qa_s, qb_s, rt_s, fs_norms, fs_proj, fs_query, fs_keyval,
        ),
    )

    at_fl, pack_fl, (dmid_l, dheads_l, vec_l) = ffn_back(
        large, index, 0, lane_l, dyl, cross_l, dcls_new,
        (hid_l, slope_l, n2_l, mid_l, ho_l), lb_norms, lb_out, lb_up, lb_down,
    )
    at_fs, pack_fs, (dmid_s, dheads_s, vec_s) = ffn_back(
        small, index, wl, lane_s, dys, cross_s, dcls_new,
        (hid_s, slope_s, n2_s, mid_s, ho_s), sb_norms, sb_out, sb_up, sb_down,
    )

    vec3 = [wl, ws]
    items = []
    for cx, name in zip(cxs, "ls"):
        items += [
            ("proj" + name, mat_rows(cx.wa, cx.wb)),
            ("query" + name, mat_rows(cx.wb, cx.wb)),
            ("keyval" + name, mat_rows(cx.wb, 2 * cx.wb)),
            ("out" + name, mat_rows(cx.wb, cx.wb)),
            ("back" + name, mat_rows(cx.wb, cx.wa)),
        ]
    widths = {"vec1": vec1, "vec2": vec2, "vec3": vec3}
    items += [(name, vec_rows(of)) for name, of in widths.items()]
    at_c, rows_c = layout(items)
    at_c["rows"], at_c["end"] = rows_c, sum(r for _, r in items)
    at_c["widths"] = widths
    half = sds((rows_c // 2, 128), BF16)
    ins = (
        index, *dcls_all, block1, block2,
        qa_l, qb_l, rt_l, gk_l, dm_l, qa_s, qb_s, rt_s, gk_s, dm_s,
    )
    pack_c = call(
        functools.partial(cross_grads_kernel, cxs, at_c, share),
        (half, half),
        ins,
        [SMEM] + [VMEM] * (len(ins) - 1),
        [pltpu.VMEM((rows_c, 128), BF16), pltpu.SemaphoreType.DMA((2,))],
        out_specs=(ANY, ANY),
    )

    sum_e = Sum(index, [pack_fl, pack_fs])
    sum_c = Sum(index, [pack_c])
    sum_e.fold(1)
    dheads_l = after(sum_e.ins[0], dheads_l)
    at_ql, pack_ql, (dx_l, dxl_l, dxr_l) = attn_back(
        large, index, meta_l, qkv_l[0], kwin_l, vwin_l, dheads_l, lse_l, xl, halo_l,
        lb_norms, lb_qkv, dmid_l, vec_l,
    )
    sum_c.ins = after(dx_l, sum_c.ins)
    sum_c.fold(1)
    sum_e.ins = after((dx_l, sum_c.ins[0]), sum_e.ins)
    sum_e.fold(2)
    dheads_s = after((sum_e.ins[0], sum_c.ins[0]), dheads_s)
    at_qs, pack_qs, (dx_s, dxl_s, dxr_s) = attn_back(
        small, index, meta_s, qkv_s[0], kwin_s, vwin_s, dheads_s, lse_s, xs, halo_s,
        sb_norms, sb_qkv, dmid_s, vec_s,
    )

    sum_q = Sum(index, [pack_ql, pack_qs])
    sum_c.ins = after(dx_s, sum_c.ins)
    sum_c.fold(2)
    sum_e.ins = after(dx_s, sum_e.ins)

    def from_sides(left, right):
        count = lax.axis_size("head")
        return (
            lax.ppermute(right, "head", [(i, i + 1) for i in range(count - 1)]),
            lax.ppermute(left, "head", [(i + 1, i) for i in range(count - 1)]),
        )

    grad_xl, grad_xs = call(
        functools.partial(settle_kernel, (large, small)),
        (
            sds((large.n, wl), BF16),
            sds((ws, small.n) if small.turned else (small.n, ws), BF16),
        ),
        (dx_l, *from_sides(dxl_l, dxr_l), dx_s, *from_sides(dxl_s, dxr_s)),
    )

    def unpack(kernel, outs, halves, rows):
        return call(
            kernel,
            outs,
            (index, *halves),
            [SMEM, ANY, ANY],
            [pltpu.VMEM((r, 128), BF16) for r in rows] + [pltpu.SemaphoreType.DMA((2 * len(rows),))],
        )

    count = len(stages())
    sum_c.folds(3, count)
    sum_e.folds(3, count)
    sum_q.folds(1, count)
    half_c, half_e, half_q = sum_c.joins(), sum_e.joins(), sum_q.joins()
    brs = (large, small)
    outs = []
    for br in brs:
        outs += [
            sds((br.w, br.w), F32),
            sds((br.w, br.f), F32),
            sds((br.w, br.f) if br.turned else (br.f, br.w), F32),
        ]
    o_l, u_l, d_l, o_s, u_s, d_s = unpack(
        functools.partial(unpack_ffn_kernel, brs, (at_fl, at_fs)),
        tuple(outs),
        half_e,
        (at_fl["rows"], at_fs["rows"]),
    )
    outs = []
    for cx in cxs:
        wa, wb = cx.wa, cx.wb
        less, more = min(wa, wb), max(wa, wb)
        outs += [
            sds((2, wa + 2 * wb), F32),
            sds((less, more), F32),
            sds((wb, wb), F32),
            sds((wb, 2 * wb), F32),
            sds((wb, wb), F32),
            sds((less, more), F32),
            sds((wa + 2 * wb,), F32),
        ]
    crossed = unpack(
        functools.partial(unpack_cross_kernel, cxs, at_c), tuple(outs), half_c, (rows_c,)
    )
    outs = []
    for br in brs:
        outs += [
            sds((br.w, 3 * br.w), F32),
            sds((2, 2, br.w), F32),
            sds((2, br.w), F32),
            sds((br.f,), F32),
        ]
    q_l, norms_l, bias_l, upbias_l, q_s, norms_s, bias_s, upbias_s = unpack(
        functools.partial(unpack_qkv_kernel, brs, (at_ql, at_qs)),
        tuple(outs),
        half_q,
        (at_ql["rows"], at_qs["rows"]),
    )
    fl, fs = list(crossed[:7]), list(crossed[7:])
    fl[1], fs[5] = fl[1].T, fs[5].T
    if small.turned:
        out_s, grad_xs, d_s = out_s.T, grad_xs.T, d_s.T
    return (
        out_l[None],
        out_s[None],
        grad_xl[None],
        grad_xs[None],
        norms_l,
        q_l,
        o_l,
        u_l,
        d_l,
        bias_l,
        upbias_l,
        norms_s,
        q_s,
        o_s,
        u_s,
        d_s,
        bias_s,
        upbias_s,
        *fl,
        *fs,
    )


def solution(mesh):
    rows = P("dp", "head", None)
    return jax.shard_map(
        on_device,
        mesh=mesh,
        in_specs=(P("dp", None),) * 2 + (rows,) * 4 + (P(),) * 28,
        out_specs=(rows,) * 4 + (P(),) * 28,
        check_vma=False,
    )
```

```python
import functools
import math

import jax
import jax.numpy as jnp
from jax import lax
from jax.experimental import pallas as pl
from jax.experimental.pallas import tpu as pltpu
from jax.sharding import PartitionSpec as P

HEADS = 6
IMGS = 10
ROWS = 16
MOST_L = 197
MOST_S = 401
EPS = 1e-6
NEG = -1e30
LOG2E = math.log2(math.e)
F32 = jnp.float32
BF16 = jnp.bfloat16
VMEM = pl.BlockSpec(memory_space=pltpu.VMEM)
SMEM = pl.BlockSpec(memory_space=pltpu.SMEM)
ANY = pl.BlockSpec(memory_space=pl.ANY)
HBM = pl.BlockSpec(memory_space=pltpu.HBM)


COSTLY = 40 * 10**6
SCHEDULE = (
    "F", "loop_s", "post_s", "F", "G", "loop_l", "F", "post_l", "F", "Q", "f", "q", "f", "q", "q",
    "q", "dx", "f", "q", "out_f", "q", "out_q",
)
ORDER = []


def round_up(value, unit):
    return -(-value // unit) * unit


class Branch:
    def __init__(self, rows, width, hidden, most, before=0):
        self.n = rows
        self.w = width
        self.f = hidden
        self.dh = width // HEADS
        self.halo = round_up(most - 1, 16)
        self.kw = self.halo + 16
        self.r = rows + 2 * self.halo
        self.t = rows // 128
        self.cols = round_up(width, 128) // 128
        self.at = before
        self.end = before + self.halo * self.cols
        self.scale = self.dh ** (-0.5)
        self.turned = width % 128 != 0
        if width % 128 == 0:
            per = 128 // self.dh
            self.groups = [
                (i * 128, (i + 1) * 128, list(range(i * per, (i + 1) * per)))
                for i in range(width // 128)
            ]
        else:
            self.groups = [(0, width, list(range(HEADS)))]


def nn(a, b):
    return jnp.dot(a, b, preferred_element_type=F32)


def nt(a, b):
    return lax.dot_general(a, b, (((1,), (1,)), ((), ())), preferred_element_type=F32)


def tn(a, b):
    return lax.dot_general(a, b, (((0,), (0,)), ((), ())), preferred_element_type=F32)


def split(x):
    high = x.astype(BF16)
    return high, (x - high.astype(F32)).astype(BF16)


def nn_exact(a, b):
    return jnp.dot(a, b, preferred_element_type=F32, precision=lax.Precision.HIGHEST)


def nt_exact(a, b):
    return lax.dot_general(
        a,
        b,
        (((1,), (1,)), ((), ())),
        preferred_element_type=F32,
        precision=lax.Precision.HIGHEST,
    )


def normalize(x):
    center = x - jnp.mean(x, axis=-1, keepdims=True)
    rstd = lax.rsqrt(jnp.mean(center * center, axis=-1, keepdims=True) + EPS)
    return center * rstd, rstd


def norm_grad(unit, rstd, gain, upstream):
    scaled = upstream * gain
    mean_one = jnp.mean(scaled, axis=-1, keepdims=True)
    mean_two = jnp.mean(scaled * unit, axis=-1, keepdims=True)
    return (scaled - mean_one - unit * mean_two) * rstd


def col_sum(x):
    return jnp.sum(x, axis=0, keepdims=True)


def gelu_pair(x):
    cumulative = 0.5 * (1.0 + lax.erf(x * 0.7071067811865476))
    density = jnp.exp(-0.5 * x * x) * 0.3989422804014327
    return x * cumulative, cumulative + x * density


def iota(shape, dim):
    return lax.broadcasted_iota(jnp.int32, shape, dim)


def padded_bytes(item):
    *lead, rows, cols = (1, 1, *item.shape)
    unit = 32 // item.dtype.itemsize
    return math.prod(lead) * round_up(rows, unit) * round_up(cols, 128) * item.dtype.itemsize


class FarIn:
    def __init__(self, far, near, sem):
        self.copy = pltpu.make_async_copy(far, near, sem)
        self.copy.start()
        self.near = near
        self.landed = False

    def land(self):
        if not self.landed:
            self.landed = True
            self.copy.wait()

    @property
    def shape(self):
        return self.near.shape

    def __getitem__(self, where):
        self.land()
        return self.near[where]


class FarOut:
    def __init__(self, far, near, sem):
        self.copy = pltpu.make_async_copy(near, far, sem)
        self.near = near
        self.sent = False

    def send(self):
        if not self.sent:
            self.sent = True
            self.copy.start()

    @property
    def shape(self):
        return self.near.shape

    def __getitem__(self, where):
        return self.near[where]

    def __setitem__(self, where, value):
        self.near[where] = value


def land(*refs):
    for ref in refs:
        if isinstance(ref, FarIn):
            ref.land()


def send(*refs):
    for ref in refs:
        if isinstance(ref, FarOut):
            ref.send()


def call(
    kernel,
    outs,
    ins,
    in_specs=None,
    scratch=(),
    flops=0,
    moved=1,
    out_specs=None,
    spare=10,
    far=(),
    far_out=(),
):
    in_specs = [VMEM] * len(ins) if in_specs is None else list(in_specs)
    flat = list(jax.tree.leaves(outs))
    specs = [VMEM] * len(flat) if out_specs is None else list(jax.tree.leaves(out_specs))
    for i in far:
        in_specs[i] = HBM
    for i in far_out:
        specs[i] = HBM
    held = list(zip(ins, in_specs)) + list(zip(flat, specs))
    need = sum(padded_bytes(item) for item, spec in held if spec is VMEM)
    near = [pltpu.VMEM(ins[i].shape, ins[i].dtype) for i in far]
    near += [pltpu.VMEM(flat[i].shape, flat[i].dtype) for i in far_out]
    scratch = list(scratch)
    for item in scratch + near:
        if getattr(item, "memory_space", None) == pltpu.VMEM:
            need += padded_bytes(sds(item.shape, jnp.dtype(item.dtype)))
    count = len(near)

    def wrapped(*refs):
        refs = list(refs)
        if not count:
            return kernel(*refs)
        refs, held, sems = refs[: -count - 1], refs[-count - 1 : -1], refs[-1]
        found = []
        for k, i in enumerate(far):
            refs[i] = FarIn(refs[i], held[k], sems.at[k])
            found.append(refs[i])
        for k, i in enumerate(far_out, len(far)):
            i += len(ins)
            refs[i] = FarOut(refs[i], held[k], sems.at[k])
            found.append(refs[i])
        kernel(*refs)
        land(*found)
        send(*found)
        for ref in found:
            if isinstance(ref, FarOut):
                ref.copy.wait()

    extra = near + [pltpu.SemaphoreType.DMA((count,))] if count else []
    ins = list(ins)
    if ORDER:
        i = next(i for i, spec in enumerate(in_specs) if spec is not SMEM)
        ins[i] = after(ORDER[-1], ins[i])
    for i in far:
        ins[i] = pltpu.with_memory_space_constraint(ins[i], pltpu.HBM)
    for i in far_out:
        flat[i] = pltpu.HBM(flat[i].shape, flat[i].dtype)
    results = pl.pallas_call(
        wrapped,
        out_shape=jax.tree.unflatten(jax.tree.structure(outs), flat),
        in_specs=in_specs,
        out_specs=jax.tree.unflatten(jax.tree.structure(outs), specs),
        scratch_shapes=scratch + extra,
        compiler_params=pltpu.CompilerParams(
            vmem_limit_bytes=min(need + spare * 2**20, 60 * 2**20)
        ),
        cost_estimate=pl.CostEstimate(flops=moved * 500, bytes_accessed=moved, transcendentals=0),
    )(*ins)
    if ORDER:
        ORDER[:] = [min(jax.tree.leaves(results), key=lambda item: item.size)]
    return results


def after(first, then):
    return lax.optimization_barrier((first, then))[1]


def sds(shape, dtype):
    return jax.ShapeDtypeStruct(shape, dtype)


def mat_rows(rows, cols):
    return rows * cols // 128


def put_halo(br, ref, value):
    low = value.astype(BF16)
    for i in range(br.cols):
        part = low[:, i * 128 : min((i + 1) * 128, br.w)]
        if part.shape[1] < 128:
            part = jnp.concatenate([part, jnp.zeros((br.halo, 128 - part.shape[1]), BF16)], axis=1)
        ref[br.at + i * br.halo : br.at + (i + 1) * br.halo, :] = part


def get_halo(br, ref):
    parts = [
        ref[br.at + i * br.halo : br.at + (i + 1) * br.halo, : min(128, br.w - i * 128)]
        for i in range(br.cols)
    ]
    return jnp.concatenate(parts, axis=1).astype(F32)


def vec_rows(widths):
    return round_up(sum(round_up(w, 128) // 128 for w in widths), 16)


def layout(items, unit=32):
    at, row = {}, 0
    for name, rows in items:
        at[name] = row
        row += rows
    return at, round_up(row, unit)


def pack_mat(ref, at, rows, cols, value):
    low = value.astype(BF16)
    full = cols // 128
    for i in range(full):
        ref[at + i * rows : at + (i + 1) * rows, :] = low[:, i * 128 : (i + 1) * 128]
    if cols % 128:
        tail = low[:, full * 128 :]
        at = at + full * rows
        half = rows // 2
        ref[at : at + half, :] = jnp.concatenate([tail[:half], tail[half:]], axis=1)


def unpack_mat(ref, at, rows, cols, out):
    full = cols // 128
    for i in range(full):
        out[:, i * 128 : (i + 1) * 128] = ref[at + i * rows : at + (i + 1) * rows, :].astype(F32)
    if cols % 128:
        at = at + full * rows
        half = rows // 2
        block = ref[at : at + half, :].astype(F32)
        out[:half, full * 128 :] = block[:, :64]
        out[half:, full * 128 :] = block[:, 64:]


def vec_block(values):
    pieces = []
    for value in values:
        width = value.shape[1]
        for i in range(0, width, 128):
            piece = value[:, i : min(i + 128, width)]
            if piece.shape[1] < 128:
                piece = jnp.concatenate(
                    [piece, jnp.zeros((1, 128 - piece.shape[1]), F32)], axis=1
                )
            pieces.append(piece)
    total = round_up(len(pieces), 16)
    if total > len(pieces):
        pieces.append(jnp.zeros((total - len(pieces), 128), F32))
    return jnp.concatenate(pieces, axis=0)


def vecs_of(block, widths):
    out, i = [], 0
    for width in widths:
        parts = []
        for j in range(0, width, 128):
            parts.append(block[i : i + 1, : min(128, width - j)])
            i += 1
        out.append(parts[0] if len(parts) == 1 else jnp.concatenate(parts, axis=1))
    return out


def emit(src_ref, outs, index, sems):
    size = src_ref.shape[0] // len(outs)
    copies = []
    for d, out in enumerate(outs):
        at = pl.multiple_of((index ^ d) * size, 16)
        copies.append(pltpu.make_async_copy(src_ref.at[pl.ds(at, size)], out, sems.at[d]))
        copies[-1].start()
    for copy in copies:
        copy.wait()


def edge_kernel(brs, xl_ref, xs_ref, last_ref, first_ref):
    for br, ref in zip(brs, (xl_ref, xs_ref)):
        put_halo(br, last_ref, ref[br.n - br.halo :, :])
        put_halo(br, first_ref, ref[: br.halo, :])


def start_kernel(
    br_l,
    br_s,
    here_ref,
    seg_l_ref,
    seg_s_ref,
    xl_ref,
    xs_ref,
    dyl_ref,
    dys_ref,
    nl_ref,
    ns_ref,
    wl_ref,
    ws_ref,
    ql_ref,
    kl_ref,
    vl_ref,
    qs_ref,
    ks_ref,
    vs_ref,
    meta_l_ref,
    meta_s_ref,
    lane_l_ref,
    lane_s_ref,
    sub_l_ref,
    sub_s_ref,
    dcls_ref,
    vector_ref,
    scalar_ref,
    sem,
):
    col = 0
    dcls_ref[...] = jnp.zeros_like(dcls_ref)
    for br, seg_ref, dy_ref, meta_ref, lane_ref, sub_ref in (
        (br_l, seg_l_ref, dyl_ref, meta_l_ref, lane_l_ref, sub_l_ref),
        (br_s, seg_s_ref, dys_ref, meta_s_ref, lane_s_ref, sub_s_ref),
    ):
        own = here_ref[0] * br.n
        seg = seg_ref[...]
        image = iota((ROWS, seg.shape[1]), 0)
        starts = jnp.sum((seg < image).astype(jnp.int32), axis=1, keepdims=True)
        ends = jnp.sum((seg <= image).astype(jnp.int32), axis=1, keepdims=True)
        starts = jnp.broadcast_to(starts, (ROWS, 128))
        ends = jnp.broadcast_to(ends, (ROWS, 128))
        lane = iota((ROWS, 128), 1)
        diagonal = (lane - (lane // ROWS) * ROWS) == iota((ROWS, 128), 0)
        lo = jnp.sum(jnp.where(diagonal, starts, 0), axis=0, keepdims=True) - own
        hi = jnp.sum(jnp.where(diagonal, ends, 0), axis=0, keepdims=True) - own
        lane_ref[...] = jnp.concatenate([lo, hi, jnp.zeros((6, 128), jnp.int32)], axis=0)
        sub_ref[...] = starts - own
        real = iota((ROWS, 128), 0) < IMGS
        first = jnp.sum(jnp.where(real & (starts <= own), 1, 0), axis=0, keepdims=True) - 1
        last = jnp.sum(jnp.where(real & (starts < own + br.n), 1, 0), axis=0, keepdims=True) - 1
        vector_ref[0:ROWS, :] = starts
        vector_ref[ROWS : ROWS + 8, :] = jnp.concatenate(
            [first, last, jnp.zeros((6, 128), jnp.int32)], axis=0
        )
        copy = pltpu.make_async_copy(vector_ref, scalar_ref, sem)
        copy.start()
        copy.wait()
        for j in range(IMGS + 1):
            meta_ref[j] = scalar_ref[j, 0]
        meta_ref[11] = own
        meta_ref[12] = scalar_ref[ROWS, 0]
        meta_ref[13] = scalar_ref[ROWS + 1, 0]
        meta_ref[14] = 0
        meta_ref[15] = 0
        pick = (iota((ROWS, br.n), 1) == (starts - own)[:, 0:1]).astype(F32).astype(BF16)
        dcls_ref[:, col : col + br.w] = nn(pick, dy_ref[...])
        col += br.w
    for x_ref, norms_ref, w_ref, outs in (
        (xl_ref, nl_ref, wl_ref, (ql_ref, kl_ref, vl_ref)),
        (xs_ref, ns_ref, ws_ref, (qs_ref, ks_ref, vs_ref)),
    ):
        width = x_ref.shape[1]
        unit, _ = normalize(x_ref[...].astype(F32))
        normed = (unit * norms_ref[0, 0:1, :] + norms_ref[0, 1:2, :]).astype(BF16)
        for i, ref in enumerate(outs):
            ref[...] = nn(normed, w_ref[:, i * width : (i + 1) * width]).astype(BF16)


def head_mask(br, head, c0, c1):
    lane = iota((1, c1 - c0), 1) + c0
    return jnp.logical_and(lane >= head * br.dh, lane < (head + 1) * br.dh)


def stack_heads(br, rows, group):
    c0, c1, heads = group
    part = rows[:, c0:c1]
    zero = jnp.zeros_like(part)
    return jnp.concatenate(
        [jnp.where(head_mask(br, h, c0, c1), part, zero) for h in heads], axis=0
    )


def image_span(br, meta_ref, j):
    base = meta_ref[11]
    lo = meta_ref[j] - base
    hi = meta_ref[j + 1] - base
    k0 = pl.multiple_of(((lo + br.halo) // 16) * 16, 16)
    t0 = jnp.maximum(lo, 0) // 128
    t1 = (jnp.minimum(hi, br.n) + 127) // 128
    return lo, hi, k0, t0, t1


def forward_kernel(
    br,
    meta_ref,
    x_ref,
    xl_ref,
    xr_ref,
    q_ref,
    k_ref,
    v_ref,
    norms_ref,
    wqkv_ref,
    wout_ref,
    wup_ref,
    wdown_ref,
    bias_ref,
    upbias_ref,
    sub_ref,
    y_ref,
    cls_ref,
    kwin_ref,
    vwin_ref,
    lse_ref,
    ho_ref,
    mid_ref,
    n2_ref,
    hid_ref,
    slope_ref,
    ot_ref,
):
    n, w, f, dh, halo = br.n, br.w, br.f, br.dh, br.halo
    for ref, at in ((xl_ref, 0), (xr_ref, halo + n)):
        unit, _ = normalize(get_halo(br, ref))
        normed = (unit * norms_ref[0, 0:1, :] + norms_ref[0, 1:2, :]).astype(BF16)
        kwin_ref[at : at + halo, :] = nn(normed, wqkv_ref[:, w : 2 * w]).astype(BF16)
        vwin_ref[at : at + halo, :] = nn(normed, wqkv_ref[:, 2 * w :]).astype(BF16)
    kwin_ref[halo : halo + n, :] = k_ref[...]
    vwin_ref[halo : halo + n, :] = v_ref[...]
    send(vwin_ref)
    ot_ref[...] = jnp.zeros_like(ot_ref)
    lse_ref[...] = jnp.zeros(lse_ref.shape, F32)
    factor = br.scale * LOG2E
    land(q_ref)

    def image(j, carry):
        lo, hi, k0, t0, t1 = image_span(br, meta_ref, j)
        keys = kwin_ref[pl.ds(k0, br.kw), :]
        values_t = vwin_ref[pl.ds(k0, br.kw), :].T
        row = iota((br.kw, 128), 0) + (k0 - br.halo)
        mask = jnp.logical_and(row >= lo, row < hi)

        def tile(t, carry):
            rows = q_ref[pl.ds(pl.multiple_of(t * 128, 128), 128), :]
            lane = iota((1, 128), 1) + t * 128
            inside = jnp.logical_and(lane >= lo, lane < hi)
            for group in br.groups:
                c0, c1, heads = group
                scores = nt(keys[:, c0:c1], stack_heads(br, rows, group))
                for i, h in enumerate(heads):
                    s = jnp.where(mask, scores[:, i * 128 : (i + 1) * 128] * factor, NEG)
                    top = jnp.max(s, axis=0, keepdims=True)
                    p = jnp.exp2(s - top)
                    total = col_sum(p)
                    o = nn(values_t[h * dh : (h + 1) * dh, :], p.astype(BF16))
                    ot_ref[t, h * dh : (h + 1) * dh, :] += o * jnp.where(inside, 1.0 / total, 0.0)
                    lse_ref[t, h : h + 1, :] = jnp.where(
                        inside, top + jnp.log2(total), lse_ref[t, h : h + 1, :]
                    )
            return carry

        return lax.fori_loop(t0, t1, tile, carry)

    lax.fori_loop(meta_ref[12], meta_ref[13] + 1, image, 0)
    send(kwin_ref, lse_ref)
    for t in range(br.t):
        ho_ref[t * 128 : (t + 1) * 128, :] = ot_ref[t].T.astype(BF16)
    mid = x_ref[...].astype(F32) + (nn(ho_ref[...], wout_ref[...]) + bias_ref[0:1, :])
    mid_ref[...] = mid
    unit, _ = normalize(mid)
    normed = (unit * norms_ref[1, 0:1, :] + norms_ref[1, 1:2, :]).astype(BF16)
    n2_ref[...] = normed
    send(ho_ref, mid_ref, n2_ref)
    total = mid + bias_ref[1:2, :]
    step = 256
    upbias = upbias_ref[...].reshape(1, f)
    for c in range(0, f, step):
        pre = nn(normed, wup_ref[:, c : c + step]) + upbias[:, c : c + step]
        act, slope = gelu_pair(pre)
        act = act.astype(BF16)
        hid_ref[:, c : c + step] = act
        slope_ref[:, c : c + step] = slope.astype(BF16)
        if br.turned:
            total = total + nt(act, wdown_ref[:, c : c + step])
        else:
            total = total + nn(act, wdown_ref[c : c + step, :])
    send(hid_ref, slope_ref)
    y = total.astype(BF16)
    y_ref[...] = y
    pick = (iota((ROWS, n), 1) == sub_ref[:, 0:1]).astype(F32).astype(BF16)
    cls_ref[...] = nn(pick, y)


def ffn_back_kernel(
    br,
    at,
    index_ref,
    lane_ref,
    dy_ref,
    cross_ref,
    dcls_ref,
    hid_ref,
    slope_ref,
    n2_ref,
    mid_ref,
    ho_ref,
    norms_ref,
    wout_ref,
    wup_ref,
    wdown_ref,
    keep_ref,
    send_ref,
    dmid_ref,
    dheads_ref,
    vec_ref,
    pack_ref,
    sems,
):
    n, w, f = br.n, br.w, br.f
    c0 = at["col"]
    cls = dcls_ref[:, c0 : c0 + w].astype(BF16)
    hit = (iota((n, 128), 0) == lane_ref[0:1, :]).astype(F32)
    hit = jnp.where(iota((1, 128), 1) < IMGS, hit, 0.0)
    first = jnp.sum(hit, axis=1, keepdims=True) > 0.5
    placed = nn(hit[:, :ROWS].astype(BF16), cls)
    gy = jnp.where(first, placed, dy_ref[...].astype(F32) + cross_ref[...]).astype(BF16)
    gy_float = gy.astype(F32)
    dn2 = jnp.zeros((n, w), F32)
    step = 256
    upbias = []
    normed = n2_ref[...]
    if br.turned:
        gy_t = gy.T
    normed_t = normed.T
    if at["rows"] > at["end"]:
        pack_ref[at["end"] :, :] = jnp.zeros((at["rows"] - at["end"], 128), BF16)
    for i, c in enumerate(range(0, f, step)):
        if br.turned:
            dpre = nn(gy, wdown_ref[:, c : c + step])
        else:
            dpre = nt(gy, wdown_ref[c : c + step, :])
        dpre = (dpre * slope_ref[:, c : c + step].astype(F32)).astype(BF16)
        upbias.append(col_sum(dpre.astype(F32)))
        pack_mat(pack_ref, at["up"] + i * mat_rows(w, step), w, step, nn(normed_t, dpre))
        dn2 = dn2 + nt(dpre, wup_ref[:, c : c + step])
        if br.turned:
            down = nn(gy_t, hid_ref[:, c : c + step])
            pack_mat(pack_ref, at["down"] + i * mat_rows(w, step), w, step, down)
        else:
            down = tn(hid_ref[:, c : c + step], gy)
            for k in range(w // 128):
                a = at["down"] + k * f + c
                pack_ref[a : a + step, :] = down[:, k * 128 : (k + 1) * 128].astype(BF16)
    unit, rstd = normalize(mid_ref[...])
    dmid = gy_float + norm_grad(unit, rstd, norms_ref[1, 0:1, :], dn2)
    dmid_ref[...] = dmid
    dattn = dmid.astype(BF16)
    pack_mat(pack_ref, at["out"], w, w, tn(ho_ref[...], dattn))
    dheads_ref[...] = nt(dattn, wout_ref[...]).astype(BF16)
    vec_ref[...] = vec_block(
        [col_sum(dn2 * unit), col_sum(dn2), col_sum(dattn.astype(F32)), col_sum(gy_float)] + upbias
    )
    emit(pack_ref, (keep_ref, send_ref), index_ref[0], sems)


def attn_loop_kernel(
    br,
    meta_ref,
    q_ref,
    kwin_ref,
    vwin_ref,
    dheads_ref,
    lse_ref,
    dk_ref,
    dv_ref,
    dq_ref,
    dqt_ref,
    p_ref,
    ds_ref,
):
    dh = br.dh
    dk_ref[...] = jnp.zeros(dk_ref.shape, F32)
    dv_ref[...] = jnp.zeros_like(dv_ref)
    dqt_ref[...] = jnp.zeros_like(dqt_ref)
    factor = br.scale * LOG2E
    land(q_ref, kwin_ref, vwin_ref, dheads_ref, lse_ref)

    def image(j, carry):
        lo, hi, k0, t0, t1 = image_span(br, meta_ref, j)
        span = pl.ds(k0, br.kw)
        keys = kwin_ref[span, :]
        keys_t = keys.T
        values = vwin_ref[span, :]
        row = iota((br.kw, 128), 0) + (k0 - br.halo)
        mask = jnp.logical_and(row >= lo, row < hi)

        def tile(t, carry):
            here = pl.ds(pl.multiple_of(t * 128, 128), 128)
            rows = q_ref[here, :]
            outs = dheads_ref[here, :]
            lane = iota((1, 128), 1) + t * 128
            inside = jnp.logical_and(lane >= lo, lane < hi)
            for group in br.groups:
                c0, c1, heads = group
                queries = stack_heads(br, rows, group)
                upstream = stack_heads(br, outs, group)
                scores = nt(keys[:, c0:c1], queries)
                dprobs = nt(values[:, c0:c1], upstream)
                for i, h in enumerate(heads):
                    part = slice(i * 128, (i + 1) * 128)
                    lse = jnp.where(inside, lse_ref[t, h : h + 1, :], -NEG)
                    p = jnp.exp2(scores[:, part] * factor - lse)
                    p = jnp.where(mask, p, 0.0)
                    dp = dprobs[:, part]
                    ds = (p * (dp - col_sum(p * dp))).astype(BF16)
                    p_ref[:, part] = p.astype(BF16)
                    ds_ref[:, part] = ds
                    dqt_ref[t, h * dh : (h + 1) * dh, :] += nn(
                        keys_t[h * dh : (h + 1) * dh, :], ds
                    )
                size = 128 * len(heads)
                dv_ref[span, c0:c1] += nn(p_ref[:, :size], upstream)
                dk_ref[span, c0:c1] += nn(ds_ref[:, :size], queries)
            return carry

        return lax.fori_loop(t0, t1, tile, carry)

    lax.fori_loop(meta_ref[12], meta_ref[13] + 1, image, 0)
    for t in range(br.t):
        dq_ref[t * 128 : (t + 1) * 128, :] = (dqt_ref[t].T * br.scale).astype(BF16)


def attn_post_kernel(
    br,
    at,
    index_ref,
    x_ref,
    xl_ref,
    xr_ref,
    norms_ref,
    wqkv_ref,
    dmid_ref,
    vec_ref,
    dk_ref,
    dv_ref,
    dq_ref,
    *refs,
):
    before, refs = refs[:-8], refs[-8:]
    keep_ref, send_ref, dx_ref, dxl_ref, dxr_ref, normed_ref, pack_ref, sems = refs
    for ref, out in zip(before, (dxl_ref, dxr_ref)):
        out[: br.at, :] = ref[...]
    n, w, halo = br.n, br.w, br.halo
    dk = (dk_ref[...] * br.scale).astype(BF16)
    dv = dv_ref[...].astype(BF16)
    gain, shift = norms_ref[0, 0:1, :], norms_ref[0, 1:2, :]
    dgain = jnp.zeros((1, w), F32)
    dshift = jnp.zeros((1, w), F32)
    for ref, lo, size, out in (
        (xl_ref, 0, halo, dxl_ref),
        (x_ref, halo, n, dx_ref),
        (xr_ref, halo + n, halo, dxr_ref),
    ):
        rows = ref[...].astype(F32) if ref is x_ref else get_halo(br, ref)
        unit, rstd = normalize(rows)
        normed_ref[lo : lo + size, :] = (unit * gain + shift).astype(BF16)
        up = nt(dk[lo : lo + size], wqkv_ref[:, w : 2 * w])
        up = up + nt(dv[lo : lo + size], wqkv_ref[:, 2 * w :])
        if out is dx_ref:
            up = up + nt(dq_ref[...], wqkv_ref[:, :w])
        dgain = dgain + col_sum(up * unit)
        dshift = dshift + col_sum(up)
        dx = norm_grad(unit, rstd, gain, up)
        if out is dx_ref:
            out[...] = dx + dmid_ref[...]
        else:
            put_halo(br, out, dx)
    whole = jnp.concatenate(
        [
            tn(normed_ref[halo : halo + n, :], dq_ref[...]),
            tn(normed_ref[...], dk),
            tn(normed_ref[...], dv),
        ],
        axis=1,
    )
    pack_mat(pack_ref, at["qkv"], w, 3 * w, whole)
    block = vec_block([dgain, dshift])
    pack_ref[at["vec1"] : at["vec1"] + block.shape[0], :] = block.astype(BF16)
    pack_ref[at["vec2"] : at["vec2"] + vec_ref.shape[0], :] = vec_ref[...].astype(BF16)
    if at["rows"] > at["end"]:
        pack_ref[at["end"] :, :] = jnp.zeros((at["rows"] - at["end"], 128), BF16)
    emit(pack_ref, (keep_ref, send_ref), index_ref[0], sems)


class Cross:
    def __init__(self, wa, wb, rows_b):
        self.wa = wa
        self.wb = wb
        self.dh = wb // HEADS
        self.n = rows_b
        self.scale = self.dh ** (-0.5)
        self.proj = nt if wa > wb else nn
        self.proj_back = nn if wa > wb else nt
        self.back = nn if wa > wb else nt
        self.back_back = nt if wa > wb else nn

    def by_head(self):
        head = iota((128, self.wb), 0) // ROWS
        col = iota((128, self.wb), 1)
        return jnp.logical_and(col >= head * self.dh, col < (head + 1) * self.dh).astype(F32)

    def by_image(self):
        lane = iota((ROWS, 128), 1)
        return jnp.logical_and(
            lane - (lane // ROWS) * ROWS == iota((ROWS, 128), 0), lane < HEADS * ROWS
        ).astype(F32)


def spread(cx, low_rows):
    return jnp.concatenate([low_rows] * 8, axis=0) * cx.by_head().astype(low_rows.dtype)


def gather_heads(cx, wide):
    kept = wide * cx.by_head()
    total = kept[0:ROWS]
    for h in range(1, HEADS):
        total = total + kept[h * ROWS : (h + 1) * ROWS]
    return total


def to_lane(cx, rows):
    return col_sum(cx.by_image() * nt_exact(rows, cx.by_head()))


def from_lane(cx, lane):
    return nn_exact(cx.by_image() * lane, cx.by_head())


def cross_query(cx, cls, norms_ref, proj_ref, query_ref, keyval_ref, bias_ref, qa_ref, qb_ref):
    wa, wb = cx.wa, cx.wb
    unit_a, rstd_a = normalize(cls)
    lifted = unit_a * norms_ref[0:1, :wa] + norms_ref[1:2, :wa]
    act, slope = gelu_pair(lifted)
    act = act.astype(BF16)
    bias = bias_ref[...].reshape(1, bias_ref.shape[0])[:, :wb]
    moved = cx.proj(act, proj_ref[...]) + bias
    gain, shift = norms_ref[0:1, wa : wa + wb], norms_ref[1:2, wa : wa + wb]
    unit_q, rstd_q = normalize(moved)
    query_in = (unit_q * gain + shift).astype(BF16)
    fquery = nn(query_in, query_ref[...]).astype(BF16)
    kself = nn(query_in, keyval_ref[:, :wb]).astype(BF16)
    vself = nn(query_in, keyval_ref[:, wb:]).astype(BF16)
    for i, item in enumerate((unit_a, slope, act, jnp.broadcast_to(rstd_a, unit_a.shape))):
        qa_ref[i] = item.astype(F32)
    for i, item in enumerate(
        (moved, unit_q, query_in, fquery, kself, vself, jnp.broadcast_to(rstd_q, moved.shape))
    ):
        qb_ref[i] = item.astype(F32)
    return fquery


def allowed_rows(cx, lane_ref):
    row = iota((cx.n, 128), 0)
    return jnp.logical_and(row > lane_ref[0:1, :], row < lane_ref[1:2, :])


def keys_kernel(cxs, ys_ref, fln_ref, yl_ref, fsn_ref, ks_ref, kl_ref):
    for cx, y_ref, norms_ref, out_ref in (
        (cxs[0], ys_ref, fln_ref, ks_ref),
        (cxs[1], yl_ref, fsn_ref, kl_ref),
    ):
        wa, wb = cx.wa, cx.wb
        unit, _ = normalize(y_ref[...].astype(F32))
        out_ref[...] = (
            unit * norms_ref[0:1, wa : wa + wb] + norms_ref[1:2, wa : wa + wb]
        ).astype(BF16)


def cross_front_kernel(
    cxs,
    c0_ref,
    c1_ref,
    c2_ref,
    c3_ref,
    lane_s_ref,
    lane_l_ref,
    key_s_ref,
    key_l_ref,
    fln_ref,
    flp_ref,
    flq_ref,
    flk_ref,
    flb_ref,
    fsn_ref,
    fsp_ref,
    fsq_ref,
    fsk_ref,
    fsb_ref,
    part_ref,
    sc_l_ref,
    sc_s_ref,
    ab_l_ref,
    ab_s_ref,
    qa_l_ref,
    qb_l_ref,
    qa_s_ref,
    qb_s_ref,
):
    cls = c0_ref[...] + c1_ref[...] + c2_ref[...] + c3_ref[...]
    wl, ws = cxs[0].wa, cxs[1].wa
    col = 0
    stats = []
    for cx, rows, key_ref, lane_ref, keyval_ref, weights, kept, sc_ref, ab_ref in (
        (
            cxs[0],
            cls[:, :wl],
            key_s_ref,
            lane_s_ref,
            flk_ref,
            (fln_ref, flp_ref, flq_ref, flk_ref, flb_ref),
            (qa_l_ref, qb_l_ref),
            sc_l_ref,
            ab_l_ref,
        ),
        (
            cxs[1],
            cls[:, wl : wl + ws],
            key_l_ref,
            lane_l_ref,
            fsk_ref,
            (fsn_ref, fsp_ref, fsq_ref, fsk_ref, fsb_ref),
            (qa_s_ref, qb_s_ref),
            sc_s_ref,
            ab_s_ref,
        ),
    ):
        fquery = cross_query(cx, rows, *weights, *kept)
        absorbed = nt(spread(cx, fquery), keyval_ref[:, : cx.wb]).astype(BF16)
        ab_ref[...] = absorbed
        key = key_ref[...]
        allowed = allowed_rows(cx, lane_ref)
        scores = jnp.where(allowed, nt(key, absorbed) * (cx.scale * LOG2E), NEG)
        sc_ref[...] = scores
        top = jnp.max(scores, axis=0, keepdims=True)
        p = jnp.where(allowed, jnp.exp2(scores - top), 0.0)
        high, low = split(p)
        mixed_high, mixed_low = split(tn(high, key) + tn(low, key))
        value_part = keyval_ref[:, cx.wb :]
        out = gather_heads(cx, nn(mixed_high, value_part) + nn(mixed_low, value_part))
        part_ref[0:ROWS, col : col + cx.wb] = out
        col += cx.wb
        stats += [top, col_sum(p)]
    width = part_ref.shape[1]
    part_ref[0:ROWS, col:] = jnp.zeros((ROWS, width - col), F32)
    part_ref[ROWS:, :] = jnp.zeros((8, width), F32)
    part_ref[ROWS : ROWS + 4, :128] = jnp.concatenate(stats, axis=0)


def cross_back_kernel(
    cxs,
    share,
    g0_ref,
    g1_ref,
    g2_ref,
    g3_ref,
    p0_ref,
    p1_ref,
    p2_ref,
    p3_ref,
    lane_s_ref,
    lane_l_ref,
    ys_ref,
    yl_ref,
    key_s_ref,
    key_l_ref,
    sc_l_ref,
    sc_s_ref,
    ab_l_ref,
    ab_s_ref,
    qb_l_ref,
    qb_s_ref,
    fln_ref,
    flk_ref,
    flo_ref,
    flw_ref,
    flb_ref,
    fsn_ref,
    fsk_ref,
    fso_ref,
    fsw_ref,
    fsb_ref,
    dq_ref,
    cross_s_ref,
    cross_l_ref,
    out_s_ref,
    out_l_ref,
    rt_l_ref,
    rt_s_ref,
    gk_l_ref,
    gk_s_ref,
    vec_ref,
):
    dcls = g0_ref[...] + g1_ref[...] + g2_ref[...] + g3_ref[...]
    parts = [p0_ref, p1_ref, p2_ref, p3_ref]
    vecs = []
    col_b = 0
    col_a = 0
    for index, (
        cx,
        key_ref,
        y_ref,
        lane_ref,
        lane_a_ref,
        a_ref,
        out_ref,
        cross_ref,
        sc_ref,
        ab_ref,
        qb_ref,
        rt_ref,
        gk_ref,
        weights,
    ) in enumerate(
        (
            (
                cxs[0],
                key_s_ref,
                ys_ref,
                lane_s_ref,
                lane_l_ref,
                yl_ref,
                out_l_ref,
                cross_s_ref,
                sc_l_ref,
                ab_l_ref,
                qb_l_ref,
                rt_l_ref,
                gk_l_ref,
                (fln_ref, flk_ref, flo_ref, flw_ref, flb_ref),
            ),
            (
                cxs[1],
                key_l_ref,
                yl_ref,
                lane_l_ref,
                lane_s_ref,
                ys_ref,
                out_s_ref,
                cross_l_ref,
                sc_s_ref,
                ab_s_ref,
                qb_s_ref,
                rt_s_ref,
                gk_s_ref,
                (fsn_ref, fsk_ref, fso_ref, fsw_ref, fsb_ref),
            ),
        )
    ):
        norms_ref, keyval_ref, wout_ref, wback_ref, bias_ref = weights
        wa, wb = cx.wa, cx.wb
        bias = bias_ref[...].reshape(1, bias_ref.shape[0])
        moved, fquery, kself, vself = qb_ref[0], qb_ref[3], qb_ref[4], qb_ref[5]
        self_score = to_lane(cx, fquery * kself) * (cx.scale * LOG2E)
        tops = [p[ROWS + 2 * index : ROWS + 2 * index + 1, :128] for p in parts]
        sums = [p[ROWS + 2 * index + 1 : ROWS + 2 * index + 2, :128] for p in parts]
        top = self_score
        for item in tops:
            top = jnp.maximum(top, item)
        own = jnp.exp2(self_score - top)
        total = own
        weights_of = []
        for item, amount in zip(tops, sums):
            weight = jnp.exp2(item - top)
            weights_of.append(weight)
            total = total + amount * weight
        inverse = 1.0 / total
        p_self = own * inverse
        fheads = from_lane(cx, p_self) * vself
        for part, weight in zip(parts, weights_of):
            fheads = fheads + part[0:ROWS, col_b : col_b + wb] * from_lane(cx, weight * inverse)
        fheads_low = fheads.astype(BF16)
        joined = moved + (nn(fheads_low, wout_ref[...]) + bias[:, wb : 2 * wb])
        unit_r, rstd_r = normalize(joined)
        gain_r = norms_ref[0:1, wa + wb :]
        reverted = unit_r * gain_r + norms_ref[1:2, wa + wb :]
        act_r, slope_r = gelu_pair(reverted)
        act_r = act_r.astype(BF16)
        back = cx.back(act_r, wback_ref[...]) + bias[:, 2 * wb :]
        n_a = a_ref.shape[0]
        hit = (iota((n_a, 128), 0) == lane_a_ref[0:1, :]).astype(F32)
        hit = jnp.where(iota((1, 128), 1) < IMGS, hit, 0.0)
        first = jnp.sum(hit, axis=1, keepdims=True) > 0.5
        placed = nn(hit[:, :ROWS].astype(BF16), back.astype(BF16))
        result = jnp.where(first, placed, a_ref[...].astype(F32))
        out_ref[...] = (result.T if wa % 128 else result).astype(BF16)
        dback = dcls[:, col_a : col_a + wa]
        dback_low = dback.astype(BF16)
        drev = cx.back_back(dback_low, wback_ref[...]) * slope_r
        djoined = norm_grad(unit_r, rstd_r, gain_r, drev)
        dattn = djoined.astype(BF16)
        dheads_low = nt(dattn, wout_ref[...]).astype(BF16)
        dheads = dheads_low.astype(F32)
        delta = to_lane(cx, dheads * fheads)
        ds_self = p_self * (to_lane(cx, dheads * vself) - delta)
        ds_self_rows = from_lane(cx, ds_self.astype(BF16).astype(F32))
        p_self_rows = from_lane(cx, p_self.astype(BF16).astype(F32))
        upstream = spread(cx, dheads_low)
        absorbed_high, absorbed_low = split(nt(upstream, keyval_ref[:, wb:]))
        key = key_ref[...]
        allowed = allowed_rows(cx, lane_ref)
        p = jnp.where(allowed, jnp.exp2(sc_ref[...] - (top + jnp.log2(total))), 0.0)
        dp = nt(key, absorbed_high) + nt(key, absorbed_low)
        ds = (p * (dp - delta)).astype(BF16)
        p_low = p.astype(BF16)
        dkey = nn(ds, ab_ref[...]) * cx.scale + nn(p_low, absorbed_high)
        g_k = tn(ds, key)
        gk_ref[0] = g_k
        gk_ref[1] = tn(p_low, key)
        g_high, g_low = split(g_k)
        key_part = keyval_ref[:, :wb]
        dquery = gather_heads(cx, nn(g_high, key_part) + nn(g_low, key_part)) * cx.scale
        dq_ref[:, col_b : col_b + wb] = dquery + ds_self_rows * kself * (cx.scale * share)
        unit_b, rstd_b = normalize(y_ref[...].astype(F32))
        gain_b = norms_ref[0:1, wa : wa + wb]
        cross_ref[...] = norm_grad(unit_b, rstd_b, gain_b, dkey)
        for i, item in enumerate(
            (
                fheads_low,
                act_r,
                dattn,
                djoined,
                dheads_low,
                ds_self_rows * fquery * cx.scale,
                p_self_rows * dheads,
            )
        ):
            rt_ref[i] = item.astype(F32)
        vecs += [
            col_sum(dkey * unit_b),
            col_sum(drev * unit_r) * share,
            col_sum(dkey),
            col_sum(drev) * share,
        ]
        col_a += wa
        col_b += wb
    dq_ref[:, col_b:] = jnp.zeros((ROWS, dq_ref.shape[1] - col_b), F32)
    vec_ref[...] = vec_block(vecs)


def cross_query_back_kernel(
    cxs,
    share,
    d0_ref,
    d1_ref,
    d2_ref,
    d3_ref,
    qa_l_ref,
    qb_l_ref,
    rt_l_ref,
    fln_ref,
    flp_ref,
    flq_ref,
    flk_ref,
    qa_s_ref,
    qb_s_ref,
    rt_s_ref,
    fsn_ref,
    fsp_ref,
    fsq_ref,
    fsk_ref,
    dcls_ref,
    dm_l_ref,
    dm_s_ref,
    vec_ref,
):
    dquery_all = d0_ref[...] + d1_ref[...] + d2_ref[...] + d3_ref[...]
    col_a = col_b = 0
    vecs = []
    for cx, qa_ref, qb_ref, rt_ref, norms_ref, proj_ref, query_ref, keyval_ref, dm_ref in (
        (cxs[0], qa_l_ref, qb_l_ref, rt_l_ref, fln_ref, flp_ref, flq_ref, flk_ref, dm_l_ref),
        (cxs[1], qa_s_ref, qb_s_ref, rt_s_ref, fsn_ref, fsp_ref, fsq_ref, fsk_ref, dm_s_ref),
    ):
        wa, wb = cx.wa, cx.wb
        dquery = dquery_all[:, col_b : col_b + wb].astype(BF16)
        dkself = rt_ref[5].astype(BF16)
        dvself = rt_ref[6].astype(BF16)
        dquery_in = (
            nt(dquery, query_ref[...])
            + nt(dkself, keyval_ref[:, :wb])
            + nt(dvself, keyval_ref[:, wb:])
        )
        unit_q, rstd_q = qb_ref[1], qb_ref[6]
        gain = norms_ref[0:1, wa : wa + wb]
        dmoved = norm_grad(unit_q, rstd_q, gain, dquery_in) + rt_ref[3]
        high, low = split(dmoved)
        dlifted = (cx.proj_back(high, proj_ref[...]) + cx.proj_back(low, proj_ref[...])) * qa_ref[1]
        unit_a = qa_ref[0]
        dcls_ref[:, col_a : col_a + wa] = norm_grad(
            unit_a, qa_ref[3], norms_ref[0:1, :wa], dlifted
        )
        dm_ref[0] = dmoved
        dm_ref[1] = dquery.astype(F32)
        vecs += [
            col_sum(dlifted * unit_a) * share,
            col_sum(dquery_in * unit_q) * share,
            col_sum(dlifted) * share,
            col_sum(dquery_in) * share,
            col_sum(dmoved) * share,
            col_sum(rt_ref[2]) * share,
        ]
        col_a += wa
        col_b += wb
    dcls_ref[:, col_a:] = jnp.zeros((ROWS, dcls_ref.shape[1] - col_a), F32)
    vec_ref[...] = vec_block(vecs)


def cross_grads_one_kernel(
    cxs,
    at,
    share,
    index_ref,
    g0_ref,
    g1_ref,
    g2_ref,
    g3_ref,
    qb_l_ref,
    rt_l_ref,
    gk_l_ref,
    qb_s_ref,
    rt_s_ref,
    gk_s_ref,
    keep_ref,
    send_ref,
    pack_ref,
    sems,
):
    dcls = g0_ref[...] + g1_ref[...] + g2_ref[...] + g3_ref[...]
    col_a = 0
    for cx, name, qb_ref, rt_ref, gk_ref in (
        (cxs[0], "l", qb_l_ref, rt_l_ref, gk_l_ref),
        (cxs[1], "s", qb_s_ref, rt_s_ref, gk_s_ref),
    ):
        wa, wb = cx.wa, cx.wb
        dback = dcls[:, col_a : col_a + wa].astype(BF16)
        query_in, fquery = qb_ref[2].astype(BF16), qb_ref[3].astype(BF16)
        fheads, act_r, dattn, dheads, dkself, dvself = (
            rt_ref[i].astype(BF16) for i in (0, 1, 2, 4, 5, 6)
        )
        back = tn(act_r, dback) if wa > wb else tn(dback, act_r)
        pack_mat(pack_ref, at["back" + name], *back.shape, back * share)
        pack_mat(pack_ref, at["out" + name], wb, wb, tn(fheads, dattn) * share)
        keys = (
            tn(gk_ref[0].astype(BF16), spread(cx, fquery)) * cx.scale
            + tn(query_in, dkself) * share
        )
        values = tn(gk_ref[1].astype(BF16), spread(cx, dheads)) + tn(query_in, dvself) * share
        pack_mat(pack_ref, at["keyval" + name], wb, 2 * wb, jnp.concatenate([keys, values], axis=1))
        col_a += wa
    if at["rows"] > at["end"]:
        pack_ref[at["end"] :, :] = jnp.zeros((at["rows"] - at["end"], 128), BF16)
    emit(pack_ref, (keep_ref, send_ref), index_ref[0], sems)


def cross_grads_two_kernel(
    cxs,
    at,
    share,
    index_ref,
    g0_ref,
    g1_ref,
    g2_ref,
    g3_ref,
    vec1_ref,
    vec2_ref,
    qa_l_ref,
    qb_l_ref,
    dm_l_ref,
    qa_s_ref,
    qb_s_ref,
    dm_s_ref,
    keep_ref,
    send_ref,
    pack_ref,
    sems,
):
    dcls = g0_ref[...] + g1_ref[...] + g2_ref[...] + g3_ref[...]
    col_a = 0
    dbacks = []
    for cx, name, qa_ref, qb_ref, dm_ref in (
        (cxs[0], "l", qa_l_ref, qb_l_ref, dm_l_ref),
        (cxs[1], "s", qa_s_ref, qb_s_ref, dm_s_ref),
    ):
        wa, wb = cx.wa, cx.wb
        dbacks.append(col_sum(dcls[:, col_a : col_a + wa]) * share)
        act, query_in = qa_ref[2].astype(BF16), qb_ref[2].astype(BF16)
        dmoved = dm_ref[0].astype(BF16)
        proj = tn(dmoved, act) if wa > wb else tn(act, dmoved)
        pack_mat(pack_ref, at["proj" + name], *proj.shape, proj * share)
        query = tn(query_in, dm_ref[1].astype(BF16)) * share
        pack_mat(pack_ref, at["query" + name], wb, wb, query)
        col_a += wa
    for name, block in (
        ("vec1", vec1_ref[...]),
        ("vec2", vec2_ref[...]),
        ("vec3", vec_block(dbacks)),
    ):
        pack_ref[at[name] : at[name] + block.shape[0], :] = block.astype(BF16)
    if at["rows"] > at["end"]:
        pack_ref[at["end"] :, :] = jnp.zeros((at["rows"] - at["end"], 128), BF16)
    emit(pack_ref, (keep_ref, send_ref), index_ref[0], sems)


def fold_kernel(counts, group, rows, index_ref, *refs):
    total = sum(counts)
    ins, refs = refs[:total], refs[total:]
    outs, (sum_ref, sems) = refs[:-2], refs[-2:]
    at = i = 0
    for count in counts:
        value = ins[i][...].astype(F32)
        for other in ins[i + 1 : i + count]:
            value = value + other[...].astype(F32)
        size = value.shape[0]
        sum_ref[at : at + size, :] = value.astype(BF16)
        at += size
        i += count
    if rows > at:
        sum_ref[at:, :] = jnp.zeros((rows - at, 128), BF16)
    emit(sum_ref, outs, index_at(index_ref, *group), sems)


def join_kernel(group, index_ref, *refs):
    *parts, out_ref = refs
    index = index_at(index_ref, *group)
    for d, part in enumerate(parts):
        size = part.shape[0]
        at = pl.multiple_of((index ^ d) * size, 16)
        out_ref[pl.ds(at, size), :] = part[...]


def settle_kernel(brs, dxl_ref, dxs_ref, left_ref, right_ref, *outs):
    for br, dx_ref, out in zip(brs, (dxl_ref, dxs_ref), outs):
        rest = jnp.zeros((br.n - br.halo, br.w), F32)
        dx = dx_ref[...] + jnp.concatenate([get_halo(br, left_ref), rest], axis=0)
        dx = dx + jnp.concatenate([rest, get_halo(br, right_ref)], axis=0)
        out[...] = (dx.T if br.turned else dx).astype(BF16)


def halves_of(sizes, shared=None):
    pieces, at = [], 0
    for pack, size in enumerate(sizes):
        done, half = 0, size // 2
        while done < half:
            row, count = at + done, half - done
            if shared:
                mine, both, first = shared
                count = min(count, mine - row % mine)
                row = row // mine * both + first + row % mine
            pieces.append((pack, done, row, count))
            done += count
        at += half
    return pieces


def gather_packs(index, own_ref, got_ref, packs, pieces, sems):
    copies = []
    for pack, row, at, count in pieces:
        half = packs[pack].shape[0] // 2
        for d, part in enumerate((own_ref, got_ref)):
            to = pl.multiple_of((index ^ d) * half + row, 16)
            copies.append(
                pltpu.make_async_copy(
                    part.at[pl.ds(at, count)],
                    packs[pack].at[pl.ds(to, count)],
                    sems.at[len(copies)],
                )
            )
            copies[-1].start()
    for copy in copies:
        copy.wait()


def unpack_block(br, at, ref, out_ref, up_ref, down_ref):
    w, f, step = br.w, br.f, 256
    unpack_mat(ref, at["out"], w, w, out_ref)
    for j, c in enumerate(range(0, f, step)):
        rows, cols = j * mat_rows(w, step), slice(c, c + step)
        unpack_mat(ref, at["up"] + rows, w, step, up_ref.at[:, cols])
        if br.turned:
            unpack_mat(ref, at["down"] + rows, w, step, down_ref.at[:, cols])
    if not br.turned:
        unpack_mat(ref, at["down"], f, w, down_ref)


def unpack_early_kernel(br, cxs, at, at1, pieces, index_ref, own_ref, got_ref, *refs):
    outs, (ref1, ref, sems) = refs[:-3], refs[-3:]
    gather_packs(index_ref[0], own_ref, got_ref, (ref1, ref), pieces, sems)
    unpack_block(br, at, ref, *outs[:3])
    for i, (cx, name) in enumerate(zip(cxs, "ls")):
        keyval_ref, out_ref, back_ref = outs[3 + 3 * i : 6 + 3 * i]
        wa, wb = cx.wa, cx.wb
        unpack_mat(ref1, at1["keyval" + name], wb, 2 * wb, keyval_ref)
        unpack_mat(ref1, at1["out" + name], wb, wb, out_ref)
        unpack_mat(ref1, at1["back" + name], min(wa, wb), max(wa, wb), back_ref)


def unpack_late_kernel(br, cxs, brs, ats, at, at2, pieces, index_ref, own_ref, got_ref, *refs):
    outs, (ref2, ref, *packs, sems) = refs[:-5], refs[-5:]
    gather_packs(index_ref[0], own_ref, got_ref, (ref2, ref, *packs), pieces, sems)
    unpack_block(br, at, ref, *outs[:3])

    def vectors(name):
        widths = at2["widths"][name]
        return vecs_of(ref2[at2[name] : at2[name] + vec_rows(widths), :].astype(F32), widths)

    vec1, vec2, vec3 = vectors("vec1"), vectors("vec2"), vectors("vec3")
    for i, (cx, name) in enumerate(zip(cxs, "ls")):
        norms_ref, proj_ref, query_ref, bias_ref = outs[3 + 4 * i : 7 + 4 * i]
        wa, wb = cx.wa, cx.wb
        unpack_mat(ref2, at2["proj" + name], min(wa, wb), max(wa, wb), proj_ref)
        unpack_mat(ref2, at2["query" + name], wb, wb, query_ref)
        gain_key, gain_rev, shift_key, shift_rev = vec1[4 * i : 4 * i + 4]
        gain_a, gain_q, shift_a, shift_q, bias_a, bias_b = vec2[6 * i : 6 * i + 6]
        norms_ref[0:1, :] = jnp.concatenate([gain_a, gain_q + gain_key, gain_rev], axis=1)
        norms_ref[1:2, :] = jnp.concatenate([shift_a, shift_q + shift_key, shift_rev], axis=1)
        bias_ref[...] = jnp.concatenate([bias_a, bias_b, vec3[i]], axis=1).reshape(wa + 2 * wb)
    unpack_qkv(brs, ats, packs, outs[11:])


def unpack_qkv(brs, ats, packs, outs):
    for i, (br, at, ref) in enumerate(zip(brs, ats, packs)):
        qkv_ref, norms_ref, bias_ref, upbias_ref = outs[4 * i : 4 * i + 4]
        w, f = br.w, br.f
        unpack_mat(ref, at["qkv"], w, 3 * w, qkv_ref)
        block = ref[at["vec1"] : at["vec1"] + vec_rows([w, w]), :].astype(F32)
        gain, shift = vecs_of(block, [w, w])
        norms_ref[0, 0:1, :] = gain
        norms_ref[0, 1:2, :] = shift
        block = ref[at["vec2"] : at["vec2"] + vec_rows([w] * 4 + [f]), :].astype(F32)
        gain, shift, bias0, bias1, upbias = vecs_of(block, [w] * 4 + [f])
        norms_ref[1, 0:1, :] = gain
        norms_ref[1, 1:2, :] = shift
        bias_ref[0:1, :] = bias0
        bias_ref[1:2, :] = bias1
        upbias_ref[...] = upbias.reshape(f)


def bits():
    head = [("head", 1 << i) for i in range(lax.axis_size("head").bit_length() - 1)]
    dp = [("dp", 1 << i) for i in range(lax.axis_size("dp").bit_length() - 1)]
    return head + dp


def bit_here(axis, bit):
    return (lax.axis_index(axis) // bit) % 2


def index_at(index_ref, first, count):
    index = 0
    for i in range(count):
        index = index * 2 + index_ref[first + i]
    return index


def swap(x, group, d):
    heads = lax.axis_size("head")
    flip = {"dp": 0, "head": 0}
    for k, (axis, bit) in enumerate(group[::-1]):
        if d >> k & 1:
            flip[axis] |= bit
    pairs = [
        (i * heads + j, (i ^ flip["dp"]) * heads + (j ^ flip["head"]))
        for i in range(lax.axis_size("dp"))
        for j in range(heads)
    ]
    return lax.ppermute(x, ("dp", "head"), pairs)


def others(x):
    count = lax.axis_size("head")
    return [
        lax.ppermute(x, "head", [(i, i ^ d) for i in range(count)]) for d in range(1, count)
    ]


class Sum:
    def __init__(self, index, order):
        self.index = index
        self.bits = order
        self.devices = 1 << len(self.bits)
        self.ins, self.counts, self.halves = [], [], []
        self.done = 1
        self.cost = 1

    def add(self, pack):
        keep, send = pack
        self.halves.append(keep.shape[0])
        self.ins += [keep, swap(send, self.bits[:1], 1)]
        self.counts.append(2)
        self.rows = round_up(sum(self.halves), self.devices // 2 * 16)

    def step(self, cost=1):
        self.cost = cost
        if self.plan:
            what, count = self.plan.pop(0)
            what(self, count)
            if what is Sum.meet:
                self.step(cost)

    def meet(self, other):
        while other.plan:
            other.step()
        self.shared = (other.rows, self.rows)
        self.ins = [*other.ins, *self.ins]
        self.counts = other.counts + self.counts
        self.rows += other.rows

    def fold(self, count):
        group = self.bits[self.done : self.done + count]
        cuts = 1 << count
        pieces = call(
            functools.partial(fold_kernel, self.counts, (self.done, count), self.rows),
            (sds((self.rows // cuts, 128), BF16),) * cuts,
            (self.index, *self.ins),
            [SMEM] + [VMEM] * len(self.ins),
            [pltpu.VMEM((self.rows, 128), BF16), pltpu.SemaphoreType.DMA((cuts,))],
            out_specs=(ANY,) * cuts,
            moved=self.cost,
            spare=2,
        )
        self.rows = self.rows // cuts
        self.counts = [cuts]
        self.done += count
        self.ins = [pieces[0]] + [swap(pieces[d], group, d) for d in range(1, cuts)]

    def turn(self, count):
        self.fold(0)
        self.spread(self.ins[0], count)

    def spread(self, whole, count):
        group = self.bits[self.done - count : self.done]
        self.ins = [whole] + [swap(whole, group, d) for d in range(1, 1 << count)]
        self.done -= count
        self.last = count

    def join(self, count):
        rows = self.ins[0].shape[0] * len(self.ins)
        whole = call(
            functools.partial(join_kernel, (self.done, self.last)),
            sds((rows, 128), BF16),
            (self.index, *self.ins),
            [SMEM] + [VMEM] * len(self.ins),
            moved=self.cost,
            spare=2,
        )
        self.spread(whole, count)


def from_sides(left, right):
    count = lax.axis_size("head")
    return (
        lax.ppermute(left, "head", [(i, i + 1) for i in range(count - 1)]),
        lax.ppermute(right, "head", [(i + 1, i) for i in range(count - 1)]),
    )


def block_forward(br, meta, sub, x, halo, qkv, norms, w_qkv, w_out, w_up, w_down, bias, upbias):
    n, w, f = br.n, br.w, br.f
    outs = (
        sds((n, w), BF16),
        sds((ROWS, w), F32),
        sds((br.r, w), BF16),
        sds((br.r, w), BF16),
        sds((br.t, 8, 128), F32),
        sds((n, w), BF16),
        sds((n, w), F32),
        sds((n, w), BF16),
        sds((n, f), BF16),
        sds((n, f), BF16),
    )
    ins = (meta, x, *halo, *qkv, norms, w_qkv, w_out, w_up, w_down, bias, upbias, sub)
    return call(
        functools.partial(forward_kernel, br),
        outs,
        ins,
        [SMEM] + [VMEM] * (len(ins) - 1),
        [pltpu.VMEM((br.t, w, 128), F32)],
        far=(2, 3, 7, 8, 4, 1, 9, 12, 13, 10, 11),
        far_out=range(2, 10),
    )


def ffn_back(br, index, col, lane, dy, cross, dcls, kept, norms, w_out, w_up, w_down):
    n, w, f = br.n, br.w, br.f
    parts = [("up", mat_rows(w, f)), ("down", mat_rows(f, w)), ("out", mat_rows(w, w))]
    at, rows = layout(parts)
    at["rows"], at["end"], at["col"] = rows, sum(r for _, r in parts), col
    ins = (index, lane, dy, cross, dcls, *kept, norms, w_out, w_up, w_down)
    half = sds((rows // 2, 128), BF16)
    vec = sds((vec_rows([w] * 4 + [f]), 128), F32)
    keep, send, *outs = call(
        functools.partial(ffn_back_kernel, br, at),
        (half, half, sds((n, w), F32), sds((n, w), BF16), vec),
        ins,
        [SMEM] + [VMEM] * (len(ins) - 1),
        [pltpu.VMEM((rows, 128), BF16), pltpu.SemaphoreType.DMA((2,))],
        out_specs=(ANY, ANY, VMEM, VMEM, VMEM),
        far=(2, 7, 13, 6, 12, 5, 8, 10, 9, 11),
        far_out=(2, 3),
    )
    return at, (keep, send), outs


def attn_loop(br, meta, q, kwin, vwin, dheads, lse):
    size = 128 * max(len(g[2]) for g in br.groups)
    ins = (meta, q, kwin, vwin, dheads, lse)
    return call(
        functools.partial(attn_loop_kernel, br),
        (sds((br.r, br.w), F32),) * 2 + (sds((br.n, br.w), BF16),),
        ins,
        [SMEM] + [VMEM] * (len(ins) - 1),
        [
            pltpu.VMEM((br.t, br.w, 128), F32),
            pltpu.VMEM((br.kw, size), BF16),
            pltpu.VMEM((br.kw, size), BF16),
        ],
        far=range(1, 6),
    )


def attn_post(br, index, grads, x, halo, norms, w_qkv, dmid, vec, before):
    n, w = br.n, br.w
    parts = [("qkv", mat_rows(w, 3 * w)), ("vec1", vec_rows([w, w])), ("vec2", vec.shape[0])]
    at, rows = layout(parts)
    at["rows"], at["end"] = rows, sum(r for _, r in parts)
    ins = (index, x, *halo, norms, w_qkv, dmid, vec, *grads, *before)
    half = sds((rows // 2, 128), BF16)
    keep, send, *outs = call(
        functools.partial(attn_post_kernel, br, at),
        (half, half, sds((n, w), F32), sds((br.end, 128), BF16), sds((br.end, 128), BF16)),
        ins,
        [SMEM] + [VMEM] * (len(ins) - 1),
        [
            pltpu.VMEM((br.r, w), BF16),
            pltpu.VMEM((rows, 128), BF16),
            pltpu.SemaphoreType.DMA((2,)),
        ],
        out_specs=(ANY, ANY, VMEM, VMEM, VMEM),
        far=range(1, 7),
    )
    return at, (keep, send), outs


def on_device(
    seg_large,
    seg_small,
    x_large,
    x_small,
    dy_large,
    dy_small,
    lb_norms,
    lb_qkv,
    lb_out,
    lb_up,
    lb_down,
    lb_bias,
    lb_upbias,
    sb_norms,
    sb_qkv,
    sb_out,
    sb_up,
    sb_down,
    sb_bias,
    sb_upbias,
    fl_norms,
    fl_proj,
    fl_query,
    fl_keyval,
    fl_out,
    fl_back,
    fl_bias,
    fs_norms,
    fs_proj,
    fs_query,
    fs_keyval,
    fs_out,
    fs_back,
    fs_bias,
):
    xl, xs, dyl, dys = x_large[0], x_small[0], dy_large[0], dy_small[0]
    small = Branch(*xs.shape, sb_up.shape[1], MOST_S)
    large = Branch(*xl.shape, lb_up.shape[1], MOST_L, small.end)
    cxs = (Cross(large.w, small.w, small.n), Cross(small.w, large.w, large.n))
    share = 1.0 / lax.axis_size("head")
    wide = round_up(large.w + small.w, 128)
    sb_down, fl_proj, fs_back = sb_down.T, fl_proj.T, fs_back.T
    order = bits()
    index = [bit_here(axis, bit) for axis, bit in order]
    index = jnp.stack(index + [jnp.zeros((), jnp.int32)] * (16 - len(order))).astype(jnp.int32)
    ORDER.clear()
    here = lax.axis_index("head").astype(jnp.int32)[None]

    edge = sds((large.end, 128), BF16)
    halo = from_sides(
        *call(functools.partial(edge_kernel, (large, small)), (edge, edge), (xl, xs))
    )
    words = sds((16,), jnp.int32)
    lanes = sds((8, 128), jnp.int32)
    subs = sds((ROWS, 128), jnp.int32)
    start = call(
        functools.partial(start_kernel, large, small),
        (sds((large.n, large.w), BF16),) * 3
        + (sds((small.n, small.w), BF16),) * 3
        + (words, words, lanes, lanes, subs, subs, sds((ROWS, wide), F32)),
        (here, seg_large, seg_small, xl, xs, dyl, dys, lb_norms, sb_norms, lb_qkv, sb_qkv),
        [SMEM] + [VMEM] * 10,
        [
            pltpu.VMEM((ROWS + 8, 128), jnp.int32),
            pltpu.SMEM((ROWS + 8, 128), jnp.int32),
            pltpu.SemaphoreType.DMA,
        ],
        out_specs=(VMEM,) * 6 + (SMEM, SMEM) + (VMEM,) * 5,
        far=range(1, 11),
        far_out=(0, 3),
    )
    qkv_l, qkv_s = start[:3], start[3:6]
    meta_l, meta_s, lane_l, lane_s, sub_l, sub_s, dcls = start[6:]
    dcls_all = [dcls] + others(dcls)

    ys, cls_s, kwin_s, vwin_s, lse_s, ho_s, mid_s, n2_s, hid_s, slope_s = block_forward(
        small, meta_s, sub_s, xs, halo, qkv_s, sb_norms, sb_qkv, sb_out, sb_up, sb_down,
        sb_bias, sb_upbias,
    )
    yl, cls_l, kwin_l, vwin_l, lse_l, ho_l, mid_l, n2_l, hid_l, slope_l = block_forward(
        large, meta_l, sub_l, xl, halo, qkv_l, lb_norms, lb_qkv, lb_out, lb_up, lb_down,
        lb_bias, lb_upbias,
    )

    cls = jnp.concatenate(
        [cls_l, cls_s, jnp.zeros((ROWS, wide - large.w - small.w), F32)], axis=1
    )
    cls_all = [cls] + others(cls)
    key_s, key_l = call(
        functools.partial(keys_kernel, cxs),
        (sds((small.n, small.w), BF16), sds((large.n, large.w), BF16)),
        (ys, fl_norms, yl, fs_norms),
        far=(1, 3),
    )
    wl, ws = large.w, small.w
    part, sc_l, sc_s, ab_l, ab_s, qa_l, qb_l, qa_s, qb_s = call(
        functools.partial(cross_front_kernel, cxs),
        (
            sds((ROWS + 8, wide), F32),
            sds((small.n, 128), F32),
            sds((large.n, 128), F32),
            sds((128, ws), BF16),
            sds((128, wl), BF16),
            sds((4, ROWS, wl), F32),
            sds((7, ROWS, ws), F32),
            sds((4, ROWS, ws), F32),
            sds((7, ROWS, wl), F32),
        ),
        (
            *cls_all, lane_s, lane_l, key_s, key_l,
            fl_norms, fl_proj, fl_query, fl_keyval, fl_bias,
            fs_norms, fs_proj, fs_query, fs_keyval, fs_bias,
        ),
        far=range(8, 18),
    )
    part_all = [part] + others(part)
    vec1 = [ws, ws, ws, ws, wl, wl, wl, wl]
    dquery, cross_s, cross_l, out_s, out_l, rt_l, rt_s, gk_l, gk_s, block1 = call(
        functools.partial(cross_back_kernel, cxs, share),
        (
            sds((ROWS, wide), F32),
            sds((small.n, ws), F32),
            sds((large.n, wl), F32),
            sds((ws, small.n) if small.turned else (small.n, ws), BF16),
            sds((large.n, wl), BF16),
            sds((7, ROWS, ws), F32),
            sds((7, ROWS, wl), F32),
            sds((2, 128, ws), F32),
            sds((2, 128, wl), F32),
            sds((vec_rows(vec1), 128), F32),
        ),
        (
            *dcls_all, *part_all, lane_s, lane_l, ys, yl, key_s, key_l,
            sc_l, sc_s, ab_l, ab_s, qb_l, qb_s,
            fl_norms, fl_keyval, fl_out, fl_back, fl_bias,
            fs_norms, fs_keyval, fs_out, fs_back, fs_bias,
        ),
        far=range(20, 30),
    )
    far = len(order) - 3
    sum_f, sum_g, sum_q = (Sum(index, order) for _ in range(3))
    fold, join = (Sum.fold, 1), (Sum.join, 1)
    rest = [fold] * far + [(Sum.turn, 1)] + [join] * (far - 1) + [(Sum.join, 2), join]
    sum_f.plan = [(Sum.fold, 2)] + rest
    sum_g.plan = [(Sum.fold, 2)]
    sum_q.plan = [(Sum.fold, 2), (Sum.meet, sum_g)] + rest

    def packed(kernel, items, unit, ins):
        at, rows = layout(items, unit)
        at["rows"], at["end"] = rows, sum(r for _, r in items)
        half = sds((rows // 2, 128), BF16)
        pack = call(
            functools.partial(kernel, cxs, at, share),
            (half, half),
            ins,
            [SMEM] + [VMEM] * (len(ins) - 1),
            [pltpu.VMEM((rows, 128), BF16), pltpu.SemaphoreType.DMA((2,))],
            out_specs=(ANY, ANY),
        )
        return at, pack

    def query_backward(dquery_all):
        return call(
            functools.partial(cross_query_back_kernel, cxs, share),
            (
                sds((ROWS, wide), F32),
                sds((2, ROWS, ws), F32),
                sds((2, ROWS, wl), F32),
                sds((vec_rows(vec2), 128), F32),
            ),
            (
                *dquery_all, qa_l, qb_l, rt_l, fl_norms, fl_proj, fl_query, fl_keyval,
                qa_s, qb_s, rt_s, fs_norms, fs_proj, fs_query, fs_keyval,
            ),
            far=(7, 8, 9, 10, 14, 15, 16, 17),
        )

    ORDER[:] = [block1]
    dquery_all = [dquery] + others(dquery)
    vec2 = [wl, ws, wl, ws, ws, ws, ws, wl, ws, wl, wl, wl]
    items = []
    for cx, name in zip(cxs, "ls"):
        items += [
            ("keyval" + name, mat_rows(cx.wb, 2 * cx.wb)),
            ("out" + name, mat_rows(cx.wb, cx.wb)),
            ("back" + name, mat_rows(cx.wb, cx.wa)),
        ]
    at_c1, pack_c1 = packed(
        cross_grads_one_kernel,
        items,
        32,
        (index, *dcls_all, qb_l, rt_l, gk_l, qb_s, rt_s, gk_s),
    )
    sum_f.add(pack_c1)
    dcls_new, dm_l, dm_s, block2 = query_backward(dquery_all)
    widths = {"vec1": vec1, "vec2": vec2, "vec3": [wl, ws]}
    items = []
    for cx, name in zip(cxs, "ls"):
        items += [("proj" + name, mat_rows(cx.wa, cx.wb)), ("query" + name, mat_rows(cx.wb, cx.wb))]
    items += [(name, vec_rows(of)) for name, of in widths.items()]
    at_c2, pack_c2 = packed(
        cross_grads_two_kernel,
        items,
        32,
        (index, *dcls_all, block1, block2, qa_l, qb_l, dm_l, qa_s, qb_s, dm_s),
    )
    at_c2["widths"] = widths
    sum_g.add(pack_c2)
    at_fl, pack_fl, (dmid_l, dheads_l, vec_l) = ffn_back(
        large, index, 0, lane_l, dyl, cross_l, dcls_new,
        (hid_l, slope_l, n2_l, mid_l, ho_l), lb_norms, lb_out, lb_up, lb_down,
    )
    sum_f.add(pack_fl)
    at_fs, pack_fs, (dmid_s, dheads_s, vec_s) = ffn_back(
        small, index, wl, lane_s, dys, cross_s, dcls_new,
        (hid_s, slope_s, n2_s, mid_s, ho_s), sb_norms, sb_out, sb_up, sb_down,
    )
    sum_g.add(pack_fs)

    def settled(dx_l, dx_s, first, last):
        return call(
            functools.partial(settle_kernel, (large, small)),
            (
                sds((large.n, wl), BF16),
                sds((ws, small.n) if small.turned else (small.n, ws), BF16),
            ),
            (dx_l, dx_s, *from_sides(last, first)),
        )

    def unpack(kernel, outs, done, rows, shared=None):
        while done.plan:
            done.step()
        pieces = halves_of(rows[0], shared and (done.shared[0], sum(done.shared), 0))
        if shared:
            first = len(rows[0])
            more = halves_of(rows[1], (done.shared[1], sum(done.shared), done.shared[0]))
            pieces += [(first + pack, *rest) for pack, *rest in more]
        return call(
            functools.partial(kernel, pieces),
            outs,
            (index, *done.ins),
            [SMEM, ANY, ANY],
            [pltpu.VMEM((r, 128), BF16) for part in rows for r in part]
            + [pltpu.SemaphoreType.DMA((2 * len(pieces),))],
        )

    def block_outs(br):
        return [
            sds((br.w, br.w), F32),
            sds((br.w, br.f), F32),
            sds((br.w, br.f) if br.turned else (br.f, br.w), F32),
        ]

    def unpack_early():
        outs = block_outs(large)
        for cx in cxs:
            less, more = min(cx.wa, cx.wb), max(cx.wa, cx.wb)
            outs += [sds((cx.wb, 2 * cx.wb), F32), sds((cx.wb, cx.wb), F32), sds((less, more), F32)]

        def kernel(pieces, *refs):
            unpack_early_kernel(large, cxs, at_fl, at_c1, pieces, *refs)

        return unpack(kernel, tuple(outs), sum_f, [(at_c1["rows"], at_fl["rows"])])

    def unpack_late():
        outs, found = block_outs(small), {"l": (large, made["at_l"]), "s": (small, made["at_s"])}
        for cx in cxs:
            wa, wb = cx.wa, cx.wb
            outs += [
                sds((2, wa + 2 * wb), F32),
                sds((min(wa, wb), max(wa, wb)), F32),
                sds((wb, wb), F32),
                sds((wa + 2 * wb,), F32),
            ]
        brs, ats = zip(*(found[name] for name in made["packs"]))
        for br in brs:
            outs += [
                sds((br.w, 3 * br.w), F32),
                sds((2, 2, br.w), F32),
                sds((2, br.w), F32),
                sds((br.f,), F32),
            ]

        def kernel(pieces, *refs):
            unpack_late_kernel(small, cxs, brs, ats, at_fs, at_c2, pieces, *refs)

        rows = [(at_c2["rows"], at_fs["rows"]), tuple(at["rows"] for at in ats)]
        got = unpack(kernel, tuple(outs), sum_q, rows, True)
        return got[:11], {name: got[11 + 4 * i : 15 + 4 * i] for i, name in enumerate(made["packs"])}

    made = {"packs": ""}
    sums = {"f": sum_f, "g": sum_g, "q": sum_q}

    def do(what):
        if what == "loop_l":
            made["grads"] = attn_loop(large, meta_l, qkv_l[0], kwin_l, vwin_l, dheads_l, lse_l)
        elif what == "loop_s":
            made["grads"] = attn_loop(small, meta_s, qkv_s[0], kwin_s, vwin_s, dheads_s, lse_s)
        elif what == "post_l":
            made["at_l"], pack, made["dx_l"] = attn_post(
                large, index, made["grads"], xl, halo, lb_norms, lb_qkv, dmid_l, vec_l,
                made["dx_s"][1:],
            )
            sum_q.add(pack)
            made["packs"] += "l"
        elif what == "post_s":
            made["at_s"], pack, made["dx_s"] = attn_post(
                small, index, made["grads"], xs, halo, sb_norms, sb_qkv, dmid_s, vec_s, ()
            )
            sum_q.add(pack)
            made["packs"] += "s"
        elif what == "dx":
            made["dx"] = settled(made["dx_l"][0], made["dx_s"][0], *made["dx_l"][1:])
        elif what == "out_f":
            made["f"] = unpack_early()
        elif what == "out_q":
            made["g"], made["q"] = unpack_late()
        else:
            sums[what.lower()].step(COSTLY if what.isupper() else 1)

    for what in SCHEDULE:
        do(what)
    o_l, u_l, d_l, *others_c = made["f"]
    o_s, u_s, d_s, *crossed = made["g"]
    q_l, norms_l, bias_l, upbias_l = made["q"]["l"]
    q_s, norms_s, bias_s, upbias_s = made["q"]["s"]
    grad_xl, grad_xs = made["dx"]
    ORDER.clear()
    fl, fs = (
        [*crossed[4 * i : 4 * i + 3], *others_c[3 * i : 3 * i + 3], crossed[4 * i + 3]]
        for i in range(2)
    )
    fl[1], fs[5] = fl[1].T, fs[5].T
    if small.turned:
        out_s, grad_xs, d_s = out_s.T, grad_xs.T, d_s.T
    return (
        out_l[None],
        out_s[None],
        grad_xl[None],
        grad_xs[None],
        norms_l,
        q_l,
        o_l,
        u_l,
        d_l,
        bias_l,
        upbias_l,
        norms_s,
        q_s,
        o_s,
        u_s,
        d_s,
        bias_s,
        upbias_s,
        *fl,
        *fs,
    )


def solution(mesh):
    rows = P("dp", "head", None)
    return jax.shard_map(
        on_device,
        mesh=mesh,
        in_specs=(P("dp", None),) * 2 + (rows,) * 4 + (P(),) * 28,
        out_specs=(rows,) * 4 + (P(),) * 28,
        check_vma=False,
    )
```

```python
import functools
import math

import jax
import jax.numpy as jnp
from jax import lax
from jax.experimental import pallas as pl
from jax.experimental.pallas import tpu as pltpu
from jax.sharding import PartitionSpec as P

HEADS = 6
IMGS = 10
ROWS = 16
MOST_L = 197
MOST_S = 401
EPS = 1e-6
NEG = -1e30
LOG2E = math.log2(math.e)
F32 = jnp.float32
BF16 = jnp.bfloat16
VMEM = pl.BlockSpec(memory_space=pltpu.VMEM)
SMEM = pl.BlockSpec(memory_space=pltpu.SMEM)
HBM = pl.BlockSpec(memory_space=pltpu.HBM)


COSTLY = 40 * 10**6
SCHEDULE = (
    "F", "loop_s", "post_s", "F", "G", "loop_l", "F", "post_l", "F", "Q", "f", "q", "f", "q", "dx",
    "q", "q", "place", "f", "Q", "out_f", "q", "out_q",
)
ORDER = []


def round_up(value, unit):
    return -(-value // unit) * unit


class Branch:
    def __init__(self, rows, width, hidden, most, before=0):
        self.n = rows
        self.w = width
        self.f = hidden
        self.dh = width // HEADS
        self.halo = round_up(most - 1, 16)
        self.kw = self.halo + 16
        self.r = rows + 2 * self.halo
        self.t = rows // 128
        self.cols = round_up(width, 128) // 128
        self.at = before
        self.end = before + self.halo * self.cols
        self.scale = self.dh ** (-0.5)
        self.turned = width % 128 != 0
        if width % 128 == 0:
            per = 128 // self.dh
            self.groups = [
                (i * 128, (i + 1) * 128, list(range(i * per, (i + 1) * per)))
                for i in range(width // 128)
            ]
        else:
            self.groups = [(0, width, list(range(HEADS)))]


def nn(a, b):
    return jnp.dot(a, b, preferred_element_type=F32)


def nt(a, b):
    return lax.dot_general(a, b, (((1,), (1,)), ((), ())), preferred_element_type=F32)


def tn(a, b):
    return lax.dot_general(a, b, (((0,), (0,)), ((), ())), preferred_element_type=F32)


def split(x):
    high = x.astype(BF16)
    return high, (x - high.astype(F32)).astype(BF16)


def normalize(x):
    center = x - jnp.mean(x, axis=-1, keepdims=True)
    rstd = lax.rsqrt(jnp.mean(center * center, axis=-1, keepdims=True) + EPS)
    return center * rstd, rstd


def norm_grad(unit, rstd, gain, upstream):
    scaled = upstream * gain
    mean_one = jnp.mean(scaled, axis=-1, keepdims=True)
    mean_two = jnp.mean(scaled * unit, axis=-1, keepdims=True)
    return (scaled - mean_one - unit * mean_two) * rstd


def col_sum(x):
    return jnp.sum(x, axis=0, keepdims=True)


def gelu_pair(x):
    cumulative = 0.5 * (1.0 + lax.erf(x * 0.7071067811865476))
    density = jnp.exp(-0.5 * x * x) * 0.3989422804014327
    return x * cumulative, cumulative + x * density


def iota(shape, dim):
    return lax.broadcasted_iota(jnp.int32, shape, dim)


def padded_bytes(item):
    *lead, rows, cols = (1, 1, *item.shape)
    unit = 32 // item.dtype.itemsize
    return math.prod(lead) * round_up(rows, unit) * round_up(cols, 128) * item.dtype.itemsize


def parts_of(item):
    return item.shape[0] if len(item.shape) == 3 and item.shape[1] * item.shape[2] > 1 << 14 else 1


class FarIn:
    def __init__(self, far, near, sems):
        pairs = [(far, near)]
        if len(sems) > 1:
            pairs = [(far.at[i], near.at[i]) for i in range(len(sems))]
        self.copies = [
            pltpu.make_async_copy(*pair, sem) for pair, sem in zip(pairs, sems, strict=True)
        ]
        for copy in self.copies:
            copy.start()
        self.near = near
        self.landed = [False] * len(sems)

    def land(self, i=None):
        for k, copy in enumerate(self.copies):
            if not self.landed[k] and i in (None, k):
                self.landed[k] = True
                copy.wait()

    @property
    def shape(self):
        return self.near.shape

    def __getitem__(self, where):
        self.land(where if isinstance(where, int) and len(self.copies) > 1 else None)
        return self.near[where]


class FarOut:
    def __init__(self, far, near, sems):
        pairs = [(near, far)]
        if len(sems) > 1:
            pairs = [(near.at[i], far.at[i]) for i in range(len(sems))]
        self.copies = [
            pltpu.make_async_copy(*pair, sem) for pair, sem in zip(pairs, sems, strict=True)
        ]
        self.near = near
        self.sent = [False] * len(sems)

    def send(self, i=None):
        for k, copy in enumerate(self.copies):
            if not self.sent[k] and i in (None, k):
                self.sent[k] = True
                copy.start()

    @property
    def shape(self):
        return self.near.shape

    def __getitem__(self, where):
        return self.near[where]

    def __setitem__(self, where, value):
        self.near[where] = value


def land(*refs):
    for ref in refs:
        if isinstance(ref, FarIn):
            ref.land()


def near(ref):
    return ref.near if isinstance(ref, (FarIn, FarOut)) else ref


def send(*refs):
    for ref in refs:
        if isinstance(ref, FarOut):
            ref.send()


def call(
    kernel,
    outs,
    ins,
    in_specs=None,
    scratch=(),
    flops=0,
    moved=1,
    out_specs=None,
    spare=10,
    far=(),
    far_out=(),
):
    in_specs = [VMEM] * len(ins) if in_specs is None else list(in_specs)
    flat = list(jax.tree.leaves(outs))
    specs = [VMEM] * len(flat) if out_specs is None else list(jax.tree.leaves(out_specs))
    for i in far:
        in_specs[i] = HBM
    for i in far_out:
        specs[i] = HBM
    held = list(zip(ins, in_specs)) + list(zip(flat, specs))
    need = sum(padded_bytes(item) for item, spec in held if spec is VMEM)
    near = [pltpu.VMEM(ins[i].shape, ins[i].dtype) for i in far]
    near += [pltpu.VMEM(flat[i].shape, flat[i].dtype) for i in far_out]
    scratch = list(scratch)
    for item in scratch + near:
        if getattr(item, "memory_space", None) == pltpu.VMEM:
            need += padded_bytes(sds(item.shape, jnp.dtype(item.dtype)))
    count = len(near)

    def wrapped(*refs):
        refs = list(refs)
        if not count:
            return kernel(*refs)
        refs, held, sems = refs[: -count - 1], refs[-count - 1 : -1], refs[-1]
        found, at = [], 0
        for k, i in enumerate([*far, *(i + len(ins) for i in far_out)]):
            size = parts_of(near[k])
            own = [sems.at[at + j] for j in range(size)]
            at += size
            refs[i] = (FarIn if k < len(far) else FarOut)(refs[i], held[k], own)
            found.append(refs[i])
        kernel(*refs)
        land(*found)
        send(*found)
        for ref in found:
            if isinstance(ref, FarOut):
                for copy in ref.copies:
                    copy.wait()

    total = sum(parts_of(item) for item in near)
    extra = near + [pltpu.SemaphoreType.DMA((total,))] if count else []
    ins = list(ins)
    if ORDER:
        i = next(i for i, spec in enumerate(in_specs) if spec is not SMEM)
        ins[i] = after(ORDER[-1], ins[i])
    for i in far:
        ins[i] = pltpu.with_memory_space_constraint(ins[i], pltpu.HBM)
    for i in far_out:
        flat[i] = pltpu.HBM(flat[i].shape, flat[i].dtype)
    results = pl.pallas_call(
        wrapped,
        out_shape=jax.tree.unflatten(jax.tree.structure(outs), flat),
        in_specs=in_specs,
        out_specs=jax.tree.unflatten(jax.tree.structure(outs), specs),
        scratch_shapes=scratch + extra,
        compiler_params=pltpu.CompilerParams(
            vmem_limit_bytes=min(need + spare * 2**20, 60 * 2**20)
        ),
        cost_estimate=pl.CostEstimate(flops=moved * 500, bytes_accessed=moved, transcendentals=0),
    )(*ins)
    if ORDER:
        ORDER[:] = [min(jax.tree.leaves(results), key=lambda item: item.size)]
    return results


def after(first, then):
    return lax.optimization_barrier((first, then))[1]


def sds(shape, dtype):
    return jax.ShapeDtypeStruct(shape, dtype)


def mat_rows(rows, cols):
    return rows * cols // 128


def put_halo(br, ref, value):
    low = value.astype(BF16)
    for i in range(br.cols):
        part = low[:, i * 128 : min((i + 1) * 128, br.w)]
        if part.shape[1] < 128:
            part = jnp.concatenate([part, jnp.zeros((br.halo, 128 - part.shape[1]), BF16)], axis=1)
        ref[br.at + i * br.halo : br.at + (i + 1) * br.halo, :] = part


def get_halo(br, ref):
    parts = [
        ref[br.at + i * br.halo : br.at + (i + 1) * br.halo, : min(128, br.w - i * 128)]
        for i in range(br.cols)
    ]
    return jnp.concatenate(parts, axis=1).astype(F32)


def vec_rows(widths):
    return round_up(sum(round_up(w, 128) // 128 for w in widths), 16)


def layout(items, unit=32):
    at, row = {}, 0
    for name, rows in items:
        at[name] = row
        row += rows
    return at, round_up(row, unit)


def pack_mat(ref, at, rows, cols, value):
    low = value.astype(BF16)
    full = cols // 128
    for i in range(full):
        ref[at + i * rows : at + (i + 1) * rows, :] = low[:, i * 128 : (i + 1) * 128]
    if cols % 128:
        tail = low[:, full * 128 :]
        at = at + full * rows
        half = rows // 2
        ref[at : at + half, :] = jnp.concatenate([tail[:half], tail[half:]], axis=1)


def unpack_mat(ref, at, rows, cols, out):
    full = cols // 128
    for i in range(full):
        out[:, i * 128 : (i + 1) * 128] = ref[at + i * rows : at + (i + 1) * rows, :].astype(F32)
    if cols % 128:
        at = at + full * rows
        half = rows // 2
        block = ref[at : at + half, :].astype(F32)
        out[:half, full * 128 :] = block[:, :64]
        out[half:, full * 128 :] = block[:, 64:]


def vec_block(values):
    pieces = []
    for value in values:
        width = value.shape[1]
        for i in range(0, width, 128):
            piece = value[:, i : min(i + 128, width)]
            if piece.shape[1] < 128:
                piece = jnp.concatenate(
                    [piece, jnp.zeros((1, 128 - piece.shape[1]), F32)], axis=1
                )
            pieces.append(piece)
    total = round_up(len(pieces), 16)
    if total > len(pieces):
        pieces.append(jnp.zeros((total - len(pieces), 128), F32))
    return jnp.concatenate(pieces, axis=0)


def vecs_of(block, widths):
    out, i = [], 0
    for width in widths:
        parts = []
        for j in range(0, width, 128):
            parts.append(block[i : i + 1, : min(128, width - j)])
            i += 1
        out.append(parts[0] if len(parts) == 1 else jnp.concatenate(parts, axis=1))
    return out


def emit(src_ref, outs, index):
    size = src_ref.shape[0] // len(outs)
    for d, out in enumerate(outs):
        at = pl.multiple_of((index ^ d) * size, 16)
        out[...] = src_ref[pl.ds(at, size), :]


def edge_kernel(brs, xl_ref, xs_ref, last_ref, first_ref):
    for br, ref in zip(brs, (xl_ref, xs_ref)):
        put_halo(br, last_ref, ref[br.n - br.halo :, :])
        put_halo(br, first_ref, ref[: br.halo, :])


def start_kernel(
    br_l,
    br_s,
    index_ref,
    seg_l_ref,
    seg_s_ref,
    xl_ref,
    xs_ref,
    dyl_ref,
    dys_ref,
    nl_ref,
    ns_ref,
    wl_ref,
    ws_ref,
    ql_ref,
    kl_ref,
    vl_ref,
    qs_ref,
    ks_ref,
    vs_ref,
    meta_l_ref,
    meta_s_ref,
    lane_l_ref,
    lane_s_ref,
    sub_l_ref,
    sub_s_ref,
    dcls_ref,
    vector_ref,
    scalar_ref,
    sem,
):
    col = 0
    dcls_ref[...] = jnp.zeros_like(dcls_ref)
    for br, seg_ref, dy_ref, meta_ref, lane_ref, sub_ref in (
        (br_l, seg_l_ref, dyl_ref, meta_l_ref, lane_l_ref, sub_l_ref),
        (br_s, seg_s_ref, dys_ref, meta_s_ref, lane_s_ref, sub_s_ref),
    ):
        own = index_ref[15] * br.n
        seg = seg_ref[...]
        image = iota((ROWS, seg.shape[1]), 0)
        starts = jnp.sum((seg < image).astype(jnp.int32), axis=1, keepdims=True)
        ends = jnp.sum((seg <= image).astype(jnp.int32), axis=1, keepdims=True)
        starts = jnp.broadcast_to(starts, (ROWS, 128))
        ends = jnp.broadcast_to(ends, (ROWS, 128))
        lane = iota((ROWS, 128), 1)
        diagonal = (lane - (lane // ROWS) * ROWS) == iota((ROWS, 128), 0)
        lo = jnp.sum(jnp.where(diagonal, starts, 0), axis=0, keepdims=True) - own
        hi = jnp.sum(jnp.where(diagonal, ends, 0), axis=0, keepdims=True) - own
        lane_ref[...] = jnp.concatenate([lo, hi, jnp.zeros((6, 128), jnp.int32)], axis=0)
        sub_ref[...] = starts - own
        real = iota((ROWS, 128), 0) < IMGS
        first = jnp.sum(jnp.where(real & (starts <= own), 1, 0), axis=0, keepdims=True) - 1
        last = jnp.sum(jnp.where(real & (starts < own + br.n), 1, 0), axis=0, keepdims=True) - 1
        at = 0 if br is br_l else ROWS + 8
        vector_ref[at : at + ROWS, :] = starts
        vector_ref[at + ROWS : at + ROWS + 8, :] = jnp.concatenate(
            [first, last, jnp.zeros((6, 128), jnp.int32)], axis=0
        )
        pick = (iota((ROWS, br.n), 1) == (starts - own)[:, 0:1]).astype(F32).astype(BF16)
        dcls_ref[:, col : col + br.w] = nn(pick, dy_ref[...])
        col += br.w
    copy = pltpu.make_async_copy(vector_ref, scalar_ref, sem)
    copy.start()
    for x_ref, norms_ref, w_ref, outs in (
        (xl_ref, nl_ref, wl_ref, (ql_ref, kl_ref, vl_ref)),
        (xs_ref, ns_ref, ws_ref, (qs_ref, ks_ref, vs_ref)),
    ):
        width = x_ref.shape[1]
        unit, _ = normalize(x_ref[...].astype(F32))
        normed = (unit * norms_ref[0, 0:1, :] + norms_ref[0, 1:2, :]).astype(BF16)
        for i, ref in enumerate(outs):
            ref[...] = nn(normed, w_ref[:, i * width : (i + 1) * width]).astype(BF16)
    copy.wait()
    for br, meta_ref, at in ((br_l, meta_l_ref, 0), (br_s, meta_s_ref, ROWS + 8)):
        for j in range(IMGS + 1):
            meta_ref[j] = scalar_ref[at + j, 0]
        meta_ref[11] = index_ref[15] * br.n
        meta_ref[12] = scalar_ref[at + ROWS, 0]
        meta_ref[13] = scalar_ref[at + ROWS + 1, 0]
        meta_ref[14] = 0
        meta_ref[15] = 0


def head_mask(br, head, c0, c1):
    lane = iota((1, c1 - c0), 1) + c0
    return jnp.logical_and(lane >= head * br.dh, lane < (head + 1) * br.dh)


def stack_heads(br, rows, group):
    c0, c1, heads = group
    part = rows[:, c0:c1]
    zero = jnp.zeros_like(part)
    return jnp.concatenate(
        [jnp.where(head_mask(br, h, c0, c1), part, zero) for h in heads], axis=0
    )


def image_span(br, meta_ref, j):
    base = meta_ref[11]
    lo = meta_ref[j] - base
    hi = meta_ref[j + 1] - base
    k0 = pl.multiple_of(((lo + br.halo) // 16) * 16, 16)
    t0 = jnp.maximum(lo, 0) // 128
    t1 = (jnp.minimum(hi, br.n) + 127) // 128
    return lo, hi, k0, t0, t1


def forward_kernel(
    br,
    meta_ref,
    x_ref,
    xl_ref,
    xr_ref,
    q_ref,
    k_ref,
    v_ref,
    norms_ref,
    wqkv_ref,
    wout_ref,
    wup_ref,
    wdown_ref,
    bias_ref,
    upbias_ref,
    sub_ref,
    y_ref,
    cls_ref,
    kwin_ref,
    vwin_ref,
    lse_ref,
    ho_ref,
    mid_ref,
    hid_ref,
    slope_ref,
    far_y_ref,
    ot_ref,
):
    n, w, f, dh, halo = br.n, br.w, br.f, br.dh, br.halo
    for ref, at in ((xl_ref, 0), (xr_ref, halo + n)):
        unit, _ = normalize(get_halo(br, ref))
        normed = (unit * norms_ref[0, 0:1, :] + norms_ref[0, 1:2, :]).astype(BF16)
        kwin_ref[at : at + halo, :] = nn(normed, wqkv_ref[:, w : 2 * w]).astype(BF16)
        vwin_ref[at : at + halo, :] = nn(normed, wqkv_ref[:, 2 * w :]).astype(BF16)
    kwin_ref[halo : halo + n, :] = k_ref[...]
    vwin_ref[halo : halo + n, :] = v_ref[...]
    send(vwin_ref)
    ot_ref[...] = jnp.zeros_like(ot_ref)
    lse_ref[...] = jnp.zeros(lse_ref.shape, F32)
    factor = br.scale * LOG2E
    land(q_ref)

    def image(j, carry):
        lo, hi, k0, t0, t1 = image_span(br, meta_ref, j)
        keys = kwin_ref[pl.ds(k0, br.kw), :]
        values_t = vwin_ref[pl.ds(k0, br.kw), :].T
        row = iota((br.kw, 128), 0) + (k0 - br.halo)
        mask = jnp.logical_and(row >= lo, row < hi)

        def tile(t, carry):
            rows = q_ref[pl.ds(pl.multiple_of(t * 128, 128), 128), :]
            lane = iota((1, 128), 1) + t * 128
            inside = jnp.logical_and(lane >= lo, lane < hi)
            for group in br.groups:
                c0, c1, heads = group
                scores = nt(keys[:, c0:c1], stack_heads(br, rows, group))
                for i, h in enumerate(heads):
                    s = jnp.where(mask, scores[:, i * 128 : (i + 1) * 128] * factor, NEG)
                    top = jnp.max(s, axis=0, keepdims=True)
                    p = jnp.exp2(s - top)
                    total = col_sum(p)
                    o = nn(values_t[h * dh : (h + 1) * dh, :], p.astype(BF16))
                    ot_ref[t, h * dh : (h + 1) * dh, :] += o * jnp.where(inside, 1.0 / total, 0.0)
                    lse_ref[t, h : h + 1, :] = jnp.where(
                        inside, top + jnp.log2(total), lse_ref[t, h : h + 1, :]
                    )
            return carry

        return lax.fori_loop(t0, t1, tile, carry)

    lax.fori_loop(meta_ref[12], meta_ref[13] + 1, image, 0)
    send(kwin_ref, lse_ref)
    for t in range(br.t):
        ho_ref[t * 128 : (t + 1) * 128, :] = ot_ref[t].T.astype(BF16)
    mid = x_ref[...].astype(F32) + (nn(ho_ref[...], wout_ref[...]) + bias_ref[0:1, :])
    mid_ref[...] = mid
    unit, _ = normalize(mid)
    normed = (unit * norms_ref[1, 0:1, :] + norms_ref[1, 1:2, :]).astype(BF16)
    send(ho_ref, mid_ref)
    total = mid + bias_ref[1:2, :]
    step = 256
    upbias = upbias_ref[...].reshape(1, f)
    for c in range(0, f, step):
        pre = nn(normed, wup_ref[:, c : c + step]) + upbias[:, c : c + step]
        act, slope = gelu_pair(pre)
        act = act.astype(BF16)
        i = c // step
        hid_ref[i] = act
        slope_ref[i] = slope.astype(BF16)
        hid_ref.send(i)
        slope_ref.send(i)
        if br.turned:
            total = total + nt(act, wdown_ref[:, c : c + step])
        else:
            total = total + nn(act, wdown_ref[c : c + step, :])
    y = total.astype(BF16)
    y_ref[...] = y
    far_y_ref[...] = y
    send(far_y_ref)
    pick = (iota((ROWS, n), 1) == sub_ref[:, 0:1]).astype(F32).astype(BF16)
    cls_ref[...] = nn(pick, y)


def ffn_back_kernel(
    br,
    at,
    index_ref,
    lane_ref,
    dy_ref,
    cross_ref,
    dcls_ref,
    hid_ref,
    slope_ref,
    mid_ref,
    ho_ref,
    norms_ref,
    wout_ref,
    wup_ref,
    wdown_ref,
    keep_ref,
    send_ref,
    dmid_ref,
    dheads_ref,
    vec_ref,
    pack_ref,
):
    n, w, f = br.n, br.w, br.f
    c0 = at["col"]
    cls = dcls_ref[:, c0 : c0 + w].astype(BF16)
    hit = (iota((n, 128), 0) == lane_ref[0:1, :]).astype(F32)
    hit = jnp.where(iota((1, 128), 1) < IMGS, hit, 0.0)
    first = jnp.sum(hit, axis=1, keepdims=True) > 0.5
    placed = nn(hit[:, :ROWS].astype(BF16), cls)
    gy = jnp.where(first, placed, dy_ref[...].astype(F32) + cross_ref[...]).astype(BF16)
    gy_float = gy.astype(F32)
    dn2 = jnp.zeros((n, w), F32)
    step = 256
    upbias = []
    unit, rstd = normalize(mid_ref[...])
    normed_t = (unit * norms_ref[1, 0:1, :] + norms_ref[1, 1:2, :]).astype(BF16).T
    gy_t = gy.T
    if at["rows"] > at["end"]:
        pack_ref[at["end"] :, :] = jnp.zeros((at["rows"] - at["end"], 128), BF16)
    for i, c in enumerate(range(0, f, step)):
        if br.turned:
            dpre = nn(gy, wdown_ref[:, c : c + step])
        else:
            dpre = nt(gy, wdown_ref[c : c + step, :])
        dpre = (dpre * slope_ref[i].astype(F32)).astype(BF16)
        upbias.append(col_sum(dpre.astype(F32)))
        rows = i * mat_rows(w, step)
        pack_mat(pack_ref, at["up"] + rows, w, step, nn(normed_t, dpre))
        dn2 = dn2 + nt(dpre, wup_ref[:, c : c + step])
        pack_mat(pack_ref, at["down"] + rows, w, step, nn(gy_t, hid_ref[i]))
    dmid = gy_float + norm_grad(unit, rstd, norms_ref[1, 0:1, :], dn2)
    dmid_ref[...] = dmid
    send(dmid_ref)
    dattn = dmid.astype(BF16)
    dheads_ref[...] = nt(dattn, wout_ref[...]).astype(BF16)
    send(dheads_ref)
    pack_mat(pack_ref, at["out"], w, w, tn(ho_ref[...], dattn))
    vec_ref[...] = vec_block(
        [col_sum(dn2 * unit), col_sum(dn2), col_sum(dattn.astype(F32)), col_sum(gy_float)] + upbias
    )
    emit(pack_ref, (keep_ref, send_ref), index_ref[0])


def attn_loop_kernel(
    br,
    meta_ref,
    q_ref,
    kwin_ref,
    vwin_ref,
    dheads_ref,
    lse_ref,
    dk_ref,
    dv_ref,
    dq_ref,
    dqt_ref,
    p_ref,
    ds_ref,
):
    dh = br.dh
    dk_ref[...] = jnp.zeros(dk_ref.shape, F32)
    dv_ref[...] = jnp.zeros_like(dv_ref)
    dqt_ref[...] = jnp.zeros_like(dqt_ref)
    factor = br.scale * LOG2E
    land(q_ref, kwin_ref, vwin_ref, dheads_ref, lse_ref)

    def image(j, carry):
        lo, hi, k0, t0, t1 = image_span(br, meta_ref, j)
        span = pl.ds(k0, br.kw)
        keys = kwin_ref[span, :]
        keys_t = keys.T
        values = vwin_ref[span, :]
        row = iota((br.kw, 128), 0) + (k0 - br.halo)
        mask = jnp.logical_and(row >= lo, row < hi)

        def tile(t, carry):
            here = pl.ds(pl.multiple_of(t * 128, 128), 128)
            rows = q_ref[here, :]
            outs = dheads_ref[here, :]
            lane = iota((1, 128), 1) + t * 128
            inside = jnp.logical_and(lane >= lo, lane < hi)
            for group in br.groups:
                c0, c1, heads = group
                queries = stack_heads(br, rows, group)
                upstream = stack_heads(br, outs, group)
                scores = nt(keys[:, c0:c1], queries)
                dprobs = nt(values[:, c0:c1], upstream)
                for i, h in enumerate(heads):
                    part = slice(i * 128, (i + 1) * 128)
                    lse = jnp.where(inside, lse_ref[t, h : h + 1, :], -NEG)
                    p = jnp.exp2(scores[:, part] * factor - lse)
                    p = jnp.where(mask, p, 0.0)
                    dp = dprobs[:, part]
                    ds = (p * (dp - col_sum(p * dp))).astype(BF16)
                    p_ref[:, part] = p.astype(BF16)
                    ds_ref[:, part] = ds
                    dqt_ref[t, h * dh : (h + 1) * dh, :] += nn(
                        keys_t[h * dh : (h + 1) * dh, :], ds
                    )
                size = 128 * len(heads)
                dv_ref[span, c0:c1] += nn(p_ref[:, :size], upstream)
                dk_ref[span, c0:c1] += nn(ds_ref[:, :size], queries)
            return carry

        return lax.fori_loop(t0, t1, tile, carry)

    lax.fori_loop(meta_ref[12], meta_ref[13] + 1, image, 0)
    for t in range(br.t):
        dq_ref[t * 128 : (t + 1) * 128, :] = (dqt_ref[t].T * br.scale).astype(BF16)


def attn_post_kernel(
    br,
    at,
    index_ref,
    x_ref,
    xl_ref,
    xr_ref,
    norms_ref,
    wqkv_ref,
    dmid_ref,
    vec_ref,
    dk_ref,
    dv_ref,
    dq_ref,
    *refs,
):
    before, refs = refs[:-7], refs[-7:]
    keep_ref, send_ref, dx_ref, dxl_ref, dxr_ref, normed_ref, pack_ref = refs
    for ref, out in zip(before, (dxl_ref, dxr_ref)):
        out[: br.at, :] = ref[...]
    n, w, halo = br.n, br.w, br.halo
    dk = (dk_ref[...] * br.scale).astype(BF16)
    dv = dv_ref[...].astype(BF16)
    gain, shift = norms_ref[0, 0:1, :], norms_ref[0, 1:2, :]
    dgain = jnp.zeros((1, w), F32)
    dshift = jnp.zeros((1, w), F32)
    for ref, lo, size, out in (
        (xl_ref, 0, halo, dxl_ref),
        (x_ref, halo, n, dx_ref),
        (xr_ref, halo + n, halo, dxr_ref),
    ):
        rows = ref[...].astype(F32) if ref is x_ref else get_halo(br, ref)
        unit, rstd = normalize(rows)
        normed_ref[lo : lo + size, :] = (unit * gain + shift).astype(BF16)
        up = nt(dk[lo : lo + size], wqkv_ref[:, w : 2 * w])
        up = up + nt(dv[lo : lo + size], wqkv_ref[:, 2 * w :])
        if out is dx_ref:
            up = up + nt(dq_ref[...], wqkv_ref[:, :w])
        dgain = dgain + col_sum(up * unit)
        dshift = dshift + col_sum(up)
        dx = norm_grad(unit, rstd, gain, up)
        if out is dx_ref:
            out[...] = dx + dmid_ref[...]
        else:
            put_halo(br, out, dx)
    whole = jnp.concatenate(
        [
            tn(normed_ref[halo : halo + n, :], dq_ref[...]),
            tn(normed_ref[...], dk),
            tn(normed_ref[...], dv),
        ],
        axis=1,
    )
    pack_mat(pack_ref, at["qkv"], w, 3 * w, whole)
    block = vec_block([dgain, dshift])
    pack_ref[at["vec1"] : at["vec1"] + block.shape[0], :] = block.astype(BF16)
    pack_ref[at["vec2"] : at["vec2"] + vec_ref.shape[0], :] = vec_ref[...].astype(BF16)
    if at["rows"] > at["end"]:
        pack_ref[at["end"] :, :] = jnp.zeros((at["rows"] - at["end"], 128), BF16)
    emit(pack_ref, (keep_ref, send_ref), index_ref[0])


class Cross:
    def __init__(self, wa, wb, rows_b):
        self.wa = wa
        self.wb = wb
        self.dh = wb // HEADS
        self.n = rows_b
        self.scale = self.dh ** (-0.5)
        self.proj = nt if wa > wb else nn
        self.proj_back = nn if wa > wb else nt
        self.back = nn if wa > wb else nt
        self.back_back = nt if wa > wb else nn

    def by_head(self):
        head = iota((128, self.wb), 0) // ROWS
        col = iota((128, self.wb), 1)
        return jnp.logical_and(col >= head * self.dh, col < (head + 1) * self.dh).astype(F32)

    def by_image(self):
        lane = iota((ROWS, 128), 1)
        return jnp.logical_and(
            lane - (lane // ROWS) * ROWS == iota((ROWS, 128), 0), lane < HEADS * ROWS
        ).astype(F32)


def spread(cx, low_rows):
    return jnp.concatenate([low_rows] * 8, axis=0) * cx.by_head().astype(low_rows.dtype)


def gather_heads(cx, wide):
    kept = wide * cx.by_head()
    total = kept[0:ROWS]
    for h in range(1, HEADS):
        total = total + kept[h * ROWS : (h + 1) * ROWS]
    return total


def to_lane(cx, *items):
    stack = jnp.concatenate([part for item in items for part in split(item)], axis=0)
    wide = nt(stack, cx.by_head().astype(BF16))
    image = cx.by_image()
    found = []
    for i in range(0, 2 * ROWS * len(items), 2 * ROWS):
        found.append(col_sum(image * (wide[i : i + ROWS] + wide[i + ROWS : i + 2 * ROWS])))
    return found


def from_lane(cx, *items):
    image = cx.by_image()
    stack = jnp.concatenate([part for item in items for part in split(image * item)], axis=0)
    wide = nn(stack, cx.by_head().astype(BF16))
    return [
        wide[i : i + ROWS] + wide[i + ROWS : i + 2 * ROWS]
        for i in range(0, 2 * ROWS * len(items), 2 * ROWS)
    ]


def cross_query(cx, cls, norms_ref, proj_ref, query_ref, keyval_ref, bias_ref, qa_ref, qb_ref):
    wa, wb = cx.wa, cx.wb
    unit_a, rstd_a = normalize(cls)
    lifted = unit_a * norms_ref[0:1, :wa] + norms_ref[1:2, :wa]
    act, slope = gelu_pair(lifted)
    act = act.astype(BF16)
    bias = bias_ref[...].reshape(1, bias_ref.shape[0])[:, :wb]
    moved = cx.proj(act, proj_ref[...]) + bias
    gain, shift = norms_ref[0:1, wa : wa + wb], norms_ref[1:2, wa : wa + wb]
    unit_q, rstd_q = normalize(moved)
    query_in = (unit_q * gain + shift).astype(BF16)
    fquery = nn(query_in, query_ref[...]).astype(BF16)
    kself = nn(query_in, keyval_ref[:, :wb]).astype(BF16)
    vself = nn(query_in, keyval_ref[:, wb:]).astype(BF16)
    for i, item in enumerate((unit_a, slope, act, jnp.broadcast_to(rstd_a, unit_a.shape))):
        qa_ref[i] = item.astype(F32)
    for i, item in enumerate(
        (moved, unit_q, query_in, fquery, kself, vself, jnp.broadcast_to(rstd_q, moved.shape))
    ):
        qb_ref[i] = item.astype(F32)
    return fquery


def allowed_rows(cx, lane_ref):
    row = iota((cx.n, 128), 0)
    return jnp.logical_and(row > lane_ref[0:1, :], row < lane_ref[1:2, :])


def keys_kernel(cxs, ys_ref, fln_ref, yl_ref, fsn_ref, ks_ref, kl_ref):
    for cx, y_ref, norms_ref, out_ref in (
        (cxs[0], ys_ref, fln_ref, ks_ref),
        (cxs[1], yl_ref, fsn_ref, kl_ref),
    ):
        wa, wb = cx.wa, cx.wb
        unit, _ = normalize(y_ref[...].astype(F32))
        out_ref[...] = (
            unit * norms_ref[0:1, wa : wa + wb] + norms_ref[1:2, wa : wa + wb]
        ).astype(BF16)


def cross_front_kernel(
    cxs,
    c0_ref,
    c1_ref,
    c2_ref,
    c3_ref,
    lane_s_ref,
    lane_l_ref,
    key_s_ref,
    key_l_ref,
    fln_ref,
    flp_ref,
    flq_ref,
    flk_ref,
    flb_ref,
    fsn_ref,
    fsp_ref,
    fsq_ref,
    fsk_ref,
    fsb_ref,
    part_ref,
    sc_l_ref,
    sc_s_ref,
    ab_l_ref,
    ab_s_ref,
    qa_l_ref,
    qb_l_ref,
    qa_s_ref,
    qb_s_ref,
):
    cls = c0_ref[...] + c1_ref[...] + c2_ref[...] + c3_ref[...]
    wl, ws = cxs[0].wa, cxs[1].wa
    col = 0
    stats = []
    for cx, rows, key_ref, lane_ref, keyval_ref, weights, kept, sc_ref, ab_ref in (
        (
            cxs[0],
            cls[:, :wl],
            key_s_ref,
            lane_s_ref,
            flk_ref,
            (fln_ref, flp_ref, flq_ref, flk_ref, flb_ref),
            (qa_l_ref, qb_l_ref),
            sc_l_ref,
            ab_l_ref,
        ),
        (
            cxs[1],
            cls[:, wl : wl + ws],
            key_l_ref,
            lane_l_ref,
            fsk_ref,
            (fsn_ref, fsp_ref, fsq_ref, fsk_ref, fsb_ref),
            (qa_s_ref, qb_s_ref),
            sc_s_ref,
            ab_s_ref,
        ),
    ):
        fquery = cross_query(cx, rows, *weights, *kept)
        absorbed = nt(spread(cx, fquery), keyval_ref[:, : cx.wb]).astype(BF16)
        ab_ref[...] = absorbed
        key = key_ref[...]
        allowed = allowed_rows(cx, lane_ref)
        scores = jnp.where(allowed, nt(key, absorbed) * (cx.scale * LOG2E), NEG)
        sc_ref[...] = scores
        top = jnp.max(scores, axis=0, keepdims=True)
        p = jnp.where(allowed, jnp.exp2(scores - top), 0.0)
        high, low = split(p)
        mixed_high, mixed_low = split(tn(high, key) + tn(low, key))
        value_part = keyval_ref[:, cx.wb :]
        out = gather_heads(cx, nn(mixed_high, value_part) + nn(mixed_low, value_part))
        part_ref[0:ROWS, col : col + cx.wb] = out
        col += cx.wb
        stats += [top, col_sum(p)]
    width = part_ref.shape[1]
    part_ref[0:ROWS, col:] = jnp.zeros((ROWS, width - col), F32)
    part_ref[ROWS:, :] = jnp.zeros((8, width), F32)
    part_ref[ROWS : ROWS + 4, :128] = jnp.concatenate(stats, axis=0)


def cross_back_kernel(
    cxs,
    share,
    g0_ref,
    g1_ref,
    g2_ref,
    g3_ref,
    p0_ref,
    p1_ref,
    p2_ref,
    p3_ref,
    lane_s_ref,
    lane_l_ref,
    key_s_ref,
    key_l_ref,
    sc_l_ref,
    sc_s_ref,
    qb_l_ref,
    qb_s_ref,
    fln_ref,
    flk_ref,
    flo_ref,
    flw_ref,
    flb_ref,
    fsn_ref,
    fsk_ref,
    fso_ref,
    fsw_ref,
    fsb_ref,
    dq_ref,
    rt_l_ref,
    rt_s_ref,
    gk_l_ref,
    gk_s_ref,
    ds_l_ref,
    ds_s_ref,
    p_l_ref,
    p_s_ref,
    av_l_ref,
    av_s_ref,
    back_ref,
    vec_ref,
):
    dcls = g0_ref[...] + g1_ref[...] + g2_ref[...] + g3_ref[...]
    parts = [p0_ref, p1_ref, p2_ref, p3_ref]
    vecs = []
    col_b = 0
    col_a = 0
    for index, (cx, key_ref, lane_ref, sc_ref, qb_ref, weights, outs) in enumerate(
        (
            (
                cxs[0],
                key_s_ref,
                lane_s_ref,
                sc_l_ref,
                qb_l_ref,
                (fln_ref, flk_ref, flo_ref, flw_ref, flb_ref),
                (rt_l_ref, gk_l_ref, ds_l_ref, p_l_ref, av_l_ref),
            ),
            (
                cxs[1],
                key_l_ref,
                lane_l_ref,
                sc_s_ref,
                qb_s_ref,
                (fsn_ref, fsk_ref, fso_ref, fsw_ref, fsb_ref),
                (rt_s_ref, gk_s_ref, ds_s_ref, p_s_ref, av_s_ref),
            ),
        )
    ):
        norms_ref, keyval_ref, wout_ref, wback_ref, bias_ref = weights
        rt_ref, gk_ref, ds_ref, p_ref, av_ref = outs
        wa, wb = cx.wa, cx.wb
        moved, fquery, kself, vself = qb_ref[0], qb_ref[3], qb_ref[4], qb_ref[5]
        self_score = to_lane(cx, fquery * kself)[0] * (cx.scale * LOG2E)
        tops = [p[ROWS + 2 * index : ROWS + 2 * index + 1, :128] for p in parts]
        sums = [p[ROWS + 2 * index + 1 : ROWS + 2 * index + 2, :128] for p in parts]
        top = self_score
        for item in tops:
            top = jnp.maximum(top, item)
        own = jnp.exp2(self_score - top)
        total = own
        weights_of = []
        for item, amount in zip(tops, sums):
            weight = jnp.exp2(item - top)
            weights_of.append(weight)
            total = total + amount * weight
        inverse = 1.0 / total
        p_self = own * inverse
        spans = from_lane(cx, p_self, *(weight * inverse for weight in weights_of))
        fheads = spans[0] * vself
        for part, span in zip(parts, spans[1:]):
            fheads = fheads + part[0:ROWS, col_b : col_b + wb] * span
        fheads_low = fheads.astype(BF16)
        bias = bias_ref[...].reshape(1, bias_ref.shape[0])
        joined = moved + (nn(fheads_low, wout_ref[...]) + bias[:, wb : 2 * wb])
        unit_r, rstd_r = normalize(joined)
        gain_r = norms_ref[0:1, wa + wb :]
        reverted = unit_r * gain_r + norms_ref[1:2, wa + wb :]
        act_r, slope_r = gelu_pair(reverted)
        act_r = act_r.astype(BF16)
        back_ref[:, col_a : col_a + wa] = cx.back(act_r, wback_ref[...]) + bias[:, 2 * wb :]
        dback_low = dcls[:, col_a : col_a + wa].astype(BF16)
        drev = cx.back_back(dback_low, wback_ref[...]) * slope_r
        djoined = norm_grad(unit_r, rstd_r, gain_r, drev)
        dattn = djoined.astype(BF16)
        dheads_low = nt(dattn, wout_ref[...]).astype(BF16)
        dheads = dheads_low.astype(F32)
        delta, dp_self = to_lane(cx, dheads * fheads, dheads * vself)
        ds_self = p_self * (dp_self - delta)
        ds_self_rows, p_self_rows = from_lane(
            cx, ds_self.astype(BF16).astype(F32), p_self.astype(BF16).astype(F32)
        )
        absorbed_high, absorbed_low = split(nt(spread(cx, dheads_low), keyval_ref[:, wb:]))
        av_ref[...] = absorbed_high
        key = key_ref[...]
        allowed = allowed_rows(cx, lane_ref)
        p = jnp.where(allowed, jnp.exp2(sc_ref[...] - (top + jnp.log2(total))), 0.0)
        dp = nt(key, absorbed_high) + nt(key, absorbed_low)
        ds = (p * (dp - delta)).astype(BF16)
        ds_ref[...] = ds
        p_ref[...] = p.astype(BF16)
        g_k = tn(ds, key)
        gk_ref[...] = g_k
        g_high, g_low = split(g_k)
        key_part = keyval_ref[:, :wb]
        dquery = gather_heads(cx, nn(g_high, key_part) + nn(g_low, key_part)) * cx.scale
        dq_ref[:, col_b : col_b + wb] = dquery + ds_self_rows * kself * (cx.scale * share)
        for i, item in enumerate(
            (
                fheads_low,
                act_r,
                dattn,
                djoined,
                dheads_low,
                ds_self_rows * fquery * cx.scale,
                p_self_rows * dheads,
            )
        ):
            rt_ref[i] = item.astype(F32)
        vecs += [col_sum(drev * unit_r) * share, col_sum(drev) * share]
        col_a += wa
        col_b += wb
    dq_ref[:, col_b:] = jnp.zeros((ROWS, dq_ref.shape[1] - col_b), F32)
    back_ref[:, col_a:] = jnp.zeros((ROWS, back_ref.shape[1] - col_a), F32)
    vec_ref[...] = vec_block(vecs)


def place_kernel(brs, back_ref, lane_l_ref, lane_s_ref, yl_ref, ys_ref, *outs):
    col = 0
    for br, lane_ref, y_ref, out_ref in zip(brs, (lane_l_ref, lane_s_ref), (yl_ref, ys_ref), outs):
        hit = (iota((br.n, 128), 0) == lane_ref[0:1, :]).astype(F32)
        hit = jnp.where(iota((1, 128), 1) < IMGS, hit, 0.0)
        first = jnp.sum(hit, axis=1, keepdims=True) > 0.5
        placed = nn(hit[:, :ROWS].astype(BF16), back_ref[:, col : col + br.w].astype(BF16))
        result = jnp.where(first, placed, y_ref[...].astype(F32))
        out_ref[...] = (result.T if br.turned else result).astype(BF16)
        col += br.w


def cross_query_back_kernel(
    cxs,
    share,
    d0_ref,
    d1_ref,
    d2_ref,
    d3_ref,
    qa_l_ref,
    qb_l_ref,
    rt_l_ref,
    fln_ref,
    flp_ref,
    flq_ref,
    flk_ref,
    qa_s_ref,
    qb_s_ref,
    rt_s_ref,
    fsn_ref,
    fsp_ref,
    fsq_ref,
    fsk_ref,
    dcls_ref,
    dm_l_ref,
    dm_s_ref,
    vec_ref,
):
    dquery_all = d0_ref[...] + d1_ref[...] + d2_ref[...] + d3_ref[...]
    col_a = col_b = 0
    vecs = []
    for cx, qa_ref, qb_ref, rt_ref, norms_ref, proj_ref, query_ref, keyval_ref, dm_ref in (
        (cxs[0], qa_l_ref, qb_l_ref, rt_l_ref, fln_ref, flp_ref, flq_ref, flk_ref, dm_l_ref),
        (cxs[1], qa_s_ref, qb_s_ref, rt_s_ref, fsn_ref, fsp_ref, fsq_ref, fsk_ref, dm_s_ref),
    ):
        wa, wb = cx.wa, cx.wb
        dquery = dquery_all[:, col_b : col_b + wb].astype(BF16)
        dkself = rt_ref[5].astype(BF16)
        dvself = rt_ref[6].astype(BF16)
        dquery_in = (
            nt(dquery, query_ref[...])
            + nt(dkself, keyval_ref[:, :wb])
            + nt(dvself, keyval_ref[:, wb:])
        )
        unit_q, rstd_q = qb_ref[1], qb_ref[6]
        gain = norms_ref[0:1, wa : wa + wb]
        dmoved = norm_grad(unit_q, rstd_q, gain, dquery_in) + rt_ref[3]
        high, low = split(dmoved)
        dlifted = (cx.proj_back(high, proj_ref[...]) + cx.proj_back(low, proj_ref[...])) * qa_ref[1]
        unit_a = qa_ref[0]
        dcls_ref[:, col_a : col_a + wa] = norm_grad(
            unit_a, qa_ref[3], norms_ref[0:1, :wa], dlifted
        )
        dm_ref[0] = dmoved
        dm_ref[1] = dquery.astype(F32)
        vecs += [
            col_sum(dlifted * unit_a) * share,
            col_sum(dquery_in * unit_q) * share,
            col_sum(dlifted) * share,
            col_sum(dquery_in) * share,
            col_sum(dmoved) * share,
            col_sum(rt_ref[2]) * share,
        ]
        col_a += wa
        col_b += wb
    dcls_ref[:, col_a:] = jnp.zeros((ROWS, dcls_ref.shape[1] - col_a), F32)
    vec_ref[...] = vec_block(vecs)


def cross_grads_one_kernel(
    cxs,
    at,
    share,
    index_ref,
    g0_ref,
    g1_ref,
    g2_ref,
    g3_ref,
    qb_l_ref,
    rt_l_ref,
    gk_l_ref,
    ds_l_ref,
    p_l_ref,
    ab_l_ref,
    av_l_ref,
    key_s_ref,
    ys_ref,
    fln_ref,
    qb_s_ref,
    rt_s_ref,
    gk_s_ref,
    ds_s_ref,
    p_s_ref,
    ab_s_ref,
    av_s_ref,
    key_l_ref,
    yl_ref,
    fsn_ref,
    keep_ref,
    send_ref,
    cross_s_ref,
    cross_l_ref,
    vec_ref,
    pack_ref,
):
    dcls = g0_ref[...] + g1_ref[...] + g2_ref[...] + g3_ref[...]
    col_a = 0
    vecs = []
    for cx, name, cross_ref, ins in (
        (
            cxs[0],
            "l",
            cross_s_ref,
            (qb_l_ref, rt_l_ref, gk_l_ref, ds_l_ref, p_l_ref, ab_l_ref, av_l_ref)
            + (key_s_ref, ys_ref, fln_ref),
        ),
        (
            cxs[1],
            "s",
            cross_l_ref,
            (qb_s_ref, rt_s_ref, gk_s_ref, ds_s_ref, p_s_ref, ab_s_ref, av_s_ref)
            + (key_l_ref, yl_ref, fsn_ref),
        ),
    ):
        qb_ref, rt_ref, gk_ref, ds_ref, p_ref, ab_ref, av_ref, key_ref, y_ref, norms_ref = ins
        wa, wb = cx.wa, cx.wb
        p = p_ref[...]
        dkey = nn(ds_ref[...], ab_ref[...]) * cx.scale + nn(p, av_ref[...])
        unit_b, rstd_b = normalize(y_ref[...].astype(F32))
        cross_ref[...] = norm_grad(unit_b, rstd_b, norms_ref[0:1, wa : wa + wb], dkey)
        vecs += [col_sum(dkey * unit_b), col_sum(dkey)]
        dback = dcls[:, col_a : col_a + wa].astype(BF16)
        query_in, fquery = qb_ref[2].astype(BF16), qb_ref[3].astype(BF16)
        fheads, act_r, dattn, dheads, dkself, dvself = (
            rt_ref[i].astype(BF16) for i in (0, 1, 2, 4, 5, 6)
        )
        back = tn(act_r, dback) if wa > wb else tn(dback, act_r)
        pack_mat(pack_ref, at["back" + name], *back.shape, back * share)
        pack_mat(pack_ref, at["out" + name], wb, wb, tn(fheads, dattn) * share)
        keys = (
            tn(gk_ref[...].astype(BF16), spread(cx, fquery)) * cx.scale
            + tn(query_in, dkself) * share
        )
        values = tn(tn(p, key_ref[...]).astype(BF16), spread(cx, dheads))
        values = values + tn(query_in, dvself) * share
        pack_mat(pack_ref, at["keyval" + name], wb, 2 * wb, jnp.concatenate([keys, values], axis=1))
        col_a += wa
    vec_ref[...] = vec_block(vecs)
    if at["rows"] > at["end"]:
        pack_ref[at["end"] :, :] = jnp.zeros((at["rows"] - at["end"], 128), BF16)
    emit(pack_ref, (keep_ref, send_ref), index_ref[0])


def cross_grads_two_kernel(
    cxs,
    at,
    share,
    index_ref,
    g0_ref,
    g1_ref,
    g2_ref,
    g3_ref,
    vec0_ref,
    vec1_ref,
    vec2_ref,
    qa_l_ref,
    qb_l_ref,
    dm_l_ref,
    qa_s_ref,
    qb_s_ref,
    dm_s_ref,
    keep_ref,
    send_ref,
    pack_ref,
):
    dcls = g0_ref[...] + g1_ref[...] + g2_ref[...] + g3_ref[...]
    col_a = 0
    dbacks = []
    for cx, name, qa_ref, qb_ref, dm_ref in (
        (cxs[0], "l", qa_l_ref, qb_l_ref, dm_l_ref),
        (cxs[1], "s", qa_s_ref, qb_s_ref, dm_s_ref),
    ):
        wa, wb = cx.wa, cx.wb
        dbacks.append(col_sum(dcls[:, col_a : col_a + wa]) * share)
        act, query_in = qa_ref[2].astype(BF16), qb_ref[2].astype(BF16)
        dmoved = dm_ref[0].astype(BF16)
        proj = tn(dmoved, act) if wa > wb else tn(act, dmoved)
        pack_mat(pack_ref, at["proj" + name], *proj.shape, proj * share)
        query = tn(query_in, dm_ref[1].astype(BF16)) * share
        pack_mat(pack_ref, at["query" + name], wb, wb, query)
        col_a += wa
    for name, block in (
        ("vec0", vec0_ref[...]),
        ("vec1", vec1_ref[...]),
        ("vec2", vec2_ref[...]),
        ("vec3", vec_block(dbacks)),
    ):
        pack_ref[at[name] : at[name] + block.shape[0], :] = block.astype(BF16)
    if at["rows"] > at["end"]:
        pack_ref[at["end"] :, :] = jnp.zeros((at["rows"] - at["end"], 128), BF16)
    emit(pack_ref, (keep_ref, send_ref), index_ref[0])


def fold_kernel(counts, group, rows, index_ref, *refs):
    total = sum(counts)
    ins, refs = refs[:total], refs[total:]
    outs, sum_ref = refs[:-1], refs[-1]
    at = i = 0
    for count in counts:
        value = ins[i][...].astype(F32)
        for other in ins[i + 1 : i + count]:
            value = value + other[...].astype(F32)
        size = value.shape[0]
        sum_ref[at : at + size, :] = value.astype(BF16)
        at += size
        i += count
    if rows > at:
        sum_ref[at:, :] = jnp.zeros((rows - at, 128), BF16)
    emit(sum_ref, outs, index_at(index_ref, *group))


def join_kernel(group, index_ref, *refs):
    *parts, out_ref = refs
    index = index_at(index_ref, *group)
    for d, part in enumerate(parts):
        size = part.shape[0]
        at = pl.multiple_of((index ^ d) * size, 16)
        out_ref[pl.ds(at, size), :] = part[...]


def settle_kernel(brs, dxl_ref, dxs_ref, left_ref, right_ref, *outs):
    for br, dx_ref, out in zip(brs, (dxl_ref, dxs_ref), outs):
        rest = jnp.zeros((br.n - br.halo, br.w), F32)
        dx = dx_ref[...] + jnp.concatenate([get_halo(br, left_ref), rest], axis=0)
        dx = dx + jnp.concatenate([rest, get_halo(br, right_ref)], axis=0)
        out[...] = (dx.T if br.turned else dx).astype(BF16)


def halves_of(sizes, shared=None):
    pieces, at = [], 0
    for pack, size in enumerate(sizes):
        done, half = 0, size // 2
        while done < half:
            row, count = at + done, half - done
            if shared:
                mine, both, first = shared
                count = min(count, mine - row % mine)
                row = row // mine * both + first + row % mine
            pieces.append((pack, done, row, count))
            done += count
        at += half
    return pieces


def gather_packs(index, own_ref, got_ref, packs, pieces):
    for pack, row, at, size in pieces:
        half = packs[pack].shape[0] // 2
        for d, part in enumerate((own_ref, got_ref)):
            to = pl.multiple_of((index ^ d) * half + row, 16)
            packs[pack][pl.ds(to, size), :] = part[at : at + size, :]


def unpack_block(br, at, ref, out_ref, up_ref, down_ref):
    w, f, step = br.w, br.f, 256
    unpack_mat(ref, at["out"], w, w, out_ref)
    for j, c in enumerate(range(0, f, step)):
        rows, cols = j * mat_rows(w, step), slice(c, c + step)
        unpack_mat(ref, at["up"] + rows, w, step, near(up_ref).at[:, cols])
        if br.turned:
            unpack_mat(ref, at["down"] + rows, w, step, near(down_ref).at[:, cols])
            continue
        for k in range(step // 128):
            a = at["down"] + rows + k * w
            down_ref[c + k * 128 : c + (k + 1) * 128, :] = ref[a : a + w, :].astype(F32).T
    send(out_ref, up_ref, down_ref)


def unpack_early_kernel(br, cxs, at, at1, pieces, index_ref, own_ref, got_ref, *refs):
    outs, (ref1, ref) = refs[:-2], refs[-2:]
    gather_packs(index_ref[0], own_ref, got_ref, (ref1, ref), pieces)
    unpack_block(br, at, ref, *outs[:3])
    for i, (cx, name) in enumerate(zip(cxs, "ls")):
        keyval_ref, out_ref, back_ref = outs[3 + 3 * i : 6 + 3 * i]
        wa, wb = cx.wa, cx.wb
        unpack_mat(ref1, at1["keyval" + name], wb, 2 * wb, keyval_ref)
        unpack_mat(ref1, at1["out" + name], wb, wb, out_ref)
        unpack_mat(ref1, at1["back" + name], min(wa, wb), max(wa, wb), back_ref)
        send(keyval_ref, out_ref, back_ref)


def unpack_late_kernel(br, cxs, brs, ats, at, at2, pieces, index_ref, own_ref, got_ref, *refs):
    outs, (ref2, ref, *packs) = refs[:-4], refs[-4:]
    gather_packs(index_ref[0], own_ref, got_ref, (ref2, ref, *packs), pieces)
    unpack_qkv(brs, ats, packs, outs[11:])
    unpack_block(br, at, ref, *outs[:3])

    def vectors(name):
        widths = at2["widths"][name]
        return vecs_of(ref2[at2[name] : at2[name] + vec_rows(widths), :].astype(F32), widths)

    vec0, vec1, vec2, vec3 = (vectors("vec%d" % i) for i in range(4))
    for i, (cx, name) in enumerate(zip(cxs, "ls")):
        norms_ref, proj_ref, query_ref, bias_ref = outs[3 + 4 * i : 7 + 4 * i]
        wa, wb = cx.wa, cx.wb
        unpack_mat(ref2, at2["proj" + name], min(wa, wb), max(wa, wb), proj_ref)
        unpack_mat(ref2, at2["query" + name], wb, wb, query_ref)
        (gain_rev, shift_rev), (gain_key, shift_key) = (v[2 * i : 2 * i + 2] for v in (vec0, vec1))
        gain_a, gain_q, shift_a, shift_q, bias_a, bias_b = vec2[6 * i : 6 * i + 6]
        norms_ref[0:1, :] = jnp.concatenate([gain_a, gain_q + gain_key, gain_rev], axis=1)
        norms_ref[1:2, :] = jnp.concatenate([shift_a, shift_q + shift_key, shift_rev], axis=1)
        bias_ref[...] = jnp.concatenate([bias_a, bias_b, vec3[i]], axis=1).reshape(wa + 2 * wb)
        send(proj_ref, query_ref)


def unpack_qkv(brs, ats, packs, outs):
    for i, (br, at, ref) in enumerate(zip(brs, ats, packs)):
        qkv_ref, norms_ref, bias_ref, upbias_ref = outs[4 * i : 4 * i + 4]
        w, f = br.w, br.f
        unpack_mat(ref, at["qkv"], w, 3 * w, qkv_ref)
        send(qkv_ref)
        block = ref[at["vec1"] : at["vec1"] + vec_rows([w, w]), :].astype(F32)
        gain, shift = vecs_of(block, [w, w])
        norms_ref[0, 0:1, :] = gain
        norms_ref[0, 1:2, :] = shift
        block = ref[at["vec2"] : at["vec2"] + vec_rows([w] * 4 + [f]), :].astype(F32)
        gain, shift, bias0, bias1, upbias = vecs_of(block, [w] * 4 + [f])
        norms_ref[1, 0:1, :] = gain
        norms_ref[1, 1:2, :] = shift
        bias_ref[0:1, :] = bias0
        bias_ref[1:2, :] = bias1
        upbias_ref[...] = upbias.reshape(f)


def bits():
    head = [("head", 1 << i) for i in range(lax.axis_size("head").bit_length() - 1)]
    dp = [("dp", 1 << i) for i in range(lax.axis_size("dp").bit_length() - 1)]
    return head + dp


def bit_here(axis, bit):
    return (lax.axis_index(axis) // bit) % 2


def index_at(index_ref, first, count):
    index = 0
    for i in range(count):
        index = index * 2 + index_ref[first + i]
    return index


def swap(x, group, d):
    heads = lax.axis_size("head")
    flip = {"dp": 0, "head": 0}
    for k, (axis, bit) in enumerate(group[::-1]):
        if d >> k & 1:
            flip[axis] |= bit
    pairs = [
        (i * heads + j, (i ^ flip["dp"]) * heads + (j ^ flip["head"]))
        for i in range(lax.axis_size("dp"))
        for j in range(heads)
    ]
    return lax.ppermute(x, ("dp", "head"), pairs)


def others(x):
    count = lax.axis_size("head")
    return [
        lax.ppermute(x, "head", [(i, i ^ d) for i in range(count)]) for d in range(1, count)
    ]


class Sum:
    def __init__(self, index, order):
        self.index = index
        self.bits = order
        self.devices = 1 << len(self.bits)
        self.ins, self.counts, self.halves = [], [], []
        self.done = 1
        self.cost = 1

    def add(self, pack):
        keep, send = pack
        self.halves.append(keep.shape[0])
        self.ins += [keep, swap(send, self.bits[:1], 1)]
        self.counts.append(2)
        self.rows = round_up(sum(self.halves), self.devices // 2 * 16)

    def step(self, cost=1):
        self.cost = cost
        if self.plan:
            what, count = self.plan.pop(0)
            what(self, count)
            if what is Sum.meet:
                self.step(cost)

    def meet(self, other):
        while other.plan:
            other.step()
        self.shared = (other.rows, self.rows)
        self.ins = [*other.ins, *self.ins]
        self.counts = other.counts + self.counts
        self.rows += other.rows

    def fold(self, count):
        group = self.bits[self.done : self.done + count]
        cuts = 1 << count
        pieces = call(
            functools.partial(fold_kernel, self.counts, (self.done, count), self.rows),
            (sds((self.rows // cuts, 128), BF16),) * cuts,
            (self.index, *self.ins),
            [SMEM] + [VMEM] * len(self.ins),
            [pltpu.VMEM((self.rows, 128), BF16)],
            moved=self.cost,
            spare=2,
        )
        self.rows = self.rows // cuts
        self.counts = [cuts]
        self.done += count
        self.ins = [pieces[0]] + [swap(pieces[d], group, d) for d in range(1, cuts)]

    def turn(self, count):
        self.fold(0)
        self.spread(self.ins[0], count)

    def spread(self, whole, count):
        group = self.bits[self.done - count : self.done]
        self.ins = [whole] + [swap(whole, group, d) for d in range(1, 1 << count)]
        self.done -= count
        self.last = count

    def join(self, count):
        rows = self.ins[0].shape[0] * len(self.ins)
        whole = call(
            functools.partial(join_kernel, (self.done, self.last)),
            sds((rows, 128), BF16),
            (self.index, *self.ins),
            [SMEM] + [VMEM] * len(self.ins),
            moved=self.cost,
            spare=2,
        )
        self.spread(whole, count)


def from_sides(left, right):
    count = lax.axis_size("head")
    return (
        lax.ppermute(left, "head", [(i, i + 1) for i in range(count - 1)]),
        lax.ppermute(right, "head", [(i + 1, i) for i in range(count - 1)]),
    )


def block_forward(br, meta, sub, x, halo, qkv, norms, w_qkv, w_out, w_up, w_down, bias, upbias):
    n, w, f = br.n, br.w, br.f
    outs = (
        sds((n, w), BF16),
        sds((ROWS, w), F32),
        sds((br.r, w), BF16),
        sds((br.r, w), BF16),
        sds((br.t, 8, 128), F32),
        sds((n, w), BF16),
        sds((n, w), F32),
        sds((f // 256, n, 256), BF16),
        sds((f // 256, n, 256), BF16),
        sds((n, w), BF16),
    )
    ins = (meta, x, *halo, *qkv, norms, w_qkv, w_out, w_up, w_down, bias, upbias, sub)
    return call(
        functools.partial(forward_kernel, br),
        outs,
        ins,
        [SMEM] + [VMEM] * (len(ins) - 1),
        [pltpu.VMEM((br.t, w, 128), F32)],
        far=(7, 8, 4, 1, 9, 12, 13, 10, 11),
        far_out=range(2, 10),
    )


def ffn_back(br, index, col, lane, dy, cross, dcls, kept, norms, w_out, w_up, w_down):
    n, w, f = br.n, br.w, br.f
    parts = [("up", mat_rows(w, f)), ("down", mat_rows(f, w)), ("out", mat_rows(w, w))]
    at, rows = layout(parts)
    at["rows"], at["end"], at["col"] = rows, sum(r for _, r in parts), col
    ins = (index, lane, dy, cross, dcls, *kept, norms, w_out, w_up, w_down)
    half = sds((rows // 2, 128), BF16)
    vec = sds((vec_rows([w] * 4 + [f]), 128), F32)
    keep, send, *outs = call(
        functools.partial(ffn_back_kernel, br, at),
        (half, half, sds((n, w), F32), sds((n, w), BF16), vec),
        ins,
        [SMEM] + [VMEM] * (len(ins) - 1),
        [pltpu.VMEM((rows, 128), BF16)],
        far=(2, 7, 9, 12, 6, 11, 5, 10, 8),
        far_out=(2, 3),
    )
    return at, (keep, send), outs


def attn_loop(br, meta, q, kwin, vwin, dheads, lse):
    size = 128 * max(len(g[2]) for g in br.groups)
    ins = (meta, q, kwin, vwin, dheads, lse)
    return call(
        functools.partial(attn_loop_kernel, br),
        (sds((br.r, br.w), F32),) * 2 + (sds((br.n, br.w), BF16),),
        ins,
        [SMEM] + [VMEM] * (len(ins) - 1),
        [
            pltpu.VMEM((br.t, br.w, 128), F32),
            pltpu.VMEM((br.kw, size), BF16),
            pltpu.VMEM((br.kw, size), BF16),
        ],
        far=range(1, 6),
    )


def attn_post(br, index, grads, x, halo, norms, w_qkv, dmid, vec, before):
    n, w = br.n, br.w
    parts = [("qkv", mat_rows(w, 3 * w)), ("vec1", vec_rows([w, w])), ("vec2", vec.shape[0])]
    at, rows = layout(parts)
    at["rows"], at["end"] = rows, sum(r for _, r in parts)
    ins = (index, x, *halo, norms, w_qkv, dmid, vec, *grads, *before)
    half = sds((rows // 2, 128), BF16)
    keep, send, *outs = call(
        functools.partial(attn_post_kernel, br, at),
        (half, half, sds((n, w), F32), sds((br.end, 128), BF16), sds((br.end, 128), BF16)),
        ins,
        [SMEM] + [VMEM] * (len(ins) - 1),
        [
            pltpu.VMEM((br.r, w), BF16),
            pltpu.VMEM((rows, 128), BF16),
        ],
        far=range(1, 7),
    )
    return at, (keep, send), outs


def on_device(
    seg_large,
    seg_small,
    x_large,
    x_small,
    dy_large,
    dy_small,
    lb_norms,
    lb_qkv,
    lb_out,
    lb_up,
    lb_down,
    lb_bias,
    lb_upbias,
    sb_norms,
    sb_qkv,
    sb_out,
    sb_up,
    sb_down,
    sb_bias,
    sb_upbias,
    fl_norms,
    fl_proj,
    fl_query,
    fl_keyval,
    fl_out,
    fl_back,
    fl_bias,
    fs_norms,
    fs_proj,
    fs_query,
    fs_keyval,
    fs_out,
    fs_back,
    fs_bias,
):
    xl, xs, dyl, dys = x_large[0], x_small[0], dy_large[0], dy_small[0]
    small = Branch(*xs.shape, sb_up.shape[1], MOST_S)
    large = Branch(*xl.shape, lb_up.shape[1], MOST_L, small.end)
    cxs = (Cross(large.w, small.w, small.n), Cross(small.w, large.w, large.n))
    share = 1.0 / lax.axis_size("head")
    wide = round_up(large.w + small.w, 128)
    sb_down, fl_proj, fs_back = sb_down.T, fl_proj.T, fs_back.T
    order = bits()
    index = [bit_here(axis, bit) for axis, bit in order]
    index += [jnp.zeros((), jnp.int32)] * (15 - len(order)) + [lax.axis_index("head")]
    index = jnp.stack(index).astype(jnp.int32)
    ORDER.clear()

    edge = sds((large.end, 128), BF16)
    halo = from_sides(
        *call(functools.partial(edge_kernel, (large, small)), (edge, edge), (xl, xs))
    )
    words = sds((16,), jnp.int32)
    lanes = sds((8, 128), jnp.int32)
    subs = sds((ROWS, 128), jnp.int32)
    start = call(
        functools.partial(start_kernel, large, small),
        (sds((large.n, large.w), BF16),) * 3
        + (sds((small.n, small.w), BF16),) * 3
        + (words, words, lanes, lanes, subs, subs, sds((ROWS, wide), F32)),
        (index, seg_large, seg_small, xl, xs, dyl, dys, lb_norms, sb_norms, lb_qkv, sb_qkv),
        [SMEM] + [VMEM] * 10,
        [
            pltpu.VMEM((2 * ROWS + 16, 128), jnp.int32),
            pltpu.SMEM((2 * ROWS + 16, 128), jnp.int32),
            pltpu.SemaphoreType.DMA,
        ],
        out_specs=(VMEM,) * 6 + (SMEM, SMEM) + (VMEM,) * 5,
        far=range(1, 11),
        far_out=(0, 3),
    )
    qkv_l, qkv_s = start[:3], start[3:6]
    meta_l, meta_s, lane_l, lane_s, sub_l, sub_s, dcls = start[6:]
    dcls_all = [dcls] + others(dcls)

    ys, cls_s, kwin_s, vwin_s, lse_s, ho_s, mid_s, hid_s, slope_s, ys_far = block_forward(
        small, meta_s, sub_s, xs, halo, qkv_s, sb_norms, sb_qkv, sb_out, sb_up, sb_down,
        sb_bias, sb_upbias,
    )
    yl, cls_l, kwin_l, vwin_l, lse_l, ho_l, mid_l, hid_l, slope_l, yl_far = block_forward(
        large, meta_l, sub_l, xl, halo, qkv_l, lb_norms, lb_qkv, lb_out, lb_up, lb_down,
        lb_bias, lb_upbias,
    )

    cls = jnp.concatenate(
        [cls_l, cls_s, jnp.zeros((ROWS, wide - large.w - small.w), F32)], axis=1
    )
    cls_all = [cls] + others(cls)
    key_s, key_l = call(
        functools.partial(keys_kernel, cxs),
        (sds((small.n, small.w), BF16), sds((large.n, large.w), BF16)),
        (ys, fl_norms, yl, fs_norms),
        far=(1, 3),
    )
    wl, ws = large.w, small.w
    part, sc_l, sc_s, ab_l, ab_s, qa_l, qb_l, qa_s, qb_s = call(
        functools.partial(cross_front_kernel, cxs),
        (
            sds((ROWS + 8, wide), F32),
            sds((small.n, 128), F32),
            sds((large.n, 128), F32),
            sds((128, ws), BF16),
            sds((128, wl), BF16),
            sds((4, ROWS, wl), F32),
            sds((7, ROWS, ws), F32),
            sds((4, ROWS, ws), F32),
            sds((7, ROWS, wl), F32),
        ),
        (
            *cls_all, lane_s, lane_l, key_s, key_l,
            fl_norms, fl_proj, fl_query, fl_keyval, fl_bias,
            fs_norms, fs_proj, fs_query, fs_keyval, fs_bias,
        ),
        far=range(8, 18),
        far_out=(3, 4),
    )
    part_all = [part] + others(part)
    vec1 = [ws, ws, wl, wl]
    both = lambda shape: (sds(shape[:1] + (ws,), shape[1]), sds(shape[:1] + (wl,), shape[1]))
    (
        dquery, rt_l, rt_s, gk_l, gk_s, ds_l, ds_s, p_l, p_s, av_l, av_s, back_cls, block0,
    ) = call(
        functools.partial(cross_back_kernel, cxs, share),
        (
            sds((ROWS, wide), F32),
            sds((7, ROWS, ws), F32),
            sds((7, ROWS, wl), F32),
            *both((128, F32)),
            *(sds((small.n, 128), BF16), sds((large.n, 128), BF16)) * 2,
            *both((128, BF16)),
            sds((ROWS, wide), F32),
            sds((vec_rows(vec1), 128), F32),
        ),
        (
            *dcls_all, *part_all, lane_s, lane_l, key_s, key_l, sc_l, sc_s, qb_l, qb_s,
            fl_norms, fl_keyval, fl_out, fl_back, fl_bias,
            fs_norms, fs_keyval, fs_out, fs_back, fs_bias,
        ),
        far=range(16, 26),
        far_out=(9, 10, 11),
    )
    far = len(order) - 3
    sum_f, sum_g, sum_q = (Sum(index, order) for _ in range(3))
    fold, join = (Sum.fold, 1), (Sum.join, 1)
    rest = [fold] * far + [(Sum.turn, 1)] + [join] * (far - 1) + [(Sum.join, 2), join]
    sum_f.plan = [(Sum.fold, 2)] + rest
    sum_g.plan = [(Sum.fold, 2)]
    sum_q.plan = [(Sum.fold, 2), (Sum.meet, sum_g)] + rest

    def packed(kernel, items, unit, ins, more=(), far=()):
        at, rows = layout(items, unit)
        at["rows"], at["end"] = rows, sum(r for _, r in items)
        half = sds((rows // 2, 128), BF16)
        keep, send, *rest = call(
            functools.partial(kernel, cxs, at, share),
            (half, half, *more),
            ins,
            [SMEM] + [VMEM] * (len(ins) - 1),
            [pltpu.VMEM((rows, 128), BF16)],
            far=far,
        )
        return at, (keep, send), rest

    def query_backward(dquery_all):
        return call(
            functools.partial(cross_query_back_kernel, cxs, share),
            (
                sds((ROWS, wide), F32),
                sds((2, ROWS, ws), F32),
                sds((2, ROWS, wl), F32),
                sds((vec_rows(vec2), 128), F32),
            ),
            (
                *dquery_all, qa_l, qb_l, rt_l, fl_norms, fl_proj, fl_query, fl_keyval,
                qa_s, qb_s, rt_s, fs_norms, fs_proj, fs_query, fs_keyval,
            ),
            far=(7, 8, 9, 10, 14, 15, 16, 17),
        )

    ORDER[:] = [block0]
    dquery_all = [dquery] + others(dquery)
    vec2 = [wl, ws, wl, ws, ws, ws, ws, wl, ws, wl, wl, wl]
    items = []
    for cx, name in zip(cxs, "ls"):
        items += [
            ("keyval" + name, mat_rows(cx.wb, 2 * cx.wb)),
            ("out" + name, mat_rows(cx.wb, cx.wb)),
            ("back" + name, mat_rows(cx.wb, cx.wa)),
        ]
    at_c1, pack_c1, (cross_s, cross_l, block1) = packed(
        cross_grads_one_kernel,
        items,
        32,
        (
            index, *dcls_all, qb_l, rt_l, gk_l, ds_l, p_l, ab_l, av_l, key_s, ys, fl_norms,
            qb_s, rt_s, gk_s, ds_s, p_s, ab_s, av_s, key_l, yl, fs_norms,
        ),
        (
            sds((small.n, ws), F32),
            sds((large.n, wl), F32),
            sds((vec_rows(vec1), 128), F32),
        ),
        (14, 24, 10, 11, 20, 21),
    )
    sum_f.add(pack_c1)
    dcls_new, dm_l, dm_s, block2 = query_backward(dquery_all)
    widths = {"vec0": vec1, "vec1": vec1, "vec2": vec2, "vec3": [wl, ws]}
    items = []
    for cx, name in zip(cxs, "ls"):
        items += [("proj" + name, mat_rows(cx.wa, cx.wb)), ("query" + name, mat_rows(cx.wb, cx.wb))]
    items += [(name, vec_rows(of)) for name, of in widths.items()]
    at_c2, pack_c2, _ = packed(
        cross_grads_two_kernel,
        items,
        32,
        (index, *dcls_all, block0, block1, block2, qa_l, qb_l, dm_l, qa_s, qb_s, dm_s),
    )
    at_c2["widths"] = widths
    sum_g.add(pack_c2)
    at_fl, pack_fl, (dmid_l, dheads_l, vec_l) = ffn_back(
        large, index, 0, lane_l, dyl, cross_l, dcls_new,
        (hid_l, slope_l, mid_l, ho_l), lb_norms, lb_out, lb_up, lb_down,
    )
    sum_f.add(pack_fl)
    at_fs, pack_fs, (dmid_s, dheads_s, vec_s) = ffn_back(
        small, index, wl, lane_s, dys, cross_s, dcls_new,
        (hid_s, slope_s, mid_s, ho_s), sb_norms, sb_out, sb_up, sb_down,
    )
    sum_g.add(pack_fs)

    def settled(dx_l, dx_s, first, last):
        return call(
            functools.partial(settle_kernel, (large, small)),
            (
                sds((large.n, wl), BF16),
                sds((ws, small.n) if small.turned else (small.n, ws), BF16),
            ),
            (dx_l, dx_s, *from_sides(last, first)),
        )

    def unpack(kernel, outs, done, rows, shared=None):
        while done.plan:
            done.step()
        pieces = halves_of(rows[0], shared and (done.shared[0], sum(done.shared), 0))
        if shared:
            first = len(rows[0])
            more = halves_of(rows[1], (done.shared[1], sum(done.shared), done.shared[0]))
            pieces += [(first + pack, *rest) for pack, *rest in more]
        return call(
            functools.partial(kernel, pieces),
            outs,
            (index, *done.ins),
            [SMEM, VMEM, VMEM],
            [pltpu.VMEM((r, 128), BF16) for part in rows for r in part],
            far_out=[i for i, out in enumerate(outs) if math.prod(out.shape) > 1 << 13],
        )

    def block_outs(br):
        return [
            sds((br.w, br.w), F32),
            sds((br.w, br.f), F32),
            sds((br.w, br.f) if br.turned else (br.f, br.w), F32),
        ]

    def unpack_early():
        outs = block_outs(large)
        for cx in cxs:
            less, more = min(cx.wa, cx.wb), max(cx.wa, cx.wb)
            outs += [sds((cx.wb, 2 * cx.wb), F32), sds((cx.wb, cx.wb), F32), sds((less, more), F32)]

        def kernel(pieces, *refs):
            unpack_early_kernel(large, cxs, at_fl, at_c1, pieces, *refs)

        return unpack(kernel, tuple(outs), sum_f, [(at_c1["rows"], at_fl["rows"])])

    def unpack_late():
        outs, found = block_outs(small), {"l": (large, made["at_l"]), "s": (small, made["at_s"])}
        for cx in cxs:
            wa, wb = cx.wa, cx.wb
            outs += [
                sds((2, wa + 2 * wb), F32),
                sds((min(wa, wb), max(wa, wb)), F32),
                sds((wb, wb), F32),
                sds((wa + 2 * wb,), F32),
            ]
        brs, ats = zip(*(found[name] for name in made["packs"]))
        for br in brs:
            outs += [
                sds((br.w, 3 * br.w), F32),
                sds((2, 2, br.w), F32),
                sds((2, br.w), F32),
                sds((br.f,), F32),
            ]

        def kernel(pieces, *refs):
            unpack_late_kernel(small, cxs, brs, ats, at_fs, at_c2, pieces, *refs)

        rows = [(at_c2["rows"], at_fs["rows"]), tuple(at["rows"] for at in ats)]
        got = unpack(kernel, tuple(outs), sum_q, rows, True)
        return got[:11], {name: got[11 + 4 * i : 15 + 4 * i] for i, name in enumerate(made["packs"])}

    made = {"packs": ""}
    sums = {"f": sum_f, "g": sum_g, "q": sum_q}

    def do(what):
        if what == "loop_l":
            made["grads"] = attn_loop(large, meta_l, qkv_l[0], kwin_l, vwin_l, dheads_l, lse_l)
        elif what == "loop_s":
            made["grads"] = attn_loop(small, meta_s, qkv_s[0], kwin_s, vwin_s, dheads_s, lse_s)
        elif what == "post_l":
            made["at_l"], pack, made["dx_l"] = attn_post(
                large, index, made["grads"], xl, halo, lb_norms, lb_qkv, dmid_l, vec_l,
                made["dx_s"][1:],
            )
            sum_q.add(pack)
            made["packs"] += "l"
        elif what == "post_s":
            made["at_s"], pack, made["dx_s"] = attn_post(
                small, index, made["grads"], xs, halo, sb_norms, sb_qkv, dmid_s, vec_s, ()
            )
            sum_q.add(pack)
            made["packs"] += "s"
        elif what == "place":
            made["out"] = call(
                functools.partial(place_kernel, (large, small)),
                (
                    sds((large.n, wl), BF16),
                    sds((ws, small.n) if small.turned else (small.n, ws), BF16),
                ),
                (back_cls, lane_l, lane_s, yl_far, ys_far),
                far=(0, 3, 4),
            )
        elif what == "dx":
            made["dx"] = settled(made["dx_l"][0], made["dx_s"][0], *made["dx_l"][1:])
        elif what == "out_f":
            made["f"] = unpack_early()
        elif what == "out_q":
            made["g"], made["q"] = unpack_late()
        else:
            sums[what.lower()].step(COSTLY if what.isupper() else 1)

    for what in SCHEDULE:
        do(what)
    o_l, u_l, d_l, *others_c = made["f"]
    o_s, u_s, d_s, *crossed = made["g"]
    q_l, norms_l, bias_l, upbias_l = made["q"]["l"]
    q_s, norms_s, bias_s, upbias_s = made["q"]["s"]
    grad_xl, grad_xs = made["dx"]
    out_l, out_s = made["out"]
    ORDER.clear()
    fl, fs = (
        [*crossed[4 * i : 4 * i + 3], *others_c[3 * i : 3 * i + 3], crossed[4 * i + 3]]
        for i in range(2)
    )
    fl[1], fs[5] = fl[1].T, fs[5].T
    if small.turned:
        out_s, grad_xs, d_s = out_s.T, grad_xs.T, d_s.T
    return (
        out_l[None],
        out_s[None],
        grad_xl[None],
        grad_xs[None],
        norms_l,
        q_l,
        o_l,
        u_l,
        d_l,
        bias_l,
        upbias_l,
        norms_s,
        q_s,
        o_s,
        u_s,
        d_s,
        bias_s,
        upbias_s,
        *fl,
        *fs,
    )


def solution(mesh):
    rows = P("dp", "head", None)
    return jax.shard_map(
        on_device,
        mesh=mesh,
        in_specs=(P("dp", None),) * 2 + (rows,) * 4 + (P(),) * 28,
        out_specs=(rows,) * 4 + (P(),) * 28,
        check_vma=False,
    )
```

```python
import functools
import math

import jax
import jax.numpy as jnp
from jax import lax
from jax.experimental import pallas as pl
from jax.experimental.pallas import tpu as pltpu
from jax.sharding import PartitionSpec as P

HEADS = 6
IMGS = 10
ROWS = 16
MOST_L = 197
MOST_S = 401
EPS = 1e-6
NEG = -1e30
LOG2E = math.log2(math.e)
F32 = jnp.float32
BF16 = jnp.bfloat16
VMEM = pl.BlockSpec(memory_space=pltpu.VMEM)
SMEM = pl.BlockSpec(memory_space=pltpu.SMEM)
HBM = pl.BlockSpec(memory_space=pltpu.HBM)


COSTLY = 40 * 10**6
SCHEDULE = (
    "F", "loop_s", "post_s", "F", "G", "loop_l", "F", "post_l", "F", "Q", "f", "q", "f", "q", "dx",
    "q", "q", "place", "f", "Q", "out_f", "q", "out_q",
)
ORDER = []


def round_up(value, unit):
    return -(-value // unit) * unit


class Branch:
    def __init__(self, rows, width, hidden, most, before=0):
        self.n = rows
        self.w = width
        self.f = hidden
        self.dh = width // HEADS
        self.halo = round_up(most - 1, 16)
        self.kw = self.halo + 16
        self.r = rows + 2 * self.halo
        self.t = rows // 128
        self.cols = round_up(width, 128) // 128
        self.at = before
        self.end = before + self.halo * self.cols
        self.scale = self.dh ** (-0.5)
        self.turned = width % 128 != 0
        if width % 128 == 0:
            per = 128 // self.dh
            self.groups = [
                (i * 128, (i + 1) * 128, list(range(i * per, (i + 1) * per)))
                for i in range(width // 128)
            ]
        else:
            self.groups = [(0, width, list(range(HEADS)))]


def nn(a, b):
    return jnp.dot(a, b, preferred_element_type=F32)


def nt(a, b):
    return lax.dot_general(a, b, (((1,), (1,)), ((), ())), preferred_element_type=F32)


def tn(a, b):
    return lax.dot_general(a, b, (((0,), (0,)), ((), ())), preferred_element_type=F32)


def split(x):
    high = x.astype(BF16)
    return high, (x - high.astype(F32)).astype(BF16)


def normalize(x):
    center = x - jnp.mean(x, axis=-1, keepdims=True)
    rstd = lax.rsqrt(jnp.mean(center * center, axis=-1, keepdims=True) + EPS)
    return center * rstd, rstd


def norm_grad(unit, rstd, gain, upstream):
    scaled = upstream * gain
    mean_one = jnp.mean(scaled, axis=-1, keepdims=True)
    mean_two = jnp.mean(scaled * unit, axis=-1, keepdims=True)
    return (scaled - mean_one - unit * mean_two) * rstd


def col_sum(x):
    return jnp.sum(x, axis=0, keepdims=True)


def gelu_pair(x):
    cumulative = 0.5 * (1.0 + lax.erf(x * 0.7071067811865476))
    density = jnp.exp(-0.5 * x * x) * 0.3989422804014327
    return x * cumulative, cumulative + x * density


def iota(shape, dim):
    return lax.broadcasted_iota(jnp.int32, shape, dim)


def padded_bytes(item):
    *lead, rows, cols = (1, 1, *item.shape)
    unit = 32 // item.dtype.itemsize
    return math.prod(lead) * round_up(rows, unit) * round_up(cols, 128) * item.dtype.itemsize


def parts_of(item):
    return item.shape[0] if len(item.shape) == 3 and item.shape[1] * item.shape[2] > 1 << 14 else 1


class FarIn:
    def __init__(self, far, near, sems):
        pairs = [(far, near)]
        if len(sems) > 1:
            pairs = [(far.at[i], near.at[i]) for i in range(len(sems))]
        self.copies = [
            pltpu.make_async_copy(*pair, sem) for pair, sem in zip(pairs, sems, strict=True)
        ]
        for copy in self.copies:
            copy.start()
        self.near = near
        self.landed = [False] * len(sems)

    def land(self, i=None):
        for k, copy in enumerate(self.copies):
            if not self.landed[k] and i in (None, k):
                self.landed[k] = True
                copy.wait()

    @property
    def shape(self):
        return self.near.shape

    def __getitem__(self, where):
        self.land(where if isinstance(where, int) and len(self.copies) > 1 else None)
        return self.near[where]


class FarOut:
    def __init__(self, far, near, sems):
        pairs = [(near, far)]
        if len(sems) > 1:
            pairs = [(near.at[i], far.at[i]) for i in range(len(sems))]
        self.copies = [
            pltpu.make_async_copy(*pair, sem) for pair, sem in zip(pairs, sems, strict=True)
        ]
        self.near = near
        self.sent = [False] * len(sems)

    def send(self, i=None):
        for k, copy in enumerate(self.copies):
            if not self.sent[k] and i in (None, k):
                self.sent[k] = True
                copy.start()

    @property
    def shape(self):
        return self.near.shape

    def __getitem__(self, where):
        return self.near[where]

    def __setitem__(self, where, value):
        self.near[where] = value


def land(*refs):
    for ref in refs:
        if isinstance(ref, FarIn):
            ref.land()


def near(ref):
    return ref.near if isinstance(ref, (FarIn, FarOut)) else ref


def send(*refs):
    for ref in refs:
        if isinstance(ref, FarOut):
            ref.send()


def call(
    kernel,
    outs,
    ins,
    in_specs=None,
    scratch=(),
    moved=1,
    busy=0,
    out_specs=None,
    spare=10,
    far=(),
    far_out=(),
):
    in_specs = [VMEM] * len(ins) if in_specs is None else list(in_specs)
    flat = list(jax.tree.leaves(outs))
    specs = [VMEM] * len(flat) if out_specs is None else list(jax.tree.leaves(out_specs))
    for i in far:
        in_specs[i] = HBM
    for i in far_out:
        specs[i] = HBM
    held = list(zip(ins, in_specs)) + list(zip(flat, specs))
    need = sum(padded_bytes(item) for item, spec in held if spec is VMEM)
    near = [pltpu.VMEM(ins[i].shape, ins[i].dtype) for i in far]
    near += [pltpu.VMEM(flat[i].shape, flat[i].dtype) for i in far_out]
    scratch = list(scratch)
    for item in scratch + near:
        if getattr(item, "memory_space", None) == pltpu.VMEM:
            need += padded_bytes(sds(item.shape, jnp.dtype(item.dtype)))
    count = len(near)

    def wrapped(*refs):
        refs = list(refs)
        if not count:
            return kernel(*refs)
        refs, held, sems = refs[: -count - 1], refs[-count - 1 : -1], refs[-1]
        found, at = [], 0
        for k, i in enumerate([*far, *(i + len(ins) for i in far_out)]):
            size = parts_of(near[k])
            own = [sems.at[at + j] for j in range(size)]
            at += size
            refs[i] = (FarIn if k < len(far) else FarOut)(refs[i], held[k], own)
            found.append(refs[i])
        kernel(*refs)
        land(*found)
        send(*found)
        for ref in found:
            if isinstance(ref, FarOut):
                for copy in ref.copies:
                    copy.wait()

    total = sum(parts_of(item) for item in near)
    extra = near + [pltpu.SemaphoreType.DMA((total,))] if count else []
    ins = list(ins)
    if ORDER:
        i = next(i for i, spec in enumerate(in_specs) if spec is not SMEM)
        ins[i] = after(ORDER[-1], ins[i])
    for i in far:
        ins[i] = pltpu.with_memory_space_constraint(ins[i], pltpu.HBM)
    for i in far_out:
        flat[i] = pltpu.HBM(flat[i].shape, flat[i].dtype)
    results = pl.pallas_call(
        wrapped,
        out_shape=jax.tree.unflatten(jax.tree.structure(outs), flat),
        in_specs=in_specs,
        out_specs=jax.tree.unflatten(jax.tree.structure(outs), specs),
        scratch_shapes=scratch + extra,
        compiler_params=pltpu.CompilerParams(
            vmem_limit_bytes=min(need + spare * 2**20, 60 * 2**20)
        ),
        cost_estimate=pl.CostEstimate(
            flops=moved * 500 + busy * 10**9, bytes_accessed=moved, transcendentals=0
        ),
    )(*ins)
    if ORDER:
        ORDER[:] = [min(jax.tree.leaves(results), key=lambda item: item.size)]
    return results


def after(first, then):
    return lax.optimization_barrier((first, then))[1]


def sds(shape, dtype):
    return jax.ShapeDtypeStruct(shape, dtype)


def mat_rows(rows, cols):
    return rows * cols // 128


def put_halo(br, ref, value):
    low = value.astype(BF16)
    for i in range(br.cols):
        part = low[:, i * 128 : min((i + 1) * 128, br.w)]
        if part.shape[1] < 128:
            part = jnp.concatenate([part, jnp.zeros((br.halo, 128 - part.shape[1]), BF16)], axis=1)
        ref[br.at + i * br.halo : br.at + (i + 1) * br.halo, :] = part


def get_halo(br, ref):
    parts = [
        ref[br.at + i * br.halo : br.at + (i + 1) * br.halo, : min(128, br.w - i * 128)]
        for i in range(br.cols)
    ]
    return jnp.concatenate(parts, axis=1).astype(F32)


def vec_rows(widths):
    return round_up(sum(round_up(w, 128) // 128 for w in widths), 16)


def layout(items, unit=32):
    at, row = {}, 0
    for name, rows in items:
        at[name] = row
        row += rows
    return at, round_up(row, unit)


def pack_mat(ref, at, rows, cols, value):
    low = value.astype(BF16)
    full = cols // 128
    for i in range(full):
        ref[at + i * rows : at + (i + 1) * rows, :] = low[:, i * 128 : (i + 1) * 128]
    if cols % 128:
        tail = low[:, full * 128 :]
        at = at + full * rows
        half = rows // 2
        ref[at : at + half, :] = jnp.concatenate([tail[:half], tail[half:]], axis=1)


def unpack_mat(ref, at, rows, cols, out):
    full = cols // 128
    for i in range(full):
        out[:, i * 128 : (i + 1) * 128] = ref[at + i * rows : at + (i + 1) * rows, :].astype(F32)
    if cols % 128:
        at = at + full * rows
        half = rows // 2
        block = ref[at : at + half, :].astype(F32)
        out[:half, full * 128 :] = block[:, :64]
        out[half:, full * 128 :] = block[:, 64:]


def vec_block(values):
    pieces = []
    for value in values:
        width = value.shape[1]
        for i in range(0, width, 128):
            piece = value[:, i : min(i + 128, width)]
            if piece.shape[1] < 128:
                piece = jnp.concatenate(
                    [piece, jnp.zeros((1, 128 - piece.shape[1]), F32)], axis=1
                )
            pieces.append(piece)
    total = round_up(len(pieces), 16)
    if total > len(pieces):
        pieces.append(jnp.zeros((total - len(pieces), 128), F32))
    return jnp.concatenate(pieces, axis=0)


def vecs_of(block, widths):
    out, i = [], 0
    for width in widths:
        parts = []
        for j in range(0, width, 128):
            parts.append(block[i : i + 1, : min(128, width - j)])
            i += 1
        out.append(parts[0] if len(parts) == 1 else jnp.concatenate(parts, axis=1))
    return out


def emit(src_ref, outs, index):
    size = src_ref.shape[0] // len(outs)
    for d, out in enumerate(outs):
        at = pl.multiple_of((index ^ d) * size, 16)
        out[...] = src_ref[pl.ds(at, size), :]


def edge_kernel(brs, xl_ref, xs_ref, last_ref, first_ref):
    for br, ref in zip(brs, (xl_ref, xs_ref)):
        put_halo(br, last_ref, ref[br.n - br.halo :, :])
        put_halo(br, first_ref, ref[: br.halo, :])


def start_kernel(
    br_l,
    br_s,
    index_ref,
    seg_l_ref,
    seg_s_ref,
    xl_ref,
    xs_ref,
    dyl_ref,
    dys_ref,
    nl_ref,
    ns_ref,
    wl_ref,
    ws_ref,
    ql_ref,
    kl_ref,
    vl_ref,
    qs_ref,
    ks_ref,
    vs_ref,
    meta_l_ref,
    meta_s_ref,
    lane_l_ref,
    lane_s_ref,
    sub_l_ref,
    sub_s_ref,
    dcls_ref,
    vector_ref,
    scalar_ref,
    sem,
):
    col = 0
    dcls_ref[...] = jnp.zeros_like(dcls_ref)
    for br, seg_ref, dy_ref, meta_ref, lane_ref, sub_ref in (
        (br_l, seg_l_ref, dyl_ref, meta_l_ref, lane_l_ref, sub_l_ref),
        (br_s, seg_s_ref, dys_ref, meta_s_ref, lane_s_ref, sub_s_ref),
    ):
        own = index_ref[15] * br.n
        seg = seg_ref[...]
        image = iota((ROWS, seg.shape[1]), 0)
        starts = jnp.sum((seg < image).astype(jnp.int32), axis=1, keepdims=True)
        ends = jnp.sum((seg <= image).astype(jnp.int32), axis=1, keepdims=True)
        starts = jnp.broadcast_to(starts, (ROWS, 128))
        ends = jnp.broadcast_to(ends, (ROWS, 128))
        lane = iota((ROWS, 128), 1)
        diagonal = (lane - (lane // ROWS) * ROWS) == iota((ROWS, 128), 0)
        lo = jnp.sum(jnp.where(diagonal, starts, 0), axis=0, keepdims=True) - own
        hi = jnp.sum(jnp.where(diagonal, ends, 0), axis=0, keepdims=True) - own
        lane_ref[...] = jnp.concatenate([lo, hi, jnp.zeros((6, 128), jnp.int32)], axis=0)
        sub_ref[...] = starts - own
        real = iota((ROWS, 128), 0) < IMGS
        first = jnp.sum(jnp.where(real & (starts <= own), 1, 0), axis=0, keepdims=True) - 1
        last = jnp.sum(jnp.where(real & (starts < own + br.n), 1, 0), axis=0, keepdims=True) - 1
        at = 0 if br is br_l else ROWS + 8
        vector_ref[at : at + ROWS, :] = starts
        vector_ref[at + ROWS : at + ROWS + 8, :] = jnp.concatenate(
            [first, last, jnp.zeros((6, 128), jnp.int32)], axis=0
        )
        pick = (iota((ROWS, br.n), 1) == (starts - own)[:, 0:1]).astype(F32).astype(BF16)
        dcls_ref[:, col : col + br.w] = nn(pick, dy_ref[...])
        col += br.w
    copy = pltpu.make_async_copy(vector_ref, scalar_ref, sem)
    copy.start()
    for x_ref, norms_ref, w_ref, outs in (
        (xl_ref, nl_ref, wl_ref, (ql_ref, kl_ref, vl_ref)),
        (xs_ref, ns_ref, ws_ref, (qs_ref, ks_ref, vs_ref)),
    ):
        width = x_ref.shape[1]
        unit, _ = normalize(x_ref[...].astype(F32))
        normed = (unit * norms_ref[0, 0:1, :] + norms_ref[0, 1:2, :]).astype(BF16)
        for i, ref in enumerate(outs):
            ref[...] = nn(normed, w_ref[:, i * width : (i + 1) * width]).astype(BF16)
    copy.wait()
    for br, meta_ref, at in ((br_l, meta_l_ref, 0), (br_s, meta_s_ref, ROWS + 8)):
        for j in range(IMGS + 1):
            meta_ref[j] = scalar_ref[at + j, 0]
        meta_ref[11] = index_ref[15] * br.n
        meta_ref[12] = scalar_ref[at + ROWS, 0]
        meta_ref[13] = scalar_ref[at + ROWS + 1, 0]
        meta_ref[14] = 0
        meta_ref[15] = 0


def head_mask(br, head, c0, c1):
    lane = iota((1, c1 - c0), 1) + c0
    return jnp.logical_and(lane >= head * br.dh, lane < (head + 1) * br.dh)


def stack_heads(br, rows, group):
    c0, c1, heads = group
    part = rows[:, c0:c1]
    zero = jnp.zeros_like(part)
    return jnp.concatenate(
        [jnp.where(head_mask(br, h, c0, c1), part, zero) for h in heads], axis=0
    )


def image_span(br, meta_ref, j):
    base = meta_ref[11]
    lo = meta_ref[j] - base
    hi = meta_ref[j + 1] - base
    k0 = pl.multiple_of(((lo + br.halo) // 16) * 16, 16)
    t0 = jnp.maximum(lo, 0) // 128
    t1 = (jnp.minimum(hi, br.n) + 127) // 128
    return lo, hi, k0, t0, t1


def forward_kernel(
    br,
    meta_ref,
    x_ref,
    xl_ref,
    xr_ref,
    q_ref,
    k_ref,
    v_ref,
    norms_ref,
    wqkv_ref,
    wout_ref,
    wup_ref,
    wdown_ref,
    bias_ref,
    upbias_ref,
    sub_ref,
    y_ref,
    cls_ref,
    kwin_ref,
    vwin_ref,
    lse_ref,
    ho_ref,
    mid_ref,
    hid_ref,
    slope_ref,
    far_y_ref,
    ot_ref,
):
    n, w, f, dh, halo = br.n, br.w, br.f, br.dh, br.halo
    for ref, at in ((xl_ref, 0), (xr_ref, halo + n)):
        unit, _ = normalize(get_halo(br, ref))
        normed = (unit * norms_ref[0, 0:1, :] + norms_ref[0, 1:2, :]).astype(BF16)
        kwin_ref[at : at + halo, :] = nn(normed, wqkv_ref[:, w : 2 * w]).astype(BF16)
        vwin_ref[at : at + halo, :] = nn(normed, wqkv_ref[:, 2 * w :]).astype(BF16)
    kwin_ref[halo : halo + n, :] = k_ref[...]
    vwin_ref[halo : halo + n, :] = v_ref[...]
    send(vwin_ref)
    ot_ref[...] = jnp.zeros_like(ot_ref)
    lse_ref[...] = jnp.zeros(lse_ref.shape, F32)
    factor = br.scale * LOG2E
    land(q_ref)

    def image(j, carry):
        lo, hi, k0, t0, t1 = image_span(br, meta_ref, j)
        keys = kwin_ref[pl.ds(k0, br.kw), :]
        values_t = vwin_ref[pl.ds(k0, br.kw), :].T
        row = iota((br.kw, 128), 0) + (k0 - br.halo)
        mask = jnp.logical_and(row >= lo, row < hi)

        def tile(t, carry):
            rows = q_ref[pl.ds(pl.multiple_of(t * 128, 128), 128), :]
            lane = iota((1, 128), 1) + t * 128
            inside = jnp.logical_and(lane >= lo, lane < hi)
            for group in br.groups:
                c0, c1, heads = group
                scores = nt(keys[:, c0:c1], stack_heads(br, rows, group))
                for i, h in enumerate(heads):
                    s = jnp.where(mask, scores[:, i * 128 : (i + 1) * 128] * factor, NEG)
                    top = jnp.max(s, axis=0, keepdims=True)
                    p = jnp.exp2(s - top)
                    total = col_sum(p)
                    o = nn(values_t[h * dh : (h + 1) * dh, :], p.astype(BF16))
                    ot_ref[t, h * dh : (h + 1) * dh, :] += o * jnp.where(inside, 1.0 / total, 0.0)
                    lse_ref[t, h : h + 1, :] = jnp.where(
                        inside, top + jnp.log2(total), lse_ref[t, h : h + 1, :]
                    )
            return carry

        return lax.fori_loop(t0, t1, tile, carry)

    lax.fori_loop(meta_ref[12], meta_ref[13] + 1, image, 0)
    send(kwin_ref, lse_ref)
    for t in range(br.t):
        ho_ref[t * 128 : (t + 1) * 128, :] = ot_ref[t].T.astype(BF16)
    mid = x_ref[...].astype(F32) + (nn(ho_ref[...], wout_ref[...]) + bias_ref[0:1, :])
    mid_ref[...] = mid
    unit, _ = normalize(mid)
    normed = (unit * norms_ref[1, 0:1, :] + norms_ref[1, 1:2, :]).astype(BF16)
    send(ho_ref, mid_ref)
    total = mid + bias_ref[1:2, :]
    step = 256
    upbias = upbias_ref[...].reshape(1, f)
    for c in range(0, f, step):
        pre = nn(normed, wup_ref[:, c : c + step]) + upbias[:, c : c + step]
        act, slope = gelu_pair(pre)
        act = act.astype(BF16)
        i = c // step
        hid_ref[i] = act
        slope_ref[i] = slope.astype(BF16)
        if br.turned:
            total = total + nt(act, wdown_ref[:, c : c + step])
        else:
            total = total + nn(act, wdown_ref[c : c + step, :])
    y = total.astype(BF16)
    y_ref[...] = y
    far_y_ref[...] = y
    send(far_y_ref)
    pick = (iota((ROWS, n), 1) == sub_ref[:, 0:1]).astype(F32).astype(BF16)
    cls_ref[...] = nn(pick, y)


def ffn_back_kernel(
    br,
    at,
    index_ref,
    lane_ref,
    dy_ref,
    cross_ref,
    dcls_ref,
    hid_ref,
    slope_ref,
    mid_ref,
    ho_ref,
    norms_ref,
    wout_ref,
    wup_ref,
    wdown_ref,
    keep_ref,
    send_ref,
    dmid_ref,
    dheads_ref,
    vec_ref,
    pack_ref,
):
    n, w, f = br.n, br.w, br.f
    c0 = at["col"]
    cls = dcls_ref[:, c0 : c0 + w].astype(BF16)
    hit = (iota((n, 128), 0) == lane_ref[0:1, :]).astype(F32)
    hit = jnp.where(iota((1, 128), 1) < IMGS, hit, 0.0)
    first = jnp.sum(hit, axis=1, keepdims=True) > 0.5
    placed = nn(hit[:, :ROWS].astype(BF16), cls)
    gy = jnp.where(first, placed, dy_ref[...].astype(F32) + cross_ref[...]).astype(BF16)
    gy_float = gy.astype(F32)
    dn2 = jnp.zeros((n, w), F32)
    step = 256
    upbias = []
    unit, rstd = normalize(mid_ref[...])
    normed_t = (unit * norms_ref[1, 0:1, :] + norms_ref[1, 1:2, :]).astype(BF16).T
    gy_t = gy.T
    if at["rows"] > at["end"]:
        pack_ref[at["end"] :, :] = jnp.zeros((at["rows"] - at["end"], 128), BF16)
    for i, c in enumerate(range(0, f, step)):
        if br.turned:
            dpre = nn(gy, wdown_ref[:, c : c + step])
        else:
            dpre = nt(gy, wdown_ref[c : c + step, :])
        dpre = (dpre * slope_ref[i].astype(F32)).astype(BF16)
        upbias.append(col_sum(dpre.astype(F32)))
        rows = i * mat_rows(w, step)
        pack_mat(pack_ref, at["up"] + rows, w, step, nn(normed_t, dpre))
        dn2 = dn2 + nt(dpre, wup_ref[:, c : c + step])
        pack_mat(pack_ref, at["down"] + rows, w, step, nn(gy_t, hid_ref[i]))
    dmid = gy_float + norm_grad(unit, rstd, norms_ref[1, 0:1, :], dn2)
    dmid_ref[...] = dmid
    send(dmid_ref)
    dattn = dmid.astype(BF16)
    dheads_ref[...] = nt(dattn, wout_ref[...]).astype(BF16)
    send(dheads_ref)
    pack_mat(pack_ref, at["out"], w, w, tn(ho_ref[...], dattn))
    vec_ref[...] = vec_block(
        [col_sum(dn2 * unit), col_sum(dn2), col_sum(dattn.astype(F32)), col_sum(gy_float)] + upbias
    )
    emit(pack_ref, (keep_ref, send_ref), index_ref[0])


def attn_loop_kernel(
    br,
    meta_ref,
    q_ref,
    kwin_ref,
    vwin_ref,
    dheads_ref,
    lse_ref,
    dk_ref,
    dv_ref,
    dq_ref,
    dqt_ref,
    p_ref,
    ds_ref,
):
    dh = br.dh
    dk_ref[...] = jnp.zeros(dk_ref.shape, F32)
    dv_ref[...] = jnp.zeros_like(dv_ref)
    dqt_ref[...] = jnp.zeros_like(dqt_ref)
    factor = br.scale * LOG2E
    land(q_ref, kwin_ref, vwin_ref, dheads_ref, lse_ref)

    def image(j, carry):
        lo, hi, k0, t0, t1 = image_span(br, meta_ref, j)
        span = pl.ds(k0, br.kw)
        keys = kwin_ref[span, :]
        keys_t = keys.T
        values = vwin_ref[span, :]
        row = iota((br.kw, 128), 0) + (k0 - br.halo)
        mask = jnp.logical_and(row >= lo, row < hi)

        def tile(t, carry):
            here = pl.ds(pl.multiple_of(t * 128, 128), 128)
            rows = q_ref[here, :]
            outs = dheads_ref[here, :]
            lane = iota((1, 128), 1) + t * 128
            inside = jnp.logical_and(lane >= lo, lane < hi)
            for group in br.groups:
                c0, c1, heads = group
                queries = stack_heads(br, rows, group)
                upstream = stack_heads(br, outs, group)
                scores = nt(keys[:, c0:c1], queries)
                dprobs = nt(values[:, c0:c1], upstream)
                for i, h in enumerate(heads):
                    part = slice(i * 128, (i + 1) * 128)
                    lse = jnp.where(inside, lse_ref[t, h : h + 1, :], -NEG)
                    p = jnp.exp2(scores[:, part] * factor - lse)
                    p = jnp.where(mask, p, 0.0)
                    dp = dprobs[:, part]
                    ds = (p * (dp - col_sum(p * dp))).astype(BF16)
                    p_ref[:, part] = p.astype(BF16)
                    ds_ref[:, part] = ds
                    dqt_ref[t, h * dh : (h + 1) * dh, :] += nn(
                        keys_t[h * dh : (h + 1) * dh, :], ds
                    )
                size = 128 * len(heads)
                dv_ref[span, c0:c1] += nn(p_ref[:, :size], upstream)
                dk_ref[span, c0:c1] += nn(ds_ref[:, :size], queries)
            return carry

        return lax.fori_loop(t0, t1, tile, carry)

    lax.fori_loop(meta_ref[12], meta_ref[13] + 1, image, 0)
    for t in range(br.t):
        dq_ref[t * 128 : (t + 1) * 128, :] = (dqt_ref[t].T * br.scale).astype(BF16)


def attn_post_kernel(
    br,
    at,
    index_ref,
    x_ref,
    xl_ref,
    xr_ref,
    norms_ref,
    wqkv_ref,
    dmid_ref,
    vec_ref,
    dk_ref,
    dv_ref,
    dq_ref,
    *refs,
):
    before, refs = refs[:-7], refs[-7:]
    keep_ref, send_ref, dx_ref, dxl_ref, dxr_ref, normed_ref, pack_ref = refs
    for ref, out in zip(before, (dxl_ref, dxr_ref)):
        out[: br.at, :] = ref[...]
    n, w, halo = br.n, br.w, br.halo
    dk = (dk_ref[...] * br.scale).astype(BF16)
    dv = dv_ref[...].astype(BF16)
    gain, shift = norms_ref[0, 0:1, :], norms_ref[0, 1:2, :]
    dgain = jnp.zeros((1, w), F32)
    dshift = jnp.zeros((1, w), F32)
    for ref, lo, size, out in (
        (xl_ref, 0, halo, dxl_ref),
        (x_ref, halo, n, dx_ref),
        (xr_ref, halo + n, halo, dxr_ref),
    ):
        rows = ref[...].astype(F32) if ref is x_ref else get_halo(br, ref)
        unit, rstd = normalize(rows)
        normed_ref[lo : lo + size, :] = (unit * gain + shift).astype(BF16)
        up = nt(dk[lo : lo + size], wqkv_ref[:, w : 2 * w])
        up = up + nt(dv[lo : lo + size], wqkv_ref[:, 2 * w :])
        if out is dx_ref:
            up = up + nt(dq_ref[...], wqkv_ref[:, :w])
        dgain = dgain + col_sum(up * unit)
        dshift = dshift + col_sum(up)
        dx = norm_grad(unit, rstd, gain, up)
        if out is dx_ref:
            out[...] = dx + dmid_ref[...]
        else:
            put_halo(br, out, dx)
    whole = jnp.concatenate(
        [
            tn(normed_ref[halo : halo + n, :], dq_ref[...]),
            tn(normed_ref[...], dk),
            tn(normed_ref[...], dv),
        ],
        axis=1,
    )
    pack_mat(pack_ref, at["qkv"], w, 3 * w, whole)
    block = vec_block([dgain, dshift])
    pack_ref[at["vec1"] : at["vec1"] + block.shape[0], :] = block.astype(BF16)
    pack_ref[at["vec2"] : at["vec2"] + vec_ref.shape[0], :] = vec_ref[...].astype(BF16)
    if at["rows"] > at["end"]:
        pack_ref[at["end"] :, :] = jnp.zeros((at["rows"] - at["end"], 128), BF16)
    emit(pack_ref, (keep_ref, send_ref), index_ref[0])


class Cross:
    def __init__(self, wa, wb, rows_b):
        self.wa = wa
        self.wb = wb
        self.dh = wb // HEADS
        self.n = rows_b
        self.scale = self.dh ** (-0.5)
        self.proj = nt if wa > wb else nn
        self.proj_back = nn if wa > wb else nt
        self.back = nn if wa > wb else nt
        self.back_back = nt if wa > wb else nn

    def by_head(self):
        head = iota((128, self.wb), 0) // ROWS
        col = iota((128, self.wb), 1)
        return jnp.logical_and(col >= head * self.dh, col < (head + 1) * self.dh).astype(F32)

    def by_image(self):
        lane = iota((ROWS, 128), 1)
        return jnp.logical_and(
            lane - (lane // ROWS) * ROWS == iota((ROWS, 128), 0), lane < HEADS * ROWS
        ).astype(F32)


def spread(cx, low_rows):
    return jnp.concatenate([low_rows] * 8, axis=0) * cx.by_head().astype(low_rows.dtype)


def gather_heads(cx, wide):
    kept = wide * cx.by_head()
    total = kept[0:ROWS]
    for h in range(1, HEADS):
        total = total + kept[h * ROWS : (h + 1) * ROWS]
    return total


def to_lane(cx, *items):
    stack = jnp.concatenate([part for item in items for part in split(item)], axis=0)
    wide = nt(stack, cx.by_head().astype(BF16))
    image = cx.by_image()
    found = []
    for i in range(0, 2 * ROWS * len(items), 2 * ROWS):
        found.append(col_sum(image * (wide[i : i + ROWS] + wide[i + ROWS : i + 2 * ROWS])))
    return found


def from_lane(cx, *items):
    image = cx.by_image()
    stack = jnp.concatenate([part for item in items for part in split(image * item)], axis=0)
    wide = nn(stack, cx.by_head().astype(BF16))
    return [
        wide[i : i + ROWS] + wide[i + ROWS : i + 2 * ROWS]
        for i in range(0, 2 * ROWS * len(items), 2 * ROWS)
    ]


def cross_query(cx, cls, norms_ref, proj_ref, query_ref, keyval_ref, bias_ref, qa_ref, qb_ref):
    wa, wb = cx.wa, cx.wb
    unit_a, rstd_a = normalize(cls)
    lifted = unit_a * norms_ref[0:1, :wa] + norms_ref[1:2, :wa]
    act, slope = gelu_pair(lifted)
    act = act.astype(BF16)
    bias = bias_ref[...].reshape(1, bias_ref.shape[0])[:, :wb]
    moved = cx.proj(act, proj_ref[...]) + bias
    gain, shift = norms_ref[0:1, wa : wa + wb], norms_ref[1:2, wa : wa + wb]
    unit_q, rstd_q = normalize(moved)
    query_in = (unit_q * gain + shift).astype(BF16)
    fquery = nn(query_in, query_ref[...]).astype(BF16)
    kself = nn(query_in, keyval_ref[:, :wb]).astype(BF16)
    vself = nn(query_in, keyval_ref[:, wb:]).astype(BF16)
    for i, item in enumerate((unit_a, slope, act, jnp.broadcast_to(rstd_a, unit_a.shape))):
        qa_ref[i] = item.astype(F32)
    for i, item in enumerate(
        (moved, unit_q, query_in, fquery, kself, vself, jnp.broadcast_to(rstd_q, moved.shape))
    ):
        qb_ref[i] = item.astype(F32)
    return fquery


def allowed_rows(cx, lane_ref):
    row = iota((cx.n, 128), 0)
    return jnp.logical_and(row > lane_ref[0:1, :], row < lane_ref[1:2, :])


def keys_kernel(cxs, ys_ref, fln_ref, yl_ref, fsn_ref, ks_ref, kl_ref):
    for cx, y_ref, norms_ref, out_ref in (
        (cxs[0], ys_ref, fln_ref, ks_ref),
        (cxs[1], yl_ref, fsn_ref, kl_ref),
    ):
        wa, wb = cx.wa, cx.wb
        unit, _ = normalize(y_ref[...].astype(F32))
        out_ref[...] = (
            unit * norms_ref[0:1, wa : wa + wb] + norms_ref[1:2, wa : wa + wb]
        ).astype(BF16)


def cross_front_kernel(
    cxs,
    c0_ref,
    c1_ref,
    c2_ref,
    c3_ref,
    lane_s_ref,
    lane_l_ref,
    key_s_ref,
    key_l_ref,
    fln_ref,
    flp_ref,
    flq_ref,
    flk_ref,
    flb_ref,
    fsn_ref,
    fsp_ref,
    fsq_ref,
    fsk_ref,
    fsb_ref,
    part_ref,
    sc_l_ref,
    sc_s_ref,
    ab_l_ref,
    ab_s_ref,
    qa_l_ref,
    qb_l_ref,
    qa_s_ref,
    qb_s_ref,
):
    cls = c0_ref[...] + c1_ref[...] + c2_ref[...] + c3_ref[...]
    wl, ws = cxs[0].wa, cxs[1].wa
    col = 0
    stats = []
    for cx, rows, key_ref, lane_ref, keyval_ref, weights, kept, sc_ref, ab_ref in (
        (
            cxs[0],
            cls[:, :wl],
            key_s_ref,
            lane_s_ref,
            flk_ref,
            (fln_ref, flp_ref, flq_ref, flk_ref, flb_ref),
            (qa_l_ref, qb_l_ref),
            sc_l_ref,
            ab_l_ref,
        ),
        (
            cxs[1],
            cls[:, wl : wl + ws],
            key_l_ref,
            lane_l_ref,
            fsk_ref,
            (fsn_ref, fsp_ref, fsq_ref, fsk_ref, fsb_ref),
            (qa_s_ref, qb_s_ref),
            sc_s_ref,
            ab_s_ref,
        ),
    ):
        fquery = cross_query(cx, rows, *weights, *kept)
        absorbed = nt(spread(cx, fquery), keyval_ref[:, : cx.wb]).astype(BF16)
        ab_ref[...] = absorbed
        key = key_ref[...]
        allowed = allowed_rows(cx, lane_ref)
        scores = jnp.where(allowed, nt(key, absorbed) * (cx.scale * LOG2E), NEG)
        sc_ref[...] = scores
        top = jnp.max(scores, axis=0, keepdims=True)
        p = jnp.where(allowed, jnp.exp2(scores - top), 0.0)
        high, low = split(p)
        mixed_high, mixed_low = split(tn(high, key) + tn(low, key))
        value_part = keyval_ref[:, cx.wb :]
        out = gather_heads(cx, nn(mixed_high, value_part) + nn(mixed_low, value_part))
        part_ref[0:ROWS, col : col + cx.wb] = out
        col += cx.wb
        stats += [top, col_sum(p)]
    width = part_ref.shape[1]
    part_ref[0:ROWS, col:] = jnp.zeros((ROWS, width - col), F32)
    part_ref[ROWS:, :] = jnp.zeros((8, width), F32)
    part_ref[ROWS : ROWS + 4, :128] = jnp.concatenate(stats, axis=0)


def cross_back_kernel(
    cxs,
    share,
    g0_ref,
    g1_ref,
    g2_ref,
    g3_ref,
    p0_ref,
    p1_ref,
    p2_ref,
    p3_ref,
    lane_s_ref,
    lane_l_ref,
    key_s_ref,
    key_l_ref,
    sc_l_ref,
    sc_s_ref,
    qb_l_ref,
    qb_s_ref,
    fln_ref,
    flk_ref,
    flo_ref,
    flw_ref,
    flb_ref,
    fsn_ref,
    fsk_ref,
    fso_ref,
    fsw_ref,
    fsb_ref,
    dq_ref,
    rt_l_ref,
    rt_s_ref,
    gk_l_ref,
    gk_s_ref,
    ds_l_ref,
    ds_s_ref,
    p_l_ref,
    p_s_ref,
    av_l_ref,
    av_s_ref,
    back_ref,
    vec_ref,
):
    dcls = g0_ref[...] + g1_ref[...] + g2_ref[...] + g3_ref[...]
    parts = [p0_ref, p1_ref, p2_ref, p3_ref]
    vecs = []
    col_b = 0
    col_a = 0
    for index, (cx, key_ref, lane_ref, sc_ref, qb_ref, weights, outs) in enumerate(
        (
            (
                cxs[0],
                key_s_ref,
                lane_s_ref,
                sc_l_ref,
                qb_l_ref,
                (fln_ref, flk_ref, flo_ref, flw_ref, flb_ref),
                (rt_l_ref, gk_l_ref, ds_l_ref, p_l_ref, av_l_ref),
            ),
            (
                cxs[1],
                key_l_ref,
                lane_l_ref,
                sc_s_ref,
                qb_s_ref,
                (fsn_ref, fsk_ref, fso_ref, fsw_ref, fsb_ref),
                (rt_s_ref, gk_s_ref, ds_s_ref, p_s_ref, av_s_ref),
            ),
        )
    ):
        norms_ref, keyval_ref, wout_ref, wback_ref, bias_ref = weights
        rt_ref, gk_ref, ds_ref, p_ref, av_ref = outs
        wa, wb = cx.wa, cx.wb
        moved, fquery, kself, vself = qb_ref[0], qb_ref[3], qb_ref[4], qb_ref[5]
        self_score = to_lane(cx, fquery * kself)[0] * (cx.scale * LOG2E)
        tops = [p[ROWS + 2 * index : ROWS + 2 * index + 1, :128] for p in parts]
        sums = [p[ROWS + 2 * index + 1 : ROWS + 2 * index + 2, :128] for p in parts]
        top = self_score
        for item in tops:
            top = jnp.maximum(top, item)
        own = jnp.exp2(self_score - top)
        total = own
        weights_of = []
        for item, amount in zip(tops, sums):
            weight = jnp.exp2(item - top)
            weights_of.append(weight)
            total = total + amount * weight
        inverse = 1.0 / total
        p_self = own * inverse
        spans = from_lane(cx, p_self, *(weight * inverse for weight in weights_of))
        fheads = spans[0] * vself
        for part, span in zip(parts, spans[1:]):
            fheads = fheads + part[0:ROWS, col_b : col_b + wb] * span
        fheads_low = fheads.astype(BF16)
        bias = bias_ref[...].reshape(1, bias_ref.shape[0])
        joined = moved + (nn(fheads_low, wout_ref[...]) + bias[:, wb : 2 * wb])
        unit_r, rstd_r = normalize(joined)
        gain_r = norms_ref[0:1, wa + wb :]
        reverted = unit_r * gain_r + norms_ref[1:2, wa + wb :]
        act_r, slope_r = gelu_pair(reverted)
        act_r = act_r.astype(BF16)
        back_ref[:, col_a : col_a + wa] = cx.back(act_r, wback_ref[...]) + bias[:, 2 * wb :]
        dback_low = dcls[:, col_a : col_a + wa].astype(BF16)
        drev = cx.back_back(dback_low, wback_ref[...]) * slope_r
        djoined = norm_grad(unit_r, rstd_r, gain_r, drev)
        dattn = djoined.astype(BF16)
        dheads_low = nt(dattn, wout_ref[...]).astype(BF16)
        dheads = dheads_low.astype(F32)
        delta, dp_self = to_lane(cx, dheads * fheads, dheads * vself)
        ds_self = p_self * (dp_self - delta)
        ds_self_rows, p_self_rows = from_lane(
            cx, ds_self.astype(BF16).astype(F32), p_self.astype(BF16).astype(F32)
        )
        absorbed_high, absorbed_low = split(nt(spread(cx, dheads_low), keyval_ref[:, wb:]))
        av_ref[...] = absorbed_high
        key = key_ref[...]
        allowed = allowed_rows(cx, lane_ref)
        p = jnp.where(allowed, jnp.exp2(sc_ref[...] - (top + jnp.log2(total))), 0.0)
        dp = nt(key, absorbed_high) + nt(key, absorbed_low)
        ds = (p * (dp - delta)).astype(BF16)
        ds_ref[...] = ds
        p_ref[...] = p.astype(BF16)
        g_k = tn(ds, key)
        gk_ref[...] = g_k
        g_high, g_low = split(g_k)
        key_part = keyval_ref[:, :wb]
        dquery = gather_heads(cx, nn(g_high, key_part) + nn(g_low, key_part)) * cx.scale
        dq_ref[:, col_b : col_b + wb] = dquery + ds_self_rows * kself * (cx.scale * share)
        for i, item in enumerate(
            (
                fheads_low,
                act_r,
                dattn,
                djoined,
                dheads_low,
                ds_self_rows * fquery * cx.scale,
                p_self_rows * dheads,
            )
        ):
            rt_ref[i] = item.astype(F32)
        vecs += [col_sum(drev * unit_r) * share, col_sum(drev) * share]
        col_a += wa
        col_b += wb
    dq_ref[:, col_b:] = jnp.zeros((ROWS, dq_ref.shape[1] - col_b), F32)
    back_ref[:, col_a:] = jnp.zeros((ROWS, back_ref.shape[1] - col_a), F32)
    vec_ref[...] = vec_block(vecs)


def place_kernel(brs, back_ref, lane_l_ref, lane_s_ref, yl_ref, ys_ref, *outs):
    col = 0
    for br, lane_ref, y_ref, out_ref in zip(brs, (lane_l_ref, lane_s_ref), (yl_ref, ys_ref), outs):
        hit = (iota((br.n, 128), 0) == lane_ref[0:1, :]).astype(F32)
        hit = jnp.where(iota((1, 128), 1) < IMGS, hit, 0.0)
        first = jnp.sum(hit, axis=1, keepdims=True) > 0.5
        placed = nn(hit[:, :ROWS].astype(BF16), back_ref[:, col : col + br.w].astype(BF16))
        result = jnp.where(first, placed, y_ref[...].astype(F32))
        out_ref[...] = (result.T if br.turned else result).astype(BF16)
        col += br.w


def cross_query_back_kernel(
    cxs,
    share,
    d0_ref,
    d1_ref,
    d2_ref,
    d3_ref,
    qa_l_ref,
    qb_l_ref,
    rt_l_ref,
    fln_ref,
    flp_ref,
    flq_ref,
    flk_ref,
    qa_s_ref,
    qb_s_ref,
    rt_s_ref,
    fsn_ref,
    fsp_ref,
    fsq_ref,
    fsk_ref,
    dcls_ref,
    dm_l_ref,
    dm_s_ref,
    vec_ref,
):
    dquery_all = d0_ref[...] + d1_ref[...] + d2_ref[...] + d3_ref[...]
    col_a = col_b = 0
    vecs = []
    for cx, qa_ref, qb_ref, rt_ref, norms_ref, proj_ref, query_ref, keyval_ref, dm_ref in (
        (cxs[0], qa_l_ref, qb_l_ref, rt_l_ref, fln_ref, flp_ref, flq_ref, flk_ref, dm_l_ref),
        (cxs[1], qa_s_ref, qb_s_ref, rt_s_ref, fsn_ref, fsp_ref, fsq_ref, fsk_ref, dm_s_ref),
    ):
        wa, wb = cx.wa, cx.wb
        dquery = dquery_all[:, col_b : col_b + wb].astype(BF16)
        dkself = rt_ref[5].astype(BF16)
        dvself = rt_ref[6].astype(BF16)
        dquery_in = (
            nt(dquery, query_ref[...])
            + nt(dkself, keyval_ref[:, :wb])
            + nt(dvself, keyval_ref[:, wb:])
        )
        unit_q, rstd_q = qb_ref[1], qb_ref[6]
        gain = norms_ref[0:1, wa : wa + wb]
        dmoved = norm_grad(unit_q, rstd_q, gain, dquery_in) + rt_ref[3]
        high, low = split(dmoved)
        dlifted = (cx.proj_back(high, proj_ref[...]) + cx.proj_back(low, proj_ref[...])) * qa_ref[1]
        unit_a = qa_ref[0]
        dcls_ref[:, col_a : col_a + wa] = norm_grad(
            unit_a, qa_ref[3], norms_ref[0:1, :wa], dlifted
        )
        dm_ref[0] = dmoved
        dm_ref[1] = dquery.astype(F32)
        vecs += [
            col_sum(dlifted * unit_a) * share,
            col_sum(dquery_in * unit_q) * share,
            col_sum(dlifted) * share,
            col_sum(dquery_in) * share,
            col_sum(dmoved) * share,
            col_sum(rt_ref[2]) * share,
        ]
        col_a += wa
        col_b += wb
    dcls_ref[:, col_a:] = jnp.zeros((ROWS, dcls_ref.shape[1] - col_a), F32)
    vec_ref[...] = vec_block(vecs)


def cross_grads_one_kernel(
    cxs,
    at,
    share,
    index_ref,
    g0_ref,
    g1_ref,
    g2_ref,
    g3_ref,
    qb_l_ref,
    rt_l_ref,
    gk_l_ref,
    ds_l_ref,
    p_l_ref,
    ab_l_ref,
    av_l_ref,
    key_s_ref,
    ys_ref,
    fln_ref,
    qb_s_ref,
    rt_s_ref,
    gk_s_ref,
    ds_s_ref,
    p_s_ref,
    ab_s_ref,
    av_s_ref,
    key_l_ref,
    yl_ref,
    fsn_ref,
    keep_ref,
    send_ref,
    cross_s_ref,
    cross_l_ref,
    vec_ref,
    pack_ref,
):
    dcls = g0_ref[...] + g1_ref[...] + g2_ref[...] + g3_ref[...]
    col_a = 0
    vecs = []
    for cx, name, cross_ref, ins in (
        (
            cxs[0],
            "l",
            cross_s_ref,
            (qb_l_ref, rt_l_ref, gk_l_ref, ds_l_ref, p_l_ref, ab_l_ref, av_l_ref)
            + (key_s_ref, ys_ref, fln_ref),
        ),
        (
            cxs[1],
            "s",
            cross_l_ref,
            (qb_s_ref, rt_s_ref, gk_s_ref, ds_s_ref, p_s_ref, ab_s_ref, av_s_ref)
            + (key_l_ref, yl_ref, fsn_ref),
        ),
    ):
        qb_ref, rt_ref, gk_ref, ds_ref, p_ref, ab_ref, av_ref, key_ref, y_ref, norms_ref = ins
        wa, wb = cx.wa, cx.wb
        p = p_ref[...]
        dkey = nn(ds_ref[...], ab_ref[...]) * cx.scale + nn(p, av_ref[...])
        unit_b, rstd_b = normalize(y_ref[...].astype(F32))
        cross_ref[...] = norm_grad(unit_b, rstd_b, norms_ref[0:1, wa : wa + wb], dkey)
        vecs += [col_sum(dkey * unit_b), col_sum(dkey)]
        dback = dcls[:, col_a : col_a + wa].astype(BF16)
        query_in, fquery = qb_ref[2].astype(BF16), qb_ref[3].astype(BF16)
        fheads, act_r, dattn, dheads, dkself, dvself = (
            rt_ref[i].astype(BF16) for i in (0, 1, 2, 4, 5, 6)
        )
        back = tn(act_r, dback) if wa > wb else tn(dback, act_r)
        pack_mat(pack_ref, at["back" + name], *back.shape, back * share)
        pack_mat(pack_ref, at["out" + name], wb, wb, tn(fheads, dattn) * share)
        keys = (
            tn(gk_ref[...].astype(BF16), spread(cx, fquery)) * cx.scale
            + tn(query_in, dkself) * share
        )
        values = tn(tn(p, key_ref[...]).astype(BF16), spread(cx, dheads))
        values = values + tn(query_in, dvself) * share
        pack_mat(pack_ref, at["keyval" + name], wb, 2 * wb, jnp.concatenate([keys, values], axis=1))
        col_a += wa
    vec_ref[...] = vec_block(vecs)
    if at["rows"] > at["end"]:
        pack_ref[at["end"] :, :] = jnp.zeros((at["rows"] - at["end"], 128), BF16)
    emit(pack_ref, (keep_ref, send_ref), index_ref[0])


def cross_grads_two_kernel(
    cxs,
    at,
    share,
    index_ref,
    g0_ref,
    g1_ref,
    g2_ref,
    g3_ref,
    vec0_ref,
    vec1_ref,
    vec2_ref,
    qa_l_ref,
    qb_l_ref,
    dm_l_ref,
    qa_s_ref,
    qb_s_ref,
    dm_s_ref,
    keep_ref,
    send_ref,
    pack_ref,
):
    dcls = g0_ref[...] + g1_ref[...] + g2_ref[...] + g3_ref[...]
    col_a = 0
    dbacks = []
    for cx, name, qa_ref, qb_ref, dm_ref in (
        (cxs[0], "l", qa_l_ref, qb_l_ref, dm_l_ref),
        (cxs[1], "s", qa_s_ref, qb_s_ref, dm_s_ref),
    ):
        wa, wb = cx.wa, cx.wb
        dbacks.append(col_sum(dcls[:, col_a : col_a + wa]) * share)
        act, query_in = qa_ref[2].astype(BF16), qb_ref[2].astype(BF16)
        dmoved = dm_ref[0].astype(BF16)
        proj = tn(dmoved, act) if wa > wb else tn(act, dmoved)
        pack_mat(pack_ref, at["proj" + name], *proj.shape, proj * share)
        query = tn(query_in, dm_ref[1].astype(BF16)) * share
        pack_mat(pack_ref, at["query" + name], wb, wb, query)
        col_a += wa
    for name, block in (
        ("vec0", vec0_ref[...]),
        ("vec1", vec1_ref[...]),
        ("vec2", vec2_ref[...]),
        ("vec3", vec_block(dbacks)),
    ):
        pack_ref[at[name] : at[name] + block.shape[0], :] = block.astype(BF16)
    if at["rows"] > at["end"]:
        pack_ref[at["end"] :, :] = jnp.zeros((at["rows"] - at["end"], 128), BF16)
    emit(pack_ref, (keep_ref, send_ref), index_ref[0])


def fold_kernel(counts, group, rows, index_ref, *refs):
    total = sum(counts)
    ins, refs = refs[:total], refs[total:]
    outs, sum_ref = refs[:-1], refs[-1]
    at = i = 0
    for count in counts:
        value = ins[i][...].astype(F32)
        for other in ins[i + 1 : i + count]:
            value = value + other[...].astype(F32)
        size = value.shape[0]
        sum_ref[at : at + size, :] = value.astype(BF16)
        at += size
        i += count
    if rows > at:
        sum_ref[at:, :] = jnp.zeros((rows - at, 128), BF16)
    emit(sum_ref, outs, index_at(index_ref, *group))


def join_kernel(group, index_ref, *refs):
    *parts, out_ref = refs
    index = index_at(index_ref, *group)
    for d, part in enumerate(parts):
        size = part.shape[0]
        at = pl.multiple_of((index ^ d) * size, 16)
        out_ref[pl.ds(at, size), :] = part[...]


def settle_kernel(brs, dxl_ref, dxs_ref, left_ref, right_ref, *outs):
    for br, dx_ref, out in zip(brs, (dxl_ref, dxs_ref), outs):
        rest = jnp.zeros((br.n - br.halo, br.w), F32)
        dx = dx_ref[...] + jnp.concatenate([get_halo(br, left_ref), rest], axis=0)
        dx = dx + jnp.concatenate([rest, get_halo(br, right_ref)], axis=0)
        out[...] = (dx.T if br.turned else dx).astype(BF16)


def halves_of(sizes, shared=None):
    pieces, at = [], 0
    for pack, size in enumerate(sizes):
        done, half = 0, size // 2
        while done < half:
            row, count = at + done, half - done
            if shared:
                mine, both, first = shared
                count = min(count, mine - row % mine)
                row = row // mine * both + first + row % mine
            pieces.append((pack, done, row, count))
            done += count
        at += half
    return pieces


def gather_packs(index, own_ref, got_ref, packs, pieces):
    for pack, row, at, size in pieces:
        half = packs[pack].shape[0] // 2
        for d, part in enumerate((own_ref, got_ref)):
            to = pl.multiple_of((index ^ d) * half + row, 16)
            packs[pack][pl.ds(to, size), :] = part[at : at + size, :]


def unpack_block(br, at, ref, out_ref, up_ref, down_ref):
    w, f, step = br.w, br.f, 256
    unpack_mat(ref, at["out"], w, w, out_ref)
    for j, c in enumerate(range(0, f, step)):
        rows, cols = j * mat_rows(w, step), slice(c, c + step)
        unpack_mat(ref, at["up"] + rows, w, step, near(up_ref).at[:, cols])
        if br.turned:
            unpack_mat(ref, at["down"] + rows, w, step, near(down_ref).at[:, cols])
            continue
        for k in range(step // 128):
            a = at["down"] + rows + k * w
            down_ref[c + k * 128 : c + (k + 1) * 128, :] = ref[a : a + w, :].astype(F32).T
    send(out_ref, up_ref, down_ref)


def unpack_early_kernel(br, cxs, at, at1, pieces, index_ref, own_ref, got_ref, *refs):
    outs, (ref1, ref) = refs[:-2], refs[-2:]
    gather_packs(index_ref[0], own_ref, got_ref, (ref1, ref), pieces)
    unpack_block(br, at, ref, *outs[:3])
    for i, (cx, name) in enumerate(zip(cxs, "ls")):
        keyval_ref, out_ref, back_ref = outs[3 + 3 * i : 6 + 3 * i]
        wa, wb = cx.wa, cx.wb
        unpack_mat(ref1, at1["keyval" + name], wb, 2 * wb, keyval_ref)
        unpack_mat(ref1, at1["out" + name], wb, wb, out_ref)
        unpack_mat(ref1, at1["back" + name], min(wa, wb), max(wa, wb), back_ref)
        send(keyval_ref, out_ref, back_ref)


def unpack_late_kernel(br, cxs, brs, ats, at, at2, pieces, index_ref, own_ref, got_ref, *refs):
    outs, (ref2, ref, *packs) = refs[:-4], refs[-4:]
    gather_packs(index_ref[0], own_ref, got_ref, (ref2, ref, *packs), pieces)
    unpack_qkv(brs, ats, packs, outs[11:])
    unpack_block(br, at, ref, *outs[:3])

    def vectors(name):
        widths = at2["widths"][name]
        return vecs_of(ref2[at2[name] : at2[name] + vec_rows(widths), :].astype(F32), widths)

    vec0, vec1, vec2, vec3 = (vectors("vec%d" % i) for i in range(4))
    for i, (cx, name) in enumerate(zip(cxs, "ls")):
        norms_ref, proj_ref, query_ref, bias_ref = outs[3 + 4 * i : 7 + 4 * i]
        wa, wb = cx.wa, cx.wb
        unpack_mat(ref2, at2["proj" + name], min(wa, wb), max(wa, wb), proj_ref)
        unpack_mat(ref2, at2["query" + name], wb, wb, query_ref)
        (gain_rev, shift_rev), (gain_key, shift_key) = (v[2 * i : 2 * i + 2] for v in (vec0, vec1))
        gain_a, gain_q, shift_a, shift_q, bias_a, bias_b = vec2[6 * i : 6 * i + 6]
        norms_ref[0:1, :] = jnp.concatenate([gain_a, gain_q + gain_key, gain_rev], axis=1)
        norms_ref[1:2, :] = jnp.concatenate([shift_a, shift_q + shift_key, shift_rev], axis=1)
        bias_ref[...] = jnp.concatenate([bias_a, bias_b, vec3[i]], axis=1).reshape(wa + 2 * wb)
        send(proj_ref, query_ref)


def unpack_qkv(brs, ats, packs, outs):
    for i, (br, at, ref) in enumerate(zip(brs, ats, packs)):
        qkv_ref, norms_ref, bias_ref, upbias_ref = outs[4 * i : 4 * i + 4]
        w, f = br.w, br.f
        unpack_mat(ref, at["qkv"], w, 3 * w, qkv_ref)
        send(qkv_ref)
        block = ref[at["vec1"] : at["vec1"] + vec_rows([w, w]), :].astype(F32)
        gain, shift = vecs_of(block, [w, w])
        norms_ref[0, 0:1, :] = gain
        norms_ref[0, 1:2, :] = shift
        block = ref[at["vec2"] : at["vec2"] + vec_rows([w] * 4 + [f]), :].astype(F32)
        gain, shift, bias0, bias1, upbias = vecs_of(block, [w] * 4 + [f])
        norms_ref[1, 0:1, :] = gain
        norms_ref[1, 1:2, :] = shift
        bias_ref[0:1, :] = bias0
        bias_ref[1:2, :] = bias1
        upbias_ref[...] = upbias.reshape(f)


def bits():
    head = [("head", 1 << i) for i in range(lax.axis_size("head").bit_length() - 1)]
    dp = [("dp", 1 << i) for i in range(lax.axis_size("dp").bit_length() - 1)]
    return head + dp


def bit_here(axis, bit):
    return (lax.axis_index(axis) // bit) % 2


def index_at(index_ref, first, count):
    index = 0
    for i in range(count):
        index = index * 2 + index_ref[first + i]
    return index


def swap(x, group, d):
    heads = lax.axis_size("head")
    flip = {"dp": 0, "head": 0}
    for k, (axis, bit) in enumerate(group[::-1]):
        if d >> k & 1:
            flip[axis] |= bit
    pairs = [
        (i * heads + j, (i ^ flip["dp"]) * heads + (j ^ flip["head"]))
        for i in range(lax.axis_size("dp"))
        for j in range(heads)
    ]
    return lax.ppermute(x, ("dp", "head"), pairs)


def others(x):
    count = lax.axis_size("head")
    return [
        lax.ppermute(x, "head", [(i, i ^ d) for i in range(count)]) for d in range(1, count)
    ]


class Sum:
    def __init__(self, index, order):
        self.index = index
        self.bits = order
        self.devices = 1 << len(self.bits)
        self.ins, self.counts, self.halves = [], [], []
        self.done = 1
        self.cost = 1

    def add(self, pack):
        keep, send = pack
        self.halves.append(keep.shape[0])
        self.ins += [keep, swap(send, self.bits[:1], 1)]
        self.counts.append(2)
        self.rows = round_up(sum(self.halves), self.devices // 2 * 16)

    def step(self, cost=1):
        self.cost = cost
        if self.plan:
            what, count = self.plan.pop(0)
            what(self, count)
            if what is Sum.meet:
                self.step(cost)

    def meet(self, other):
        while other.plan:
            other.step()
        self.shared = (other.rows, self.rows)
        self.ins = [*other.ins, *self.ins]
        self.counts = other.counts + self.counts
        self.rows += other.rows

    def fold(self, count):
        group = self.bits[self.done : self.done + count]
        cuts = 1 << count
        pieces = call(
            functools.partial(fold_kernel, self.counts, (self.done, count), self.rows),
            (sds((self.rows // cuts, 128), BF16),) * cuts,
            (self.index, *self.ins),
            [SMEM] + [VMEM] * len(self.ins),
            [pltpu.VMEM((self.rows, 128), BF16)],
            moved=self.cost,
            spare=2,
        )
        self.rows = self.rows // cuts
        self.counts = [cuts]
        self.done += count
        self.ins = [pieces[0]] + [swap(pieces[d], group, d) for d in range(1, cuts)]

    def turn(self, count):
        self.fold(0)
        self.spread(self.ins[0], count)

    def spread(self, whole, count):
        group = self.bits[self.done - count : self.done]
        self.ins = [whole] + [swap(whole, group, d) for d in range(1, 1 << count)]
        self.done -= count
        self.last = count

    def join(self, count):
        rows = self.ins[0].shape[0] * len(self.ins)
        whole = call(
            functools.partial(join_kernel, (self.done, self.last)),
            sds((rows, 128), BF16),
            (self.index, *self.ins),
            [SMEM] + [VMEM] * len(self.ins),
            moved=self.cost,
            spare=2,
        )
        self.spread(whole, count)


def from_sides(left, right):
    count = lax.axis_size("head")
    return (
        lax.ppermute(left, "head", [(i, i + 1) for i in range(count - 1)]),
        lax.ppermute(right, "head", [(i + 1, i) for i in range(count - 1)]),
    )


def block_forward(br, meta, sub, x, halo, qkv, norms, w_qkv, w_out, w_up, w_down, bias, upbias):
    n, w, f = br.n, br.w, br.f
    outs = (
        sds((n, w), BF16),
        sds((ROWS, w), F32),
        sds((br.r, w), BF16),
        sds((br.r, w), BF16),
        sds((br.t, 8, 128), F32),
        sds((n, w), BF16),
        sds((n, w), F32),
        sds((f // 256, n, 256), BF16),
        sds((f // 256, n, 256), BF16),
        sds((n, w), BF16),
    )
    ins = (meta, x, *halo, *qkv, norms, w_qkv, w_out, w_up, w_down, bias, upbias, sub)
    return call(
        functools.partial(forward_kernel, br),
        outs,
        ins,
        [SMEM] + [VMEM] * (len(ins) - 1),
        [pltpu.VMEM((br.t, w, 128), F32)],
        busy=10,
        far_out=(2, 3, 4, 9),
    )


def ffn_back(br, index, col, lane, dy, cross, dcls, kept, norms, w_out, w_up, w_down):
    n, w, f = br.n, br.w, br.f
    parts = [("up", mat_rows(w, f)), ("down", mat_rows(f, w)), ("out", mat_rows(w, w))]
    at, rows = layout(parts)
    at["rows"], at["end"], at["col"] = rows, sum(r for _, r in parts), col
    ins = (index, lane, dy, cross, dcls, *kept, norms, w_out, w_up, w_down)
    half = sds((rows // 2, 128), BF16)
    vec = sds((vec_rows([w] * 4 + [f]), 128), F32)
    keep, send, *outs = call(
        functools.partial(ffn_back_kernel, br, at),
        (half, half, sds((n, w), F32), sds((n, w), BF16), vec),
        ins,
        [SMEM] + [VMEM] * (len(ins) - 1),
        [pltpu.VMEM((rows, 128), BF16)],
        far=(2,) if br.turned else (),
        busy=7,
    )
    return at, (keep, send), outs


def attn_loop(br, meta, q, kwin, vwin, dheads, lse):
    size = 128 * max(len(g[2]) for g in br.groups)
    ins = (meta, q, kwin, vwin, dheads, lse)
    return call(
        functools.partial(attn_loop_kernel, br),
        (sds((br.r, br.w), F32),) * 2 + (sds((br.n, br.w), BF16),),
        ins,
        [SMEM] + [VMEM] * (len(ins) - 1),
        [
            pltpu.VMEM((br.t, br.w, 128), F32),
            pltpu.VMEM((br.kw, size), BF16),
            pltpu.VMEM((br.kw, size), BF16),
        ],
    )


def attn_post(br, index, grads, x, halo, norms, w_qkv, dmid, vec, before):
    n, w = br.n, br.w
    parts = [("qkv", mat_rows(w, 3 * w)), ("vec1", vec_rows([w, w])), ("vec2", vec.shape[0])]
    at, rows = layout(parts)
    at["rows"], at["end"] = rows, sum(r for _, r in parts)
    ins = (index, x, *halo, norms, w_qkv, dmid, vec, *grads, *before)
    half = sds((rows // 2, 128), BF16)
    keep, send, *outs = call(
        functools.partial(attn_post_kernel, br, at),
        (half, half, sds((n, w), F32), sds((br.end, 128), BF16), sds((br.end, 128), BF16)),
        ins,
        [SMEM] + [VMEM] * (len(ins) - 1),
        [
            pltpu.VMEM((br.r, w), BF16),
            pltpu.VMEM((rows, 128), BF16),
        ],
    )
    return at, (keep, send), outs


def on_device(
    seg_large,
    seg_small,
    x_large,
    x_small,
    dy_large,
    dy_small,
    lb_norms,
    lb_qkv,
    lb_out,
    lb_up,
    lb_down,
    lb_bias,
    lb_upbias,
    sb_norms,
    sb_qkv,
    sb_out,
    sb_up,
    sb_down,
    sb_bias,
    sb_upbias,
    fl_norms,
    fl_proj,
    fl_query,
    fl_keyval,
    fl_out,
    fl_back,
    fl_bias,
    fs_norms,
    fs_proj,
    fs_query,
    fs_keyval,
    fs_out,
    fs_back,
    fs_bias,
):
    xl, xs, dyl, dys = x_large[0], x_small[0], dy_large[0], dy_small[0]
    small = Branch(*xs.shape, sb_up.shape[1], MOST_S)
    large = Branch(*xl.shape, lb_up.shape[1], MOST_L, small.end)
    cxs = (Cross(large.w, small.w, small.n), Cross(small.w, large.w, large.n))
    share = 1.0 / lax.axis_size("head")
    wide = round_up(large.w + small.w, 128)
    sb_down, fl_proj, fs_back = sb_down.T, fl_proj.T, fs_back.T
    order = bits()
    index = [bit_here(axis, bit) for axis, bit in order]
    index += [jnp.zeros((), jnp.int32)] * (15 - len(order)) + [lax.axis_index("head")]
    index = jnp.stack(index).astype(jnp.int32)
    ORDER.clear()

    edge = sds((large.end, 128), BF16)
    halo = from_sides(
        *call(functools.partial(edge_kernel, (large, small)), (edge, edge), (xl, xs))
    )
    words = sds((16,), jnp.int32)
    lanes = sds((8, 128), jnp.int32)
    subs = sds((ROWS, 128), jnp.int32)
    start = call(
        functools.partial(start_kernel, large, small),
        (sds((large.n, large.w), BF16),) * 3
        + (sds((small.n, small.w), BF16),) * 3
        + (words, words, lanes, lanes, subs, subs, sds((ROWS, wide), F32)),
        (index, seg_large, seg_small, xl, xs, dyl, dys, lb_norms, sb_norms, lb_qkv, sb_qkv),
        [SMEM] + [VMEM] * 10,
        [
            pltpu.VMEM((2 * ROWS + 16, 128), jnp.int32),
            pltpu.SMEM((2 * ROWS + 16, 128), jnp.int32),
            pltpu.SemaphoreType.DMA,
        ],
        out_specs=(VMEM,) * 6 + (SMEM, SMEM) + (VMEM,) * 5,
        busy=4,
    )
    qkv_l, qkv_s = start[:3], start[3:6]
    meta_l, meta_s, lane_l, lane_s, sub_l, sub_s, dcls = start[6:]
    dcls_all = [dcls] + others(dcls)

    ys, cls_s, kwin_s, vwin_s, lse_s, ho_s, mid_s, hid_s, slope_s, ys_far = block_forward(
        small, meta_s, sub_s, xs, halo, qkv_s, sb_norms, sb_qkv, sb_out, sb_up, sb_down,
        sb_bias, sb_upbias,
    )
    yl, cls_l, kwin_l, vwin_l, lse_l, ho_l, mid_l, hid_l, slope_l, yl_far = block_forward(
        large, meta_l, sub_l, xl, halo, qkv_l, lb_norms, lb_qkv, lb_out, lb_up, lb_down,
        lb_bias, lb_upbias,
    )

    cls = jnp.concatenate(
        [cls_l, cls_s, jnp.zeros((ROWS, wide - large.w - small.w), F32)], axis=1
    )
    cls_all = [cls] + others(cls)
    key_s, key_l = call(
        functools.partial(keys_kernel, cxs),
        (sds((small.n, small.w), BF16), sds((large.n, large.w), BF16)),
        (ys, fl_norms, yl, fs_norms),
        busy=1,
    )
    wl, ws = large.w, small.w
    part, sc_l, sc_s, ab_l, ab_s, qa_l, qb_l, qa_s, qb_s = call(
        functools.partial(cross_front_kernel, cxs),
        (
            sds((ROWS + 8, wide), F32),
            sds((small.n, 128), F32),
            sds((large.n, 128), F32),
            sds((128, ws), BF16),
            sds((128, wl), BF16),
            sds((4, ROWS, wl), F32),
            sds((7, ROWS, ws), F32),
            sds((4, ROWS, ws), F32),
            sds((7, ROWS, wl), F32),
        ),
        (
            *cls_all, lane_s, lane_l, key_s, key_l,
            fl_norms, fl_proj, fl_query, fl_keyval, fl_bias,
            fs_norms, fs_proj, fs_query, fs_keyval, fs_bias,
        ),
        far_out=(3, 4),
        busy=4,
    )
    part_all = [part] + others(part)
    vec1 = [ws, ws, wl, wl]
    both = lambda shape: (sds(shape[:1] + (ws,), shape[1]), sds(shape[:1] + (wl,), shape[1]))
    (
        dquery, rt_l, rt_s, gk_l, gk_s, ds_l, ds_s, p_l, p_s, av_l, av_s, back_cls, block0,
    ) = call(
        functools.partial(cross_back_kernel, cxs, share),
        (
            sds((ROWS, wide), F32),
            sds((7, ROWS, ws), F32),
            sds((7, ROWS, wl), F32),
            *both((128, F32)),
            *(sds((small.n, 128), BF16), sds((large.n, 128), BF16)) * 2,
            *both((128, BF16)),
            sds((ROWS, wide), F32),
            sds((vec_rows(vec1), 128), F32),
        ),
        (
            *dcls_all, *part_all, lane_s, lane_l, key_s, key_l, sc_l, sc_s, qb_l, qb_s,
            fl_norms, fl_keyval, fl_out, fl_back, fl_bias,
            fs_norms, fs_keyval, fs_out, fs_back, fs_bias,
        ),
        far_out=(9, 10, 11),
        busy=6,
    )
    far = len(order) - 3
    sum_f, sum_g, sum_q = (Sum(index, order) for _ in range(3))
    fold, join = (Sum.fold, 1), (Sum.join, 1)
    rest = [fold] * far + [(Sum.turn, 1)] + [join] * (far - 1) + [(Sum.join, 2), join]
    sum_f.plan = [(Sum.fold, 2)] + rest
    sum_g.plan = [(Sum.fold, 2)]
    sum_q.plan = [(Sum.fold, 2), (Sum.meet, sum_g)] + rest

    def packed(kernel, items, unit, ins, more=(), far=()):
        at, rows = layout(items, unit)
        at["rows"], at["end"] = rows, sum(r for _, r in items)
        half = sds((rows // 2, 128), BF16)
        keep, send, *rest = call(
            functools.partial(kernel, cxs, at, share),
            (half, half, *more),
            ins,
            [SMEM] + [VMEM] * (len(ins) - 1),
            [pltpu.VMEM((rows, 128), BF16)],
            far=far,
        )
        return at, (keep, send), rest

    def query_backward(dquery_all):
        return call(
            functools.partial(cross_query_back_kernel, cxs, share),
            (
                sds((ROWS, wide), F32),
                sds((2, ROWS, ws), F32),
                sds((2, ROWS, wl), F32),
                sds((vec_rows(vec2), 128), F32),
            ),
            (
                *dquery_all, qa_l, qb_l, rt_l, fl_norms, fl_proj, fl_query, fl_keyval,
                qa_s, qb_s, rt_s, fs_norms, fs_proj, fs_query, fs_keyval,
            ),
            busy=2,
        )

    ORDER[:] = [block0]
    dquery_all = [dquery] + others(dquery)
    vec2 = [wl, ws, wl, ws, ws, ws, ws, wl, ws, wl, wl, wl]
    items = []
    for cx, name in zip(cxs, "ls"):
        items += [
            ("keyval" + name, mat_rows(cx.wb, 2 * cx.wb)),
            ("out" + name, mat_rows(cx.wb, cx.wb)),
            ("back" + name, mat_rows(cx.wb, cx.wa)),
        ]
    at_c1, pack_c1, (cross_s, cross_l, block1) = packed(
        cross_grads_one_kernel,
        items,
        32,
        (
            index, *dcls_all, qb_l, rt_l, gk_l, ds_l, p_l, ab_l, av_l, key_s, ys, fl_norms,
            qb_s, rt_s, gk_s, ds_s, p_s, ab_s, av_s, key_l, yl, fs_norms,
        ),
        (
            sds((small.n, ws), F32),
            sds((large.n, wl), F32),
            sds((vec_rows(vec1), 128), F32),
        ),
        (14, 24, 10, 11, 20, 21),
    )
    sum_f.add(pack_c1)
    dcls_new, dm_l, dm_s, block2 = query_backward(dquery_all)
    widths = {"vec0": vec1, "vec1": vec1, "vec2": vec2, "vec3": [wl, ws]}
    items = []
    for cx, name in zip(cxs, "ls"):
        items += [("proj" + name, mat_rows(cx.wa, cx.wb)), ("query" + name, mat_rows(cx.wb, cx.wb))]
    items += [(name, vec_rows(of)) for name, of in widths.items()]
    at_c2, pack_c2, _ = packed(
        cross_grads_two_kernel,
        items,
        32,
        (index, *dcls_all, block0, block1, block2, qa_l, qb_l, dm_l, qa_s, qb_s, dm_s),
    )
    at_c2["widths"] = widths
    sum_g.add(pack_c2)
    at_fl, pack_fl, (dmid_l, dheads_l, vec_l) = ffn_back(
        large, index, 0, lane_l, dyl, cross_l, dcls_new,
        (hid_l, slope_l, mid_l, ho_l), lb_norms, lb_out, lb_up, lb_down,
    )
    sum_f.add(pack_fl)
    at_fs, pack_fs, (dmid_s, dheads_s, vec_s) = ffn_back(
        small, index, wl, lane_s, dys, cross_s, dcls_new,
        (hid_s, slope_s, mid_s, ho_s), sb_norms, sb_out, sb_up, sb_down,
    )
    sum_g.add(pack_fs)

    def settled(dx_l, dx_s, first, last):
        return call(
            functools.partial(settle_kernel, (large, small)),
            (
                sds((large.n, wl), BF16),
                sds((ws, small.n) if small.turned else (small.n, ws), BF16),
            ),
            (dx_l, dx_s, *from_sides(last, first)),
        )

    def unpack(kernel, outs, done, rows, shared=None):
        while done.plan:
            done.step()
        pieces = halves_of(rows[0], shared and (done.shared[0], sum(done.shared), 0))
        if shared:
            first = len(rows[0])
            more = halves_of(rows[1], (done.shared[1], sum(done.shared), done.shared[0]))
            pieces += [(first + pack, *rest) for pack, *rest in more]
        return call(
            functools.partial(kernel, pieces),
            outs,
            (index, *done.ins),
            [SMEM, VMEM, VMEM],
            [pltpu.VMEM((r, 128), BF16) for part in rows for r in part],
            far_out=[i for i, out in enumerate(outs) if math.prod(out.shape) > 1 << 13],
        )

    def block_outs(br):
        return [
            sds((br.w, br.w), F32),
            sds((br.w, br.f), F32),
            sds((br.w, br.f) if br.turned else (br.f, br.w), F32),
        ]

    def unpack_early():
        outs = block_outs(large)
        for cx in cxs:
            less, more = min(cx.wa, cx.wb), max(cx.wa, cx.wb)
            outs += [sds((cx.wb, 2 * cx.wb), F32), sds((cx.wb, cx.wb), F32), sds((less, more), F32)]

        def kernel(pieces, *refs):
            unpack_early_kernel(large, cxs, at_fl, at_c1, pieces, *refs)

        return unpack(kernel, tuple(outs), sum_f, [(at_c1["rows"], at_fl["rows"])])

    def unpack_late():
        outs, found = block_outs(small), {"l": (large, made["at_l"]), "s": (small, made["at_s"])}
        for cx in cxs:
            wa, wb = cx.wa, cx.wb
            outs += [
                sds((2, wa + 2 * wb), F32),
                sds((min(wa, wb), max(wa, wb)), F32),
                sds((wb, wb), F32),
                sds((wa + 2 * wb,), F32),
            ]
        brs, ats = zip(*(found[name] for name in made["packs"]))
        for br in brs:
            outs += [
                sds((br.w, 3 * br.w), F32),
                sds((2, 2, br.w), F32),
                sds((2, br.w), F32),
                sds((br.f,), F32),
            ]

        def kernel(pieces, *refs):
            unpack_late_kernel(small, cxs, brs, ats, at_fs, at_c2, pieces, *refs)

        rows = [(at_c2["rows"], at_fs["rows"]), tuple(at["rows"] for at in ats)]
        got = unpack(kernel, tuple(outs), sum_q, rows, True)
        return got[:11], {name: got[11 + 4 * i : 15 + 4 * i] for i, name in enumerate(made["packs"])}

    made = {"packs": ""}
    sums = {"f": sum_f, "g": sum_g, "q": sum_q}

    def do(what):
        if what == "loop_l":
            made["grads"] = attn_loop(large, meta_l, qkv_l[0], kwin_l, vwin_l, dheads_l, lse_l)
        elif what == "loop_s":
            made["grads"] = attn_loop(small, meta_s, qkv_s[0], kwin_s, vwin_s, dheads_s, lse_s)
        elif what == "post_l":
            made["at_l"], pack, made["dx_l"] = attn_post(
                large, index, made["grads"], xl, halo, lb_norms, lb_qkv, dmid_l, vec_l,
                made["dx_s"][1:],
            )
            sum_q.add(pack)
            made["packs"] += "l"
        elif what == "post_s":
            made["at_s"], pack, made["dx_s"] = attn_post(
                small, index, made["grads"], xs, halo, sb_norms, sb_qkv, dmid_s, vec_s, ()
            )
            sum_q.add(pack)
            made["packs"] += "s"
        elif what == "place":
            made["out"] = call(
                functools.partial(place_kernel, (large, small)),
                (
                    sds((large.n, wl), BF16),
                    sds((ws, small.n) if small.turned else (small.n, ws), BF16),
                ),
                (back_cls, lane_l, lane_s, yl_far, ys_far),
                far=(0, 3, 4),
            )
        elif what == "dx":
            made["dx"] = settled(made["dx_l"][0], made["dx_s"][0], *made["dx_l"][1:])
        elif what == "out_f":
            made["f"] = unpack_early()
        elif what == "out_q":
            made["g"], made["q"] = unpack_late()
        else:
            sums[what.lower()].step(COSTLY if what.isupper() else 1)

    for what in SCHEDULE:
        do(what)
    o_l, u_l, d_l, *others_c = made["f"]
    o_s, u_s, d_s, *crossed = made["g"]
    q_l, norms_l, bias_l, upbias_l = made["q"]["l"]
    q_s, norms_s, bias_s, upbias_s = made["q"]["s"]
    grad_xl, grad_xs = made["dx"]
    out_l, out_s = made["out"]
    ORDER.clear()
    fl, fs = (
        [*crossed[4 * i : 4 * i + 3], *others_c[3 * i : 3 * i + 3], crossed[4 * i + 3]]
        for i in range(2)
    )
    fl[1], fs[5] = fl[1].T, fs[5].T
    if small.turned:
        out_s, grad_xs, d_s = out_s.T, grad_xs.T, d_s.T
    return (
        out_l[None],
        out_s[None],
        grad_xl[None],
        grad_xs[None],
        norms_l,
        q_l,
        o_l,
        u_l,
        d_l,
        bias_l,
        upbias_l,
        norms_s,
        q_s,
        o_s,
        u_s,
        d_s,
        bias_s,
        upbias_s,
        *fl,
        *fs,
    )


def solution(mesh):
    rows = P("dp", "head", None)
    return jax.shard_map(
        on_device,
        mesh=mesh,
        in_specs=(P("dp", None),) * 2 + (rows,) * 4 + (P(),) * 28,
        out_specs=(rows,) * 4 + (P(),) * 28,
        check_vma=False,
    )
```

```python
import functools
import math

import jax
import jax.numpy as jnp
from jax import lax
from jax.experimental import pallas as pl
from jax.experimental.pallas import tpu as pltpu
from jax.sharding import PartitionSpec as P

HEADS = 6
IMGS = 10
ROWS = 16
MOST_L = 197
MOST_S = 401
EPS = 1e-6
NEG = -1e30
LOG2E = math.log2(math.e)
F32 = jnp.float32
BF16 = jnp.bfloat16
VMEM = pl.BlockSpec(memory_space=pltpu.VMEM)
SMEM = pl.BlockSpec(memory_space=pltpu.SMEM)
HBM = pl.BlockSpec(memory_space=pltpu.HBM)


COSTLY = 40 * 10**6
SCHEDULE = (
    "F", "cross", "loop_s", "post_s", "F", "loop_l", "G", "F", "post_l", "F", "Q", "f", "q", "f",
    "q", "dx", "q", "q", "f", "Q", "place", "out_f", "q", "out_q",
)
ORDER = []


def round_up(value, unit):
    return -(-value // unit) * unit


class Branch:
    def __init__(self, rows, width, hidden, most, before=0):
        self.n = rows
        self.w = width
        self.f = hidden
        self.dh = width // HEADS
        self.halo = round_up(most - 1, 16)
        self.kw = self.halo + 16
        self.r = rows + 2 * self.halo
        self.t = rows // 128
        self.cols = round_up(width, 128) // 128
        self.at = before
        self.end = before + self.halo * self.cols
        self.scale = self.dh ** (-0.5)
        self.turned = width % 128 != 0
        if width % 128 == 0:
            per = 128 // self.dh
            self.groups = [
                (i * 128, (i + 1) * 128, list(range(i * per, (i + 1) * per)))
                for i in range(width // 128)
            ]
        else:
            self.groups = [(0, width, list(range(HEADS)))]


def nn(a, b):
    return jnp.dot(a, b, preferred_element_type=F32)


def nt(a, b):
    return lax.dot_general(a, b, (((1,), (1,)), ((), ())), preferred_element_type=F32)


def tn(a, b):
    return lax.dot_general(a, b, (((0,), (0,)), ((), ())), preferred_element_type=F32)


def split(x):
    high = x.astype(BF16)
    return high, (x - high.astype(F32)).astype(BF16)


def normalize(x):
    center = x - jnp.mean(x, axis=-1, keepdims=True)
    rstd = lax.rsqrt(jnp.mean(center * center, axis=-1, keepdims=True) + EPS)
    return center * rstd, rstd


def norm_grad(unit, rstd, gain, upstream):
    scaled = upstream * gain
    mean_one = jnp.mean(scaled, axis=-1, keepdims=True)
    mean_two = jnp.mean(scaled * unit, axis=-1, keepdims=True)
    return (scaled - mean_one - unit * mean_two) * rstd


def col_sum(x):
    return jnp.sum(x, axis=0, keepdims=True)


def gelu_pair(x):
    cumulative = 0.5 * (1.0 + lax.erf(x * 0.7071067811865476))
    density = jnp.exp(-0.5 * x * x) * 0.3989422804014327
    return x * cumulative, cumulative + x * density


def iota(shape, dim):
    return lax.broadcasted_iota(jnp.int32, shape, dim)


def padded_bytes(item):
    *lead, rows, cols = (1, 1, *item.shape)
    unit = 32 // item.dtype.itemsize
    return math.prod(lead) * round_up(rows, unit) * round_up(cols, 128) * item.dtype.itemsize


def parts_of(item):
    return item.shape[0] if len(item.shape) == 3 and item.shape[1] * item.shape[2] > 1 << 14 else 1


class FarIn:
    def __init__(self, far, near, sems):
        pairs = [(far, near)]
        if len(sems) > 1:
            pairs = [(far.at[i], near.at[i]) for i in range(len(sems))]
        self.copies = [
            pltpu.make_async_copy(*pair, sem) for pair, sem in zip(pairs, sems, strict=True)
        ]
        for copy in self.copies:
            copy.start()
        self.near = near
        self.landed = [False] * len(sems)

    def land(self, i=None):
        for k, copy in enumerate(self.copies):
            if not self.landed[k] and i in (None, k):
                self.landed[k] = True
                copy.wait()

    @property
    def shape(self):
        return self.near.shape

    def __getitem__(self, where):
        self.land(where if isinstance(where, int) and len(self.copies) > 1 else None)
        return self.near[where]


class FarOut:
    def __init__(self, far, near, sems):
        pairs = [(near, far)]
        if len(sems) > 1:
            pairs = [(near.at[i], far.at[i]) for i in range(len(sems))]
        self.copies = [
            pltpu.make_async_copy(*pair, sem) for pair, sem in zip(pairs, sems, strict=True)
        ]
        self.near = near
        self.sent = [False] * len(sems)

    def send(self, i=None):
        for k, copy in enumerate(self.copies):
            if not self.sent[k] and i in (None, k):
                self.sent[k] = True
                copy.start()

    @property
    def shape(self):
        return self.near.shape

    def __getitem__(self, where):
        return self.near[where]

    def __setitem__(self, where, value):
        self.near[where] = value


def land(*refs):
    for ref in refs:
        if isinstance(ref, FarIn):
            ref.land()


def near(ref):
    return ref.near if isinstance(ref, (FarIn, FarOut)) else ref


def send(*refs):
    for ref in refs:
        if isinstance(ref, FarOut):
            ref.send()


def call(
    kernel,
    outs,
    ins,
    in_specs=None,
    scratch=(),
    moved=1,
    busy=0,
    out_specs=None,
    spare=10,
    far=(),
    far_out=(),
):
    in_specs = [VMEM] * len(ins) if in_specs is None else list(in_specs)
    flat = list(jax.tree.leaves(outs))
    specs = [VMEM] * len(flat) if out_specs is None else list(jax.tree.leaves(out_specs))
    for i in far:
        in_specs[i] = HBM
    for i in far_out:
        specs[i] = HBM
    held = list(zip(ins, in_specs)) + list(zip(flat, specs))
    need = sum(padded_bytes(item) for item, spec in held if spec is VMEM)
    near = [pltpu.VMEM(ins[i].shape, ins[i].dtype) for i in far]
    near += [pltpu.VMEM(flat[i].shape, flat[i].dtype) for i in far_out]
    scratch = list(scratch)
    for item in scratch + near:
        if getattr(item, "memory_space", None) == pltpu.VMEM:
            need += padded_bytes(sds(item.shape, jnp.dtype(item.dtype)))
    count = len(near)

    def wrapped(*refs):
        refs = list(refs)
        if not count:
            return kernel(*refs)
        refs, held, sems = refs[: -count - 1], refs[-count - 1 : -1], refs[-1]
        found, at = [], 0
        for k, i in enumerate([*far, *(i + len(ins) for i in far_out)]):
            size = parts_of(near[k])
            own = [sems.at[at + j] for j in range(size)]
            at += size
            refs[i] = (FarIn if k < len(far) else FarOut)(refs[i], held[k], own)
            found.append(refs[i])
        kernel(*refs)
        land(*found)
        send(*found)
        for ref in found:
            if isinstance(ref, FarOut):
                for copy in ref.copies:
                    copy.wait()

    total = sum(parts_of(item) for item in near)
    extra = near + [pltpu.SemaphoreType.DMA((total,))] if count else []
    ins = list(ins)
    if ORDER:
        i = next(i for i, spec in enumerate(in_specs) if spec is not SMEM)
        ins[i] = after(ORDER[-1], ins[i])
    for i in far:
        ins[i] = pltpu.with_memory_space_constraint(ins[i], pltpu.HBM)
    for i in far_out:
        flat[i] = pltpu.HBM(flat[i].shape, flat[i].dtype)
    results = pl.pallas_call(
        wrapped,
        out_shape=jax.tree.unflatten(jax.tree.structure(outs), flat),
        in_specs=in_specs,
        out_specs=jax.tree.unflatten(jax.tree.structure(outs), specs),
        scratch_shapes=scratch + extra,
        compiler_params=pltpu.CompilerParams(
            vmem_limit_bytes=min(need + spare * 2**20, 60 * 2**20)
        ),
        cost_estimate=pl.CostEstimate(
            flops=moved * 500 + busy * 10**9, bytes_accessed=moved, transcendentals=0
        ),
    )(*ins)
    if ORDER:
        ORDER[:] = [min(jax.tree.leaves(results), key=lambda item: item.size)]
    return results


def after(first, then):
    return lax.optimization_barrier((first, then))[1]


def sds(shape, dtype):
    return jax.ShapeDtypeStruct(shape, dtype)


def mat_rows(rows, cols):
    return rows * cols // 128


def put_halo(br, ref, value):
    low = value.astype(BF16)
    for i in range(br.cols):
        part = low[:, i * 128 : min((i + 1) * 128, br.w)]
        if part.shape[1] < 128:
            part = jnp.concatenate([part, jnp.zeros((br.halo, 128 - part.shape[1]), BF16)], axis=1)
        ref[br.at + i * br.halo : br.at + (i + 1) * br.halo, :] = part


def get_halo(br, ref):
    parts = [
        ref[br.at + i * br.halo : br.at + (i + 1) * br.halo, : min(128, br.w - i * 128)]
        for i in range(br.cols)
    ]
    return jnp.concatenate(parts, axis=1).astype(F32)


def vec_rows(widths):
    return round_up(sum(round_up(w, 128) // 128 for w in widths), 16)


def layout(items, unit=32):
    at, row = {}, 0
    for name, rows in items:
        at[name] = row
        row += rows
    return at, round_up(row, unit)


def pack_mat(ref, at, rows, cols, value):
    low = value.astype(BF16)
    full = cols // 128
    for i in range(full):
        ref[at + i * rows : at + (i + 1) * rows, :] = low[:, i * 128 : (i + 1) * 128]
    if cols % 128:
        tail = low[:, full * 128 :]
        at = at + full * rows
        half = rows // 2
        ref[at : at + half, :] = jnp.concatenate([tail[:half], tail[half:]], axis=1)


def unpack_mat(ref, at, rows, cols, out):
    full = cols // 128
    for i in range(full):
        out[:, i * 128 : (i + 1) * 128] = ref[at + i * rows : at + (i + 1) * rows, :].astype(F32)
    if cols % 128:
        at = at + full * rows
        half = rows // 2
        block = ref[at : at + half, :].astype(F32)
        out[:half, full * 128 :] = block[:, :64]
        out[half:, full * 128 :] = block[:, 64:]


def vec_block(values):
    pieces = []
    for value in values:
        width = value.shape[1]
        for i in range(0, width, 128):
            piece = value[:, i : min(i + 128, width)]
            if piece.shape[1] < 128:
                piece = jnp.concatenate(
                    [piece, jnp.zeros((1, 128 - piece.shape[1]), F32)], axis=1
                )
            pieces.append(piece)
    total = round_up(len(pieces), 16)
    if total > len(pieces):
        pieces.append(jnp.zeros((total - len(pieces), 128), F32))
    return jnp.concatenate(pieces, axis=0)


def vecs_of(block, widths):
    out, i = [], 0
    for width in widths:
        parts = []
        for j in range(0, width, 128):
            parts.append(block[i : i + 1, : min(128, width - j)])
            i += 1
        out.append(parts[0] if len(parts) == 1 else jnp.concatenate(parts, axis=1))
    return out


def emit(src_ref, outs, index):
    size = src_ref.shape[0] // len(outs)
    for d, out in enumerate(outs):
        at = pl.multiple_of((index ^ d) * size, 16)
        out[...] = src_ref[pl.ds(at, size), :]


def edge_kernel(brs, xl_ref, xs_ref, last_ref, first_ref):
    for br, ref in zip(brs, (xl_ref, xs_ref)):
        put_halo(br, last_ref, ref[br.n - br.halo :, :])
        put_halo(br, first_ref, ref[: br.halo, :])


def start_kernel(
    br_l,
    br_s,
    index_ref,
    seg_l_ref,
    seg_s_ref,
    xl_ref,
    xs_ref,
    dyl_ref,
    dys_ref,
    nl_ref,
    ns_ref,
    wl_ref,
    ws_ref,
    ql_ref,
    kl_ref,
    vl_ref,
    qs_ref,
    ks_ref,
    vs_ref,
    meta_l_ref,
    meta_s_ref,
    lane_l_ref,
    lane_s_ref,
    sub_l_ref,
    sub_s_ref,
    dcls_ref,
    vector_ref,
    scalar_ref,
    sem,
):
    col = 0
    dcls_ref[...] = jnp.zeros_like(dcls_ref)
    for br, seg_ref, dy_ref, meta_ref, lane_ref, sub_ref in (
        (br_l, seg_l_ref, dyl_ref, meta_l_ref, lane_l_ref, sub_l_ref),
        (br_s, seg_s_ref, dys_ref, meta_s_ref, lane_s_ref, sub_s_ref),
    ):
        own = index_ref[15] * br.n
        seg = seg_ref[...]
        image = iota((ROWS, seg.shape[1]), 0)
        starts = jnp.sum((seg < image).astype(jnp.int32), axis=1, keepdims=True)
        ends = jnp.sum((seg <= image).astype(jnp.int32), axis=1, keepdims=True)
        starts = jnp.broadcast_to(starts, (ROWS, 128))
        ends = jnp.broadcast_to(ends, (ROWS, 128))
        lane = iota((ROWS, 128), 1)
        diagonal = (lane - (lane // ROWS) * ROWS) == iota((ROWS, 128), 0)
        lo = jnp.sum(jnp.where(diagonal, starts, 0), axis=0, keepdims=True) - own
        hi = jnp.sum(jnp.where(diagonal, ends, 0), axis=0, keepdims=True) - own
        lane_ref[...] = jnp.concatenate([lo, hi, jnp.zeros((6, 128), jnp.int32)], axis=0)
        sub_ref[...] = starts - own
        real = iota((ROWS, 128), 0) < IMGS
        first = jnp.sum(jnp.where(real & (starts <= own), 1, 0), axis=0, keepdims=True) - 1
        last = jnp.sum(jnp.where(real & (starts < own + br.n), 1, 0), axis=0, keepdims=True) - 1
        at = 0 if br is br_l else ROWS + 8
        vector_ref[at : at + ROWS, :] = starts
        vector_ref[at + ROWS : at + ROWS + 8, :] = jnp.concatenate(
            [first, last, jnp.zeros((6, 128), jnp.int32)], axis=0
        )
        pick = (iota((ROWS, br.n), 1) == (starts - own)[:, 0:1]).astype(F32).astype(BF16)
        dcls_ref[:, col : col + br.w] = nn(pick, dy_ref[...])
        col += br.w
    copy = pltpu.make_async_copy(vector_ref, scalar_ref, sem)
    copy.start()
    for x_ref, norms_ref, w_ref, outs in (
        (xl_ref, nl_ref, wl_ref, (ql_ref, kl_ref, vl_ref)),
        (xs_ref, ns_ref, ws_ref, (qs_ref, ks_ref, vs_ref)),
    ):
        width = x_ref.shape[1]
        unit, _ = normalize(x_ref[...].astype(F32))
        normed = (unit * norms_ref[0, 0:1, :] + norms_ref[0, 1:2, :]).astype(BF16)
        for i, ref in enumerate(outs):
            ref[...] = nn(normed, w_ref[:, i * width : (i + 1) * width]).astype(BF16)
    copy.wait()
    for br, meta_ref, at in ((br_l, meta_l_ref, 0), (br_s, meta_s_ref, ROWS + 8)):
        for j in range(IMGS + 1):
            meta_ref[j] = scalar_ref[at + j, 0]
        meta_ref[11] = index_ref[15] * br.n
        meta_ref[12] = scalar_ref[at + ROWS, 0]
        meta_ref[13] = scalar_ref[at + ROWS + 1, 0]
        meta_ref[14] = 0
        meta_ref[15] = 0


def head_mask(br, head, c0, c1):
    lane = iota((1, c1 - c0), 1) + c0
    return jnp.logical_and(lane >= head * br.dh, lane < (head + 1) * br.dh)


def stack_heads(br, rows, group):
    c0, c1, heads = group
    part = rows[:, c0:c1]
    zero = jnp.zeros_like(part)
    return jnp.concatenate(
        [jnp.where(head_mask(br, h, c0, c1), part, zero) for h in heads], axis=0
    )


def image_span(br, meta_ref, j):
    base = meta_ref[11]
    lo = meta_ref[j] - base
    hi = meta_ref[j + 1] - base
    k0 = pl.multiple_of(((lo + br.halo) // 16) * 16, 16)
    t0 = jnp.maximum(lo, 0) // 128
    t1 = (jnp.minimum(hi, br.n) + 127) // 128
    return lo, hi, k0, t0, t1


def forward_kernel(
    br,
    meta_ref,
    x_ref,
    xl_ref,
    xr_ref,
    q_ref,
    k_ref,
    v_ref,
    norms_ref,
    wqkv_ref,
    wout_ref,
    wup_ref,
    wdown_ref,
    bias_ref,
    upbias_ref,
    sub_ref,
    y_ref,
    cls_ref,
    kwin_ref,
    vwin_ref,
    lse_ref,
    ho_ref,
    mid_ref,
    hid_ref,
    slope_ref,
    far_y_ref,
    ot_ref,
):
    n, w, f, dh, halo = br.n, br.w, br.f, br.dh, br.halo
    for ref, at in ((xl_ref, 0), (xr_ref, halo + n)):
        unit, _ = normalize(get_halo(br, ref))
        normed = (unit * norms_ref[0, 0:1, :] + norms_ref[0, 1:2, :]).astype(BF16)
        kwin_ref[at : at + halo, :] = nn(normed, wqkv_ref[:, w : 2 * w]).astype(BF16)
        vwin_ref[at : at + halo, :] = nn(normed, wqkv_ref[:, 2 * w :]).astype(BF16)
    kwin_ref[halo : halo + n, :] = k_ref[...]
    vwin_ref[halo : halo + n, :] = v_ref[...]
    send(vwin_ref)
    ot_ref[...] = jnp.zeros_like(ot_ref)
    lse_ref[...] = jnp.zeros(lse_ref.shape, F32)
    factor = br.scale * LOG2E
    land(q_ref)

    def image(j, carry):
        lo, hi, k0, t0, t1 = image_span(br, meta_ref, j)
        keys = kwin_ref[pl.ds(k0, br.kw), :]
        values_t = vwin_ref[pl.ds(k0, br.kw), :].T
        row = iota((br.kw, 128), 0) + (k0 - br.halo)
        mask = jnp.logical_and(row >= lo, row < hi)

        def tile(t, carry):
            rows = q_ref[pl.ds(pl.multiple_of(t * 128, 128), 128), :]
            lane = iota((1, 128), 1) + t * 128
            inside = jnp.logical_and(lane >= lo, lane < hi)
            for group in br.groups:
                c0, c1, heads = group
                scores = nt(keys[:, c0:c1], stack_heads(br, rows, group))
                for i, h in enumerate(heads):
                    s = jnp.where(mask, scores[:, i * 128 : (i + 1) * 128] * factor, NEG)
                    top = jnp.max(s, axis=0, keepdims=True)
                    p = jnp.exp2(s - top)
                    total = col_sum(p)
                    o = nn(values_t[h * dh : (h + 1) * dh, :], p.astype(BF16))
                    ot_ref[t, h * dh : (h + 1) * dh, :] += o * jnp.where(inside, 1.0 / total, 0.0)
                    lse_ref[t, h : h + 1, :] = jnp.where(
                        inside, top + jnp.log2(total), lse_ref[t, h : h + 1, :]
                    )
            return carry

        return lax.fori_loop(t0, t1, tile, carry)

    lax.fori_loop(meta_ref[12], meta_ref[13] + 1, image, 0)
    send(kwin_ref, lse_ref)
    for t in range(br.t):
        ho_ref[t * 128 : (t + 1) * 128, :] = ot_ref[t].T.astype(BF16)
    mid = x_ref[...].astype(F32) + (nn(ho_ref[...], wout_ref[...]) + bias_ref[0:1, :])
    mid_ref[...] = mid
    unit, _ = normalize(mid)
    normed = (unit * norms_ref[1, 0:1, :] + norms_ref[1, 1:2, :]).astype(BF16)
    send(ho_ref, mid_ref)
    total = mid + bias_ref[1:2, :]
    step = 256
    upbias = upbias_ref[...].reshape(1, f)
    for c in range(0, f, step):
        pre = nn(normed, wup_ref[:, c : c + step]) + upbias[:, c : c + step]
        act, slope = gelu_pair(pre)
        act = act.astype(BF16)
        i = c // step
        hid_ref[i] = act
        slope_ref[i] = slope.astype(BF16)
        if br.turned:
            total = total + nt(act, wdown_ref[:, c : c + step])
        else:
            total = total + nn(act, wdown_ref[c : c + step, :])
    y = total.astype(BF16)
    y_ref[...] = y
    far_y_ref[...] = y
    send(far_y_ref)
    pick = (iota((ROWS, n), 1) == sub_ref[:, 0:1]).astype(F32).astype(BF16)
    cls_ref[...] = nn(pick, y)


def ffn_back_kernel(
    br,
    at,
    index_ref,
    lane_ref,
    dy_ref,
    cross_ref,
    dcls_ref,
    hid_ref,
    slope_ref,
    mid_ref,
    ho_ref,
    norms_ref,
    wout_ref,
    wup_ref,
    wdown_ref,
    keep_ref,
    send_ref,
    dmid_ref,
    dheads_ref,
    vec_ref,
    pack_ref,
):
    n, w, f = br.n, br.w, br.f
    c0 = at["col"]
    cls = dcls_ref[:, c0 : c0 + w].astype(BF16)
    hit = (iota((n, 128), 0) == lane_ref[0:1, :]).astype(F32)
    hit = jnp.where(iota((1, 128), 1) < IMGS, hit, 0.0)
    first = jnp.sum(hit, axis=1, keepdims=True) > 0.5
    placed = nn(hit[:, :ROWS].astype(BF16), cls)
    gy = jnp.where(first, placed, dy_ref[...].astype(F32) + cross_ref[...]).astype(BF16)
    gy_float = gy.astype(F32)
    dn2 = jnp.zeros((n, w), F32)
    step = 256
    upbias = []
    unit, rstd = normalize(mid_ref[...])
    normed_t = (unit * norms_ref[1, 0:1, :] + norms_ref[1, 1:2, :]).astype(BF16).T
    gy_t = gy.T
    if at["rows"] > at["end"]:
        pack_ref[at["end"] :, :] = jnp.zeros((at["rows"] - at["end"], 128), BF16)
    for i, c in enumerate(range(0, f, step)):
        if br.turned:
            dpre = nn(gy, wdown_ref[:, c : c + step])
        else:
            dpre = nt(gy, wdown_ref[c : c + step, :])
        dpre = (dpre * slope_ref[i].astype(F32)).astype(BF16)
        upbias.append(col_sum(dpre.astype(F32)))
        rows = i * mat_rows(w, step)
        pack_mat(pack_ref, at["up"] + rows, w, step, nn(normed_t, dpre))
        dn2 = dn2 + nt(dpre, wup_ref[:, c : c + step])
        pack_mat(pack_ref, at["down"] + rows, w, step, nn(gy_t, hid_ref[i]))
    dmid = gy_float + norm_grad(unit, rstd, norms_ref[1, 0:1, :], dn2)
    dmid_ref[...] = dmid
    send(dmid_ref)
    dattn = dmid.astype(BF16)
    dheads_ref[...] = nt(dattn, wout_ref[...]).astype(BF16)
    send(dheads_ref)
    pack_mat(pack_ref, at["out"], w, w, tn(ho_ref[...], dattn))
    vec_ref[...] = vec_block(
        [col_sum(dn2 * unit), col_sum(dn2), col_sum(dattn.astype(F32)), col_sum(gy_float)] + upbias
    )
    emit(pack_ref, (keep_ref, send_ref), index_ref[0])


def attn_loop_kernel(
    br,
    meta_ref,
    q_ref,
    kwin_ref,
    vwin_ref,
    dheads_ref,
    lse_ref,
    dk_ref,
    dv_ref,
    dq_ref,
    dqt_ref,
    p_ref,
    ds_ref,
):
    dh = br.dh
    dk_ref[...] = jnp.zeros(dk_ref.shape, F32)
    dv_ref[...] = jnp.zeros_like(dv_ref)
    dqt_ref[...] = jnp.zeros_like(dqt_ref)
    factor = br.scale * LOG2E
    land(q_ref, kwin_ref, vwin_ref, dheads_ref, lse_ref)

    def image(j, carry):
        lo, hi, k0, t0, t1 = image_span(br, meta_ref, j)
        span = pl.ds(k0, br.kw)
        keys = kwin_ref[span, :]
        keys_t = keys.T
        values = vwin_ref[span, :]
        row = iota((br.kw, 128), 0) + (k0 - br.halo)
        mask = jnp.logical_and(row >= lo, row < hi)

        def tile(t, carry):
            here = pl.ds(pl.multiple_of(t * 128, 128), 128)
            rows = q_ref[here, :]
            outs = dheads_ref[here, :]
            lane = iota((1, 128), 1) + t * 128
            inside = jnp.logical_and(lane >= lo, lane < hi)
            for group in br.groups:
                c0, c1, heads = group
                queries = stack_heads(br, rows, group)
                upstream = stack_heads(br, outs, group)
                scores = nt(keys[:, c0:c1], queries)
                dprobs = nt(values[:, c0:c1], upstream)
                for i, h in enumerate(heads):
                    part = slice(i * 128, (i + 1) * 128)
                    lse = jnp.where(inside, lse_ref[t, h : h + 1, :], -NEG)
                    p = jnp.exp2(scores[:, part] * factor - lse)
                    p = jnp.where(mask, p, 0.0)
                    dp = dprobs[:, part]
                    ds = (p * (dp - col_sum(p * dp))).astype(BF16)
                    p_ref[:, part] = p.astype(BF16)
                    ds_ref[:, part] = ds
                    dqt_ref[t, h * dh : (h + 1) * dh, :] += nn(
                        keys_t[h * dh : (h + 1) * dh, :], ds
                    )
                size = 128 * len(heads)
                dv_ref[span, c0:c1] += nn(p_ref[:, :size], upstream)
                dk_ref[span, c0:c1] += nn(ds_ref[:, :size], queries)
            return carry

        return lax.fori_loop(t0, t1, tile, carry)

    lax.fori_loop(meta_ref[12], meta_ref[13] + 1, image, 0)
    for t in range(br.t):
        dq_ref[t * 128 : (t + 1) * 128, :] = (dqt_ref[t].T * br.scale).astype(BF16)


def attn_post_kernel(
    br,
    at,
    index_ref,
    x_ref,
    xl_ref,
    xr_ref,
    norms_ref,
    wqkv_ref,
    dmid_ref,
    vec_ref,
    dk_ref,
    dv_ref,
    dq_ref,
    *refs,
):
    before, refs = refs[:-7], refs[-7:]
    keep_ref, send_ref, dx_ref, dxl_ref, dxr_ref, normed_ref, pack_ref = refs
    for ref, out in zip(before, (dxl_ref, dxr_ref)):
        out[: br.at, :] = ref[...]
    n, w, halo = br.n, br.w, br.halo
    dk = (dk_ref[...] * br.scale).astype(BF16)
    dv = dv_ref[...].astype(BF16)
    gain, shift = norms_ref[0, 0:1, :], norms_ref[0, 1:2, :]
    dgain = jnp.zeros((1, w), F32)
    dshift = jnp.zeros((1, w), F32)
    for ref, lo, size, out in (
        (xl_ref, 0, halo, dxl_ref),
        (x_ref, halo, n, dx_ref),
        (xr_ref, halo + n, halo, dxr_ref),
    ):
        rows = ref[...].astype(F32) if ref is x_ref else get_halo(br, ref)
        unit, rstd = normalize(rows)
        normed_ref[lo : lo + size, :] = (unit * gain + shift).astype(BF16)
        up = nt(dk[lo : lo + size], wqkv_ref[:, w : 2 * w])
        up = up + nt(dv[lo : lo + size], wqkv_ref[:, 2 * w :])
        if out is dx_ref:
            up = up + nt(dq_ref[...], wqkv_ref[:, :w])
        dgain = dgain + col_sum(up * unit)
        dshift = dshift + col_sum(up)
        dx = norm_grad(unit, rstd, gain, up)
        if out is dx_ref:
            out[...] = dx + dmid_ref[...]
        else:
            put_halo(br, out, dx)
    whole = jnp.concatenate(
        [
            tn(normed_ref[halo : halo + n, :], dq_ref[...]),
            tn(normed_ref[...], dk),
            tn(normed_ref[...], dv),
        ],
        axis=1,
    )
    pack_mat(pack_ref, at["qkv"], w, 3 * w, whole)
    block = vec_block([dgain, dshift])
    pack_ref[at["vec1"] : at["vec1"] + block.shape[0], :] = block.astype(BF16)
    pack_ref[at["vec2"] : at["vec2"] + vec_ref.shape[0], :] = vec_ref[...].astype(BF16)
    if at["rows"] > at["end"]:
        pack_ref[at["end"] :, :] = jnp.zeros((at["rows"] - at["end"], 128), BF16)
    emit(pack_ref, (keep_ref, send_ref), index_ref[0])


class Cross:
    def __init__(self, wa, wb, rows_b):
        self.wa = wa
        self.wb = wb
        self.dh = wb // HEADS
        self.n = rows_b
        self.scale = self.dh ** (-0.5)
        self.proj = nt if wa > wb else nn
        self.proj_back = nn if wa > wb else nt
        self.back = nn if wa > wb else nt
        self.back_back = nt if wa > wb else nn

    def by_head(self):
        head = iota((128, self.wb), 0) // ROWS
        col = iota((128, self.wb), 1)
        return jnp.logical_and(col >= head * self.dh, col < (head + 1) * self.dh).astype(F32)

    def by_image(self):
        lane = iota((ROWS, 128), 1)
        return jnp.logical_and(
            lane - (lane // ROWS) * ROWS == iota((ROWS, 128), 0), lane < HEADS * ROWS
        ).astype(F32)


def spread(cx, low_rows):
    return jnp.concatenate([low_rows] * 8, axis=0) * cx.by_head().astype(low_rows.dtype)


def gather_heads(cx, wide):
    kept = wide * cx.by_head()
    total = kept[0:ROWS]
    for h in range(1, HEADS):
        total = total + kept[h * ROWS : (h + 1) * ROWS]
    return total


def to_lane(cx, *items):
    stack = jnp.concatenate([part for item in items for part in split(item)], axis=0)
    wide = nt(stack, cx.by_head().astype(BF16))
    image = cx.by_image()
    found = []
    for i in range(0, 2 * ROWS * len(items), 2 * ROWS):
        found.append(col_sum(image * (wide[i : i + ROWS] + wide[i + ROWS : i + 2 * ROWS])))
    return found


def from_lane(cx, *items):
    image = cx.by_image()
    stack = jnp.concatenate([part for item in items for part in split(image * item)], axis=0)
    wide = nn(stack, cx.by_head().astype(BF16))
    return [
        wide[i : i + ROWS] + wide[i + ROWS : i + 2 * ROWS]
        for i in range(0, 2 * ROWS * len(items), 2 * ROWS)
    ]


def cross_query(cx, cls, norms_ref, proj_ref, query_ref, keyval_ref, bias_ref, qa_ref, qb_ref):
    wa, wb = cx.wa, cx.wb
    unit_a, rstd_a = normalize(cls)
    lifted = unit_a * norms_ref[0:1, :wa] + norms_ref[1:2, :wa]
    act, slope = gelu_pair(lifted)
    act = act.astype(BF16)
    bias = bias_ref[...].reshape(1, bias_ref.shape[0])[:, :wb]
    moved = cx.proj(act, proj_ref[...]) + bias
    gain, shift = norms_ref[0:1, wa : wa + wb], norms_ref[1:2, wa : wa + wb]
    unit_q, rstd_q = normalize(moved)
    query_in = (unit_q * gain + shift).astype(BF16)
    fquery = nn(query_in, query_ref[...]).astype(BF16)
    kself = nn(query_in, keyval_ref[:, :wb]).astype(BF16)
    vself = nn(query_in, keyval_ref[:, wb:]).astype(BF16)
    for i, item in enumerate((unit_a, slope, act, jnp.broadcast_to(rstd_a, unit_a.shape))):
        qa_ref[i] = item.astype(F32)
    for i, item in enumerate(
        (moved, unit_q, query_in, fquery, kself, vself, jnp.broadcast_to(rstd_q, moved.shape))
    ):
        qb_ref[i] = item.astype(F32)
    return fquery


def allowed_rows(cx, lane_ref):
    row = iota((cx.n, 128), 0)
    return jnp.logical_and(row > lane_ref[0:1, :], row < lane_ref[1:2, :])


def keys_kernel(cxs, ys_ref, fln_ref, yl_ref, fsn_ref, ks_ref, kl_ref):
    for cx, y_ref, norms_ref, out_ref in (
        (cxs[0], ys_ref, fln_ref, ks_ref),
        (cxs[1], yl_ref, fsn_ref, kl_ref),
    ):
        wa, wb = cx.wa, cx.wb
        unit, _ = normalize(y_ref[...].astype(F32))
        out_ref[...] = (
            unit * norms_ref[0:1, wa : wa + wb] + norms_ref[1:2, wa : wa + wb]
        ).astype(BF16)


def cross_front_kernel(
    cxs,
    c0_ref,
    c1_ref,
    c2_ref,
    c3_ref,
    lane_s_ref,
    lane_l_ref,
    key_s_ref,
    key_l_ref,
    fln_ref,
    flp_ref,
    flq_ref,
    flk_ref,
    flb_ref,
    fsn_ref,
    fsp_ref,
    fsq_ref,
    fsk_ref,
    fsb_ref,
    part_ref,
    sc_l_ref,
    sc_s_ref,
    ab_l_ref,
    ab_s_ref,
    qa_l_ref,
    qb_l_ref,
    qa_s_ref,
    qb_s_ref,
):
    cls = c0_ref[...] + c1_ref[...] + c2_ref[...] + c3_ref[...]
    wl, ws = cxs[0].wa, cxs[1].wa
    col = 0
    stats = []
    for cx, rows, key_ref, lane_ref, keyval_ref, weights, kept, sc_ref, ab_ref in (
        (
            cxs[0],
            cls[:, :wl],
            key_s_ref,
            lane_s_ref,
            flk_ref,
            (fln_ref, flp_ref, flq_ref, flk_ref, flb_ref),
            (qa_l_ref, qb_l_ref),
            sc_l_ref,
            ab_l_ref,
        ),
        (
            cxs[1],
            cls[:, wl : wl + ws],
            key_l_ref,
            lane_l_ref,
            fsk_ref,
            (fsn_ref, fsp_ref, fsq_ref, fsk_ref, fsb_ref),
            (qa_s_ref, qb_s_ref),
            sc_s_ref,
            ab_s_ref,
        ),
    ):
        fquery = cross_query(cx, rows, *weights, *kept)
        absorbed = nt(spread(cx, fquery), keyval_ref[:, : cx.wb]).astype(BF16)
        ab_ref[...] = absorbed
        key = key_ref[...]
        allowed = allowed_rows(cx, lane_ref)
        scores = jnp.where(allowed, nt(key, absorbed) * (cx.scale * LOG2E), NEG)
        sc_ref[...] = scores
        top = jnp.max(scores, axis=0, keepdims=True)
        p = jnp.where(allowed, jnp.exp2(scores - top), 0.0)
        high, low = split(p)
        mixed_high, mixed_low = split(tn(high, key) + tn(low, key))
        value_part = keyval_ref[:, cx.wb :]
        out = gather_heads(cx, nn(mixed_high, value_part) + nn(mixed_low, value_part))
        part_ref[0:ROWS, col : col + cx.wb] = out
        col += cx.wb
        stats += [top, col_sum(p)]
    width = part_ref.shape[1]
    part_ref[0:ROWS, col:] = jnp.zeros((ROWS, width - col), F32)
    part_ref[ROWS:, :] = jnp.zeros((8, width), F32)
    part_ref[ROWS : ROWS + 4, :128] = jnp.concatenate(stats, axis=0)


def cross_back_kernel(
    cxs,
    share,
    g0_ref,
    g1_ref,
    g2_ref,
    g3_ref,
    p0_ref,
    p1_ref,
    p2_ref,
    p3_ref,
    lane_s_ref,
    lane_l_ref,
    key_s_ref,
    key_l_ref,
    sc_l_ref,
    sc_s_ref,
    qb_l_ref,
    qb_s_ref,
    fln_ref,
    flk_ref,
    flo_ref,
    flw_ref,
    flb_ref,
    fsn_ref,
    fsk_ref,
    fso_ref,
    fsw_ref,
    fsb_ref,
    dq_ref,
    rt_l_ref,
    rt_s_ref,
    gk_l_ref,
    gk_s_ref,
    ds_l_ref,
    ds_s_ref,
    p_l_ref,
    p_s_ref,
    av_l_ref,
    av_s_ref,
    back_ref,
    vec_ref,
):
    dcls = g0_ref[...] + g1_ref[...] + g2_ref[...] + g3_ref[...]
    parts = [p0_ref, p1_ref, p2_ref, p3_ref]
    vecs = []
    col_b = 0
    col_a = 0
    for index, (cx, key_ref, lane_ref, sc_ref, qb_ref, weights, outs) in enumerate(
        (
            (
                cxs[0],
                key_s_ref,
                lane_s_ref,
                sc_l_ref,
                qb_l_ref,
                (fln_ref, flk_ref, flo_ref, flw_ref, flb_ref),
                (rt_l_ref, gk_l_ref, ds_l_ref, p_l_ref, av_l_ref),
            ),
            (
                cxs[1],
                key_l_ref,
                lane_l_ref,
                sc_s_ref,
                qb_s_ref,
                (fsn_ref, fsk_ref, fso_ref, fsw_ref, fsb_ref),
                (rt_s_ref, gk_s_ref, ds_s_ref, p_s_ref, av_s_ref),
            ),
        )
    ):
        norms_ref, keyval_ref, wout_ref, wback_ref, bias_ref = weights
        rt_ref, gk_ref, ds_ref, p_ref, av_ref = outs
        wa, wb = cx.wa, cx.wb
        moved, fquery, kself, vself = qb_ref[0], qb_ref[3], qb_ref[4], qb_ref[5]
        self_score = to_lane(cx, fquery * kself)[0] * (cx.scale * LOG2E)
        tops = [p[ROWS + 2 * index : ROWS + 2 * index + 1, :128] for p in parts]
        sums = [p[ROWS + 2 * index + 1 : ROWS + 2 * index + 2, :128] for p in parts]
        top = self_score
        for item in tops:
            top = jnp.maximum(top, item)
        own = jnp.exp2(self_score - top)
        total = own
        weights_of = []
        for item, amount in zip(tops, sums):
            weight = jnp.exp2(item - top)
            weights_of.append(weight)
            total = total + amount * weight
        inverse = 1.0 / total
        p_self = own * inverse
        spans = from_lane(cx, p_self, *(weight * inverse for weight in weights_of))
        fheads = spans[0] * vself
        for part, span in zip(parts, spans[1:]):
            fheads = fheads + part[0:ROWS, col_b : col_b + wb] * span
        fheads_low = fheads.astype(BF16)
        bias = bias_ref[...].reshape(1, bias_ref.shape[0])
        joined = moved + (nn(fheads_low, wout_ref[...]) + bias[:, wb : 2 * wb])
        unit_r, rstd_r = normalize(joined)
        gain_r = norms_ref[0:1, wa + wb :]
        reverted = unit_r * gain_r + norms_ref[1:2, wa + wb :]
        act_r, slope_r = gelu_pair(reverted)
        act_r = act_r.astype(BF16)
        back_ref[:, col_a : col_a + wa] = cx.back(act_r, wback_ref[...]) + bias[:, 2 * wb :]
        dback_low = dcls[:, col_a : col_a + wa].astype(BF16)
        drev = cx.back_back(dback_low, wback_ref[...]) * slope_r
        djoined = norm_grad(unit_r, rstd_r, gain_r, drev)
        dattn = djoined.astype(BF16)
        dheads_low = nt(dattn, wout_ref[...]).astype(BF16)
        dheads = dheads_low.astype(F32)
        delta, dp_self = to_lane(cx, dheads * fheads, dheads * vself)
        ds_self = p_self * (dp_self - delta)
        ds_self_rows, p_self_rows = from_lane(
            cx, ds_self.astype(BF16).astype(F32), p_self.astype(BF16).astype(F32)
        )
        absorbed_high, absorbed_low = split(nt(spread(cx, dheads_low), keyval_ref[:, wb:]))
        av_ref[...] = absorbed_high
        key = key_ref[...]
        allowed = allowed_rows(cx, lane_ref)
        p = jnp.where(allowed, jnp.exp2(sc_ref[...] - (top + jnp.log2(total))), 0.0)
        dp = nt(key, absorbed_high) + nt(key, absorbed_low)
        ds = (p * (dp - delta)).astype(BF16)
        ds_ref[...] = ds
        p_ref[...] = p.astype(BF16)
        g_k = tn(ds, key)
        gk_ref[...] = g_k
        g_high, g_low = split(g_k)
        key_part = keyval_ref[:, :wb]
        dquery = gather_heads(cx, nn(g_high, key_part) + nn(g_low, key_part)) * cx.scale
        dq_ref[:, col_b : col_b + wb] = dquery + ds_self_rows * kself * (cx.scale * share)
        for i, item in enumerate(
            (
                fheads_low,
                act_r,
                dattn,
                djoined,
                dheads_low,
                ds_self_rows * fquery * cx.scale,
                p_self_rows * dheads,
            )
        ):
            rt_ref[i] = item.astype(F32)
        vecs += [col_sum(drev * unit_r) * share, col_sum(drev) * share]
        col_a += wa
        col_b += wb
    dq_ref[:, col_b:] = jnp.zeros((ROWS, dq_ref.shape[1] - col_b), F32)
    back_ref[:, col_a:] = jnp.zeros((ROWS, back_ref.shape[1] - col_a), F32)
    vec_ref[...] = vec_block(vecs)


def place_kernel(brs, back_ref, lane_l_ref, lane_s_ref, yl_ref, ys_ref, *outs):
    col = 0
    for br, lane_ref, y_ref, out_ref in zip(brs, (lane_l_ref, lane_s_ref), (yl_ref, ys_ref), outs):
        hit = (iota((br.n, 128), 0) == lane_ref[0:1, :]).astype(F32)
        hit = jnp.where(iota((1, 128), 1) < IMGS, hit, 0.0)
        first = jnp.sum(hit, axis=1, keepdims=True) > 0.5
        placed = nn(hit[:, :ROWS].astype(BF16), back_ref[:, col : col + br.w].astype(BF16))
        result = jnp.where(first, placed, y_ref[...].astype(F32))
        out_ref[...] = (result.T if br.turned else result).astype(BF16)
        col += br.w


def cross_query_back_kernel(
    cxs,
    share,
    d0_ref,
    d1_ref,
    d2_ref,
    d3_ref,
    qa_l_ref,
    qb_l_ref,
    rt_l_ref,
    fln_ref,
    flp_ref,
    flq_ref,
    flk_ref,
    qa_s_ref,
    qb_s_ref,
    rt_s_ref,
    fsn_ref,
    fsp_ref,
    fsq_ref,
    fsk_ref,
    dcls_ref,
    dm_l_ref,
    dm_s_ref,
    vec_ref,
):
    dquery_all = d0_ref[...] + d1_ref[...] + d2_ref[...] + d3_ref[...]
    col_a = col_b = 0
    vecs = []
    for cx, qa_ref, qb_ref, rt_ref, norms_ref, proj_ref, query_ref, keyval_ref, dm_ref in (
        (cxs[0], qa_l_ref, qb_l_ref, rt_l_ref, fln_ref, flp_ref, flq_ref, flk_ref, dm_l_ref),
        (cxs[1], qa_s_ref, qb_s_ref, rt_s_ref, fsn_ref, fsp_ref, fsq_ref, fsk_ref, dm_s_ref),
    ):
        wa, wb = cx.wa, cx.wb
        dquery = dquery_all[:, col_b : col_b + wb].astype(BF16)
        dkself = rt_ref[5].astype(BF16)
        dvself = rt_ref[6].astype(BF16)
        dquery_in = (
            nt(dquery, query_ref[...])
            + nt(dkself, keyval_ref[:, :wb])
            + nt(dvself, keyval_ref[:, wb:])
        )
        unit_q, rstd_q = qb_ref[1], qb_ref[6]
        gain = norms_ref[0:1, wa : wa + wb]
        dmoved = norm_grad(unit_q, rstd_q, gain, dquery_in) + rt_ref[3]
        high, low = split(dmoved)
        dlifted = (cx.proj_back(high, proj_ref[...]) + cx.proj_back(low, proj_ref[...])) * qa_ref[1]
        unit_a = qa_ref[0]
        dcls_ref[:, col_a : col_a + wa] = norm_grad(
            unit_a, qa_ref[3], norms_ref[0:1, :wa], dlifted
        )
        dm_ref[0] = dmoved
        dm_ref[1] = dquery.astype(F32)
        vecs += [
            col_sum(dlifted * unit_a) * share,
            col_sum(dquery_in * unit_q) * share,
            col_sum(dlifted) * share,
            col_sum(dquery_in) * share,
            col_sum(dmoved) * share,
            col_sum(rt_ref[2]) * share,
        ]
        col_a += wa
        col_b += wb
    dcls_ref[:, col_a:] = jnp.zeros((ROWS, dcls_ref.shape[1] - col_a), F32)
    vec_ref[...] = vec_block(vecs)


def cross_rows_kernel(
    cxs,
    ds_l_ref,
    p_l_ref,
    ab_l_ref,
    av_l_ref,
    ys_ref,
    fln_ref,
    ds_s_ref,
    p_s_ref,
    ab_s_ref,
    av_s_ref,
    yl_ref,
    fsn_ref,
    cross_s_ref,
    cross_l_ref,
    vec_ref,
):
    vecs = []
    for cx, cross_ref, ds_ref, p_ref, ab_ref, av_ref, y_ref, norms_ref in (
        (cxs[0], cross_s_ref, ds_l_ref, p_l_ref, ab_l_ref, av_l_ref, ys_ref, fln_ref),
        (cxs[1], cross_l_ref, ds_s_ref, p_s_ref, ab_s_ref, av_s_ref, yl_ref, fsn_ref),
    ):
        wa, wb = cx.wa, cx.wb
        dkey = nn(ds_ref[...], ab_ref[...]) * cx.scale + nn(p_ref[...], av_ref[...])
        unit_b, rstd_b = normalize(y_ref[...].astype(F32))
        cross_ref[...] = norm_grad(unit_b, rstd_b, norms_ref[0:1, wa : wa + wb], dkey)
        vecs += [col_sum(dkey * unit_b), col_sum(dkey)]
    vec_ref[...] = vec_block(vecs)


def cross_grads_one_kernel(
    cxs,
    at,
    share,
    index_ref,
    g0_ref,
    g1_ref,
    g2_ref,
    g3_ref,
    qb_l_ref,
    rt_l_ref,
    gk_l_ref,
    p_l_ref,
    key_s_ref,
    qb_s_ref,
    rt_s_ref,
    gk_s_ref,
    p_s_ref,
    key_l_ref,
    keep_ref,
    send_ref,
    pack_ref,
):
    dcls = g0_ref[...] + g1_ref[...] + g2_ref[...] + g3_ref[...]
    col_a = 0
    for cx, name, qb_ref, rt_ref, gk_ref, p_ref, key_ref in (
        (cxs[0], "l", qb_l_ref, rt_l_ref, gk_l_ref, p_l_ref, key_s_ref),
        (cxs[1], "s", qb_s_ref, rt_s_ref, gk_s_ref, p_s_ref, key_l_ref),
    ):
        wa, wb = cx.wa, cx.wb
        dback = dcls[:, col_a : col_a + wa].astype(BF16)
        query_in, fquery = qb_ref[2].astype(BF16), qb_ref[3].astype(BF16)
        fheads, act_r, dattn, dheads, dkself, dvself = (
            rt_ref[i].astype(BF16) for i in (0, 1, 2, 4, 5, 6)
        )
        back = tn(act_r, dback) if wa > wb else tn(dback, act_r)
        pack_mat(pack_ref, at["back" + name], *back.shape, back * share)
        pack_mat(pack_ref, at["out" + name], wb, wb, tn(fheads, dattn) * share)
        keys = (
            tn(gk_ref[...].astype(BF16), spread(cx, fquery)) * cx.scale
            + tn(query_in, dkself) * share
        )
        values = tn(tn(p_ref[...], key_ref[...]).astype(BF16), spread(cx, dheads))
        values = values + tn(query_in, dvself) * share
        pack_mat(pack_ref, at["keyval" + name], wb, 2 * wb, jnp.concatenate([keys, values], axis=1))
        col_a += wa
    if at["rows"] > at["end"]:
        pack_ref[at["end"] :, :] = jnp.zeros((at["rows"] - at["end"], 128), BF16)
    emit(pack_ref, (keep_ref, send_ref), index_ref[0])


def cross_grads_two_kernel(
    cxs,
    at,
    share,
    index_ref,
    g0_ref,
    g1_ref,
    g2_ref,
    g3_ref,
    vec0_ref,
    vec1_ref,
    vec2_ref,
    qa_l_ref,
    qb_l_ref,
    dm_l_ref,
    qa_s_ref,
    qb_s_ref,
    dm_s_ref,
    keep_ref,
    send_ref,
    pack_ref,
):
    dcls = g0_ref[...] + g1_ref[...] + g2_ref[...] + g3_ref[...]
    col_a = 0
    dbacks = []
    for cx, name, qa_ref, qb_ref, dm_ref in (
        (cxs[0], "l", qa_l_ref, qb_l_ref, dm_l_ref),
        (cxs[1], "s", qa_s_ref, qb_s_ref, dm_s_ref),
    ):
        wa, wb = cx.wa, cx.wb
        dbacks.append(col_sum(dcls[:, col_a : col_a + wa]) * share)
        act, query_in = qa_ref[2].astype(BF16), qb_ref[2].astype(BF16)
        dmoved = dm_ref[0].astype(BF16)
        proj = tn(dmoved, act) if wa > wb else tn(act, dmoved)
        pack_mat(pack_ref, at["proj" + name], *proj.shape, proj * share)
        query = tn(query_in, dm_ref[1].astype(BF16)) * share
        pack_mat(pack_ref, at["query" + name], wb, wb, query)
        col_a += wa
    for name, block in (
        ("vec0", vec0_ref[...]),
        ("vec1", vec1_ref[...]),
        ("vec2", vec2_ref[...]),
        ("vec3", vec_block(dbacks)),
    ):
        pack_ref[at[name] : at[name] + block.shape[0], :] = block.astype(BF16)
    if at["rows"] > at["end"]:
        pack_ref[at["end"] :, :] = jnp.zeros((at["rows"] - at["end"], 128), BF16)
    emit(pack_ref, (keep_ref, send_ref), index_ref[0])


def fold_kernel(counts, group, rows, index_ref, *refs):
    total = sum(counts)
    ins, refs = refs[:total], refs[total:]
    outs, sum_ref = refs[:-1], refs[-1]
    at = i = 0
    for count in counts:
        value = ins[i][...].astype(F32)
        for other in ins[i + 1 : i + count]:
            value = value + other[...].astype(F32)
        size = value.shape[0]
        sum_ref[at : at + size, :] = value.astype(BF16)
        at += size
        i += count
    if rows > at:
        sum_ref[at:, :] = jnp.zeros((rows - at, 128), BF16)
    emit(sum_ref, outs, index_at(index_ref, *group))


def join_kernel(group, index_ref, *refs):
    *parts, out_ref = refs
    index = index_at(index_ref, *group)
    for d, part in enumerate(parts):
        size = part.shape[0]
        at = pl.multiple_of((index ^ d) * size, 16)
        out_ref[pl.ds(at, size), :] = part[...]


def settle_kernel(brs, dxl_ref, dxs_ref, left_ref, right_ref, *outs):
    for br, dx_ref, out in zip(brs, (dxl_ref, dxs_ref), outs):
        rest = jnp.zeros((br.n - br.halo, br.w), F32)
        dx = dx_ref[...] + jnp.concatenate([get_halo(br, left_ref), rest], axis=0)
        dx = dx + jnp.concatenate([rest, get_halo(br, right_ref)], axis=0)
        out[...] = (dx.T if br.turned else dx).astype(BF16)


def halves_of(sizes, shared=None):
    pieces, at = [], 0
    for pack, size in enumerate(sizes):
        done, half = 0, size // 2
        while done < half:
            row, count = at + done, half - done
            if shared:
                mine, both, first = shared
                count = min(count, mine - row % mine)
                row = row // mine * both + first + row % mine
            pieces.append((pack, done, row, count))
            done += count
        at += half
    return pieces


def gather_packs(index, own_ref, got_ref, packs, pieces):
    for pack, row, at, size in pieces:
        half = packs[pack].shape[0] // 2
        for d, part in enumerate((own_ref, got_ref)):
            to = pl.multiple_of((index ^ d) * half + row, 16)
            packs[pack][pl.ds(to, size), :] = part[at : at + size, :]


def unpack_block(br, at, ref, out_ref, up_ref, down_ref):
    w, f, step = br.w, br.f, 256
    unpack_mat(ref, at["out"], w, w, out_ref)
    for j, c in enumerate(range(0, f, step)):
        rows, cols = j * mat_rows(w, step), slice(c, c + step)
        unpack_mat(ref, at["up"] + rows, w, step, near(up_ref).at[:, cols])
        if br.turned:
            unpack_mat(ref, at["down"] + rows, w, step, near(down_ref).at[:, cols])
            continue
        for k in range(step // 128):
            a = at["down"] + rows + k * w
            down_ref[c + k * 128 : c + (k + 1) * 128, :] = ref[a : a + w, :].astype(F32).T
    send(out_ref, up_ref, down_ref)


def unpack_early_kernel(br, cxs, at, at2, pieces, index_ref, own_ref, got_ref, *refs):
    outs, (ref2, ref) = refs[:-2], refs[-2:]
    gather_packs(index_ref[0], own_ref, got_ref, (ref2, ref), pieces)
    unpack_block(br, at, ref, *outs[:3])

    def vectors(name):
        widths = at2["widths"][name]
        return vecs_of(ref2[at2[name] : at2[name] + vec_rows(widths), :].astype(F32), widths)

    vec0, vec1, vec2, vec3 = (vectors("vec%d" % i) for i in range(4))
    for i, (cx, name) in enumerate(zip(cxs, "ls")):
        norms_ref, proj_ref, query_ref, bias_ref = outs[3 + 4 * i : 7 + 4 * i]
        wa, wb = cx.wa, cx.wb
        unpack_mat(ref2, at2["proj" + name], min(wa, wb), max(wa, wb), proj_ref)
        unpack_mat(ref2, at2["query" + name], wb, wb, query_ref)
        (gain_rev, shift_rev), (gain_key, shift_key) = (v[2 * i : 2 * i + 2] for v in (vec0, vec1))
        gain_a, gain_q, shift_a, shift_q, bias_a, bias_b = vec2[6 * i : 6 * i + 6]
        norms_ref[0:1, :] = jnp.concatenate([gain_a, gain_q + gain_key, gain_rev], axis=1)
        norms_ref[1:2, :] = jnp.concatenate([shift_a, shift_q + shift_key, shift_rev], axis=1)
        bias_ref[...] = jnp.concatenate([bias_a, bias_b, vec3[i]], axis=1).reshape(wa + 2 * wb)
        send(proj_ref, query_ref)


def unpack_late_kernel(br, cxs, brs, ats, at, at1, pieces, index_ref, own_ref, got_ref, *refs):
    outs, (ref, ref1, *packs) = refs[:-4], refs[-4:]
    gather_packs(index_ref[0], own_ref, got_ref, (ref, ref1, *packs), pieces)
    unpack_qkv(brs, ats, packs, outs[9:])
    unpack_block(br, at, ref, *outs[:3])
    for i, (cx, name) in enumerate(zip(cxs, "ls")):
        keyval_ref, out_ref, back_ref = outs[3 + 3 * i : 6 + 3 * i]
        wa, wb = cx.wa, cx.wb
        unpack_mat(ref1, at1["keyval" + name], wb, 2 * wb, keyval_ref)
        unpack_mat(ref1, at1["out" + name], wb, wb, out_ref)
        unpack_mat(ref1, at1["back" + name], min(wa, wb), max(wa, wb), back_ref)
        send(keyval_ref, out_ref, back_ref)


def unpack_qkv(brs, ats, packs, outs):
    for i, (br, at, ref) in enumerate(zip(brs, ats, packs)):
        qkv_ref, norms_ref, bias_ref, upbias_ref = outs[4 * i : 4 * i + 4]
        w, f = br.w, br.f
        unpack_mat(ref, at["qkv"], w, 3 * w, qkv_ref)
        send(qkv_ref)
        block = ref[at["vec1"] : at["vec1"] + vec_rows([w, w]), :].astype(F32)
        gain, shift = vecs_of(block, [w, w])
        norms_ref[0, 0:1, :] = gain
        norms_ref[0, 1:2, :] = shift
        block = ref[at["vec2"] : at["vec2"] + vec_rows([w] * 4 + [f]), :].astype(F32)
        gain, shift, bias0, bias1, upbias = vecs_of(block, [w] * 4 + [f])
        norms_ref[1, 0:1, :] = gain
        norms_ref[1, 1:2, :] = shift
        bias_ref[0:1, :] = bias0
        bias_ref[1:2, :] = bias1
        upbias_ref[...] = upbias.reshape(f)


def bits():
    head = [("head", 1 << i) for i in range(lax.axis_size("head").bit_length() - 1)]
    dp = [("dp", 1 << i) for i in range(lax.axis_size("dp").bit_length() - 1)]
    return head + dp


def bit_here(axis, bit):
    return (lax.axis_index(axis) // bit) % 2


def index_at(index_ref, first, count):
    index = 0
    for i in range(count):
        index = index * 2 + index_ref[first + i]
    return index


def swap(x, group, d):
    heads = lax.axis_size("head")
    flip = {"dp": 0, "head": 0}
    for k, (axis, bit) in enumerate(group[::-1]):
        if d >> k & 1:
            flip[axis] |= bit
    pairs = [
        (i * heads + j, (i ^ flip["dp"]) * heads + (j ^ flip["head"]))
        for i in range(lax.axis_size("dp"))
        for j in range(heads)
    ]
    return lax.ppermute(x, ("dp", "head"), pairs)


def others(x):
    count = lax.axis_size("head")
    return [
        lax.ppermute(x, "head", [(i, i ^ d) for i in range(count)]) for d in range(1, count)
    ]


class Sum:
    def __init__(self, index, order):
        self.index = index
        self.bits = order
        self.devices = 1 << len(self.bits)
        self.ins, self.counts, self.halves = [], [], []
        self.done = 1
        self.cost = 1

    def add(self, pack):
        keep, send = pack
        self.halves.append(keep.shape[0])
        self.ins += [keep, swap(send, self.bits[:1], 1)]
        self.counts.append(2)
        self.rows = round_up(sum(self.halves), self.devices // 2 * 16)

    def step(self, cost=1):
        self.cost = cost
        if self.plan:
            what, count = self.plan.pop(0)
            what(self, count)
            if what is Sum.meet:
                self.step(cost)

    def meet(self, other):
        while other.plan:
            other.step()
        self.shared = (other.rows, self.rows)
        self.ins = [*other.ins, *self.ins]
        self.counts = other.counts + self.counts
        self.rows += other.rows

    def fold(self, count):
        group = self.bits[self.done : self.done + count]
        cuts = 1 << count
        pieces = call(
            functools.partial(fold_kernel, self.counts, (self.done, count), self.rows),
            (sds((self.rows // cuts, 128), BF16),) * cuts,
            (self.index, *self.ins),
            [SMEM] + [VMEM] * len(self.ins),
            [pltpu.VMEM((self.rows, 128), BF16)],
            moved=self.cost,
            spare=2,
        )
        self.rows = self.rows // cuts
        self.counts = [cuts]
        self.done += count
        self.ins = [pieces[0]] + [swap(pieces[d], group, d) for d in range(1, cuts)]

    def turn(self, count):
        self.fold(0)
        self.spread(self.ins[0], count)

    def spread(self, whole, count):
        group = self.bits[self.done - count : self.done]
        self.ins = [whole] + [swap(whole, group, d) for d in range(1, 1 << count)]
        self.done -= count
        self.last = count

    def join(self, count):
        rows = self.ins[0].shape[0] * len(self.ins)
        whole = call(
            functools.partial(join_kernel, (self.done, self.last)),
            sds((rows, 128), BF16),
            (self.index, *self.ins),
            [SMEM] + [VMEM] * len(self.ins),
            moved=self.cost,
            spare=2,
        )
        self.spread(whole, count)


def from_sides(left, right):
    count = lax.axis_size("head")
    return (
        lax.ppermute(left, "head", [(i, i + 1) for i in range(count - 1)]),
        lax.ppermute(right, "head", [(i + 1, i) for i in range(count - 1)]),
    )


def block_forward(br, meta, sub, x, halo, qkv, norms, w_qkv, w_out, w_up, w_down, bias, upbias):
    n, w, f = br.n, br.w, br.f
    outs = (
        sds((n, w), BF16),
        sds((ROWS, w), F32),
        sds((br.r, w), BF16),
        sds((br.r, w), BF16),
        sds((br.t, 8, 128), F32),
        sds((n, w), BF16),
        sds((n, w), F32),
        sds((f // 256, n, 256), BF16),
        sds((f // 256, n, 256), BF16),
        sds((n, w), BF16),
    )
    ins = (meta, x, *halo, *qkv, norms, w_qkv, w_out, w_up, w_down, bias, upbias, sub)
    return call(
        functools.partial(forward_kernel, br),
        outs,
        ins,
        [SMEM] + [VMEM] * (len(ins) - 1),
        [pltpu.VMEM((br.t, w, 128), F32)],
        busy=10,
        far_out=(2, 3, 4, 9),
    )


def ffn_back(br, index, col, lane, dy, cross, dcls, kept, norms, w_out, w_up, w_down):
    n, w, f = br.n, br.w, br.f
    parts = [("up", mat_rows(w, f)), ("down", mat_rows(f, w)), ("out", mat_rows(w, w))]
    at, rows = layout(parts)
    at["rows"], at["end"], at["col"] = rows, sum(r for _, r in parts), col
    ins = (index, lane, dy, cross, dcls, *kept, norms, w_out, w_up, w_down)
    half = sds((rows // 2, 128), BF16)
    vec = sds((vec_rows([w] * 4 + [f]), 128), F32)
    keep, send, *outs = call(
        functools.partial(ffn_back_kernel, br, at),
        (half, half, sds((n, w), F32), sds((n, w), BF16), vec),
        ins,
        [SMEM] + [VMEM] * (len(ins) - 1),
        [pltpu.VMEM((rows, 128), BF16)],
        far=(2,) if br.turned else (),
        busy=7,
    )
    return at, (keep, send), outs


def attn_loop(br, meta, q, kwin, vwin, dheads, lse):
    size = 128 * max(len(g[2]) for g in br.groups)
    ins = (meta, q, kwin, vwin, dheads, lse)
    return call(
        functools.partial(attn_loop_kernel, br),
        (sds((br.r, br.w), F32),) * 2 + (sds((br.n, br.w), BF16),),
        ins,
        [SMEM] + [VMEM] * (len(ins) - 1),
        [
            pltpu.VMEM((br.t, br.w, 128), F32),
            pltpu.VMEM((br.kw, size), BF16),
            pltpu.VMEM((br.kw, size), BF16),
        ],
    )


def attn_post(br, index, grads, x, halo, norms, w_qkv, dmid, vec, before):
    n, w = br.n, br.w
    parts = [("qkv", mat_rows(w, 3 * w)), ("vec1", vec_rows([w, w])), ("vec2", vec.shape[0])]
    at, rows = layout(parts)
    at["rows"], at["end"] = rows, sum(r for _, r in parts)
    ins = (index, x, *halo, norms, w_qkv, dmid, vec, *grads, *before)
    half = sds((rows // 2, 128), BF16)
    keep, send, *outs = call(
        functools.partial(attn_post_kernel, br, at),
        (half, half, sds((n, w), F32), sds((br.end, 128), BF16), sds((br.end, 128), BF16)),
        ins,
        [SMEM] + [VMEM] * (len(ins) - 1),
        [
            pltpu.VMEM((br.r, w), BF16),
            pltpu.VMEM((rows, 128), BF16),
        ],
    )
    return at, (keep, send), outs


def on_device(
    seg_large,
    seg_small,
    x_large,
    x_small,
    dy_large,
    dy_small,
    lb_norms,
    lb_qkv,
    lb_out,
    lb_up,
    lb_down,
    lb_bias,
    lb_upbias,
    sb_norms,
    sb_qkv,
    sb_out,
    sb_up,
    sb_down,
    sb_bias,
    sb_upbias,
    fl_norms,
    fl_proj,
    fl_query,
    fl_keyval,
    fl_out,
    fl_back,
    fl_bias,
    fs_norms,
    fs_proj,
    fs_query,
    fs_keyval,
    fs_out,
    fs_back,
    fs_bias,
):
    xl, xs, dyl, dys = x_large[0], x_small[0], dy_large[0], dy_small[0]
    small = Branch(*xs.shape, sb_up.shape[1], MOST_S)
    large = Branch(*xl.shape, lb_up.shape[1], MOST_L, small.end)
    cxs = (Cross(large.w, small.w, small.n), Cross(small.w, large.w, large.n))
    share = 1.0 / lax.axis_size("head")
    wide = round_up(large.w + small.w, 128)
    sb_down, fl_proj, fs_back = sb_down.T, fl_proj.T, fs_back.T
    order = bits()
    index = [bit_here(axis, bit) for axis, bit in order]
    index += [jnp.zeros((), jnp.int32)] * (15 - len(order)) + [lax.axis_index("head")]
    index = jnp.stack(index).astype(jnp.int32)
    ORDER.clear()

    edge = sds((large.end, 128), BF16)
    halo = from_sides(
        *call(functools.partial(edge_kernel, (large, small)), (edge, edge), (xl, xs))
    )
    words = sds((16,), jnp.int32)
    lanes = sds((8, 128), jnp.int32)
    subs = sds((ROWS, 128), jnp.int32)
    start = call(
        functools.partial(start_kernel, large, small),
        (sds((large.n, large.w), BF16),) * 3
        + (sds((small.n, small.w), BF16),) * 3
        + (words, words, lanes, lanes, subs, subs, sds((ROWS, wide), F32)),
        (index, seg_large, seg_small, xl, xs, dyl, dys, lb_norms, sb_norms, lb_qkv, sb_qkv),
        [SMEM] + [VMEM] * 10,
        [
            pltpu.VMEM((2 * ROWS + 16, 128), jnp.int32),
            pltpu.SMEM((2 * ROWS + 16, 128), jnp.int32),
            pltpu.SemaphoreType.DMA,
        ],
        out_specs=(VMEM,) * 6 + (SMEM, SMEM) + (VMEM,) * 5,
        busy=4,
    )
    qkv_l, qkv_s = start[:3], start[3:6]
    meta_l, meta_s, lane_l, lane_s, sub_l, sub_s, dcls = start[6:]
    dcls_all = [dcls] + others(dcls)

    ys, cls_s, kwin_s, vwin_s, lse_s, ho_s, mid_s, hid_s, slope_s, ys_far = block_forward(
        small, meta_s, sub_s, xs, halo, qkv_s, sb_norms, sb_qkv, sb_out, sb_up, sb_down,
        sb_bias, sb_upbias,
    )
    yl, cls_l, kwin_l, vwin_l, lse_l, ho_l, mid_l, hid_l, slope_l, yl_far = block_forward(
        large, meta_l, sub_l, xl, halo, qkv_l, lb_norms, lb_qkv, lb_out, lb_up, lb_down,
        lb_bias, lb_upbias,
    )

    cls = jnp.concatenate(
        [cls_l, cls_s, jnp.zeros((ROWS, wide - large.w - small.w), F32)], axis=1
    )
    cls_all = [cls] + others(cls)
    key_s, key_l = call(
        functools.partial(keys_kernel, cxs),
        (sds((small.n, small.w), BF16), sds((large.n, large.w), BF16)),
        (ys, fl_norms, yl, fs_norms),
        busy=1,
    )
    wl, ws = large.w, small.w
    part, sc_l, sc_s, ab_l, ab_s, qa_l, qb_l, qa_s, qb_s = call(
        functools.partial(cross_front_kernel, cxs),
        (
            sds((ROWS + 8, wide), F32),
            sds((small.n, 128), F32),
            sds((large.n, 128), F32),
            sds((128, ws), BF16),
            sds((128, wl), BF16),
            sds((4, ROWS, wl), F32),
            sds((7, ROWS, ws), F32),
            sds((4, ROWS, ws), F32),
            sds((7, ROWS, wl), F32),
        ),
        (
            *cls_all, lane_s, lane_l, key_s, key_l,
            fl_norms, fl_proj, fl_query, fl_keyval, fl_bias,
            fs_norms, fs_proj, fs_query, fs_keyval, fs_bias,
        ),
        far_out=(3, 4),
        busy=4,
    )
    part_all = [part] + others(part)
    vec1 = [ws, ws, wl, wl]
    both = lambda shape: (sds(shape[:1] + (ws,), shape[1]), sds(shape[:1] + (wl,), shape[1]))
    (
        dquery, rt_l, rt_s, gk_l, gk_s, ds_l, ds_s, p_l, p_s, av_l, av_s, back_cls, block0,
    ) = call(
        functools.partial(cross_back_kernel, cxs, share),
        (
            sds((ROWS, wide), F32),
            sds((7, ROWS, ws), F32),
            sds((7, ROWS, wl), F32),
            *both((128, F32)),
            *(sds((small.n, 128), BF16), sds((large.n, 128), BF16)) * 2,
            *both((128, BF16)),
            sds((ROWS, wide), F32),
            sds((vec_rows(vec1), 128), F32),
        ),
        (
            *dcls_all, *part_all, lane_s, lane_l, key_s, key_l, sc_l, sc_s, qb_l, qb_s,
            fl_norms, fl_keyval, fl_out, fl_back, fl_bias,
            fs_norms, fs_keyval, fs_out, fs_back, fs_bias,
        ),
        far_out=(9, 10, 11),
        busy=6,
    )
    far = len(order) - 3
    sum_f, sum_g, sum_q = (Sum(index, order) for _ in range(3))
    fold, join = (Sum.fold, 1), (Sum.join, 1)
    rest = [fold] * far + [(Sum.turn, 1)] + [join] * (far - 1) + [(Sum.join, 2), join]
    sum_f.plan = [(Sum.fold, 2)] + rest
    sum_g.plan = [(Sum.fold, 2)]
    sum_q.plan = [(Sum.fold, 2), (Sum.meet, sum_g)] + rest

    def packed(kernel, items, unit, ins, more=(), far=()):
        at, rows = layout(items, unit)
        at["rows"], at["end"] = rows, sum(r for _, r in items)
        half = sds((rows // 2, 128), BF16)
        keep, send, *rest = call(
            functools.partial(kernel, cxs, at, share),
            (half, half, *more),
            ins,
            [SMEM] + [VMEM] * (len(ins) - 1),
            [pltpu.VMEM((rows, 128), BF16)],
            far=far,
        )
        return at, (keep, send), rest

    def query_backward(dquery_all):
        return call(
            functools.partial(cross_query_back_kernel, cxs, share),
            (
                sds((ROWS, wide), F32),
                sds((2, ROWS, ws), F32),
                sds((2, ROWS, wl), F32),
                sds((vec_rows(vec2), 128), F32),
            ),
            (
                *dquery_all, qa_l, qb_l, rt_l, fl_norms, fl_proj, fl_query, fl_keyval,
                qa_s, qb_s, rt_s, fs_norms, fs_proj, fs_query, fs_keyval,
            ),
            busy=2,
        )

    ORDER[:] = [block0]
    dquery_all = [dquery] + others(dquery)
    vec2 = [wl, ws, wl, ws, ws, ws, ws, wl, ws, wl, wl, wl]
    cross_s, cross_l, block1 = call(
        functools.partial(cross_rows_kernel, cxs),
        (sds((small.n, ws), F32), sds((large.n, wl), F32), sds((vec_rows(vec1), 128), F32)),
        (ds_l, p_l, ab_l, av_l, ys, fl_norms, ds_s, p_s, ab_s, av_s, yl, fs_norms),
        busy=2,
    )
    dcls_new, dm_l, dm_s, block2 = query_backward(dquery_all)
    widths = {"vec0": vec1, "vec1": vec1, "vec2": vec2, "vec3": [wl, ws]}
    items = []
    for cx, name in zip(cxs, "ls"):
        items += [("proj" + name, mat_rows(cx.wa, cx.wb)), ("query" + name, mat_rows(cx.wb, cx.wb))]
    items += [(name, vec_rows(of)) for name, of in widths.items()]
    at_c2, pack_c2, _ = packed(
        cross_grads_two_kernel,
        items,
        32,
        (index, *dcls_all, block0, block1, block2, qa_l, qb_l, dm_l, qa_s, qb_s, dm_s),
    )
    at_c2["widths"] = widths
    sum_f.add(pack_c2)
    at_fl, pack_fl, (dmid_l, dheads_l, vec_l) = ffn_back(
        large, index, 0, lane_l, dyl, cross_l, dcls_new,
        (hid_l, slope_l, mid_l, ho_l), lb_norms, lb_out, lb_up, lb_down,
    )
    sum_f.add(pack_fl)
    at_fs, pack_fs, (dmid_s, dheads_s, vec_s) = ffn_back(
        small, index, wl, lane_s, dys, cross_s, dcls_new,
        (hid_s, slope_s, mid_s, ho_s), sb_norms, sb_out, sb_up, sb_down,
    )
    sum_g.add(pack_fs)

    def cross_grads_one():
        items = []
        for cx, name in zip(cxs, "ls"):
            items += [
                ("keyval" + name, mat_rows(cx.wb, 2 * cx.wb)),
                ("out" + name, mat_rows(cx.wb, cx.wb)),
                ("back" + name, mat_rows(cx.wb, cx.wa)),
            ]
        at, pack, _ = packed(
            cross_grads_one_kernel,
            items,
            32,
            (
                index, *dcls_all, qb_l, rt_l, gk_l, p_l, key_s,
                qb_s, rt_s, gk_s, p_s, key_l,
            ),
        )
        sum_g.add(pack)
        return at

    def settled(dx_l, dx_s, first, last):
        return call(
            functools.partial(settle_kernel, (large, small)),
            (
                sds((large.n, wl), BF16),
                sds((ws, small.n) if small.turned else (small.n, ws), BF16),
            ),
            (dx_l, dx_s, *from_sides(last, first)),
        )

    def unpack(kernel, outs, done, rows, shared=None):
        while done.plan:
            done.step()
        pieces = halves_of(rows[0], shared and (done.shared[0], sum(done.shared), 0))
        if shared:
            first = len(rows[0])
            more = halves_of(rows[1], (done.shared[1], sum(done.shared), done.shared[0]))
            pieces += [(first + pack, *rest) for pack, *rest in more]
        return call(
            functools.partial(kernel, pieces),
            outs,
            (index, *done.ins),
            [SMEM, VMEM, VMEM],
            [pltpu.VMEM((r, 128), BF16) for part in rows for r in part],
            far_out=[i for i, out in enumerate(outs) if math.prod(out.shape) > 1 << 13],
        )

    def block_outs(br):
        return [
            sds((br.w, br.w), F32),
            sds((br.w, br.f), F32),
            sds((br.w, br.f) if br.turned else (br.f, br.w), F32),
        ]

    def unpack_early():
        outs = block_outs(large)
        for cx in cxs:
            wa, wb = cx.wa, cx.wb
            outs += [
                sds((2, wa + 2 * wb), F32),
                sds((min(wa, wb), max(wa, wb)), F32),
                sds((wb, wb), F32),
                sds((wa + 2 * wb,), F32),
            ]

        def kernel(pieces, *refs):
            unpack_early_kernel(large, cxs, at_fl, at_c2, pieces, *refs)

        return unpack(kernel, tuple(outs), sum_f, [(at_c2["rows"], at_fl["rows"])])

    def unpack_late():
        outs, found = block_outs(small), {"l": (large, made["at_l"]), "s": (small, made["at_s"])}
        for cx in cxs:
            less, more = min(cx.wa, cx.wb), max(cx.wa, cx.wb)
            outs += [sds((cx.wb, 2 * cx.wb), F32), sds((cx.wb, cx.wb), F32), sds((less, more), F32)]
        brs, ats = zip(*(found[name] for name in made["packs"]))
        for br in brs:
            outs += [
                sds((br.w, 3 * br.w), F32),
                sds((2, 2, br.w), F32),
                sds((2, br.w), F32),
                sds((br.f,), F32),
            ]

        def kernel(pieces, *refs):
            unpack_late_kernel(small, cxs, brs, ats, at_fs, made["at_c1"], pieces, *refs)

        rows = [(at_fs["rows"], made["at_c1"]["rows"]), tuple(at["rows"] for at in ats)]
        got = unpack(kernel, tuple(outs), sum_q, rows, True)
        return got[:9], {name: got[9 + 4 * i : 13 + 4 * i] for i, name in enumerate(made["packs"])}

    made = {"packs": ""}
    sums = {"f": sum_f, "g": sum_g, "q": sum_q}

    def do(what):
        if what == "loop_l":
            made["grads"] = attn_loop(large, meta_l, qkv_l[0], kwin_l, vwin_l, dheads_l, lse_l)
        elif what == "loop_s":
            made["grads"] = attn_loop(small, meta_s, qkv_s[0], kwin_s, vwin_s, dheads_s, lse_s)
        elif what == "post_l":
            made["at_l"], pack, made["dx_l"] = attn_post(
                large, index, made["grads"], xl, halo, lb_norms, lb_qkv, dmid_l, vec_l,
                made["dx_s"][1:],
            )
            sum_q.add(pack)
            made["packs"] += "l"
        elif what == "post_s":
            made["at_s"], pack, made["dx_s"] = attn_post(
                small, index, made["grads"], xs, halo, sb_norms, sb_qkv, dmid_s, vec_s, ()
            )
            sum_q.add(pack)
            made["packs"] += "s"
        elif what == "cross":
            made["at_c1"] = cross_grads_one()
        elif what == "place":
            made["out"] = call(
                functools.partial(place_kernel, (large, small)),
                (
                    sds((large.n, wl), BF16),
                    sds((ws, small.n) if small.turned else (small.n, ws), BF16),
                ),
                (back_cls, lane_l, lane_s, yl_far, ys_far),
                far=(0, 3, 4),
            )
        elif what == "dx":
            made["dx"] = settled(made["dx_l"][0], made["dx_s"][0], *made["dx_l"][1:])
        elif what == "out_f":
            made["f"] = unpack_early()
        elif what == "out_q":
            made["g"], made["q"] = unpack_late()
        else:
            sums[what.lower()].step(COSTLY if what.isupper() else 1)

    for what in SCHEDULE:
        do(what)
    o_l, u_l, d_l, *crossed = made["f"]
    o_s, u_s, d_s, *others_c = made["g"]
    q_l, norms_l, bias_l, upbias_l = made["q"]["l"]
    q_s, norms_s, bias_s, upbias_s = made["q"]["s"]
    grad_xl, grad_xs = made["dx"]
    out_l, out_s = made["out"]
    ORDER.clear()
    fl, fs = (
        [*crossed[4 * i : 4 * i + 3], *others_c[3 * i : 3 * i + 3], crossed[4 * i + 3]]
        for i in range(2)
    )
    fl[1], fs[5] = fl[1].T, fs[5].T
    if small.turned:
        out_s, grad_xs, d_s = out_s.T, grad_xs.T, d_s.T
    return (
        out_l[None],
        out_s[None],
        grad_xl[None],
        grad_xs[None],
        norms_l,
        q_l,
        o_l,
        u_l,
        d_l,
        bias_l,
        upbias_l,
        norms_s,
        q_s,
        o_s,
        u_s,
        d_s,
        bias_s,
        upbias_s,
        *fl,
        *fs,
    )


def solution(mesh):
    rows = P("dp", "head", None)
    return jax.shard_map(
        on_device,
        mesh=mesh,
        in_specs=(P("dp", None),) * 2 + (rows,) * 4 + (P(),) * 28,
        out_specs=(rows,) * 4 + (P(),) * 28,
        check_vma=False,
    )
```
